32 devices in a mesh: tm: 8 (over z, y), mp: 4 (over x, core).
Axes of the slice: x: 2, y: 2, z: 4, core: 2. Of those that a mesh axis runs over, the one named last changes fastest.
Arguments:
- frames_in: bfloat16 [4096, 1024], P('tm'), may hold values from -16 to 16
- queries: bfloat16 [4096, 1024], P('tm', 'mp'), may hold values from -6 to 6
- keys: bfloat16 [4096, 1024], P('tm', 'mp'), may hold values from -6 to 6
- values: bfloat16 [4096, 1024], P('tm', 'mp'), may hold values from -6 to 6
- segment_edges: int32 [2, 4096], P(None, 'tm'), may hold values from 0 to 4095, as said below
- out_proj: bfloat16 [1024, 1024], P('mp'), may hold values from -0.1875 to 0.1875
- expert_ids: int32 [4096, 2], P('tm'), may hold values from 0 to 15, all different within a row; in each aligned block of 512 rows (0 to 511, 512 to 1023, ...) at most 128 rows name the same one
- gates: float32 [4096, 2], P('tm'), may hold values from 0.25 to 1
- w_gate: bfloat16 [16, 1024, 4096], P('tm', None, 'mp'), may hold values from -0.1875 to 0.1875
- w_up: bfloat16 [16, 1024, 4096], P('tm', None, 'mp'), may hold values from -0.1875 to 0.1875
- w_down: bfloat16 [16, 4096, 1024], P('tm', 'mp'), may hold values from -0.09375 to 0.09375
Outputs:
- layer_out: bfloat16 [4096, 1024], P('tm', 'mp')
The draws below stay inside these ranges and needn't reach their ends.
Inputs may be any that keep to these rules, and one draw needn't show every extreme that they name: `segment_edges`: row 0 holds the first frame of each frame's segment and row 1 its last. Segments are runs of 1 to 64 frames; every multiple of 64 starts a segment, and some segment has exactly 64 frames. `expert_ids`: each frame names 2 different experts. Among the 512 frames of one index of tm no expert is named more than 128 times; in some of these groups one expert is named exactly 128 times.
All inputs are finite; a program needn't handle non-finite values.
Results may differ from the reference program's by a relative error of at most 0.006.
Values may be sent and summed in bfloat16 or wider, within the bound.
No kernel may reach another device: no remote copies, remote signals or barrier semaphores. Data moves between devices by JAX's collectives and lax.ppermute only.
A program may use at most 128 MiB of HBM per device.

```python
import math
import jax
import jax.numpy as jnp
import numpy as np
from jax import lax

D = 1024
HEADS = 16
HEAD = 64
FF = 4096
TOP = 2
SEGMENT = 64
LEFT = 256
F_DEV = 512
FRAMES = 4096
EXPERTS = 16
CAP = 128
N_TM = 8


def base_rows(key, salt):
    sub = jax.random.fold_in(key, salt)
    return jnp.clip(jax.random.normal(sub, (FRAMES, D), jnp.float32), -4.0, 4.0)


def draw_queries(key, part):
    rows = base_rows(key, 11)
    return rows.astype(jnp.bfloat16)


def draw_keys(key, part):
    rows = base_rows(key, 13)
    return rows.astype(jnp.bfloat16)


def draw_frames_in(key, part):
    low = jnp.log(0.2)
    high = jnp.log(2.0)
    row_scale = jnp.exp(jax.random.uniform(jax.random.fold_in(key, 1), (FRAMES, 1), jnp.float32, low, high))
    col_scale = jnp.exp(jax.random.uniform(jax.random.fold_in(key, 2), (1, D), jnp.float32, low, high))
    noise = jnp.clip(jax.random.normal(jax.random.fold_in(key, 3), (FRAMES, D), jnp.float32), -4.0, 4.0)
    return (noise * row_scale * col_scale).astype(jnp.bfloat16)


def draw_segment_edges(key, part):
    positions = jnp.arange(FRAMES, dtype=jnp.int32)
    extra = jax.random.randint(key, (FRAMES,), 0, 64) == 0
    cuts = jnp.where(positions < SEGMENT, positions == 0, (positions % SEGMENT == 0) | extra)
    first = lax.cummax(jnp.where(cuts, positions, 0), axis=0)
    starts = jnp.where(cuts, positions, FRAMES)
    following = jnp.concatenate([starts[1:], jnp.array([FRAMES], jnp.int32)])
    last = lax.cummin(following, axis=0, reverse=True) - 1
    return jnp.stack([first, last], 0).astype(jnp.int32)


def shard_levels(key, shape, shards, least, largest):
    factor_of = 1.0
    for position, parts in shards:
        heights = jax.random.uniform(jax.random.fold_in(jax.random.fold_in(key, 6), position), (parts,), jnp.float32, least / len(shards), largest / len(shards))
        factor_of = factor_of * jnp.repeat(jnp.exp(heights), shape[position] // parts).reshape((-1,) + (1,) * (len(shape) - 1 - position))
    return factor_of


def shared_out(key, own, number, rows, amount, top, bound, lean):
    sequence = jax.random.permutation(key, amount)
    packed, ordinary = shares(amount, rows * top, bound, lean, True), shares(amount, rows * top, bound, lean, False)
    places = jnp.arange(amount)

    def named(sizes, rotation):
        used = int((sizes > 0).sum())
        fixed = max(1, used // 4)
        moved = fixed + (places - fixed + rotation * (used - fixed)) % max(1, amount - fixed)
        return jnp.zeros((amount,), jnp.int32).at[sequence[jnp.where(places < fixed, places, moved)]].set(jnp.asarray(sizes, jnp.int32))

    sizes = jnp.where(number % 4 == 0, named(packed, number // 4), named(ordinary, number - number // 4 - 1))
    mixed = jax.random.permutation(jax.random.fold_in(own, 3), amount)
    giver, sink = mixed[0:amount // 2 * 2:2], mixed[1:amount // 2 * 2:2]
    margin = jnp.minimum(sizes[giver] - 1, bound - sizes[sink]) // 2
    margin = jnp.where((giver == sequence[0]) | (sink == sequence[0]) | (sizes[sink] == 0), 0, jnp.maximum(margin, 0))
    moved = jax.random.randint(jax.random.fold_in(own, 4), (amount // 2,), 0, 1 << 20) % (margin + 1)
    sizes = sizes.at[giver].add(-moved).at[sink].add(moved)
    labels = jnp.searchsorted(jnp.cumsum(sizes), jnp.arange(rows * top), side="right").astype(jnp.int32)
    listing = labels.reshape(top, rows).T
    listing = listing[jax.random.permutation(jax.random.fold_in(own, 1), rows)]
    rotation = jax.random.randint(jax.random.fold_in(own, 2), (rows, 1), 0, top)
    return jnp.take_along_axis(listing, (jnp.arange(top)[None, :] + rotation) % top, axis=1)


def shares(number_of, total, limit, skew, full):
    loads = [(1 << 20) // math.isqrt(standing ** skew) + 1 for standing in range(1, number_of + 1)]
    largest = limit if full else min(limit, max(-(-total // number_of), total * loads[0] // sum(loads)))
    least = 1 if total - largest >= number_of - 1 else 0
    given, surplus = [largest] + [least] * (number_of - 1), total - largest - least * (number_of - 1)
    while surplus > 0:
        candidates = [i for i in range(1, number_of) if given[i] < largest] or [i for i in range(1, number_of) if given[i] < limit]
        whole, remaining = sum([loads[i] for i in candidates]), surplus
        for i in candidates:
            addition = min(limit - given[i], max(1, remaining * loads[i] // whole), surplus)
            given[i] = given[i] + addition
            surplus = surplus - addition
    return np.array(given)


def gaussian(rng, shape, scale, most, shards=(), kind=jnp.bfloat16):
    values = jax.random.normal(rng, shape, jnp.float32) * scale
    if len(shards) > 0:
        values = shard_levels(rng, shape, shards, -0.22, 0.18) * values
    return jnp.clip(values, min=-most, max=most).astype(kind)


def setup_inputs(seed: int = 0) -> dict:
    key_list = jax.random.split(jax.random.key(seed), 12)
    frames_in = draw_frames_in(jax.random.fold_in(key_list[11], 71), 0)
    queries = draw_queries(jax.random.fold_in(key_list[11], 71), 0)
    keys = draw_keys(jax.random.fold_in(key_list[11], 71), 0)
    values = gaussian(key_list[3], (FRAMES, D), 1.0, 6.0, ((0, 8), (1, 4)))
    segment_edges = draw_segment_edges(jax.random.fold_in(key_list[11], 71), 0)
    out_proj = gaussian(key_list[5], (D, D), D ** -0.5, 0.1875, ((0, 4),))
    expert_ids_keys = jax.random.split(jax.random.fold_in(key_list[6], 1), FRAMES // F_DEV)
    expert_ids_turns = jax.random.permutation(jax.random.fold_in(key_list[6], 3), FRAMES // F_DEV)
    expert_ids = jax.vmap(lambda own, number: shared_out(jax.random.fold_in(key_list[6], 2), own, number, F_DEV, EXPERTS, TOP, CAP, 2))(expert_ids_keys, expert_ids_turns).reshape((FRAMES, TOP))
    gates = jnp.clip(0.25 + 0.75 * jax.random.uniform(key_list[7], (FRAMES, TOP), jnp.float32) ** shard_levels(key_list[7], (FRAMES, TOP), ((0, 8),), -0.2, 0.2), 0.25, 1.0)
    w_gate = gaussian(key_list[8], (EXPERTS, D, FF), D ** -0.5, 0.1875, ((0, 8), (2, 4)))
    w_up = gaussian(key_list[9], (EXPERTS, D, FF), D ** -0.5, 0.1875, ((0, 8), (2, 4)))
    w_down = gaussian(key_list[10], (EXPERTS, FF, D), FF ** -0.5, 0.09375, ((0, 8), (1, 4)))
    return {"frames_in": frames_in, "queries": queries, "keys": keys, "values": values, "segment_edges": segment_edges, "out_proj": out_proj, "expert_ids": expert_ids, "gates": gates, "w_gate": w_gate, "w_up": w_up, "w_down": w_down}


EPS = 1e-06

def attend(queries, keys, values, segment_edges):
    block = min(F_DEV, 512)
    head_width = HEAD
    scale = HEAD ** (-0.5)
    total = queries.shape[0]
    keys_padded = jnp.concatenate([jnp.zeros((LEFT, D), keys.dtype), keys], 0)
    values_padded = jnp.concatenate([jnp.zeros((LEFT, D), values.dtype), values], 0)

    def one_block(start):
        query_rows = lax.dynamic_slice_in_dim(queries, start, block, 0).astype(jnp.float32).reshape(block, HEADS, head_width)
        key_rows = lax.dynamic_slice_in_dim(keys_padded, start, LEFT + block, 0).astype(jnp.float32).reshape(LEFT + block, HEADS, head_width)
        value_rows = lax.dynamic_slice_in_dim(values_padded, start, LEFT + block, 0).astype(jnp.float32).reshape(LEFT + block, HEADS, head_width)
        first = lax.dynamic_slice_in_dim(segment_edges[0], start, block, 0)
        last = lax.dynamic_slice_in_dim(segment_edges[1], start, block, 0)
        places = start - LEFT + jnp.arange(LEFT + block, dtype=jnp.int32)
        lower = jnp.maximum(first - LEFT, 0)
        visible = (places[None, :] >= lower[:, None]) & (places[None, :] <= last[:, None])
        scores = jnp.einsum('qhd,khd->hqk', query_rows, key_rows) * scale
        scores = jnp.where(visible[None], scores, -jnp.inf)
        highest = lax.optimization_barrier(jnp.max(scores, -1, keepdims=True))
        expos = jnp.exp(scores - highest)
        weights = (expos / lax.optimization_barrier(jnp.sum(expos, -1, keepdims=True))).astype(jnp.bfloat16)
        mixed = jnp.einsum('hqk,khd->qhd', weights.astype(jnp.float32), value_rows)
        return mixed.reshape(block, D).astype(jnp.bfloat16)
    starts = jnp.arange(total // block, dtype=jnp.int32) * block
    return lax.map(one_block, starts).reshape(total, D)

def reference(frames_in, queries, keys, values, segment_edges, out_proj, expert_ids, gates, w_gate, w_up, w_down):
    context = attend(queries, keys, values, segment_edges)
    attended = jnp.dot(context, out_proj, preferred_element_type=jnp.float32)
    hidden_state = (frames_in.astype(jnp.float32) + attended).astype(jnp.bfloat16)
    hidden_state = lax.optimization_barrier(hidden_state)
    state = hidden_state.astype(jnp.float32)
    normed = (state * lax.rsqrt(lax.optimization_barrier(jnp.mean(state * state, -1, keepdims=True)) + EPS)).astype(jnp.bfloat16)
    grouped = expert_ids.reshape(N_TM, F_DEV * TOP)
    onehot = (grouped[:, :, None] == jnp.arange(EXPERTS, dtype=jnp.int32)[None, None, :]).astype(jnp.int32)
    ranks = jnp.cumsum(onehot, 1) - onehot
    slots = lax.optimization_barrier(jnp.sum(ranks * onehot, -1))
    sources = jnp.arange(N_TM, dtype=jnp.int32)[:, None]
    targets = ((grouped * N_TM + sources) * CAP + slots).reshape(-1).astype(jnp.int32)
    owners = jnp.arange(FRAMES * TOP, dtype=jnp.int32) // TOP
    table = jnp.full((EXPERTS * N_TM * CAP,), FRAMES, jnp.int32).at[targets].set(owners)
    padded = jnp.concatenate([normed, jnp.zeros((1, D), jnp.bfloat16)], 0)
    buffers = padded[table].reshape(EXPERTS, N_TM * CAP, D)

    def expert(operands):
        rows_in, gate_weight, up_weight, down_weight = operands
        gate_act = jnp.dot(rows_in, gate_weight, preferred_element_type=jnp.float32)
        up_act = jnp.dot(rows_in, up_weight, preferred_element_type=jnp.float32)
        activity = (jax.nn.silu(gate_act) * up_act).astype(jnp.bfloat16)
        return jnp.dot(activity, down_weight, preferred_element_type=jnp.float32)
    results = lax.map(expert, (buffers, w_gate, w_up, w_down))
    picked = results.reshape(-1, D)[targets].reshape(FRAMES, TOP, D)
    mixture = lax.optimization_barrier(jnp.sum(gates[:, :, None] * picked, 1))
    return (state + mixture).astype(jnp.bfloat16)
```

```python
import functools

import jax
import jax.numpy as jnp
from jax import lax
from jax.experimental import pallas as pl
from jax.experimental.pallas import tpu as pltpu
from jax.sharding import PartitionSpec as P

HEADS = 16
TOP = 2
LEFT = 256
EPS = 1e-06
LANES = 128
MIB = 1 << 20
F32 = jnp.float32
BF16 = jnp.bfloat16

VMEM = pl.BlockSpec(memory_space=pltpu.VMEM)
SMEM = pl.BlockSpec(memory_space=pltpu.SMEM)


def params(mib):
    return pltpu.CompilerParams(vmem_limit_bytes=mib * MIB)


def cost(flops, moved, transcendentals=0):
    return pl.CostEstimate(flops=flops, bytes_accessed=moved, transcendentals=transcendentals)


def from_behind(x, axis, by):
    size = lax.axis_size(axis)
    pairs = [(i, i + by) for i in range(size) if 0 <= i + by < size]
    return lax.ppermute(x, axis, pairs)


def core_swap(x):
    size = lax.axis_size("mp")
    return lax.ppermute(x, "mp", [(i, i ^ 1) for i in range(size)])


def from_chip(x, by):
    chips = lax.axis_size("mp") // 2
    pairs = [(c * 2 + k, ((c + by) % chips) * 2 + k) for c in range(chips) for k in range(2)]
    return lax.ppermute(x, "mp", pairs)


def gathered(x):
    chips = lax.axis_size("mp") // 2
    mine = [x] + [from_chip(x, by) for by in range(1, chips)]
    return mine + [core_swap(part) for part in mine]


def route_kernel(capacity, local_experts, n_time, ids_ref, ranks_ref, targets_ref):
    frames = ids_ref.shape[0]
    lanes = ranks_ref.shape[0]
    ids = ids_ref[...]
    experts = lax.broadcasted_iota(jnp.int32, (frames, lanes), 1)
    hits = [ids[:, k : k + 1] == experts for k in range(TOP)]
    named = functools.reduce(jnp.logical_or, hits)
    ones = jnp.where(named, 1.0, 0.0).astype(BF16)
    row = lax.broadcasted_iota(jnp.int32, (frames, frames), 0)
    column = lax.broadcasted_iota(jnp.int32, (frames, frames), 1)
    before = jnp.where(column < row, 1.0, 0.0).astype(BF16)
    ranks = jnp.dot(before, ones, preferred_element_type=F32)
    ranks_ref[...] = jnp.where(named, ranks, -1.0).T
    places = []
    for k in range(TOP):
        slot = jnp.sum(jnp.where(hits[k], ranks, 0.0), 1, keepdims=True).astype(jnp.int32)
        expert = ids[:, k : k + 1]
        owner = expert // local_experts
        local = expert - owner * local_experts
        places.append((local * n_time + owner) * capacity + slot)
    targets_ref[...] = jnp.concatenate(places, 1)


def attend_kernel(scale, head_width, start, *refs):
    if start == 0:
        meta_ref, edges_ref, q_ref, k_ref, v_ref, tails_ref, out_ref = refs
    else:
        meta_ref, edges_ref, q_ref, k_ref, v_ref, out_ref = refs
    rows, columns = out_ref.shape
    heads = columns // head_width
    block = LANES
    window = LEFT + block
    edges = edges_ref[...].astype(F32)
    edges = jnp.concatenate([edges, jnp.zeros((6, edges.shape[1]), F32)], 0).T
    lane_head = lax.broadcasted_iota(jnp.int32, (block, columns), 1) // head_width
    for r in range(0, rows, block):
        first = start + r
        if first >= LEFT:
            key = k_ref[first - LEFT : first + block, :]
            value = v_ref[first - LEFT : first + block, :]
        else:
            key = jnp.concatenate([tails_ref[0, first:LEFT, :], k_ref[0 : first + block, :]], 0)
            value = jnp.concatenate([tails_ref[1, first:LEFT, :], v_ref[0 : first + block, :]], 0)
        query = q_ref[first : first + block, :]
        places = meta_ref[0] + (first - LEFT) + lax.broadcasted_iota(jnp.int32, (block, window), 1)
        places = places.astype(F32)
        lower = jnp.maximum(edges[first : first + block, 0:1] - LEFT, 0.0)
        upper = edges[first : first + block, 1:2]
        visible = (places >= lower) & (places <= upper)
        mixed = jnp.zeros((block, columns), F32)
        for h in range(heads):
            own = jnp.where(lane_head == h, query, jnp.zeros_like(query))
            scores = lax.dot_general(own, key, (((1,), (1,)), ((), ())), preferred_element_type=F32)
            scores = jnp.where(visible, scores * scale, -1e30)
            highest = jnp.max(scores, 1, keepdims=True)
            expos = jnp.exp(scores - highest)
            weights = (expos / jnp.sum(expos, 1, keepdims=True)).astype(BF16)
            product = jnp.dot(weights, value, preferred_element_type=F32)
            mixed = jnp.where(lane_head == h, product, mixed)
        out_ref[r : r + block, :] = mixed.astype(BF16)


def scatter_rows(local, capacity, local_experts, ranks_ref, state, out_ref):
    frames = state.shape[0]
    n_time = out_ref.shape[0] // capacity
    slot = lax.broadcasted_iota(jnp.int32, (capacity, frames), 0).astype(F32)
    for owner in range(n_time):
        e = owner * local_experts + local
        pick = jnp.where(slot == ranks_ref[e : e + 1, :], 1.0, 0.0).astype(BF16)
        rows = jnp.dot(pick, state, preferred_element_type=F32)
        out_ref[owner * capacity : (owner + 1) * capacity, :] = rows.astype(BF16)


def state_kernel(pieces, capacity, local_experts, *refs):
    ctx = refs[:pieces]
    proj = refs[pieces : 2 * pieces]
    frames_ref, ranks_ref, state_ref, out_ref = refs[2 * pieces :]
    total = frames_ref[...].astype(F32)
    attended = jnp.dot(ctx[0][...], proj[0][...], preferred_element_type=F32)
    for part, weight in zip(ctx[1:], proj[1:]):
        attended = attended + jnp.dot(part[...], weight[...], preferred_element_type=F32)
    state = (total + attended).astype(BF16)
    state_ref[...] = state
    scatter_rows(0, capacity, local_experts, ranks_ref, state, out_ref)


def dispatch_kernel(local, capacity, local_experts, state_ref, ranks_ref, out_ref):
    scatter_rows(local, capacity, local_experts, ranks_ref, state_ref[...], out_ref)


def expert_kernel(pieces, order_ref, *refs):
    rows_in = refs[:pieces]
    gate_ref, up_ref, down_ref, send_ref, keep_ref, normed_ref = refs[pieces:]
    width = rows_in[0].shape[1]
    model = normed_ref.shape[1]
    parts = [part[...].astype(F32) for part in rows_in]
    squares = sum(jnp.sum(part * part, 1, keepdims=True) for part in parts)
    factor = lax.rsqrt(squares * (1.0 / model) + EPS)
    for i, part in enumerate(parts):
        at = pl.multiple_of(order_ref[i] * width, width)
        normed_ref[:, pl.ds(at, width)] = (part * factor).astype(BF16)
    normed = normed_ref[...]
    gate = jnp.dot(normed, gate_ref[...], preferred_element_type=F32)
    up = jnp.dot(normed, up_ref[...], preferred_element_type=F32)
    active = (gate / (1.0 + jnp.exp(-gate)) * up).astype(BF16)
    half = pieces // 2
    for i in range(pieces):
        at = pl.multiple_of(order_ref[i] * width, width)
        weight = down_ref[:, pl.ds(at, width)]
        result = jnp.dot(active, weight, preferred_element_type=F32)
        if i < half:
            keep_ref[:, i * width : (i + 1) * width] = result
        else:
            j = i - half
            send_ref[:, j * width : (j + 1) * width] = result.astype(BF16)


def combine_kernel(local, last, targets_ref, gates_ref, back_ref, base_ref, out_ref):
    rows = back_ref.shape[0]
    frames = targets_ref.shape[0]
    back = back_ref[...]
    places = lax.broadcasted_iota(jnp.int32, (frames, rows), 1) + local * rows
    total = base_ref[...].astype(F32)
    for k in range(TOP):
        pick = jnp.where(places == targets_ref[:, k : k + 1], 1.0, 0.0).astype(BF16)
        total = total + gates_ref[:, k : k + 1] * jnp.dot(pick, back, preferred_element_type=F32)
    out_ref[...] = total.astype(out_ref.dtype)


def per_device(
    frames_in,
    queries,
    keys,
    values,
    segment_edges,
    out_proj,
    expert_ids,
    gates,
    w_gate,
    w_up,
    w_down,
):
    frames, model = frames_in.shape
    width = queries.shape[1]
    n_model = lax.axis_size("mp")
    n_time = lax.axis_size("tm")
    chips = n_model // 2
    head_width = model // HEADS
    scale = head_width ** (-0.5)
    local_experts = w_gate.shape[0]
    hidden = w_gate.shape[2]
    experts_all = local_experts * n_time
    capacity = 4 * frames // experts_all
    rows = n_time * capacity
    lanes = -(-experts_all // LANES) * LANES
    at_time = lax.axis_index("tm")
    at_model = lax.axis_index("mp")
    chip, core = at_model // 2, at_model % 2
    mine = [((chip - by) % chips) * 2 + core for by in range(chips)]
    others = [((chip - by) % chips) * 2 + 1 - core for by in range(chips)]
    order = jnp.stack(mine + others).astype(jnp.int32)
    offset = (at_time * frames).astype(jnp.int32).reshape(1)

    tails = from_behind(jnp.stack([keys[frames - LEFT :], values[frames - LEFT :]], 0), "tm", 1)

    def column_block(x, index):
        return lax.dynamic_slice_in_dim(x, index * width, width, 1)

    proj = [column_block(out_proj, at_model)]
    for by in range(1, chips):
        proj.append(from_chip(column_block(out_proj, ((chip + by) % chips) * 2 + core), by))
    proj.append(core_swap(column_block(out_proj, chip * 2 + 1 - core)))
    for by in range(1, chips):
        to = column_block(out_proj, ((chip + by) % chips) * 2 + 1 - core)
        pairs = [
            (c * 2 + k, ((c + by) % chips) * 2 + 1 - k) for c in range(chips) for k in range(2)
        ]
        proj.append(lax.ppermute(to, "mp", pairs))

    ranks, targets = pl.pallas_call(
        functools.partial(route_kernel, capacity, local_experts, n_time),
        out_shape=(
            jax.ShapeDtypeStruct((lanes, frames), F32),
            jax.ShapeDtypeStruct((frames, TOP), jnp.int32),
        ),
        in_specs=[VMEM],
        out_specs=(VMEM, VMEM),
        compiler_params=params(16),
        cost_estimate=cost(2 * frames * frames * lanes, frames * 1024),
        name="route",
    )(expert_ids)

    def attend(start, end, *extra):
        count = end - start
        return pl.pallas_call(
            functools.partial(attend_kernel, scale, head_width, start),
            out_shape=jax.ShapeDtypeStruct((count, width), BF16),
            in_specs=[SMEM] + [VMEM] * (4 + len(extra)),
            out_specs=VMEM,
            compiler_params=params(16),
            cost_estimate=cost(count * 384 * width * 16, count * width * 8, count * 384 * 4),
            name=f"attend_{start}",
        )(offset, segment_edges, queries, keys, values, *extra)

    late = attend(LEFT, frames)
    early = attend(0, LEFT, tails)
    late_parts = gathered(late)
    early_parts = gathered(early)
    context = [jnp.concatenate([a, b], 0) for a, b in zip(early_parts, late_parts)]
    own_frames = column_block(frames_in, at_model)

    state, outgoing = pl.pallas_call(
        functools.partial(state_kernel, n_model, capacity, local_experts),
        out_shape=(
            jax.ShapeDtypeStruct((frames, width), BF16),
            jax.ShapeDtypeStruct((rows, width), BF16),
        ),
        in_specs=[VMEM] * (2 * n_model + 2),
        out_specs=(VMEM, VMEM),
        compiler_params=params(24),
        cost_estimate=cost(2 * frames * width * (model + rows), 4 * MIB),
        name="state",
    )(*context, *proj, own_frames, ranks)

    def dispatch(local):
        return pl.pallas_call(
            functools.partial(dispatch_kernel, local, capacity, local_experts),
            out_shape=jax.ShapeDtypeStruct((rows, width), BF16),
            in_specs=[VMEM, VMEM],
            out_specs=VMEM,
            compiler_params=params(16),
            cost_estimate=cost(2 * frames * width * rows, 2 * MIB),
            name=f"dispatch_{local}",
        )(state, ranks)

    def over_time(x):
        x = x.reshape(n_time, capacity, width)
        x = lax.all_to_all(x, "tm", split_axis=0, concat_axis=0, tiled=True)
        return x.reshape(rows, width)

    def experts(local, parts):
        tile = min(rows, 256)
        row_spec = pl.BlockSpec((tile, width), lambda i, _: (i, 0))
        wide_spec = pl.BlockSpec((tile, chips * width), lambda i, _: (i, 0))
        once = pl.Buffered(1)
        return pl.pallas_call(
            functools.partial(expert_kernel, n_model),
            grid_spec=pltpu.PrefetchScalarGridSpec(
                num_scalar_prefetch=1,
                grid=(rows // tile,),
                in_specs=[row_spec] * n_model
                + [
                    pl.BlockSpec(
                        (None, model, hidden), lambda i, _: (local, 0, 0), pipeline_mode=once
                    ),
                    pl.BlockSpec(
                        (None, model, hidden), lambda i, _: (local, 0, 0), pipeline_mode=once
                    ),
                    pl.BlockSpec(
                        (None, hidden, model), lambda i, _: (local, 0, 0), pipeline_mode=once
                    ),
                ],
                out_specs=(wide_spec, wide_spec),
                scratch_shapes=[pltpu.VMEM((tile, model), BF16)],
            ),
            out_shape=(
                jax.ShapeDtypeStruct((rows, chips * width), BF16),
                jax.ShapeDtypeStruct((rows, chips * width), F32),
            ),
            compiler_params=params(40),
            cost_estimate=cost(6 * rows * model * hidden, 12 * MIB, rows * hidden),
            name=f"experts_{local}",
        )(order, *parts, w_gate, w_up, w_down)

    def summed(send, keep):
        got = core_swap(send)
        both = [
            keep[:, i * width : (i + 1) * width]
            + got[:, i * width : (i + 1) * width].astype(F32)
            for i in range(chips)
        ]
        total = both[0]
        for by in range(1, chips):
            total = total + from_chip(both[by].astype(BF16), chips - by).astype(F32)
        return total.astype(BF16)

    def combine(local, back, base):
        last = local == local_experts - 1
        return pl.pallas_call(
            functools.partial(combine_kernel, local, last),
            out_shape=jax.ShapeDtypeStruct((frames, width), BF16 if last else F32),
            in_specs=[VMEM] * 4,
            out_specs=VMEM,
            compiler_params=params(24),
            cost_estimate=cost(4 * frames * width * rows, 3 * MIB),
            name=f"combine_{local}",
        )(targets, gates, back, base)

    arrived = []
    for local in range(local_experts):
        arrived.append(over_time(outgoing if local == 0 else dispatch(local)))
    result = state
    for local in range(local_experts):
        send, keep = experts(local, gathered(arrived[local]))
        result = combine(local, over_time(summed(send, keep)), result)
    return result


def solution(mesh):
    return jax.shard_map(
        per_device,
        mesh=mesh,
        in_specs=(
            P("tm", None),
            P("tm", "mp"),
            P("tm", "mp"),
            P("tm", "mp"),
            P(None, "tm"),
            P("mp", None),
            P("tm", None),
            P("tm", None),
            P("tm", None, "mp"),
            P("tm", None, "mp"),
            P("tm", "mp", None),
        ),
        out_specs=P("tm", "mp"),
        check_vma=False,
    )
```

```python
import functools

import jax
import jax.numpy as jnp
from jax import lax
from jax.experimental import pallas as pl
from jax.experimental.pallas import tpu as pltpu
from jax.sharding import PartitionSpec as P

HEADS = 16
TOP = 2
LEFT = 256
EPS = 1e-06
LANES = 128
MIB = 1 << 20
F32 = jnp.float32
BF16 = jnp.bfloat16

VMEM = pl.BlockSpec(memory_space=pltpu.VMEM)
SMEM = pl.BlockSpec(memory_space=pltpu.SMEM)
ANY = pl.BlockSpec(memory_space=pl.ANY)


def params(mib):
    return pltpu.CompilerParams(vmem_limit_bytes=mib * MIB)


def cost(flops, moved, transcendentals=0):
    return pl.CostEstimate(flops=flops, bytes_accessed=moved, transcendentals=transcendentals)


def from_behind(x, axis, by):
    size = lax.axis_size(axis)
    pairs = [(i, i + by) for i in range(size) if 0 <= i + by < size]
    return lax.ppermute(x, axis, pairs)


def core_swap(x):
    size = lax.axis_size("mp")
    return lax.ppermute(x, "mp", [(i, i ^ 1) for i in range(size)])


def from_chip(x, by):
    chips = lax.axis_size("mp") // 2
    pairs = [(c * 2 + k, ((c + by) % chips) * 2 + k) for c in range(chips) for k in range(2)]
    return lax.ppermute(x, "mp", pairs)


def gathered(x):
    chips = lax.axis_size("mp") // 2
    mine = [x] + [from_chip(x, by) for by in range(1, chips)]
    return mine + [core_swap(part) for part in mine]


def route_kernel(capacity, local_experts, n_time, ids_ref, ranks_ref, targets_ref):
    frames = ids_ref.shape[0]
    lanes = ranks_ref.shape[0]
    ids = ids_ref[...]
    experts = lax.broadcasted_iota(jnp.int32, (frames, lanes), 1)
    hits = [ids[:, k : k + 1] == experts for k in range(TOP)]
    named = functools.reduce(jnp.logical_or, hits)
    ones = jnp.where(named, 1.0, 0.0).astype(BF16)
    row = lax.broadcasted_iota(jnp.int32, (frames, frames), 0)
    column = lax.broadcasted_iota(jnp.int32, (frames, frames), 1)
    before = jnp.where(column < row, 1.0, 0.0).astype(BF16)
    ranks = jnp.dot(before, ones, preferred_element_type=F32)
    ranks_ref[...] = jnp.where(named, ranks, -1.0).T
    places = []
    for k in range(TOP):
        slot = jnp.sum(jnp.where(hits[k], ranks, 0.0), 1, keepdims=True).astype(jnp.int32)
        expert = ids[:, k : k + 1]
        owner = expert // local_experts
        local = expert - owner * local_experts
        places.append((local * n_time + owner) * capacity + slot)
    targets_ref[...] = jnp.concatenate(places, 1)


def attend_kernel(scale, head_width, start, meta_ref, *refs):
    if start == 0:
        edges_any, q_any, k_any, v_any, tails_any, out_ref = refs[:6]
        edges_ref, q_ref, k_ref, v_ref, sems = refs[6:]
    else:
        edges_any, q_any, k_any, v_any, out_ref = refs[:5]
        edges_ref, q_ref, k_ref, v_ref, sems = refs[5:]
    rows, columns = out_ref.shape
    heads = columns // head_width
    block = LANES
    window = LEFT + block
    if start == 0:
        moves = [
            (q_any.at[pl.ds(0, rows)], q_ref),
            (tails_any.at[0], k_ref.at[pl.ds(0, LEFT)]),
            (k_any.at[pl.ds(0, rows)], k_ref.at[pl.ds(LEFT, rows)]),
            (tails_any.at[1], v_ref.at[pl.ds(0, LEFT)]),
            (v_any.at[pl.ds(0, rows)], v_ref.at[pl.ds(LEFT, rows)]),
            (edges_any, edges_ref),
        ]
    else:
        moves = [
            (q_any.at[pl.ds(start, rows)], q_ref),
            (k_any.at[pl.ds(start - LEFT, rows + LEFT)], k_ref),
            (v_any.at[pl.ds(start - LEFT, rows + LEFT)], v_ref),
            (edges_any, edges_ref),
        ]
    copies = [pltpu.make_async_copy(a, b, sems.at[i]) for i, (a, b) in enumerate(moves)]
    for copy in copies:
        copy.start()
    for copy in copies:
        copy.wait()
    edges = edges_ref[:, start : start + rows].astype(F32)
    edges = jnp.concatenate([edges, jnp.zeros((6, rows), F32)], 0).T
    lane_head = lax.broadcasted_iota(jnp.int32, (block, columns), 1) // head_width
    for r in range(0, rows, block):
        key = k_ref[r : r + window, :]
        value = v_ref[r : r + window, :]
        query = q_ref[r : r + block, :]
        places = lax.broadcasted_iota(jnp.int32, (block, window), 1)
        places = (places + (meta_ref[0] + (start + r - LEFT))).astype(F32)
        lower = jnp.maximum(edges[r : r + block, 0:1] - LEFT, 0.0)
        upper = edges[r : r + block, 1:2]
        visible = (places >= lower) & (places <= upper)
        mixed = jnp.zeros((block, columns), F32)
        for h in range(heads):
            own = jnp.where(lane_head == h, query, jnp.zeros_like(query))
            scores = lax.dot_general(own, key, (((1,), (1,)), ((), ())), preferred_element_type=F32)
            scores = jnp.where(visible, scores * scale, -1e30)
            highest = jnp.max(scores, 1, keepdims=True)
            expos = jnp.exp(scores - highest)
            weights = (expos * (1.0 / jnp.sum(expos, 1, keepdims=True))).astype(BF16)
            product = jnp.dot(weights, value, preferred_element_type=F32)
            mixed = jnp.where(lane_head == h, product, mixed)
        out_ref[r : r + block, :] = mixed.astype(BF16)


def scatter_rows(local, capacity, local_experts, ranks_ref, state, out_ref):
    frames = state.shape[0]
    n_time = out_ref.shape[0] // capacity
    slot = lax.broadcasted_iota(jnp.int32, (capacity, frames), 0).astype(F32)
    for owner in range(n_time):
        e = owner * local_experts + local
        pick = jnp.where(slot == ranks_ref[e : e + 1, :], 1.0, 0.0).astype(BF16)
        rows = jnp.dot(pick, state, preferred_element_type=F32)
        out_ref[owner * capacity : (owner + 1) * capacity, :] = rows.astype(BF16)


def state_kernel(pieces, capacity, local_experts, *refs):
    ctx = refs[:pieces]
    proj = refs[pieces : 2 * pieces]
    frames_ref, ranks_ref, state_ref, out_ref = refs[2 * pieces :]
    total = frames_ref[...].astype(F32)
    attended = jnp.dot(ctx[0][...], proj[0][...], preferred_element_type=F32)
    for part, weight in zip(ctx[1:], proj[1:]):
        attended = attended + jnp.dot(part[...], weight[...], preferred_element_type=F32)
    state = (total + attended).astype(BF16)
    state_ref[...] = state
    scatter_rows(0, capacity, local_experts, ranks_ref, state, out_ref)


def dispatch_kernel(local, capacity, local_experts, state_ref, ranks_ref, out_ref):
    scatter_rows(local, capacity, local_experts, ranks_ref, state_ref[...], out_ref)


def expert_kernel(local, arrays, width, order_ref, *refs):
    rows_any = refs[:arrays]
    gate_any, up_any, down_any, after_any = refs[arrays : arrays + 4]
    send_x_any, send_any, keep_x_any, keep_any = refs[arrays + 4 : arrays + 8]
    scratch = refs[arrays + 8 :]
    rows_in = scratch[:arrays]
    gate_ref, up_ref, down_ref, normed_ref, active_ref = scratch[arrays : arrays + 5]
    send_x_ref, send_ref, keep_x_ref, keep_ref, sems = scratch[arrays + 5 :]
    rows, model = normed_ref.shape
    hidden = active_ref.shape[1]
    moves = list(zip(rows_any, rows_in)) + [
        (gate_any.at[local], gate_ref),
        (up_any.at[local], up_ref),
        (down_any.at[local], down_ref),
    ]
    copies = [pltpu.make_async_copy(a, b, sems.at[i]) for i, (a, b) in enumerate(moves)]
    for copy in copies:
        copy.start()
    for copy in copies[:arrays]:
        copy.wait()

    blocks = []
    for ref in rows_in:
        blocks += [(ref, c) for c in range(0, ref.shape[1], width)]
    step = min(rows, 256)

    def norm(i, carry):
        at_row = pl.multiple_of(i * step, step)
        parts = [ref[pl.ds(at_row, step), c : c + width].astype(F32) for ref, c in blocks]
        squares = sum(jnp.sum(part * part, 1, keepdims=True) for part in parts)
        factor = lax.rsqrt(squares * (1.0 / model) + EPS)
        for j, part in enumerate(parts):
            at = pl.multiple_of(order_ref[j] * width, width)
            normed_ref[pl.ds(at_row, step), pl.ds(at, width)] = (part * factor).astype(BF16)
        return carry

    lax.fori_loop(0, rows // step, norm, 0)
    copies[arrays].wait()
    copies[arrays + 1].wait()
    tile = min(rows, 512)
    chunk = min(hidden, 256)
    for r in range(0, rows, tile):
        normed = normed_ref[r : r + tile, :]
        for c in range(0, hidden, chunk):
            gate = jnp.dot(normed, gate_ref[:, c : c + chunk], preferred_element_type=F32)
            up = jnp.dot(normed, up_ref[:, c : c + chunk], preferred_element_type=F32)
            half = 0.5 * gate
            active = (half + half * jnp.tanh(half)) * up
            active_ref[r : r + tile, c : c + chunk] = active.astype(BF16)
    copies[arrays + 2].wait()
    count = len(blocks) // 2
    outs = [
        (send_x_ref, send_x_any),
        (send_ref, send_any),
        (keep_x_ref, keep_x_any),
        (keep_ref, keep_any),
    ]
    writes = [
        pltpu.make_async_copy(a, b, sems.at[arrays + 3 + i]) for i, (a, b) in enumerate(outs)
    ]

    def project(i, out_ref, column):
        at = pl.multiple_of(order_ref[i] * width, width)
        weight = down_ref[:, pl.ds(at, width)]
        for r in range(0, rows, tile):
            result = jnp.dot(active_ref[r : r + tile, :], weight, preferred_element_type=F32)
            out_ref[r : r + tile, column : column + width] = result.astype(out_ref.dtype)

    for by in range(1, count):
        project(count + by, send_x_ref, (by - 1) * width)
    writes[0].start()
    project(count, send_ref, 0)
    writes[1].start()
    for by in range(1, count):
        project(by, keep_x_ref, (by - 1) * width)
    writes[2].start()
    project(0, keep_ref, 0)
    writes[3].start()
    for write in writes:
        write.wait()


def add_kernel(width, keep_ref, got_ref, after_any, *out_refs):
    for i, out_ref in enumerate(out_refs):
        at = slice(i * width, (i + 1) * width)
        out_ref[...] = (keep_ref[:, at] + got_ref[:, at].astype(F32)).astype(BF16)


def total_kernel(keep_ref, *refs):
    total = keep_ref[...]
    for ref in refs[:-1]:
        total = total + ref[...].astype(F32)
    refs[-1][...] = total.astype(BF16)


def combine_kernel(local, last, targets_ref, gates_ref, back_ref, base_ref, out_ref):
    rows = back_ref.shape[0]
    frames = targets_ref.shape[0]
    back = back_ref[...]
    places = lax.broadcasted_iota(jnp.int32, (frames, rows), 1) + local * rows
    total = base_ref[...].astype(F32)
    for k in range(TOP):
        pick = jnp.where(places == targets_ref[:, k : k + 1], 1.0, 0.0).astype(BF16)
        total = total + gates_ref[:, k : k + 1] * jnp.dot(pick, back, preferred_element_type=F32)
    out_ref[...] = total.astype(out_ref.dtype)


def per_device(
    frames_in,
    queries,
    keys,
    values,
    segment_edges,
    out_proj,
    expert_ids,
    gates,
    w_gate,
    w_up,
    w_down,
):
    frames, model = frames_in.shape
    width = queries.shape[1]
    n_model = lax.axis_size("mp")
    n_time = lax.axis_size("tm")
    chips = n_model // 2
    head_width = model // HEADS
    scale = head_width ** (-0.5)
    local_experts = w_gate.shape[0]
    hidden = w_gate.shape[2]
    experts_all = local_experts * n_time
    capacity = 4 * frames // experts_all
    rows = n_time * capacity
    lanes = -(-experts_all // LANES) * LANES
    at_time = lax.axis_index("tm")
    at_model = lax.axis_index("mp")
    chip, core = at_model // 2, at_model % 2
    mine = [((chip - by) % chips) * 2 + core for by in range(chips)]
    others = [((chip - by) % chips) * 2 + 1 - core for by in range(chips)]
    order = jnp.stack(mine + others).astype(jnp.int32)
    offset = (at_time * frames).astype(jnp.int32).reshape(1)

    tails = from_behind(jnp.stack([keys[frames - LEFT :], values[frames - LEFT :]], 0), "tm", 1)

    def column_block(x, index):
        return lax.dynamic_slice_in_dim(x, index * width, width, 1)

    proj = [column_block(out_proj, at_model)]
    for by in range(1, chips):
        proj.append(from_chip(column_block(out_proj, ((chip + by) % chips) * 2 + core), by))
    proj.append(core_swap(column_block(out_proj, chip * 2 + 1 - core)))
    for by in range(1, chips):
        to = column_block(out_proj, ((chip + by) % chips) * 2 + 1 - core)
        pairs = [
            (c * 2 + k, ((c + by) % chips) * 2 + 1 - k) for c in range(chips) for k in range(2)
        ]
        proj.append(lax.ppermute(to, "mp", pairs))

    ranks, targets = pl.pallas_call(
        functools.partial(route_kernel, capacity, local_experts, n_time),
        out_shape=(
            jax.ShapeDtypeStruct((lanes, frames), F32),
            jax.ShapeDtypeStruct((frames, TOP), jnp.int32),
        ),
        in_specs=[VMEM],
        out_specs=(VMEM, VMEM),
        compiler_params=params(16),
        cost_estimate=cost(2 * frames * frames * lanes, frames * 1024),
        name="route",
    )(expert_ids)

    def attend(start, end, *extra):
        count = end - start
        return pl.pallas_call(
            functools.partial(attend_kernel, scale, head_width, start),
            out_shape=jax.ShapeDtypeStruct((count, width), BF16),
            in_specs=[SMEM] + [ANY] * (4 + len(extra)),
            out_specs=VMEM,
            scratch_shapes=[
                pltpu.VMEM((2, frames), jnp.int32),
                pltpu.VMEM((count, width), BF16),
                pltpu.VMEM((LEFT + count, width), BF16),
                pltpu.VMEM((LEFT + count, width), BF16),
                pltpu.SemaphoreType.DMA((6,)),
            ],
            compiler_params=params(60),
            cost_estimate=cost(count * 384 * width * 16, count * width * 8, count * 384 * 4),
            name=f"attend_{start}",
        )(offset, segment_edges, queries, keys, values, *extra)

    late = attend(LEFT, frames)
    tails, *proj = lax.optimization_barrier((tails, *proj))
    early = attend(0, LEFT, tails)
    late_parts = gathered(late)
    early_parts = gathered(early)
    context = [jnp.concatenate([a, b], 0) for a, b in zip(early_parts, late_parts)]
    own_frames = column_block(frames_in, at_model)

    state, outgoing = pl.pallas_call(
        functools.partial(state_kernel, n_model, capacity, local_experts),
        out_shape=(
            jax.ShapeDtypeStruct((frames, width), BF16),
            jax.ShapeDtypeStruct((rows, width), BF16),
        ),
        in_specs=[VMEM] * (2 * n_model + 2),
        out_specs=(VMEM, VMEM),
        compiler_params=params(24),
        cost_estimate=cost(2 * frames * width * (model + rows), 4 * MIB),
        name="state",
    )(*context, *proj, own_frames, ranks)

    def dispatch(local, wide):
        columns = wide.shape[1]
        return pl.pallas_call(
            functools.partial(dispatch_kernel, local, capacity, local_experts),
            out_shape=jax.ShapeDtypeStruct((rows, columns), BF16),
            in_specs=[VMEM, VMEM],
            out_specs=VMEM,
            compiler_params=params(16),
            cost_estimate=cost(2 * frames * columns * rows, 3 * MIB),
            name=f"dispatch_{local}",
        )(wide, ranks)

    def over_time(x):
        columns = x.shape[1]
        x = x.reshape(n_time, capacity, columns)
        x = lax.all_to_all(x, "tm", split_axis=0, concat_axis=0, tiled=True)
        return x.reshape(rows, columns)

    def experts(local, parts, after):
        away = (chips - 1) * width
        outs = [
            jax.ShapeDtypeStruct((rows, away), BF16),
            jax.ShapeDtypeStruct((rows, width), BF16),
            jax.ShapeDtypeStruct((rows, away), F32),
            jax.ShapeDtypeStruct((rows, width), F32),
        ]
        return pl.pallas_call(
            functools.partial(expert_kernel, local, len(parts), width),
            in_specs=[SMEM] + [ANY] * (len(parts) + 4),
            out_specs=(ANY,) * 4,
            scratch_shapes=[pltpu.VMEM(part.shape, BF16) for part in parts]
            + [
                pltpu.VMEM((model, hidden), BF16),
                pltpu.VMEM((model, hidden), BF16),
                pltpu.VMEM((hidden, model), BF16),
                pltpu.VMEM((rows, model), BF16),
                pltpu.VMEM((rows, hidden), BF16),
            ]
            + [pltpu.VMEM(out.shape, out.dtype) for out in outs]
            + [pltpu.SemaphoreType.DMA((len(parts) + 7,))],
            out_shape=tuple(outs),
            compiler_params=params(60),
            cost_estimate=cost(6 * rows * model * hidden, 12 * MIB, rows * hidden),
            name=f"experts_{local}",
        )(order, *parts, w_gate, w_up, w_down, after)

    tile = min(rows, 256)

    def tiles(columns):
        return pl.BlockSpec((tile, columns), lambda i: (i, 0))

    def add(local, keep, got, after):
        return pl.pallas_call(
            functools.partial(add_kernel, width),
            grid=(rows // tile,),
            in_specs=[tiles(keep.shape[1]), tiles(keep.shape[1]), ANY],
            out_specs=(tiles(width),) * (chips - 1),
            out_shape=(jax.ShapeDtypeStruct((rows, width), BF16),) * (chips - 1),
            cost_estimate=cost(keep.size, keep.size * 8),
            name=f"add_{local}",
        )(keep, got, after)

    def total(local, keep, parts):
        return pl.pallas_call(
            total_kernel,
            grid=(rows // tile,),
            in_specs=[tiles(width)] * (1 + len(parts)),
            out_specs=tiles(width),
            out_shape=jax.ShapeDtypeStruct((rows, width), BF16),
            cost_estimate=cost(keep.size, keep.size * 10),
            name=f"total_{local}",
        )(keep, *parts)

    def from_chips(parts):
        return [from_chip(part, chips - by) for by, part in enumerate(parts, 1)]

    def combine(local, back, base):
        last = local == local_experts - 1
        return pl.pallas_call(
            functools.partial(combine_kernel, local, last),
            out_shape=jax.ShapeDtypeStruct((frames, width), BF16 if last else F32),
            in_specs=[VMEM] * 4,
            out_specs=VMEM,
            compiler_params=params(24),
            cost_estimate=cost(4 * frames * width * rows, 3 * MIB),
            name=f"combine_{local}",
        )(targets, gates, back, base)

    arrived_0 = over_time(outgoing)
    wide = jnp.concatenate([state] + [from_chip(state, by) for by in range(1, chips)], 1)
    outgoing_1 = dispatch(1, wide)
    arrived_1 = over_time(outgoing_1)
    send_x_0, send_0, keep_x_0, keep_0 = experts(0, gathered(arrived_0), outgoing_1)
    away_0 = add(0, keep_x_0, core_swap(send_x_0), send_0)
    got_0 = from_chips(away_0)
    send_x_1, send_1, keep_x_1, keep_1 = experts(1, [arrived_1, core_swap(arrived_1)], away_0[0])
    total_0 = total(0, keep_0, [core_swap(send_0), *got_0])
    back_0 = over_time(total_0)
    got_1 = from_chips(add(1, keep_x_1, core_swap(send_x_1), total_0))
    back_1 = over_time(total(1, keep_1, [core_swap(send_1), *got_1]))
    return combine(1, back_1, combine(0, back_0, state))


def solution(mesh):
    return jax.shard_map(
        per_device,
        mesh=mesh,
        in_specs=(
            P("tm", None),
            P("tm", "mp"),
            P("tm", "mp"),
            P("tm", "mp"),
            P(None, "tm"),
            P("mp", None),
            P("tm", None),
            P("tm", None),
            P("tm", None, "mp"),
            P("tm", None, "mp"),
            P("tm", "mp", None),
        ),
        out_specs=P("tm", "mp"),
        check_vma=False,
    )
```

```python
import functools

import jax
import jax.numpy as jnp
from jax import lax
from jax.experimental import pallas as pl
from jax.experimental.pallas import tpu as pltpu
from jax.sharding import PartitionSpec as P

HEADS = 16
TOP = 2
LEFT = 256
EPS = 1e-06
LANES = 128
MIB = 1 << 20
F32 = jnp.float32
BF16 = jnp.bfloat16

VMEM = pl.BlockSpec(memory_space=pltpu.VMEM)
SMEM = pl.BlockSpec(memory_space=pltpu.SMEM)
ANY = pl.BlockSpec(memory_space=pl.ANY)
HBM = pl.BlockSpec(memory_space=pltpu.HBM)


def params(mib):
    return pltpu.CompilerParams(vmem_limit_bytes=mib * MIB)


def cost(flops, moved, transcendentals=0):
    return pl.CostEstimate(flops=flops, bytes_accessed=moved, transcendentals=transcendentals)


def from_behind(x, axis, by):
    size = lax.axis_size(axis)
    pairs = [(i, i + by) for i in range(size) if 0 <= i + by < size]
    return lax.ppermute(x, axis, pairs)


def core_swap(x):
    size = lax.axis_size("mp")
    return lax.ppermute(x, "mp", [(i, i ^ 1) for i in range(size)])


def from_chip(x, by):
    chips = lax.axis_size("mp") // 2
    pairs = [(c * 2 + k, ((c + by) % chips) * 2 + k) for c in range(chips) for k in range(2)]
    return lax.ppermute(x, "mp", pairs)


def gathered(x):
    chips = lax.axis_size("mp") // 2
    mine = [x] + [from_chip(x, by) for by in range(1, chips)]
    return mine + [core_swap(part) for part in mine]


def exchanged(blocks, sign):
    size = lax.axis_size("tm")
    moved = [
        lax.ppermute(block, "tm", [(i, (i + sign * s) % size) for i in range(size)])
        for s, block in enumerate(blocks)
        if s > 0
    ]
    return [blocks[0]] + moved


def route_kernel(capacity, local_experts, n_time, meta_ref, ids_ref, ranks_ref, targets_ref):
    frames = ids_ref.shape[0]
    lanes = ranks_ref.shape[0]
    ids = ids_ref[...]
    owner = ids // local_experts
    away = owner - meta_ref[1]
    away = jnp.where(away < 0, away + n_time, away)
    ids = (ids - owner * local_experts) * n_time + away
    experts = lax.broadcasted_iota(jnp.int32, (frames, lanes), 1)
    hits = [ids[:, k : k + 1] == experts for k in range(TOP)]
    named = functools.reduce(jnp.logical_or, hits)
    ones = jnp.where(named, 1.0, 0.0).astype(BF16)
    row = lax.broadcasted_iota(jnp.int32, (frames, frames), 0)
    column = lax.broadcasted_iota(jnp.int32, (frames, frames), 1)
    before = jnp.where(column < row, 1.0, 0.0).astype(BF16)
    ranks = jnp.dot(before, ones, preferred_element_type=F32)
    ranks_ref[...] = jnp.where(named, ranks, -1.0).T
    places = []
    for k in range(TOP):
        slot = jnp.sum(jnp.where(hits[k], ranks, 0.0), 1, keepdims=True).astype(jnp.int32)
        places.append(ids[:, k : k + 1] * capacity + slot)
    targets_ref[...] = jnp.concatenate(places, 1)


def attend_kernel(scale, head_width, start, meta_ref, *refs):
    if start == 0:
        edges_any, q_any, k_any, v_any, tails_any, out_ref = refs[:6]
        edges_ref, q_ref, k_ref, v_ref, sems = refs[6:]
    else:
        edges_any, q_any, k_any, v_any, out_ref = refs[:5]
        edges_ref, q_ref, k_ref, v_ref, sems = refs[5:]
    rows, columns = out_ref.shape
    heads = columns // head_width
    block = LANES
    window = LEFT + block
    if start == 0:
        moves = [
            (q_any.at[pl.ds(0, rows)], q_ref),
            (tails_any.at[0], k_ref.at[pl.ds(0, LEFT)]),
            (k_any.at[pl.ds(0, rows)], k_ref.at[pl.ds(LEFT, rows)]),
            (tails_any.at[1], v_ref.at[pl.ds(0, LEFT)]),
            (v_any.at[pl.ds(0, rows)], v_ref.at[pl.ds(LEFT, rows)]),
            (edges_any, edges_ref),
        ]
    else:
        moves = [
            (q_any.at[pl.ds(start, rows)], q_ref),
            (k_any.at[pl.ds(start - LEFT, rows + LEFT)], k_ref),
            (v_any.at[pl.ds(start - LEFT, rows + LEFT)], v_ref),
            (edges_any, edges_ref),
        ]
    copies = [pltpu.make_async_copy(a, b, sems.at[i]) for i, (a, b) in enumerate(moves)]
    for copy in copies:
        copy.start()
    for copy in copies:
        copy.wait()
    edges = edges_ref[:, start : start + rows].astype(F32)
    edges = jnp.concatenate([edges, jnp.zeros((6, rows), F32)], 0).T
    lane_head = lax.broadcasted_iota(jnp.int32, (block, columns), 1) // head_width
    for r in range(0, rows, block):
        key = k_ref[r : r + window, :]
        value = v_ref[r : r + window, :]
        query = q_ref[r : r + block, :]
        places = lax.broadcasted_iota(jnp.int32, (block, window), 1)
        places = (places + (meta_ref[0] + (start + r - LEFT))).astype(F32)
        lower = jnp.maximum(edges[r : r + block, 0:1] - LEFT, 0.0)
        upper = edges[r : r + block, 1:2]
        visible = (places >= lower) & (places <= upper)
        own = [jnp.where(lane_head == h, query, jnp.zeros_like(query)) for h in range(heads)]
        own = jnp.concatenate(own, 0)
        scores = lax.dot_general(own, key, (((1,), (1,)), ((), ())), preferred_element_type=F32)
        scores = (scores * scale).reshape(heads, block, window)
        scores = jnp.where(visible[None], scores, -1e30)
        highest = jnp.max(scores, 2, keepdims=True)
        expos = jnp.exp(scores - highest)
        weights = (expos * (1.0 / jnp.sum(expos, 2, keepdims=True))).astype(BF16)
        weights = weights.reshape(heads * block, window)
        product = jnp.dot(weights, value, preferred_element_type=F32)
        mixed = product[0:block]
        for h in range(1, heads):
            mixed = jnp.where(lane_head == h, product[h * block : (h + 1) * block], mixed)
        out_ref[r : r + block, :] = mixed.astype(BF16)


def scatter_rows(local, ranks_ref, state, out_refs):
    frames = state.shape[0]
    capacity = out_refs[0].shape[0]
    slot = lax.broadcasted_iota(jnp.int32, (capacity, frames), 0).astype(F32)
    for s, out_ref in enumerate(out_refs):
        e = local * len(out_refs) + s
        pick = jnp.where(slot == ranks_ref[e : e + 1, :], 1.0, 0.0).astype(BF16)
        out_ref[...] = jnp.dot(pick, state, preferred_element_type=F32).astype(BF16)


def state_kernel(pieces, *refs):
    early = refs[:pieces]
    late = refs[pieces : 2 * pieces]
    proj = refs[2 * pieces : 3 * pieces]
    frames_ref, ranks_ref, state_ref = refs[3 * pieces : 3 * pieces + 3]
    halves = []
    for ctx in (early, late):
        attended = jnp.dot(ctx[0][...], proj[0][...], preferred_element_type=F32)
        for part, weight in zip(ctx[1:], proj[1:]):
            attended = attended + jnp.dot(part[...], weight[...], preferred_element_type=F32)
        halves.append(attended)
    attended = jnp.concatenate(halves, 0)
    state = (frames_ref[...].astype(F32) + attended).astype(BF16)
    state_ref[...] = state
    scatter_rows(0, ranks_ref, state, refs[3 * pieces + 3 :])


def dispatch_kernel(local, pieces, *refs):
    state = jnp.concatenate([ref[...] for ref in refs[:pieces]], 1)
    scatter_rows(local, refs[pieces], state, refs[pieces + 1 :])


def expert_kernel(local, arrays, width, joined, order_ref, *refs):
    rows_in = refs[:arrays]
    gate_any, up_any, down_any, after_any = refs[arrays : arrays + 4]
    if joined:
        send_ref, keep_x_ref, keep_ref = refs[arrays + 4 : arrays + 7]
        scratch = refs[arrays + 7 :]
    else:
        send_x_ref, send_ref, keep_x_ref, keep_ref = refs[arrays + 4 : arrays + 8]
        scratch = refs[arrays + 8 :]
    gate_ref, up_ref, down_ref, normed_ref, active_ref, sems = scratch
    rows, model = normed_ref.shape
    hidden = active_ref.shape[1]
    moves = [
        (gate_any.at[local], gate_ref),
        (up_any.at[local], up_ref),
        (down_any.at[local], down_ref),
    ]
    copies = [pltpu.make_async_copy(a, b, sems.at[i]) for i, (a, b) in enumerate(moves)]
    for copy in copies:
        copy.start()

    blocks = []
    for ref in rows_in:
        blocks += [(ref, c) for c in range(0, ref.shape[1], width)]
    step = min(rows, 256)

    def norm(i, carry):
        at_row = pl.multiple_of(i * step, step)
        parts = [ref[pl.ds(at_row, step), c : c + width].astype(F32) for ref, c in blocks]
        squares = sum(jnp.sum(part * part, 1, keepdims=True) for part in parts)
        factor = lax.rsqrt(squares * (1.0 / model) + EPS)
        for j, part in enumerate(parts):
            at = pl.multiple_of(order_ref[j] * width, width)
            normed_ref[pl.ds(at_row, step), pl.ds(at, width)] = (part * factor).astype(BF16)
        return carry

    lax.fori_loop(0, rows // step, norm, 0)
    copies[0].wait()
    copies[1].wait()
    tile = min(rows, 1024)
    chunk = min(hidden, 256)
    for r in range(0, rows, tile):
        normed = normed_ref[r : r + tile, :]
        for c in range(0, hidden, chunk):
            gate = jnp.dot(normed, gate_ref[:, c : c + chunk], preferred_element_type=F32)
            up = jnp.dot(normed, up_ref[:, c : c + chunk], preferred_element_type=F32)
            half = 0.5 * gate
            active = (half + half * jnp.tanh(half)) * up
            active_ref[r : r + tile, c : c + chunk] = active.astype(BF16)
    copies[2].wait()
    count = len(blocks) // 2
    def project(i, out_ref, column):
        at = pl.multiple_of(order_ref[i] * width, width)
        weight = down_ref[:, pl.ds(at, width)]
        for r in range(0, rows, tile):
            result = jnp.dot(active_ref[r : r + tile, :], weight, preferred_element_type=F32)
            out_ref[r : r + tile, column : column + width] = result.astype(out_ref.dtype)

    for by in range(1, count):
        project(count + by, send_ref if joined else send_x_ref, (by - 1) * width)
    project(count, send_ref, (count - 1) * width if joined else 0)
    for by in range(1, count):
        project(by, keep_x_ref, (by - 1) * width)
    project(0, keep_ref, 0)


def add_kernel(width, keep_ref, got_ref, after_any, *out_refs):
    for i, out_ref in enumerate(out_refs):
        at = slice(i * width, (i + 1) * width)
        out_ref[...] = (keep_ref[:, at] + got_ref[:, at].astype(F32)).astype(BF16)


def total_kernel(parts, column, keep_ref, *refs):
    capacity, width = refs[parts].shape
    for s, out_ref in enumerate(refs[parts:]):
        at = slice(s * capacity, (s + 1) * capacity)
        total = keep_ref[at, :] + refs[0][at, column : column + width].astype(F32)
        for ref in refs[1:parts]:
            total = total + ref[at, :].astype(F32)
        out_ref[...] = total.astype(BF16)


def combine_kernel(local, targets_ref, gates_ref, base_ref, *refs):
    out_ref = refs[-1]
    back = jnp.concatenate([ref[...] for ref in refs[:-1]], 0)
    rows = back.shape[0]
    frames = targets_ref.shape[0]
    places = lax.broadcasted_iota(jnp.int32, (frames, rows), 1) + local * rows
    total = base_ref[...].astype(F32)
    for k in range(TOP):
        pick = jnp.where(places == targets_ref[:, k : k + 1], 1.0, 0.0).astype(BF16)
        total = total + gates_ref[:, k : k + 1] * jnp.dot(pick, back, preferred_element_type=F32)
    out_ref[...] = total.astype(out_ref.dtype)


def per_device(
    frames_in,
    queries,
    keys,
    values,
    segment_edges,
    out_proj,
    expert_ids,
    gates,
    w_gate,
    w_up,
    w_down,
):
    frames, model = frames_in.shape
    width = queries.shape[1]
    n_model = lax.axis_size("mp")
    n_time = lax.axis_size("tm")
    chips = n_model // 2
    head_width = model // HEADS
    scale = head_width ** (-0.5)
    local_experts = w_gate.shape[0]
    hidden = w_gate.shape[2]
    experts_all = local_experts * n_time
    capacity = 4 * frames // experts_all
    rows = n_time * capacity
    lanes = -(-experts_all // LANES) * LANES
    at_time = lax.axis_index("tm")
    at_model = lax.axis_index("mp")
    chip, core = at_model // 2, at_model % 2
    mine = [((chip - by) % chips) * 2 + core for by in range(chips)]
    others = [((chip - by) % chips) * 2 + 1 - core for by in range(chips)]
    order = jnp.stack(mine + others).astype(jnp.int32)
    meta = jnp.stack([at_time * frames, at_time]).astype(jnp.int32)

    tails = from_behind(jnp.stack([keys[frames - LEFT :], values[frames - LEFT :]], 0), "tm", 1)

    def column_block(x, index):
        return lax.dynamic_slice_in_dim(x, index * width, width, 1)

    proj = [column_block(out_proj, at_model)]
    for by in range(1, chips):
        proj.append(from_chip(column_block(out_proj, ((chip + by) % chips) * 2 + core), by))
    proj.append(core_swap(column_block(out_proj, chip * 2 + 1 - core)))
    for by in range(1, chips):
        to = column_block(out_proj, ((chip + by) % chips) * 2 + 1 - core)
        pairs = [
            (c * 2 + k, ((c + by) % chips) * 2 + 1 - k) for c in range(chips) for k in range(2)
        ]
        proj.append(lax.ppermute(to, "mp", pairs))

    ranks, targets = pl.pallas_call(
        functools.partial(route_kernel, capacity, local_experts, n_time),
        out_shape=(
            jax.ShapeDtypeStruct((lanes, frames), F32),
            jax.ShapeDtypeStruct((frames, TOP), jnp.int32),
        ),
        in_specs=[SMEM, VMEM],
        out_specs=(VMEM, VMEM),
        compiler_params=params(16),
        cost_estimate=cost(2 * frames * frames * lanes, frames * 1024),
        name="route",
    )(meta, expert_ids)

    def attend(start, end, *extra):
        count = end - start
        return pl.pallas_call(
            functools.partial(attend_kernel, scale, head_width, start),
            out_shape=jax.ShapeDtypeStruct((count, width), BF16),
            in_specs=[SMEM] + [HBM] * 4 + [ANY] * len(extra),
            out_specs=VMEM,
            scratch_shapes=[
                pltpu.VMEM((2, frames), jnp.int32),
                pltpu.VMEM((count, width), BF16),
                pltpu.VMEM((LEFT + count, width), BF16),
                pltpu.VMEM((LEFT + count, width), BF16),
                pltpu.SemaphoreType.DMA((6,)),
            ],
            compiler_params=params(16),
            cost_estimate=cost(count * 384 * width * 16, count * width * 8, count * 384 * 4),
            name=f"attend_{start}",
        )(meta, segment_edges, queries, keys, values, *extra)

    late = attend(LEFT, frames)
    tails, *proj = lax.optimization_barrier((tails, *proj))
    early = attend(0, LEFT, tails)
    late_parts = gathered(late)
    early_parts = gathered(early)
    own_frames = column_block(frames_in, at_model)

    def blocks_of(columns):
        return (jax.ShapeDtypeStruct((capacity, columns), BF16),) * n_time

    state, *outgoing_0 = pl.pallas_call(
        functools.partial(state_kernel, n_model),
        out_shape=(jax.ShapeDtypeStruct((frames, width), BF16),) + blocks_of(width),
        in_specs=[VMEM] * (3 * n_model + 2),
        out_specs=(VMEM,) * (1 + n_time),
        compiler_params=params(16),
        cost_estimate=cost(2 * frames * width * (model + rows), 4 * MIB),
        name="state",
    )(*early_parts, *late_parts, *proj, own_frames, ranks)

    def dispatch(local, parts):
        columns = width * len(parts)
        return pl.pallas_call(
            functools.partial(dispatch_kernel, local, len(parts)),
            out_shape=blocks_of(columns),
            in_specs=[VMEM] * (len(parts) + 1),
            out_specs=(VMEM,) * n_time,
            compiler_params=params(16),
            cost_estimate=cost(2 * frames * columns * rows, 3 * MIB),
            name=f"dispatch_{local}",
        )(*parts, ranks)

    def experts(local, parts, joined, after):
        away = (chips - 1) * width
        send = [(chips * width,)] if joined else [(away,), (width,)]
        outs = [jax.ShapeDtypeStruct((rows, *columns), BF16) for columns in send]
        outs += [jax.ShapeDtypeStruct((rows, columns), F32) for columns in (away, width)]
        return pl.pallas_call(
            functools.partial(expert_kernel, local, len(parts), width, joined),
            in_specs=[SMEM] + [VMEM] * len(parts) + [HBM] * 3 + [ANY],
            out_specs=(VMEM,) * len(outs),
            scratch_shapes=[
                pltpu.VMEM((model, hidden), BF16),
                pltpu.VMEM((model, hidden), BF16),
                pltpu.VMEM((hidden, model), BF16),
                pltpu.VMEM((rows, model), BF16),
                pltpu.VMEM((rows, hidden), BF16),
                pltpu.SemaphoreType.DMA((3,)),
            ],
            out_shape=tuple(outs),
            compiler_params=params(32),
            cost_estimate=cost(6 * rows * model * hidden, 12 * MIB, rows * hidden),
            name=f"experts_{local}",
        )(order, *parts, w_gate, w_up, w_down, after)

    def add(local, keep, got, after):
        return pl.pallas_call(
            functools.partial(add_kernel, width),
            in_specs=[VMEM, VMEM, ANY],
            out_specs=(VMEM,) * (chips - 1),
            out_shape=(jax.ShapeDtypeStruct((rows, width), BF16),) * (chips - 1),
            compiler_params=params(16),
            cost_estimate=cost(keep.size, keep.size * 8),
            name=f"add_{local}",
        )(keep, got, after)

    def total(local, column, keep, parts):
        return pl.pallas_call(
            functools.partial(total_kernel, len(parts), column),
            in_specs=[VMEM] * (1 + len(parts)),
            out_specs=(VMEM,) * n_time,
            out_shape=blocks_of(width),
            compiler_params=params(16),
            cost_estimate=cost(keep.size, keep.size * 10),
            name=f"total_{local}",
        )(keep, *parts)

    def from_chips(parts):
        return [from_chip(part, chips - by) for by, part in enumerate(parts, 1)]

    def combine(local, back, base):
        last = local == local_experts - 1
        return pl.pallas_call(
            functools.partial(combine_kernel, local),
            out_shape=jax.ShapeDtypeStruct((frames, width), BF16 if last else F32),
            in_specs=[VMEM] * (3 + n_time),
            out_specs=VMEM,
            compiler_params=params(24),
            cost_estimate=cost(4 * frames * width * rows, 3 * MIB),
            name=f"combine_{local}",
        )(targets, gates, base, *back)

    arrived_0 = jnp.concatenate(exchanged(outgoing_0, 1), 0)
    wide = [state] + [from_chip(state, by) for by in range(1, chips)]
    outgoing_1 = dispatch(1, wide)
    arrived_1 = jnp.concatenate(exchanged(outgoing_1, 1), 0)
    send_0, keep_x_0, keep_0 = experts(0, gathered(arrived_0), True, outgoing_1[0])
    swapped_0 = core_swap(send_0)
    away_0 = add(0, keep_x_0, swapped_0, swapped_0)
    got_0 = from_chips(away_0)
    parts_1 = [arrived_1, core_swap(arrived_1)]
    send_x_1, send_1, keep_x_1, keep_1 = experts(1, parts_1, False, away_0[0])
    total_0 = total(0, (chips - 1) * width, keep_0, [swapped_0, *got_0])
    back_0 = exchanged(total_0, -1)
    got_1 = from_chips(add(1, keep_x_1, core_swap(send_x_1), total_0[0]))
    back_1 = exchanged(total(1, 0, keep_1, [core_swap(send_1), *got_1]), -1)
    return combine(1, back_1, combine(0, back_0, state))


def solution(mesh):
    return jax.shard_map(
        per_device,
        mesh=mesh,
        in_specs=(
            P("tm", None),
            P("tm", "mp"),
            P("tm", "mp"),
            P("tm", "mp"),
            P(None, "tm"),
            P("mp", None),
            P("tm", None),
            P("tm", None),
            P("tm", None, "mp"),
            P("tm", None, "mp"),
            P("tm", "mp", None),
        ),
        out_specs=P("tm", "mp"),
        check_vma=False,
    )
```

```python
import functools

import jax
import jax.numpy as jnp
from jax import lax
from jax.experimental import pallas as pl
from jax.experimental.pallas import tpu as pltpu
from jax.sharding import PartitionSpec as P

HEADS = 16
TOP = 2
LEFT = 256
EPS = 1e-06
LANES = 128
MIB = 1 << 20
F32 = jnp.float32
BF16 = jnp.bfloat16

VMEM = pl.BlockSpec(memory_space=pltpu.VMEM)
SMEM = pl.BlockSpec(memory_space=pltpu.SMEM)
ANY = pl.BlockSpec(memory_space=pl.ANY)
HBM = pl.BlockSpec(memory_space=pltpu.HBM)


def params(mib):
    return pltpu.CompilerParams(vmem_limit_bytes=mib * MIB)


def cost(flops, moved, transcendentals=0):
    return pl.CostEstimate(flops=flops, bytes_accessed=moved, transcendentals=transcendentals)


def from_behind(x, axis, by):
    size = lax.axis_size(axis)
    pairs = [(i, i + by) for i in range(size) if 0 <= i + by < size]
    return lax.ppermute(x, axis, pairs)


def core_swap(x):
    size = lax.axis_size("mp")
    return lax.ppermute(x, "mp", [(i, i ^ 1) for i in range(size)])


def from_chip(x, by):
    chips = lax.axis_size("mp") // 2
    pairs = [(c * 2 + k, ((c + by) % chips) * 2 + k) for c in range(chips) for k in range(2)]
    return lax.ppermute(x, "mp", pairs)


def gathered(x):
    chips = lax.axis_size("mp") // 2
    mine = [x] + [from_chip(x, by) for by in range(1, chips)]
    return mine + [core_swap(part) for part in mine]


def route_kernel(capacity, local_experts, n_time, ids_ref, ranks_ref, targets_ref):
    frames = ids_ref.shape[0]
    lanes = ranks_ref.shape[0]
    ids = ids_ref[...]
    owner = ids // local_experts
    ids = (ids - owner * local_experts) * n_time + owner
    experts = lax.broadcasted_iota(jnp.int32, (frames, lanes), 1)
    hits = [ids[:, k : k + 1] == experts for k in range(TOP)]
    named = functools.reduce(jnp.logical_or, hits)
    ones = jnp.where(named, 1.0, 0.0).astype(BF16)
    row = lax.broadcasted_iota(jnp.int32, (frames, frames), 0)
    column = lax.broadcasted_iota(jnp.int32, (frames, frames), 1)
    before = jnp.where(column < row, 1.0, 0.0).astype(BF16)
    ranks = jnp.dot(before, ones, preferred_element_type=F32)
    ranks_ref[...] = jnp.where(named, ranks, -1.0).T
    places = []
    for k in range(TOP):
        slot = jnp.sum(jnp.where(hits[k], ranks, 0.0), 1, keepdims=True).astype(jnp.int32)
        places.append(ids[:, k : k + 1] * capacity + slot)
    targets_ref[...] = jnp.concatenate(places, 1)


def attend_kernel(scale, head_width, start, meta_ref, order_ref, *refs):
    tails_any = refs[5] if start == 0 else None
    edges_any, q_any, k_any, v_any, proj_any = refs[:5]
    refs = refs[6:] if start == 0 else refs[5:]
    send_ref, keep_x_ref, keep_ref, edges_ref, q_ref, k_ref, v_ref, proj_ref, sems = refs
    rows, columns = q_ref.shape
    heads = columns // head_width
    block = LANES
    window = LEFT + block
    if start == 0:
        moves = [
            (q_any.at[pl.ds(0, rows)], q_ref),
            (tails_any.at[0], k_ref.at[pl.ds(0, LEFT)]),
            (k_any.at[pl.ds(0, rows)], k_ref.at[pl.ds(LEFT, rows)]),
            (tails_any.at[1], v_ref.at[pl.ds(0, LEFT)]),
            (v_any.at[pl.ds(0, rows)], v_ref.at[pl.ds(LEFT, rows)]),
            (edges_any, edges_ref),
            (proj_any, proj_ref),
        ]
    else:
        moves = [
            (q_any.at[pl.ds(start, rows)], q_ref),
            (k_any.at[pl.ds(start - LEFT, rows + LEFT)], k_ref),
            (v_any.at[pl.ds(start - LEFT, rows + LEFT)], v_ref),
            (edges_any, edges_ref),
            (proj_any, proj_ref),
        ]
    copies = [pltpu.make_async_copy(a, b, sems.at[i]) for i, (a, b) in enumerate(moves)]
    for copy in copies:
        copy.start()
    for copy in copies[:-1]:
        copy.wait()
    edges = edges_ref[:, start : start + rows].astype(F32)
    edges = jnp.concatenate([edges, jnp.zeros((6, rows), F32)], 0).T
    lane_head = lax.broadcasted_iota(jnp.int32, (block, columns), 1) // head_width
    context = []
    for r in range(0, rows, block):
        key = k_ref[r : r + window, :]
        value = v_ref[r : r + window, :]
        query = q_ref[r : r + block, :]
        places = lax.broadcasted_iota(jnp.int32, (block, window), 1)
        places = (places + (meta_ref[0] + (start + r - LEFT))).astype(F32)
        lower = jnp.maximum(edges[r : r + block, 0:1] - LEFT, 0.0)
        upper = edges[r : r + block, 1:2]
        visible = (places >= lower) & (places <= upper)
        own = [jnp.where(lane_head == h, query, jnp.zeros_like(query)) for h in range(heads)]
        own = jnp.concatenate(own, 0)
        scores = lax.dot_general(own, key, (((1,), (1,)), ((), ())), preferred_element_type=F32)
        scores = (scores * scale).reshape(heads, block, window)
        scores = jnp.where(visible[None], scores, -1e30)
        highest = jnp.max(scores, 2, keepdims=True)
        expos = jnp.exp(scores - highest)
        weights = (expos * (1.0 / jnp.sum(expos, 2, keepdims=True))).astype(BF16)
        weights = weights.reshape(heads * block, window)
        product = jnp.dot(weights, value, preferred_element_type=F32)
        mixed = product[0:block]
        for h in range(1, heads):
            mixed = jnp.where(lane_head == h, product[h * block : (h + 1) * block], mixed)
        context.append(mixed.astype(BF16))
    context = jnp.concatenate(context, 0)
    copies[-1].wait()
    count = proj_ref.shape[1] // columns // 2
    for i in range(2 * count):
        at = pl.multiple_of(order_ref[i] * columns, columns)
        part = jnp.dot(context, proj_ref[:, pl.ds(at, columns)], preferred_element_type=F32)
        j = (i - 1) % count * columns
        if i >= count:
            send_ref[:, j : j + columns] = part.astype(BF16)
        elif i > 0:
            keep_x_ref[:, j : j + columns] = part
        else:
            keep_ref[...] = part


def scatter_rows(local, capacity, ranks_ref, state, out_ref):
    frames = state.shape[0]
    n_time = out_ref.shape[0] // capacity
    slot = lax.broadcasted_iota(jnp.int32, (capacity, frames), 0).astype(F32)
    for owner in range(n_time):
        e = local * n_time + owner
        pick = jnp.where(slot == ranks_ref[e : e + 1, :], 1.0, 0.0).astype(BF16)
        rows = jnp.dot(pick, state, preferred_element_type=F32)
        out_ref[owner * capacity : (owner + 1) * capacity, :] = rows.astype(BF16)


def state_kernel(parts, column, capacity, *refs):
    frames_ref, ranks_ref, state_ref = refs[2 * parts : 2 * parts + 3]
    width = state_ref.shape[1]
    halves = []
    for keep_ref, swapped_ref, *got in (refs[:parts], refs[parts : 2 * parts]):
        half = keep_ref[...] + swapped_ref[:, column : column + width].astype(F32)
        for ref in got:
            half = half + ref[...].astype(F32)
        halves.append(half)
    attended = jnp.concatenate(halves, 0)
    state = (frames_ref[...].astype(F32) + attended).astype(BF16)
    state_ref[...] = state
    scatter_rows(0, capacity, ranks_ref, state, refs[2 * parts + 3])


def dispatch_kernel(local, capacity, pieces, *refs):
    state = jnp.concatenate([ref[...] for ref in refs[:pieces]], 1)
    scatter_rows(local, capacity, refs[pieces], state, refs[pieces + 1])


def take_kernel(rows_ref, after_any, out_ref):
    out_ref[...] = rows_ref[...]


def expert_kernel(local, arrays, width, joined, order_ref, *refs):
    rows_in = refs[:arrays]
    gate_any, up_any, down_any, after_any = refs[arrays : arrays + 4]
    if joined:
        send_ref, keep_x_ref, keep_ref = refs[arrays + 4 : arrays + 7]
        scratch = refs[arrays + 7 :]
    else:
        send_x_ref, send_ref, keep_x_ref, keep_ref = refs[arrays + 4 : arrays + 8]
        scratch = refs[arrays + 8 :]
    gate_ref, up_ref, down_ref, normed_ref, active_ref, sems = scratch
    rows, model = normed_ref.shape
    hidden = active_ref.shape[1]
    moves = [
        (gate_any.at[local], gate_ref),
        (up_any.at[local], up_ref),
        (down_any.at[local], down_ref),
    ]
    copies = [pltpu.make_async_copy(a, b, sems.at[i]) for i, (a, b) in enumerate(moves)]
    for copy in copies:
        copy.start()

    blocks = []
    for ref in rows_in:
        blocks += [(ref, c) for c in range(0, ref.shape[1], width)]
    step = min(rows, 256)

    def norm(i, carry):
        at_row = pl.multiple_of(i * step, step)
        parts = [ref[pl.ds(at_row, step), c : c + width].astype(F32) for ref, c in blocks]
        squares = sum(jnp.sum(part * part, 1, keepdims=True) for part in parts)
        factor = lax.rsqrt(squares * (1.0 / model) + EPS)
        for j, part in enumerate(parts):
            at = pl.multiple_of(order_ref[j] * width, width)
            normed_ref[pl.ds(at_row, step), pl.ds(at, width)] = (part * factor).astype(BF16)
        return carry

    lax.fori_loop(0, rows // step, norm, 0)
    copies[0].wait()
    copies[1].wait()
    tile = min(rows, 1024)
    chunk = min(hidden, 256)
    for r in range(0, rows, tile):
        normed = normed_ref[r : r + tile, :]
        for c in range(0, hidden, chunk):
            gate = jnp.dot(normed, gate_ref[:, c : c + chunk], preferred_element_type=F32)
            up = jnp.dot(normed, up_ref[:, c : c + chunk], preferred_element_type=F32)
            half = 0.5 * gate
            active = (half + half * jnp.tanh(half)) * up
            active_ref[r : r + tile, c : c + chunk] = active.astype(BF16)
    copies[2].wait()
    count = len(blocks) // 2
    def project(i, out_ref, column):
        at = pl.multiple_of(order_ref[i] * width, width)
        weight = down_ref[:, pl.ds(at, width)]
        for r in range(0, rows, tile):
            result = jnp.dot(active_ref[r : r + tile, :], weight, preferred_element_type=F32)
            out_ref[r : r + tile, column : column + width] = result.astype(out_ref.dtype)

    for by in range(1, count):
        project(count + by, send_ref if joined else send_x_ref, (by - 1) * width)
    project(count, send_ref, (count - 1) * width if joined else 0)
    for by in range(1, count):
        project(by, keep_x_ref, (by - 1) * width)
    project(0, keep_ref, 0)


def add_kernel(width, keep_ref, got_ref, after_any, *out_refs):
    for i, out_ref in enumerate(out_refs):
        at = slice(i * width, (i + 1) * width)
        out_ref[...] = (keep_ref[:, at] + got_ref[:, at].astype(F32)).astype(BF16)


def total_kernel(column, keep_ref, swapped_ref, *refs):
    width = keep_ref.shape[1]
    total = keep_ref[...] + swapped_ref[:, column : column + width].astype(F32)
    for ref in refs[:-1]:
        total = total + ref[...].astype(F32)
    refs[-1][...] = total.astype(BF16)


def combine_kernel(local, targets_ref, gates_ref, base_ref, *refs):
    out_ref = refs[-1]
    back = jnp.concatenate([ref[...] for ref in refs[:-1]], 0) if len(refs) > 2 else refs[0][...]
    rows = back.shape[0]
    frames = targets_ref.shape[0]
    places = lax.broadcasted_iota(jnp.int32, (frames, rows), 1) + local * rows
    total = base_ref[...].astype(F32)
    for k in range(TOP):
        pick = jnp.where(places == targets_ref[:, k : k + 1], 1.0, 0.0).astype(BF16)
        total = total + gates_ref[:, k : k + 1] * jnp.dot(pick, back, preferred_element_type=F32)
    out_ref[...] = total.astype(out_ref.dtype)


def per_device(
    frames_in,
    queries,
    keys,
    values,
    segment_edges,
    out_proj,
    expert_ids,
    gates,
    w_gate,
    w_up,
    w_down,
):
    frames, model = frames_in.shape
    width = queries.shape[1]
    n_model = lax.axis_size("mp")
    n_time = lax.axis_size("tm")
    chips = n_model // 2
    head_width = model // HEADS
    scale = head_width ** (-0.5)
    local_experts = w_gate.shape[0]
    hidden = w_gate.shape[2]
    experts_all = local_experts * n_time
    capacity = 4 * frames // experts_all
    rows = n_time * capacity
    lanes = -(-experts_all // LANES) * LANES
    at_time = lax.axis_index("tm")
    at_model = lax.axis_index("mp")
    chip, core = at_model // 2, at_model % 2
    mine = [((chip - by) % chips) * 2 + core for by in range(chips)]
    others = [((chip - by) % chips) * 2 + 1 - core for by in range(chips)]
    order = jnp.stack(mine + others).astype(jnp.int32)
    offset = (at_time * frames).astype(jnp.int32).reshape(1)
    away = (chips - 1) * width

    tails = from_behind(jnp.stack([keys[frames - LEFT :], values[frames - LEFT :]], 0), "tm", 1)
    own_frames = lax.dynamic_slice_in_dim(frames_in, at_model * width, width, 1)

    ranks, targets = pl.pallas_call(
        functools.partial(route_kernel, capacity, local_experts, n_time),
        out_shape=(
            jax.ShapeDtypeStruct((lanes, frames), F32),
            jax.ShapeDtypeStruct((frames, TOP), jnp.int32),
        ),
        in_specs=[VMEM],
        out_specs=(VMEM, VMEM),
        compiler_params=params(16),
        cost_estimate=cost(2 * frames * frames * lanes, frames * 1024),
        name="route",
    )(expert_ids)

    def in_hbm(*arrays):
        return [pltpu.with_memory_space_constraint(x, pltpu.HBM) for x in arrays]

    def attend(start, end, *extra):
        count = end - start
        return pl.pallas_call(
            functools.partial(attend_kernel, scale, head_width, start),
            out_shape=(
                jax.ShapeDtypeStruct((count, chips * width), BF16),
                jax.ShapeDtypeStruct((count, away), F32),
                jax.ShapeDtypeStruct((count, width), F32),
            ),
            in_specs=[SMEM, SMEM] + [HBM] * 5 + [ANY] * len(extra),
            out_specs=(VMEM,) * 3,
            scratch_shapes=[
                pltpu.VMEM((2, frames), jnp.int32),
                pltpu.VMEM((count, width), BF16),
                pltpu.VMEM((LEFT + count, width), BF16),
                pltpu.VMEM((LEFT + count, width), BF16),
                pltpu.VMEM(out_proj.shape, BF16),
                pltpu.SemaphoreType.DMA((7,)),
            ],
            compiler_params=params(16),
            cost_estimate=cost(count * 384 * width * 16, count * width * 8, count * 384 * 4),
            name=f"attend_{start}",
        )(offset, order, *in_hbm(segment_edges, queries, keys, values, out_proj), *extra)

    def add(name, keep, got, after):
        count = keep.shape[0]
        return pl.pallas_call(
            functools.partial(add_kernel, width),
            in_specs=[VMEM, VMEM, ANY],
            out_specs=(VMEM,) * (chips - 1),
            out_shape=(jax.ShapeDtypeStruct((count, width), BF16),) * (chips - 1),
            compiler_params=params(16),
            cost_estimate=cost(keep.size, keep.size * 8),
            name=f"add_{name}",
        )(keep, got, after)

    def from_chips(parts):
        return [from_chip(part, chips - by) for by, part in enumerate(parts, 1)]

    def attended(name, send, keep_x, keep):
        swapped = core_swap(send)
        return [keep, swapped, *from_chips(add(name, keep_x, swapped, swapped))]

    late = attended("late", *attend(LEFT, frames))
    early = attended("early", *attend(0, LEFT, tails))

    state, outgoing_0 = pl.pallas_call(
        functools.partial(state_kernel, len(early), away, capacity),
        out_shape=(
            jax.ShapeDtypeStruct((frames, width), BF16),
            jax.ShapeDtypeStruct((rows, width), BF16),
        ),
        in_specs=[VMEM] * (2 * len(early) + 2),
        out_specs=(VMEM, VMEM),
        compiler_params=params(16),
        cost_estimate=cost(2 * frames * width * rows, 4 * MIB),
        name="state",
    )(*early, *late, own_frames, ranks)

    def dispatch(local, parts):
        columns = width * len(parts)
        return pl.pallas_call(
            functools.partial(dispatch_kernel, local, capacity, len(parts)),
            out_shape=jax.ShapeDtypeStruct((rows, columns), BF16),
            in_specs=[VMEM] * (len(parts) + 1),
            out_specs=VMEM,
            compiler_params=params(16),
            cost_estimate=cost(2 * frames * columns * rows, 3 * MIB),
            name=f"dispatch_{local}",
        )(*parts, ranks)

    def over_time(x):
        columns = x.shape[1]
        x = x.reshape(n_time, capacity, columns)
        x = lax.all_to_all(x, "tm", split_axis=0, concat_axis=0, tiled=True)
        return x.reshape(rows, columns)

    def take(x, after):
        return pl.pallas_call(
            take_kernel,
            in_specs=[VMEM, ANY],
            out_specs=VMEM,
            out_shape=jax.ShapeDtypeStruct(x.shape, x.dtype),
            compiler_params=params(16),
            cost_estimate=cost(x.size, x.size * 4),
            name="take",
        )(x, after)

    def experts(local, parts, joined, after):
        send = [(chips * width,)] if joined else [(away,), (width,)]
        outs = [jax.ShapeDtypeStruct((rows, *columns), BF16) for columns in send]
        outs += [jax.ShapeDtypeStruct((rows, columns), F32) for columns in (away, width)]
        return pl.pallas_call(
            functools.partial(expert_kernel, local, len(parts), width, joined),
            in_specs=[SMEM] + [VMEM] * len(parts) + [HBM] * 3 + [ANY],
            out_specs=(VMEM,) * len(outs),
            scratch_shapes=[
                pltpu.VMEM((model, hidden), BF16),
                pltpu.VMEM((model, hidden), BF16),
                pltpu.VMEM((hidden, model), BF16),
                pltpu.VMEM((rows, model), BF16),
                pltpu.VMEM((rows, hidden), BF16),
                pltpu.SemaphoreType.DMA((3,)),
            ],
            out_shape=tuple(outs),
            compiler_params=params(32),
            cost_estimate=cost(6 * rows * model * hidden, 12 * MIB, rows * hidden),
            name=f"experts_{local}",
        )(order, *parts, *in_hbm(w_gate, w_up, w_down), after)

    def total(local, column, keep, swapped, parts):
        return pl.pallas_call(
            functools.partial(total_kernel, column),
            in_specs=[VMEM] * (2 + len(parts)),
            out_specs=VMEM,
            out_shape=jax.ShapeDtypeStruct((rows, width), BF16),
            compiler_params=params(16),
            cost_estimate=cost(keep.size, keep.size * 10),
            name=f"total_{local}",
        )(keep, swapped, *parts)

    def combine(local, back, base):
        last = local == local_experts - 1
        return pl.pallas_call(
            functools.partial(combine_kernel, local),
            out_shape=jax.ShapeDtypeStruct((frames, width), BF16 if last else F32),
            in_specs=[VMEM] * (3 + len(back)),
            out_specs=VMEM,
            compiler_params=params(24),
            cost_estimate=cost(4 * frames * width * rows, 3 * MIB),
            name=f"combine_{local}",
        )(targets, gates, base, *back)

    arrived_0 = over_time(outgoing_0)
    wide = [state] + [from_chip(state, by) for by in range(1, chips)]
    outgoing_1 = dispatch(1, wide)
    arrived_1 = over_time(outgoing_1)
    send_0, keep_x_0, keep_0 = experts(0, gathered(arrived_0), True, outgoing_1)
    swapped_0 = core_swap(send_0)
    away_0 = add("0", keep_x_0, swapped_0, swapped_0)
    got_0 = from_chips(away_0)
    arrived_1 = take(arrived_1, send_0)
    parts_1 = [arrived_1, core_swap(arrived_1)]
    send_x_1, send_1, keep_x_1, keep_1 = experts(1, parts_1, False, away_0[0])
    total_0 = total(0, away, keep_0, swapped_0, got_0)
    back_0 = over_time(total_0)
    got_1 = from_chips(add("1", keep_x_1, core_swap(send_x_1), total_0))
    back_1 = over_time(total(1, 0, keep_1, core_swap(send_1), got_1))
    return combine(1, [back_1], combine(0, [back_0], state))


def solution(mesh):
    return jax.shard_map(
        per_device,
        mesh=mesh,
        in_specs=(
            P("tm", None),
            P("tm", "mp"),
            P("tm", "mp"),
            P("tm", "mp"),
            P(None, "tm"),
            P("mp", None),
            P("tm", None),
            P("tm", None),
            P("tm", None, "mp"),
            P("tm", None, "mp"),
            P("tm", "mp", None),
        ),
        out_specs=P("tm", "mp"),
        check_vma=False,
    )
```

```python
import functools

import jax
import jax.numpy as jnp
from jax import lax
from jax.experimental import pallas as pl
from jax.experimental.pallas import tpu as pltpu
from jax.sharding import PartitionSpec as P

HEADS = 16
TOP = 2
LEFT = 256
EPS = 1e-06
LANES = 128
MIB = 1 << 20
F32 = jnp.float32
BF16 = jnp.bfloat16

VMEM = pl.BlockSpec(memory_space=pltpu.VMEM)
SMEM = pl.BlockSpec(memory_space=pltpu.SMEM)
ANY = pl.BlockSpec(memory_space=pl.ANY)
HBM = pl.BlockSpec(memory_space=pltpu.HBM)


def params(mib):
    return pltpu.CompilerParams(vmem_limit_bytes=mib * MIB)


def cost(flops, moved, transcendentals=0):
    return pl.CostEstimate(flops=flops, bytes_accessed=moved, transcendentals=transcendentals)


def from_behind(x, axis, by):
    size = lax.axis_size(axis)
    pairs = [(i, i + by) for i in range(size) if 0 <= i + by < size]
    return lax.ppermute(x, axis, pairs)


def core_swap(x):
    size = lax.axis_size("mp")
    return lax.ppermute(x, "mp", [(i, i ^ 1) for i in range(size)])


def from_chip(x, by):
    chips = lax.axis_size("mp") // 2
    pairs = [(c * 2 + k, ((c + by) % chips) * 2 + k) for c in range(chips) for k in range(2)]
    return lax.ppermute(x, "mp", pairs)


def gathered(x):
    chips = lax.axis_size("mp") // 2
    mine = [x] + [from_chip(x, by) for by in range(1, chips)]
    return mine + [core_swap(part) for part in mine]


def exchanged(blocks):
    size = lax.axis_size("tm")
    return [blocks[0]] + [
        lax.ppermute(block, "tm", [(i, (i + s) % size) for i in range(size)])
        for s, block in enumerate(blocks)
        if s > 0
    ]


def route_kernel(capacity, local_experts, n_time, ids_ref, ranks_ref, targets_ref):
    frames = ids_ref.shape[0]
    lanes = ranks_ref.shape[0]
    ids = ids_ref[...]
    owner = ids // local_experts
    ids = (ids - owner * local_experts) * n_time + owner
    experts = lax.broadcasted_iota(jnp.int32, (frames, lanes), 1)
    hits = [ids[:, k : k + 1] == experts for k in range(TOP)]
    named = functools.reduce(jnp.logical_or, hits)
    ones = jnp.where(named, 1.0, 0.0).astype(BF16)
    row = lax.broadcasted_iota(jnp.int32, (frames, frames), 0)
    column = lax.broadcasted_iota(jnp.int32, (frames, frames), 1)
    before = jnp.where(column < row, 1.0, 0.0).astype(BF16)
    ranks = jnp.dot(before, ones, preferred_element_type=F32)
    ranks_ref[...] = jnp.where(named, ranks, -1.0).T
    places = []
    for k in range(TOP):
        slot = jnp.sum(jnp.where(hits[k], ranks, 0.0), 1, keepdims=True).astype(jnp.int32)
        places.append(ids[:, k : k + 1] * capacity + slot)
    targets_ref[...] = jnp.concatenate(places, 1)


def attend_kernel(scale, head_width, start, meta_ref, order_ref, *refs):
    tails_any = refs[5] if start == 0 else None
    edges_any, q_any, k_any, v_any, proj_any = refs[:5]
    refs = refs[6:] if start == 0 else refs[5:]
    send_ref, keep_x_ref, keep_ref, edges_ref, q_ref, k_ref, v_ref, proj_ref, sems = refs
    rows, columns = q_ref.shape
    heads = columns // head_width
    block = LANES
    window = LEFT + block
    if start == 0:
        moves = [
            (q_any.at[pl.ds(0, rows)], q_ref),
            (tails_any.at[0], k_ref.at[pl.ds(0, LEFT)]),
            (k_any.at[pl.ds(0, rows)], k_ref.at[pl.ds(LEFT, rows)]),
            (tails_any.at[1], v_ref.at[pl.ds(0, LEFT)]),
            (v_any.at[pl.ds(0, rows)], v_ref.at[pl.ds(LEFT, rows)]),
            (edges_any, edges_ref),
            (proj_any, proj_ref),
        ]
    else:
        moves = [
            (q_any.at[pl.ds(start, rows)], q_ref),
            (k_any.at[pl.ds(start - LEFT, rows + LEFT)], k_ref),
            (v_any.at[pl.ds(start - LEFT, rows + LEFT)], v_ref),
            (edges_any, edges_ref),
            (proj_any, proj_ref),
        ]
    copies = [pltpu.make_async_copy(a, b, sems.at[i]) for i, (a, b) in enumerate(moves)]
    for copy in copies:
        copy.start()
    for copy in copies[:-1]:
        copy.wait()
    edges = edges_ref[:, start : start + rows].astype(F32)
    edges = jnp.concatenate([edges, jnp.zeros((6, rows), F32)], 0).T
    lane_head = lax.broadcasted_iota(jnp.int32, (block, columns), 1) // head_width
    context = []
    for r in range(0, rows, block):
        key = k_ref[r : r + window, :]
        value = v_ref[r : r + window, :]
        query = q_ref[r : r + block, :]
        places = lax.broadcasted_iota(jnp.int32, (block, window), 1)
        places = (places + (meta_ref[0] + (start + r - LEFT))).astype(F32)
        lower = jnp.maximum(edges[r : r + block, 0:1] - LEFT, 0.0)
        upper = edges[r : r + block, 1:2]
        visible = (places >= lower) & (places <= upper)
        own = [jnp.where(lane_head == h, query, jnp.zeros_like(query)) for h in range(heads)]
        own = jnp.concatenate(own, 0)
        scores = lax.dot_general(own, key, (((1,), (1,)), ((), ())), preferred_element_type=F32)
        scores = (scores * scale).reshape(heads, block, window)
        scores = jnp.where(visible[None], scores, -1e30)
        highest = jnp.max(scores, 2, keepdims=True)
        expos = jnp.exp(scores - highest)
        weights = (expos * (1.0 / jnp.sum(expos, 2, keepdims=True))).astype(BF16)
        weights = weights.reshape(heads * block, window)
        product = jnp.dot(weights, value, preferred_element_type=F32)
        mixed = product[0:block]
        for h in range(1, heads):
            mixed = jnp.where(lane_head == h, product[h * block : (h + 1) * block], mixed)
        context.append(mixed.astype(BF16))
    context = jnp.concatenate(context, 0)
    copies[-1].wait()
    count = proj_ref.shape[1] // columns // 2
    for i in range(2 * count):
        at = pl.multiple_of(order_ref[i] * columns, columns)
        part = jnp.dot(context, proj_ref[:, pl.ds(at, columns)], preferred_element_type=F32)
        j = (i - 1) % count * columns
        if i >= count:
            send_ref[:, j : j + columns] = part.astype(BF16)
        elif i > 0:
            keep_x_ref[:, j : j + columns] = part
        else:
            keep_ref[...] = part


def scatter_rows(local, capacity, ranks_ref, state, out_ref):
    frames = state.shape[0]
    n_time = out_ref.shape[0] // capacity
    slot = lax.broadcasted_iota(jnp.int32, (capacity, frames), 0).astype(F32)
    for owner in range(n_time):
        e = local * n_time + owner
        pick = jnp.where(slot == ranks_ref[e : e + 1, :], 1.0, 0.0).astype(BF16)
        rows = jnp.dot(pick, state, preferred_element_type=F32)
        out_ref[owner * capacity : (owner + 1) * capacity, :] = rows.astype(BF16)


def state_kernel(parts, column, capacity, *refs):
    frames_ref, ranks_ref, state_ref = refs[2 * parts : 2 * parts + 3]
    width = state_ref.shape[1]
    halves = []
    for keep_ref, swapped_ref, *got in (refs[:parts], refs[parts : 2 * parts]):
        half = keep_ref[...] + swapped_ref[:, column : column + width].astype(F32)
        for ref in got:
            half = half + ref[...].astype(F32)
        halves.append(half)
    attended = jnp.concatenate(halves, 0)
    state = (frames_ref[...].astype(F32) + attended).astype(BF16)
    state_ref[...] = state
    scatter_rows(0, capacity, ranks_ref, state, refs[2 * parts + 3])


def dispatch_kernel(local, capacity, pieces, *refs):
    state = jnp.concatenate([ref[...] for ref in refs[:pieces]], 1)
    scatter_rows(local, capacity, refs[pieces], state, refs[pieces + 1])


def take_kernel(rows_ref, *refs):
    refs[-1][...] = rows_ref[...]


def expert_kernel(local, starts, width, awaited, order_ref, *refs):
    arrays = len(starts)
    rows_in = refs[:arrays]
    gate_any, up_any, down_any = refs[arrays : arrays + 3]
    *outs, gate_ref, up_ref, down_ref, normed_ref, active_ref, sems = refs[arrays + 3 + awaited :]
    *send_x_refs, send_ref, keep_x_ref, keep_ref = outs
    rows, model = normed_ref.shape
    hidden = active_ref.shape[1]
    moves = [
        (gate_any.at[local], gate_ref),
        (up_any.at[local], up_ref),
        (down_any.at[local], down_ref),
    ]
    copies = [pltpu.make_async_copy(a, b, sems.at[i]) for i, (a, b) in enumerate(moves)]
    for copy in copies:
        copy.start()

    blocks = []
    for ref, start in zip(rows_in, starts):
        blocks += [(ref, start, c) for c in range(0, ref.shape[1], width)]
    step = min(rows, 256)

    def norm(i, carry):
        at_row = pl.multiple_of(i * step, step)
        parts = [
            ref[pl.ds(pl.multiple_of(start + i * step, step), step), c : c + width].astype(F32)
            for ref, start, c in blocks
        ]
        squares = sum(jnp.sum(part * part, 1, keepdims=True) for part in parts)
        factor = lax.rsqrt(squares * (1.0 / model) + EPS)
        for j, part in enumerate(parts):
            at = pl.multiple_of(order_ref[j] * width, width)
            normed_ref[pl.ds(at_row, step), pl.ds(at, width)] = (part * factor).astype(BF16)
        return carry

    lax.fori_loop(0, rows // step, norm, 0)
    copies[0].wait()
    copies[1].wait()
    tile = min(rows, 1024)
    chunk = min(hidden, 256)
    for r in range(0, rows, tile):
        normed = normed_ref[r : r + tile, :]
        for c in range(0, hidden, chunk):
            gate = jnp.dot(normed, gate_ref[:, c : c + chunk], preferred_element_type=F32)
            up = jnp.dot(normed, up_ref[:, c : c + chunk], preferred_element_type=F32)
            half = 0.5 * gate
            active = (half + half * jnp.tanh(half)) * up
            active_ref[r : r + tile, c : c + chunk] = active.astype(BF16)
    copies[2].wait()
    count = len(blocks) // 2
    def project(i, out_refs, column):
        at = pl.multiple_of(order_ref[i] * width, width)
        weight = down_ref[:, pl.ds(at, width)]
        result = jnp.dot(active_ref[...], weight, preferred_element_type=F32)
        each = rows // len(out_refs)
        for j, out_ref in enumerate(out_refs):
            part = result[j * each : (j + 1) * each]
            out_ref[:, column : column + width] = part.astype(out_ref.dtype)

    for by in range(1, count):
        project(count + by, send_x_refs, (by - 1) * width)
    project(count, [send_ref], 0)
    for by in range(1, count):
        project(by, [keep_x_ref], (by - 1) * width)
    project(0, [keep_ref], 0)


def add_kernel(width, pieces, keep_ref, *refs):
    got_refs, out_refs = refs[:pieces], refs[pieces + 1 :]
    each = keep_ref.shape[0] // pieces
    for j, got_ref in enumerate(got_refs):
        rows = slice(j * each, (j + 1) * each)
        for i, out_ref in enumerate(out_refs):
            at = slice(i * width, (i + 1) * width)
            out_ref[rows, :] = (keep_ref[rows, at] + got_ref[:, at].astype(F32)).astype(BF16)


def total_kernel(column, *refs):
    out_ref = refs[-1]
    width = out_ref.shape[1]
    count = refs[0].shape[0]
    parts = len(refs) * count // out_ref.shape[0]
    for i in range(out_ref.shape[0] // count):
        keep_ref, swapped_ref, *got = refs[i * parts : (i + 1) * parts]
        total = keep_ref[...] + swapped_ref[:, column : column + width].astype(F32)
        for ref in got:
            total = total + ref[...].astype(F32)
        out_ref[i * count : (i + 1) * count, :] = total.astype(BF16)


def spread_kernel(n_time, at_ref, keep_ref, swapped_ref, *refs):
    got, outs = refs[: -n_time - 1], refs[-n_time:]
    capacity = outs[0].shape[0]
    for s, out_ref in enumerate(outs):
        place = at_ref[0] + s
        place = jnp.where(place >= n_time, place - n_time, place)
        at = pl.ds(pl.multiple_of(place * capacity, capacity), capacity)
        total = keep_ref[at, :] + swapped_ref[at, :].astype(F32)
        for ref in got:
            total = total + ref[at, :].astype(F32)
        out_ref[...] = total.astype(BF16)


def combine_kernel(local, at_ref, targets_ref, gates_ref, base_ref, *refs):
    if len(refs) == 2:
        back_ref, out_ref = refs
    else:
        *got, out_ref, back_ref = refs
        n_time, capacity = len(got), got[0].shape[0]
        for s, ref in enumerate(got):
            place = at_ref[0] - s
            place = jnp.where(place < 0, place + n_time, place)
            back_ref[pl.ds(pl.multiple_of(place * capacity, capacity), capacity), :] = ref[...]
    back = back_ref[...]
    rows = back.shape[0]
    frames = targets_ref.shape[0]
    places = lax.broadcasted_iota(jnp.int32, (frames, rows), 1) + local * rows
    total = base_ref[...].astype(F32)
    for k in range(TOP):
        pick = jnp.where(places == targets_ref[:, k : k + 1], 1.0, 0.0).astype(BF16)
        total = total + gates_ref[:, k : k + 1] * jnp.dot(pick, back, preferred_element_type=F32)
    out_ref[...] = total.astype(out_ref.dtype)


def per_device(
    frames_in,
    queries,
    keys,
    values,
    segment_edges,
    out_proj,
    expert_ids,
    gates,
    w_gate,
    w_up,
    w_down,
):
    frames, model = frames_in.shape
    width = queries.shape[1]
    n_model = lax.axis_size("mp")
    n_time = lax.axis_size("tm")
    chips = n_model // 2
    head_width = model // HEADS
    scale = head_width ** (-0.5)
    local_experts = w_gate.shape[0]
    hidden = w_gate.shape[2]
    experts_all = local_experts * n_time
    capacity = 4 * frames // experts_all
    rows = n_time * capacity
    lanes = -(-experts_all // LANES) * LANES
    at_time = lax.axis_index("tm")
    at_model = lax.axis_index("mp")
    chip, core = at_model // 2, at_model % 2
    mine = [((chip - by) % chips) * 2 + core for by in range(chips)]
    others = [((chip - by) % chips) * 2 + 1 - core for by in range(chips)]
    order = jnp.stack(mine + others).astype(jnp.int32)
    offset = (at_time * frames).astype(jnp.int32).reshape(1)
    place = at_time.astype(jnp.int32).reshape(1)
    away = (chips - 1) * width

    tails = from_behind(jnp.stack([keys[frames - LEFT :], values[frames - LEFT :]], 0), "tm", 1)
    own_frames = lax.dynamic_slice_in_dim(frames_in, at_model * width, width, 1)

    ranks, targets = pl.pallas_call(
        functools.partial(route_kernel, capacity, local_experts, n_time),
        out_shape=(
            jax.ShapeDtypeStruct((lanes, frames), F32),
            jax.ShapeDtypeStruct((frames, TOP), jnp.int32),
        ),
        in_specs=[VMEM],
        out_specs=(VMEM, VMEM),
        compiler_params=params(16),
        cost_estimate=cost(2 * frames * frames * lanes, frames * 1024),
        name="route",
    )(expert_ids)

    def in_hbm(*arrays):
        return [pltpu.with_memory_space_constraint(x, pltpu.HBM) for x in arrays]

    def attend(start, end, *extra):
        count = end - start
        return pl.pallas_call(
            functools.partial(attend_kernel, scale, head_width, start),
            out_shape=(
                jax.ShapeDtypeStruct((count, chips * width), BF16),
                jax.ShapeDtypeStruct((count, away), F32),
                jax.ShapeDtypeStruct((count, width), F32),
            ),
            in_specs=[SMEM, SMEM] + [HBM] * 5 + [ANY] * len(extra),
            out_specs=(VMEM,) * 3,
            scratch_shapes=[
                pltpu.VMEM((2, frames), jnp.int32),
                pltpu.VMEM((count, width), BF16),
                pltpu.VMEM((LEFT + count, width), BF16),
                pltpu.VMEM((LEFT + count, width), BF16),
                pltpu.VMEM(out_proj.shape, BF16),
                pltpu.SemaphoreType.DMA((7,)),
            ],
            compiler_params=params(16),
            cost_estimate=cost(count * 384 * width * 16, count * width * 8, count * 384 * 4),
            name=f"attend_{start}",
        )(offset, order, *in_hbm(segment_edges, queries, keys, values, out_proj), *extra)

    def add(name, keep, got, after):
        count = keep.shape[0]
        return pl.pallas_call(
            functools.partial(add_kernel, width, len(got)),
            in_specs=[VMEM] * (1 + len(got)) + [ANY],
            out_specs=(VMEM,) * (chips - 1),
            out_shape=(jax.ShapeDtypeStruct((count, width), BF16),) * (chips - 1),
            compiler_params=params(16),
            cost_estimate=cost(keep.size, keep.size * 8),
            name=f"add_{name}",
        )(keep, *got, after)

    def from_chips(parts):
        return [from_chip(part, chips - by) for by, part in enumerate(parts, 1)]

    def attended(name, send, keep_x, keep):
        swapped = core_swap(send)
        return [keep, swapped, *from_chips(add(name, keep_x, [swapped], swapped))]

    late = attended("late", *attend(LEFT, frames))
    early = attended("early", *attend(0, LEFT, tails))

    state, outgoing_0 = pl.pallas_call(
        functools.partial(state_kernel, len(early), away, capacity),
        out_shape=(
            jax.ShapeDtypeStruct((frames, width), BF16),
            jax.ShapeDtypeStruct((rows, width), BF16),
        ),
        in_specs=[VMEM] * (2 * len(early) + 2),
        out_specs=(VMEM, VMEM),
        compiler_params=params(16),
        cost_estimate=cost(2 * frames * width * rows, 4 * MIB),
        name="state",
    )(*early, *late, own_frames, ranks)

    def dispatch(local, parts):
        columns = width * len(parts)
        return pl.pallas_call(
            functools.partial(dispatch_kernel, local, capacity, len(parts)),
            out_shape=jax.ShapeDtypeStruct((rows, columns), BF16),
            in_specs=[VMEM] * (len(parts) + 1),
            out_specs=VMEM,
            compiler_params=params(16),
            cost_estimate=cost(2 * frames * columns * rows, 3 * MIB),
            name=f"dispatch_{local}",
        )(*parts, ranks)

    def over_time(x):
        columns = x.shape[1]
        x = x.reshape(n_time, capacity, columns)
        x = lax.all_to_all(x, "tm", split_axis=0, concat_axis=0, tiled=True)
        return x.reshape(rows, columns)

    def take(x, after):
        return pl.pallas_call(
            take_kernel,
            in_specs=[VMEM] + [ANY] * len(after),
            out_specs=VMEM,
            out_shape=jax.ShapeDtypeStruct(x.shape, x.dtype),
            compiler_params=params(16),
            cost_estimate=cost(x.size, x.size * 4),
            name="take",
        )(x, *after)

    def experts(local, parts, starts, count, pieces, after):
        send = [(count // pieces, away)] * pieces + [(count, width)]
        outs = [jax.ShapeDtypeStruct(shape, BF16) for shape in send]
        outs += [jax.ShapeDtypeStruct((count, columns), F32) for columns in (away, width)]
        return pl.pallas_call(
            functools.partial(expert_kernel, local, starts, width, len(after)),
            in_specs=[SMEM] + [VMEM] * len(parts) + [HBM] * 3 + [ANY] * len(after),
            out_specs=(VMEM,) * len(outs),
            scratch_shapes=[
                pltpu.VMEM((model, hidden), BF16),
                pltpu.VMEM((model, hidden), BF16),
                pltpu.VMEM((hidden, model), BF16),
                pltpu.VMEM((count, model), BF16),
                pltpu.VMEM((count, hidden), BF16),
                pltpu.SemaphoreType.DMA((3,)),
            ],
            out_shape=tuple(outs),
            compiler_params=params(20),
            cost_estimate=cost(6 * count * model * hidden, 12 * MIB, count * hidden),
            name=f"experts_{local}_{starts[0]}",
        )(order, *parts, *in_hbm(w_gate, w_up, w_down), *after)

    def total(local, column, parts):
        return pl.pallas_call(
            functools.partial(total_kernel, column),
            in_specs=[VMEM] * len(parts),
            out_specs=VMEM,
            out_shape=jax.ShapeDtypeStruct((rows, width), BF16),
            compiler_params=params(16),
            cost_estimate=cost(rows * width * 4, rows * width * 10),
            name=f"total_{local}",
        )(*parts)

    def spread(local, parts, after):
        return pl.pallas_call(
            functools.partial(spread_kernel, n_time),
            in_specs=[SMEM] + [VMEM] * len(parts) + [ANY],
            out_specs=(VMEM,) * n_time,
            out_shape=(jax.ShapeDtypeStruct((capacity, width), BF16),) * n_time,
            compiler_params=params(16),
            cost_estimate=cost(rows * width * 4, rows * width * 10),
            name=f"spread_{local}",
        )(place, *parts, after)

    def combine(local, back, base):
        last = local == local_experts - 1
        apart = [pltpu.VMEM((rows, width), BF16)] if len(back) > 1 else []
        return pl.pallas_call(
            functools.partial(combine_kernel, local),
            out_shape=jax.ShapeDtypeStruct((frames, width), BF16 if last else F32),
            in_specs=[SMEM] + [VMEM] * (3 + len(back)),
            out_specs=VMEM,
            scratch_shapes=apart,
            compiler_params=params(16),
            cost_estimate=cost(4 * frames * width * rows, 3 * MIB),
            name=f"combine_{local}",
        )(place, targets, gates, base, *back)

    half = rows // 2
    arrived_0 = over_time(outgoing_0)
    wide = [state] + [from_chip(state, by) for by in range(1, chips)]
    outgoing_1 = dispatch(1, wide)
    arrived_1 = over_time(outgoing_1)
    other_core = core_swap(arrived_0)
    after = [outgoing_1]
    sums = []
    for at in (0, half):
        part = arrived_0[at : at + half]
        others = [from_chip(part, by) for by in range(1, chips)]
        parts = [arrived_0, *others, other_core, *[core_swap(x) for x in others]]
        starts = (at, *[0] * len(others), at, *[0] * len(others))
        *send_x, send, keep_x, keep = experts(0, parts, starts, half, 2, after)
        away_sums = add(f"0_{at}", keep_x, [core_swap(x) for x in send_x], send)
        got = from_chips(away_sums)
        sums += [keep, core_swap(send), *got]
        after = [away_sums[0]]
    arrived_1 = take(arrived_1, [send, sums[2]])
    parts = [arrived_1, core_swap(arrived_1)]
    *send_x, send, keep_x, keep = experts(1, parts, (0, 0), rows, 2, after)
    total_0 = total(0, 0, sums)
    back_0 = over_time(total_0)
    got = from_chips(add("1", keep_x, [core_swap(x) for x in send_x], total_0))
    back_1 = exchanged(spread(1, [keep, core_swap(send), *got], back_0))
    return combine(1, back_1, combine(0, [back_0], state))


def solution(mesh):
    return jax.shard_map(
        per_device,
        mesh=mesh,
        in_specs=(
            P("tm", None),
            P("tm", "mp"),
            P("tm", "mp"),
            P("tm", "mp"),
            P(None, "tm"),
            P("mp", None),
            P("tm", None),
            P("tm", None),
            P("tm", None, "mp"),
            P("tm", None, "mp"),
            P("tm", "mp", None),
        ),
        out_specs=P("tm", "mp"),
        check_vma=False,
    )
```

```python
import functools

import jax
import jax.numpy as jnp
from jax import lax
from jax.experimental import pallas as pl
from jax.experimental.pallas import tpu as pltpu
from jax.sharding import PartitionSpec as P

HEADS = 16
TOP = 2
LEFT = 256
EPS = 1e-06
LANES = 128
MIB = 1 << 20
F32 = jnp.float32
BF16 = jnp.bfloat16

VMEM = pl.BlockSpec(memory_space=pltpu.VMEM)
SMEM = pl.BlockSpec(memory_space=pltpu.SMEM)
ANY = pl.BlockSpec(memory_space=pl.ANY)
HBM = pl.BlockSpec(memory_space=pltpu.HBM)


def params(mib):
    return pltpu.CompilerParams(vmem_limit_bytes=mib * MIB)


def cost(flops, moved, transcendentals=0):
    return pl.CostEstimate(flops=flops, bytes_accessed=moved, transcendentals=transcendentals)


def from_behind(x, axis, by):
    size = lax.axis_size(axis)
    pairs = [(i, i + by) for i in range(size) if 0 <= i + by < size]
    return lax.ppermute(x, axis, pairs)


def core_swap(x):
    size = lax.axis_size("mp")
    return lax.ppermute(x, "mp", [(i, i ^ 1) for i in range(size)])


def from_chip(x, by):
    chips = lax.axis_size("mp") // 2
    pairs = [(c * 2 + k, ((c + by) % chips) * 2 + k) for c in range(chips) for k in range(2)]
    return lax.ppermute(x, "mp", pairs)


def gathered(x):
    chips = lax.axis_size("mp") // 2
    mine = [x] + [from_chip(x, by) for by in range(1, chips)]
    return mine + [core_swap(part) for part in mine]


def exchanged(blocks):
    size = lax.axis_size("tm")
    return [blocks[0]] + [
        lax.ppermute(block, "tm", [(i, (i + s) % size) for i in range(size)])
        for s, block in enumerate(blocks)
        if s > 0
    ]


def route_kernel(capacity, local_experts, n_time, ids_ref, ranks_ref, targets_ref):
    frames = ids_ref.shape[0]
    lanes = ranks_ref.shape[0]
    ids = ids_ref[...]
    owner = ids // local_experts
    ids = (ids - owner * local_experts) * n_time + owner
    experts = lax.broadcasted_iota(jnp.int32, (frames, lanes), 1)
    hits = [ids[:, k : k + 1] == experts for k in range(TOP)]
    named = functools.reduce(jnp.logical_or, hits)
    ones = jnp.where(named, 1.0, 0.0).astype(BF16)
    row = lax.broadcasted_iota(jnp.int32, (frames, frames), 0)
    column = lax.broadcasted_iota(jnp.int32, (frames, frames), 1)
    before = jnp.where(column < row, 1.0, 0.0).astype(BF16)
    ranks = jnp.dot(before, ones, preferred_element_type=F32)
    ranks_ref[...] = jnp.where(named, ranks, -1.0).T
    places = []
    for k in range(TOP):
        slot = jnp.sum(jnp.where(hits[k], ranks, 0.0), 1, keepdims=True).astype(jnp.int32)
        places.append(ids[:, k : k + 1] * capacity + slot)
    targets_ref[...] = jnp.concatenate(places, 1)


def attend_kernel(scale, head_width, start, meta_ref, order_ref, *refs):
    tails_any = refs[5] if start == 0 else None
    edges_any, q_any, k_any, v_any, proj_any = refs[:5]
    refs = refs[6:] if start == 0 else refs[5:]
    send_ref, keep_x_ref, keep_ref, edges_ref, q_ref, k_ref, v_ref, proj_ref, sems = refs
    rows, columns = q_ref.shape
    heads = columns // head_width
    block = LANES
    window = LEFT + block
    if start == 0:
        moves = [
            (q_any.at[pl.ds(0, rows)], q_ref),
            (tails_any.at[0], k_ref.at[pl.ds(0, LEFT)]),
            (k_any.at[pl.ds(0, rows)], k_ref.at[pl.ds(LEFT, rows)]),
            (tails_any.at[1], v_ref.at[pl.ds(0, LEFT)]),
            (v_any.at[pl.ds(0, rows)], v_ref.at[pl.ds(LEFT, rows)]),
            (edges_any, edges_ref),
            (proj_any, proj_ref),
        ]
    else:
        moves = [
            (q_any.at[pl.ds(start, rows)], q_ref),
            (k_any.at[pl.ds(start - LEFT, rows + LEFT)], k_ref),
            (v_any.at[pl.ds(start - LEFT, rows + LEFT)], v_ref),
            (edges_any, edges_ref),
            (proj_any, proj_ref),
        ]
    copies = [pltpu.make_async_copy(a, b, sems.at[i]) for i, (a, b) in enumerate(moves)]
    for copy in copies:
        copy.start()
    for copy in copies[:-1]:
        copy.wait()
    edges = edges_ref[:, start : start + rows].astype(F32)
    edges = jnp.concatenate([edges, jnp.zeros((6, rows), F32)], 0).T
    lane_head = lax.broadcasted_iota(jnp.int32, (block, columns), 1) // head_width
    context = []
    for r in range(0, rows, block):
        key = k_ref[r : r + window, :]
        value = v_ref[r : r + window, :]
        query = q_ref[r : r + block, :]
        places = lax.broadcasted_iota(jnp.int32, (block, window), 1)
        places = (places + (meta_ref[0] + (start + r - LEFT))).astype(F32)
        lower = jnp.maximum(edges[r : r + block, 0:1] - LEFT, 0.0)
        upper = edges[r : r + block, 1:2]
        visible = (places >= lower) & (places <= upper)
        own = [jnp.where(lane_head == h, query, jnp.zeros_like(query)) for h in range(heads)]
        own = jnp.concatenate(own, 0)
        scores = lax.dot_general(own, key, (((1,), (1,)), ((), ())), preferred_element_type=F32)
        scores = (scores * scale).reshape(heads, block, window)
        scores = jnp.where(visible[None], scores, -1e30)
        highest = jnp.max(scores, 2, keepdims=True)
        expos = jnp.exp(scores - highest)
        weights = (expos * (1.0 / jnp.sum(expos, 2, keepdims=True))).astype(BF16)
        weights = weights.reshape(heads * block, window)
        product = jnp.dot(weights, value, preferred_element_type=F32)
        mixed = product[0:block]
        for h in range(1, heads):
            mixed = jnp.where(lane_head == h, product[h * block : (h + 1) * block], mixed)
        context.append(mixed.astype(BF16))
    context = jnp.concatenate(context, 0)
    copies[-1].wait()
    count = proj_ref.shape[1] // columns // 2
    for i in range(2 * count):
        at = pl.multiple_of(order_ref[i] * columns, columns)
        part = jnp.dot(context, proj_ref[:, pl.ds(at, columns)], preferred_element_type=F32)
        j = (i - 1) % count * columns
        if i >= count:
            send_ref[:, j : j + columns] = part.astype(BF16)
        elif i > 0:
            keep_x_ref[:, j : j + columns] = part
        else:
            keep_ref[...] = part


def scatter_rows(local, capacity, ranks_ref, state, out_ref):
    frames = state.shape[0]
    n_time = out_ref.shape[0] // capacity
    slot = lax.broadcasted_iota(jnp.int32, (capacity, frames), 0).astype(F32)
    for owner in range(n_time):
        e = local * n_time + owner
        pick = jnp.where(slot == ranks_ref[e : e + 1, :], 1.0, 0.0).astype(BF16)
        rows = jnp.dot(pick, state, preferred_element_type=F32)
        out_ref[owner * capacity : (owner + 1) * capacity, :] = rows.astype(BF16)


def state_kernel(parts, column, capacity, *refs):
    frames_ref, ranks_ref, state_ref = refs[2 * parts : 2 * parts + 3]
    width = state_ref.shape[1]
    halves = []
    for keep_ref, swapped_ref, *got in (refs[:parts], refs[parts : 2 * parts]):
        half = keep_ref[...] + swapped_ref[:, column : column + width].astype(F32)
        for ref in got:
            half = half + ref[...].astype(F32)
        halves.append(half)
    attended = jnp.concatenate(halves, 0)
    state = (frames_ref[...].astype(F32) + attended).astype(BF16)
    state_ref[...] = state
    scatter_rows(0, capacity, ranks_ref, state, refs[2 * parts + 3])


def dispatch_kernel(local, capacity, pieces, *refs):
    state = jnp.concatenate([ref[...] for ref in refs[:pieces]], 1)
    scatter_rows(local, capacity, refs[pieces], state, refs[pieces + 1])


def take_kernel(rows_ref, *refs):
    refs[-1][...] = rows_ref[...]


def expert_kernel(local, arrays, awaited, width, order_ref, *refs):
    rows_any = refs[:arrays]
    gate_any, up_any, down_any = refs[arrays : arrays + 3]
    send_x_ref, send_ref, keep_x_any, keep_any = refs[arrays + 3 + awaited : arrays + 7 + awaited]
    scratch = refs[arrays + 7 + awaited :]
    rows_in = scratch[:arrays]
    gate_ref, up_ref, down_ref, active_ref, keep_x_ref, keep_ref, sems = scratch[arrays:]
    model = gate_ref.shape[0]
    rows, hidden = active_ref.shape
    blocks = model // width
    count = blocks // 2

    copies = []

    def copy(source, target):
        copies.append(pltpu.make_async_copy(source, target, sems.at[len(copies)]))
        copies[-1].start()

    for source, target in zip(rows_any, rows_in):
        copy(source, target)
    for source, target in ((gate_any, gate_ref), (up_any, up_ref)):
        for i in range(blocks):
            at = pl.multiple_of(order_ref[i] * width, width)
            copy(source.at[local, pl.ds(at, width)], target.at[pl.ds(i * width, width)])
    copy(down_any.at[local], down_ref)
    for each in copies[: arrays + blocks]:
        each.wait()

    state = jnp.concatenate([ref[...] for ref in rows_in], 1)
    squares = sum(
        jnp.sum(jnp.square(ref[...].astype(F32)), 1, keepdims=True) for ref in rows_in
    )
    factor = lax.rsqrt(squares * (1.0 / model) + EPS)
    chunk = min(hidden, 256)
    for c in range(0, hidden, chunk):
        gate = jnp.dot(state, gate_ref[:, c : c + chunk], preferred_element_type=F32) * factor
        if c == 0:
            for each in copies[arrays + blocks : arrays + 2 * blocks]:
                each.wait()
        up = jnp.dot(state, up_ref[:, c : c + chunk], preferred_element_type=F32) * factor
        half = 0.5 * gate
        active = (half + half * jnp.tanh(half)) * up
        active_ref[:, c : c + chunk] = active.astype(BF16)
    copies[arrays + 2 * blocks].wait()

    def project(i, out_ref, column):
        at = pl.multiple_of(order_ref[i] * width, width)
        weight = down_ref[:, pl.ds(at, width)]
        result = jnp.dot(active_ref[...], weight, preferred_element_type=F32)
        out_ref[:, column : column + width] = result.astype(out_ref.dtype)

    for by in range(1, count):
        project(by, keep_x_ref, (by - 1) * width)
    copy(keep_x_ref, keep_x_any)
    project(0, keep_ref, 0)
    copy(keep_ref, keep_any)
    for by in range(1, count):
        project(count + by, send_x_ref, (by - 1) * width)
    project(count, send_ref, 0)
    for each in copies[-2:]:
        each.wait()


def add_kernel(width, keep_any, got_ref, after_any, *refs):
    *out_refs, keep_ref, sem = refs
    copy = pltpu.make_async_copy(keep_any, keep_ref, sem)
    copy.start()
    copy.wait()
    for i, out_ref in enumerate(out_refs):
        at = slice(i * width, (i + 1) * width)
        out_ref[...] = (keep_ref[:, at] + got_ref[:, at].astype(F32)).astype(BF16)


def total_kernel(*refs):
    keep_ref, *got, after_any, out_ref = refs
    total = keep_ref[...]
    for ref in got:
        total = total + ref[...].astype(F32)
    out_ref[...] = total.astype(BF16)


def spread_kernel(n_time, at_ref, keep_ref, swapped_ref, *refs):
    got, outs = refs[: -n_time - 1], refs[-n_time:]
    capacity = outs[0].shape[0]
    for s, out_ref in enumerate(outs):
        place = at_ref[0] + s
        place = jnp.where(place >= n_time, place - n_time, place)
        at = pl.ds(pl.multiple_of(place * capacity, capacity), capacity)
        total = keep_ref[at, :] + swapped_ref[at, :].astype(F32)
        for ref in got:
            total = total + ref[at, :].astype(F32)
        out_ref[...] = total.astype(BF16)


def combine_kernel(local, at_ref, targets_ref, gates_ref, base_ref, *refs):
    if len(refs) == 2:
        back_ref, out_ref = refs
    else:
        *got, out_ref, back_ref = refs
        n_time, capacity = len(got), got[0].shape[0]
        for s, ref in enumerate(got):
            place = at_ref[0] - s
            place = jnp.where(place < 0, place + n_time, place)
            back_ref[pl.ds(pl.multiple_of(place * capacity, capacity), capacity), :] = ref[...]
    back = back_ref[...]
    rows = back.shape[0]
    frames = targets_ref.shape[0]
    places = lax.broadcasted_iota(jnp.int32, (frames, rows), 1) + local * rows
    total = base_ref[...].astype(F32)
    for k in range(TOP):
        pick = jnp.where(places == targets_ref[:, k : k + 1], 1.0, 0.0).astype(BF16)
        total = total + gates_ref[:, k : k + 1] * jnp.dot(pick, back, preferred_element_type=F32)
    out_ref[...] = total.astype(out_ref.dtype)


def per_device(
    frames_in,
    queries,
    keys,
    values,
    segment_edges,
    out_proj,
    expert_ids,
    gates,
    w_gate,
    w_up,
    w_down,
):
    frames, model = frames_in.shape
    width = queries.shape[1]
    n_model = lax.axis_size("mp")
    n_time = lax.axis_size("tm")
    chips = n_model // 2
    head_width = model // HEADS
    scale = head_width ** (-0.5)
    local_experts = w_gate.shape[0]
    hidden = w_gate.shape[2]
    experts_all = local_experts * n_time
    capacity = 4 * frames // experts_all
    rows = n_time * capacity
    lanes = -(-experts_all // LANES) * LANES
    at_time = lax.axis_index("tm")
    at_model = lax.axis_index("mp")
    chip, core = at_model // 2, at_model % 2
    mine = [((chip - by) % chips) * 2 + core for by in range(chips)]
    others = [((chip - by) % chips) * 2 + 1 - core for by in range(chips)]
    order = jnp.stack(mine + others).astype(jnp.int32)
    offset = (at_time * frames).astype(jnp.int32).reshape(1)
    place = at_time.astype(jnp.int32).reshape(1)
    away = (chips - 1) * width

    tails = from_behind(jnp.stack([keys[frames - LEFT :], values[frames - LEFT :]], 0), "tm", 1)
    own_frames = lax.dynamic_slice_in_dim(frames_in, at_model * width, width, 1)

    ranks, targets = pl.pallas_call(
        functools.partial(route_kernel, capacity, local_experts, n_time),
        out_shape=(
            jax.ShapeDtypeStruct((lanes, frames), F32),
            jax.ShapeDtypeStruct((frames, TOP), jnp.int32),
        ),
        in_specs=[VMEM],
        out_specs=(VMEM, VMEM),
        compiler_params=params(16),
        cost_estimate=cost(2 * frames * frames * lanes, frames * 1024),
        name="route",
    )(expert_ids)

    def in_hbm(*arrays):
        return [pltpu.with_memory_space_constraint(x, pltpu.HBM) for x in arrays]

    def attend(start, end, *extra):
        count = end - start
        return pl.pallas_call(
            functools.partial(attend_kernel, scale, head_width, start),
            out_shape=(
                jax.ShapeDtypeStruct((count, chips * width), BF16),
                jax.ShapeDtypeStruct((count, away), F32),
                jax.ShapeDtypeStruct((count, width), F32),
            ),
            in_specs=[SMEM, SMEM] + [HBM] * 5 + [ANY] * len(extra),
            out_specs=(VMEM,) * 3,
            scratch_shapes=[
                pltpu.VMEM((2, frames), jnp.int32),
                pltpu.VMEM((count, width), BF16),
                pltpu.VMEM((LEFT + count, width), BF16),
                pltpu.VMEM((LEFT + count, width), BF16),
                pltpu.VMEM(out_proj.shape, BF16),
                pltpu.SemaphoreType.DMA((7,)),
            ],
            compiler_params=params(16),
            cost_estimate=cost(count * 384 * width * 16, count * width * 8, count * 384 * 4),
            name=f"attend_{start}",
        )(offset, order, *in_hbm(segment_edges, queries, keys, values, out_proj), *extra)

    def add(name, keep, got, after):
        count = keep.shape[0]
        return pl.pallas_call(
            functools.partial(add_kernel, width),
            in_specs=[ANY, VMEM, ANY],
            out_specs=(VMEM,) * (chips - 1),
            out_shape=(jax.ShapeDtypeStruct((count, width), BF16),) * (chips - 1),
            scratch_shapes=[pltpu.VMEM(keep.shape, F32), pltpu.SemaphoreType.DMA],
            compiler_params=params(16),
            cost_estimate=cost(keep.size, keep.size * 8),
            name=f"add_{name}",
        )(keep, got, after)

    def from_chips(parts):
        return [from_chip(part, chips - by) for by, part in enumerate(parts, 1)]

    def attended(name, send, keep_x, keep):
        swapped = core_swap(send)
        return [keep, swapped, *from_chips(add(name, keep_x, swapped, swapped))]

    late = attended("late", *attend(LEFT, frames))
    early = attended("early", *attend(0, LEFT, tails))

    state, outgoing_0 = pl.pallas_call(
        functools.partial(state_kernel, len(early), away, capacity),
        out_shape=(
            jax.ShapeDtypeStruct((frames, width), BF16),
            jax.ShapeDtypeStruct((rows, width), BF16),
        ),
        in_specs=[VMEM] * (2 * len(early) + 2),
        out_specs=(VMEM, VMEM),
        compiler_params=params(16),
        cost_estimate=cost(2 * frames * width * rows, 4 * MIB),
        name="state",
    )(*early, *late, own_frames, ranks)

    def dispatch(local, parts):
        columns = width * len(parts)
        return pl.pallas_call(
            functools.partial(dispatch_kernel, local, capacity, len(parts)),
            out_shape=jax.ShapeDtypeStruct((rows, columns), BF16),
            in_specs=[VMEM] * (len(parts) + 1),
            out_specs=VMEM,
            compiler_params=params(16),
            cost_estimate=cost(2 * frames * columns * rows, 3 * MIB),
            name=f"dispatch_{local}",
        )(*parts, ranks)

    def over_time(x):
        columns = x.shape[1]
        x = x.reshape(n_time, capacity, columns)
        x = lax.all_to_all(x, "tm", split_axis=0, concat_axis=0, tiled=True)
        return x.reshape(rows, columns)

    def take(x, after):
        return pl.pallas_call(
            take_kernel,
            in_specs=[VMEM] + [ANY] * len(after),
            out_specs=VMEM,
            out_shape=jax.ShapeDtypeStruct(x.shape, x.dtype),
            compiler_params=params(16),
            cost_estimate=cost(x.size, x.size * 4),
            name="take",
        )(x, *after)

    def experts(local, parts, after):
        outs = [jax.ShapeDtypeStruct((rows, columns), BF16) for columns in (away, width)]
        outs += [jax.ShapeDtypeStruct((rows, columns), F32) for columns in (away, width)]
        return pl.pallas_call(
            functools.partial(expert_kernel, local, len(parts), len(after), width),
            in_specs=[SMEM] + [ANY] * len(parts) + [HBM] * 3 + [ANY] * len(after),
            out_specs=(VMEM, VMEM, ANY, ANY),
            scratch_shapes=[pltpu.VMEM(part.shape, BF16) for part in parts]
            + [
                pltpu.VMEM((model, hidden), BF16),
                pltpu.VMEM((model, hidden), BF16),
                pltpu.VMEM((hidden, model), BF16),
                pltpu.VMEM((rows, hidden), BF16),
                pltpu.VMEM((rows, away), F32),
                pltpu.VMEM((rows, width), F32),
                pltpu.SemaphoreType.DMA((len(parts) + 2 * n_model + 3,)),
            ],
            out_shape=tuple(outs),
            compiler_params=params(28),
            cost_estimate=cost(6 * rows * model * hidden, 12 * MIB, rows * hidden),
            name=f"experts_{local}",
        )(order, *parts, *in_hbm(w_gate, w_up, w_down), *after)

    def total(local, parts, after):
        return pl.pallas_call(
            total_kernel,
            in_specs=[VMEM] * len(parts) + [ANY],
            out_specs=VMEM,
            out_shape=jax.ShapeDtypeStruct((rows, width), BF16),
            compiler_params=params(16),
            cost_estimate=cost(rows * width * 4, rows * width * 10),
            name=f"total_{local}",
        )(*parts, after)

    def spread(local, parts, after):
        return pl.pallas_call(
            functools.partial(spread_kernel, n_time),
            in_specs=[SMEM] + [VMEM] * len(parts) + [ANY],
            out_specs=(VMEM,) * n_time,
            out_shape=(jax.ShapeDtypeStruct((capacity, width), BF16),) * n_time,
            compiler_params=params(16),
            cost_estimate=cost(rows * width * 4, rows * width * 10),
            name=f"spread_{local}",
        )(place, *parts, after)

    def combine(local, back, base):
        last = local == local_experts - 1
        apart = [pltpu.VMEM((rows, width), BF16)] if len(back) > 1 else []
        return pl.pallas_call(
            functools.partial(combine_kernel, local),
            out_shape=jax.ShapeDtypeStruct((frames, width), BF16 if last else F32),
            in_specs=[SMEM] + [VMEM] * (3 + len(back)),
            out_specs=VMEM,
            scratch_shapes=apart,
            compiler_params=params(16),
            cost_estimate=cost(4 * frames * width * rows, 3 * MIB),
            name=f"combine_{local}",
        )(place, targets, gates, base, *back)

    arrived_0 = over_time(outgoing_0)
    wide = [state] + [from_chip(state, by) for by in range(1, chips)]
    outgoing_1 = dispatch(1, wide)
    arrived_1 = over_time(outgoing_1)
    send_x_0, send_0, keep_x_0, keep_0 = experts(0, gathered(arrived_0), [outgoing_1])
    away_0 = add("0", keep_x_0, core_swap(send_x_0), send_0)
    got_0 = from_chips(away_0)
    arrived_1 = take(arrived_1, [send_0])
    parts = [arrived_1, core_swap(arrived_1)]
    send_x_1, send_1, keep_x_1, keep_1 = experts(1, parts, [away_0[0]])
    total_0 = total(0, [keep_0, core_swap(send_0), *got_0], send_1)
    back_0 = over_time(total_0)
    got_1 = from_chips(add("1", keep_x_1, core_swap(send_x_1), total_0))
    back_1 = exchanged(spread(1, [keep_1, core_swap(send_1), *got_1], back_0))
    return combine(1, back_1, combine(0, [back_0], state))


def solution(mesh):
    return jax.shard_map(
        per_device,
        mesh=mesh,
        in_specs=(
            P("tm", None),
            P("tm", "mp"),
            P("tm", "mp"),
            P("tm", "mp"),
            P(None, "tm"),
            P("mp", None),
            P("tm", None),
            P("tm", None),
            P("tm", None, "mp"),
            P("tm", None, "mp"),
            P("tm", "mp", None),
        ),
        out_specs=P("tm", "mp"),
        check_vma=False,
    )
```

```python
import functools

import jax
import jax.numpy as jnp
from jax import lax
from jax.experimental import pallas as pl
from jax.experimental.pallas import tpu as pltpu
from jax.sharding import PartitionSpec as P

HEADS = 16
TOP = 2
LEFT = 256
EPS = 1e-06
LANES = 128
MIB = 1 << 20
F32 = jnp.float32
BF16 = jnp.bfloat16

VMEM = pl.BlockSpec(memory_space=pltpu.VMEM)
SMEM = pl.BlockSpec(memory_space=pltpu.SMEM)
ANY = pl.BlockSpec(memory_space=pl.ANY)
HBM = pl.BlockSpec(memory_space=pltpu.HBM)


def params(mib):
    return pltpu.CompilerParams(vmem_limit_bytes=mib * MIB)


def cost(flops, moved, transcendentals=0):
    return pl.CostEstimate(flops=flops, bytes_accessed=moved, transcendentals=transcendentals)


def from_behind(x, axis, by):
    size = lax.axis_size(axis)
    pairs = [(i, i + by) for i in range(size) if 0 <= i + by < size]
    return lax.ppermute(x, axis, pairs)


def core_swap(x):
    size = lax.axis_size("mp")
    return lax.ppermute(x, "mp", [(i, i ^ 1) for i in range(size)])


def from_chip(x, by):
    chips = lax.axis_size("mp") // 2
    pairs = [(c * 2 + k, ((c + by) % chips) * 2 + k) for c in range(chips) for k in range(2)]
    return lax.ppermute(x, "mp", pairs)


def gathered(x):
    chips = lax.axis_size("mp") // 2
    mine = [x] + [from_chip(x, by) for by in range(1, chips)]
    return mine + [core_swap(part) for part in mine]


def exchanged(blocks):
    size = lax.axis_size("tm")
    return [blocks[0]] + [
        lax.ppermute(block, "tm", [(i, (i + s) % size) for i in range(size)])
        for s, block in enumerate(blocks)
        if s > 0
    ]


def route_kernel(capacity, local_experts, n_time, ids_ref, ranks_ref, targets_ref):
    frames = ids_ref.shape[0]
    lanes = ranks_ref.shape[0]
    ids = ids_ref[...]
    owner = ids // local_experts
    ids = (ids - owner * local_experts) * n_time + owner
    experts = lax.broadcasted_iota(jnp.int32, (frames, lanes), 1)
    hits = [ids[:, k : k + 1] == experts for k in range(TOP)]
    named = functools.reduce(jnp.logical_or, hits)
    ones = jnp.where(named, 1.0, 0.0).astype(BF16)
    row = lax.broadcasted_iota(jnp.int32, (frames, frames), 0)
    column = lax.broadcasted_iota(jnp.int32, (frames, frames), 1)
    before = jnp.where(column < row, 1.0, 0.0).astype(BF16)
    ranks = jnp.dot(before, ones, preferred_element_type=F32)
    ranks_ref[...] = jnp.where(named, ranks, -1.0).T
    places = []
    for k in range(TOP):
        slot = jnp.sum(jnp.where(hits[k], ranks, 0.0), 1, keepdims=True).astype(jnp.int32)
        places.append(ids[:, k : k + 1] * capacity + slot)
    targets_ref[...] = jnp.concatenate(places, 1)


def attend_kernel(scale, head_width, start, meta_ref, order_ref, *refs):
    tails_any = refs[5] if start == 0 else None
    edges_any, q_any, k_any, v_any, proj_any = refs[:5]
    refs = refs[6:] if start == 0 else refs[5:]
    send_ref, keep_x_ref, keep_ref, edges_ref, q_ref, k_ref, v_ref, proj_ref, sems = refs
    rows, columns = q_ref.shape
    heads = columns // head_width
    block = LANES
    window = LEFT + block
    if start == 0:
        moves = [
            (q_any.at[pl.ds(0, rows)], q_ref),
            (tails_any.at[0], k_ref.at[pl.ds(0, LEFT)]),
            (k_any.at[pl.ds(0, rows)], k_ref.at[pl.ds(LEFT, rows)]),
            (tails_any.at[1], v_ref.at[pl.ds(0, LEFT)]),
            (v_any.at[pl.ds(0, rows)], v_ref.at[pl.ds(LEFT, rows)]),
            (edges_any, edges_ref),
            (proj_any, proj_ref),
        ]
    else:
        moves = [
            (q_any.at[pl.ds(start, rows)], q_ref),
            (k_any.at[pl.ds(start - LEFT, rows + LEFT)], k_ref),
            (v_any.at[pl.ds(start - LEFT, rows + LEFT)], v_ref),
            (edges_any, edges_ref),
            (proj_any, proj_ref),
        ]
    copies = [pltpu.make_async_copy(a, b, sems.at[i]) for i, (a, b) in enumerate(moves)]
    for copy in copies:
        copy.start()
    for copy in copies[:-1]:
        copy.wait()
    edges = edges_ref[:, start : start + rows].astype(F32)
    edges = jnp.concatenate([edges, jnp.zeros((6, rows), F32)], 0).T
    lane_head = lax.broadcasted_iota(jnp.int32, (block, columns), 1) // head_width
    context = []
    for r in range(0, rows, block):
        key = k_ref[r : r + window, :]
        value = v_ref[r : r + window, :]
        query = q_ref[r : r + block, :]
        places = lax.broadcasted_iota(jnp.int32, (block, window), 1)
        places = (places + (meta_ref[0] + (start + r - LEFT))).astype(F32)
        lower = jnp.maximum(edges[r : r + block, 0:1] - LEFT, 0.0)
        upper = edges[r : r + block, 1:2]
        visible = (places >= lower) & (places <= upper)
        own = [jnp.where(lane_head == h, query, jnp.zeros_like(query)) for h in range(heads)]
        own = jnp.concatenate(own, 0)
        scores = lax.dot_general(own, key, (((1,), (1,)), ((), ())), preferred_element_type=F32)
        scores = (scores * scale).reshape(heads, block, window)
        scores = jnp.where(visible[None], scores, -1e30)
        highest = jnp.max(scores, 2, keepdims=True)
        expos = jnp.exp(scores - highest)
        weights = (expos * (1.0 / jnp.sum(expos, 2, keepdims=True))).astype(BF16)
        weights = weights.reshape(heads * block, window)
        product = jnp.dot(weights, value, preferred_element_type=F32)
        mixed = product[0:block]
        for h in range(1, heads):
            mixed = jnp.where(lane_head == h, product[h * block : (h + 1) * block], mixed)
        context.append(mixed.astype(BF16))
    context = jnp.concatenate(context, 0)
    copies[-1].wait()
    count = proj_ref.shape[1] // columns // 2
    for i in range(2 * count):
        at = pl.multiple_of(order_ref[i] * columns, columns)
        part = jnp.dot(context, proj_ref[:, pl.ds(at, columns)], preferred_element_type=F32)
        j = (i - 1) % count * columns
        if i >= count:
            send_ref[:, j : j + columns] = part.astype(BF16)
        elif i > 0:
            keep_x_ref[:, j : j + columns] = part
        else:
            keep_ref[...] = part


def picked_rows(e, capacity, ranks_ref, state):
    slot = lax.broadcasted_iota(jnp.int32, (capacity, state.shape[0]), 0).astype(F32)
    pick = jnp.where(slot == ranks_ref[pl.ds(e, 1), :], 1.0, 0.0).astype(BF16)
    return jnp.dot(pick, state, preferred_element_type=F32).astype(BF16)


def scatter_rows(local, first, n_time, at_ref, ranks_ref, state, out_refs):
    for s, out_ref in enumerate(out_refs, first):
        owner = at_ref[0] + s
        owner = jnp.where(owner >= n_time, owner - n_time, owner)
        out_ref[...] = picked_rows(local * n_time + owner, out_ref.shape[0], ranks_ref, state)


def state_kernel(parts, column, n_time, at_ref, *refs):
    frames_ref, ranks_ref, state_ref = refs[2 * parts : 2 * parts + 3]
    width = state_ref.shape[1]
    halves = []
    for keep_ref, swapped_ref, *got in (refs[:parts], refs[parts : 2 * parts]):
        half = keep_ref[...] + swapped_ref[:, column : column + width].astype(F32)
        for ref in got:
            half = half + ref[...].astype(F32)
        halves.append(half)
    attended = jnp.concatenate(halves, 0)
    state = (frames_ref[...].astype(F32) + attended).astype(BF16)
    state_ref[...] = state
    scatter_rows(0, 0, n_time, at_ref, ranks_ref, state, refs[2 * parts + 3 :])


def dispatch_kernel(pieces, first, n_time, at_ref, *refs):
    own = refs[0][...]
    ranks_ref, *blocks, out_ref = refs[pieces:]
    scatter_rows(0, first, n_time, at_ref, ranks_ref, own, blocks)
    state = jnp.concatenate([own] + [ref[...] for ref in refs[1:pieces]], 1)
    capacity = out_ref.shape[0] // n_time
    for owner in range(n_time):
        rows = picked_rows(n_time + owner, capacity, ranks_ref, state)
        out_ref[owner * capacity : (owner + 1) * capacity, :] = rows


def take_kernel(rows_ref, *refs):
    refs[-1][...] = rows_ref[...]


def expert_kernel(local, starts, width, awaited, order_ref, *refs):
    arrays = len(starts)
    rows_in = refs[:arrays]
    gate_any, up_any, down_any = refs[arrays : arrays + 3]
    *outs, gate_ref, up_ref, down_ref, normed_ref, active_ref, sems = refs[arrays + 3 + awaited :]
    *send_x_refs, send_ref, keep_x_ref, keep_ref = outs
    rows, model = normed_ref.shape
    hidden = active_ref.shape[1]
    moves = [
        (gate_any.at[local], gate_ref),
        (up_any.at[local], up_ref),
        (down_any.at[local], down_ref),
    ]
    copies = [pltpu.make_async_copy(a, b, sems.at[i]) for i, (a, b) in enumerate(moves)]
    for copy in copies:
        copy.start()

    blocks = []
    for ref, start in zip(rows_in, starts):
        blocks += [(ref, start, c) for c in range(0, ref.shape[1], width)]
    step = min(rows, 256)

    def norm(i, carry):
        at_row = pl.multiple_of(i * step, step)
        parts = [
            ref[pl.ds(pl.multiple_of(start + i * step, step), step), c : c + width].astype(F32)
            for ref, start, c in blocks
        ]
        squares = sum(jnp.sum(part * part, 1, keepdims=True) for part in parts)
        factor = lax.rsqrt(squares * (1.0 / model) + EPS)
        for j, part in enumerate(parts):
            at = pl.multiple_of(order_ref[j] * width, width)
            normed_ref[pl.ds(at_row, step), pl.ds(at, width)] = (part * factor).astype(BF16)
        return carry

    lax.fori_loop(0, rows // step, norm, 0)
    copies[0].wait()
    copies[1].wait()
    tile = min(rows, 1024)
    chunk = min(hidden, 256)
    for r in range(0, rows, tile):
        normed = normed_ref[r : r + tile, :]
        for c in range(0, hidden, chunk):
            gate = jnp.dot(normed, gate_ref[:, c : c + chunk], preferred_element_type=F32)
            up = jnp.dot(normed, up_ref[:, c : c + chunk], preferred_element_type=F32)
            half = 0.5 * gate
            active = (half + half * jnp.tanh(half)) * up
            active_ref[r : r + tile, c : c + chunk] = active.astype(BF16)
    copies[2].wait()
    count = len(blocks) // 2
    def project(i, out_refs, column):
        at = pl.multiple_of(order_ref[i] * width, width)
        weight = down_ref[:, pl.ds(at, width)]
        result = jnp.dot(active_ref[...], weight, preferred_element_type=F32)
        each = rows // len(out_refs)
        for j, out_ref in enumerate(out_refs):
            part = result[j * each : (j + 1) * each]
            out_ref[:, column : column + width] = part.astype(out_ref.dtype)

    for by in range(1, count):
        project(count + by, send_x_refs, (by - 1) * width)
    project(count, [send_ref], 0)
    for by in range(1, count):
        project(by, [keep_x_ref], (by - 1) * width)
    project(0, [keep_ref], 0)


def add_kernel(width, keep_ref, got_ref, after_any, *out_refs):
    for i, out_ref in enumerate(out_refs):
        at = slice(i * width, (i + 1) * width)
        out_ref[...] = (keep_ref[:, at] + got_ref[:, at].astype(F32)).astype(BF16)


def total_kernel(n_time, at_ref, keep_ref, *refs):
    *got, after_any, out_ref = refs
    capacity = out_ref.shape[0] // n_time
    for s in range(n_time):
        rows = slice(s * capacity, (s + 1) * capacity)
        total = keep_ref[rows, :]
        for ref in got:
            total = total + ref[rows, :].astype(F32)
        place = at_ref[0] - s
        place = jnp.where(place < 0, place + n_time, place)
        out_ref[pl.ds(pl.multiple_of(place * capacity, capacity), capacity), :] = total.astype(BF16)


def spread_kernel(n_time, at_ref, keep_ref, swapped_ref, *refs):
    got, outs = refs[: -n_time - 1], refs[-n_time:]
    capacity = outs[0].shape[0]
    for s, out_ref in enumerate(outs):
        place = at_ref[0] + s
        place = jnp.where(place >= n_time, place - n_time, place)
        at = pl.ds(pl.multiple_of(place * capacity, capacity), capacity)
        total = keep_ref[at, :] + swapped_ref[at, :].astype(F32)
        for ref in got:
            total = total + ref[at, :].astype(F32)
        out_ref[...] = total.astype(BF16)


def combine_kernel(local, at_ref, targets_ref, gates_ref, base_ref, *refs):
    if len(refs) == 2:
        back_ref, out_ref = refs
    else:
        *got, out_ref, back_ref = refs
        n_time, capacity = len(got), got[0].shape[0]
        for s, ref in enumerate(got):
            place = at_ref[0] - s
            place = jnp.where(place < 0, place + n_time, place)
            back_ref[pl.ds(pl.multiple_of(place * capacity, capacity), capacity), :] = ref[...]
    back = back_ref[...]
    rows = back.shape[0]
    frames = targets_ref.shape[0]
    places = lax.broadcasted_iota(jnp.int32, (frames, rows), 1) + local * rows
    total = base_ref[...].astype(F32)
    for k in range(TOP):
        pick = jnp.where(places == targets_ref[:, k : k + 1], 1.0, 0.0).astype(BF16)
        total = total + gates_ref[:, k : k + 1] * jnp.dot(pick, back, preferred_element_type=F32)
    out_ref[...] = total.astype(out_ref.dtype)


def per_device(
    frames_in,
    queries,
    keys,
    values,
    segment_edges,
    out_proj,
    expert_ids,
    gates,
    w_gate,
    w_up,
    w_down,
):
    frames, model = frames_in.shape
    width = queries.shape[1]
    n_model = lax.axis_size("mp")
    n_time = lax.axis_size("tm")
    chips = n_model // 2
    head_width = model // HEADS
    scale = head_width ** (-0.5)
    local_experts = w_gate.shape[0]
    hidden = w_gate.shape[2]
    experts_all = local_experts * n_time
    capacity = 4 * frames // experts_all
    rows = n_time * capacity
    lanes = -(-experts_all // LANES) * LANES
    at_time = lax.axis_index("tm")
    at_model = lax.axis_index("mp")
    chip, core = at_model // 2, at_model % 2
    mine = [((chip - by) % chips) * 2 + core for by in range(chips)]
    others = [((chip - by) % chips) * 2 + 1 - core for by in range(chips)]
    order = jnp.stack(mine + others).astype(jnp.int32)
    offset = (at_time * frames).astype(jnp.int32).reshape(1)
    place = at_time.astype(jnp.int32).reshape(1)
    away = (chips - 1) * width

    tails = from_behind(jnp.stack([keys[frames - LEFT :], values[frames - LEFT :]], 0), "tm", 1)
    own_frames = lax.dynamic_slice_in_dim(frames_in, at_model * width, width, 1)

    ranks, targets = pl.pallas_call(
        functools.partial(route_kernel, capacity, local_experts, n_time),
        out_shape=(
            jax.ShapeDtypeStruct((lanes, frames), F32),
            jax.ShapeDtypeStruct((frames, TOP), jnp.int32),
        ),
        in_specs=[VMEM],
        out_specs=(VMEM, VMEM),
        compiler_params=params(16),
        cost_estimate=cost(2 * frames * frames * lanes, frames * 1024),
        name="route",
    )(expert_ids)

    def in_hbm(*arrays):
        return [pltpu.with_memory_space_constraint(x, pltpu.HBM) for x in arrays]

    def attend(start, end, *extra):
        count = end - start
        return pl.pallas_call(
            functools.partial(attend_kernel, scale, head_width, start),
            out_shape=(
                jax.ShapeDtypeStruct((count, chips * width), BF16),
                jax.ShapeDtypeStruct((count, away), F32),
                jax.ShapeDtypeStruct((count, width), F32),
            ),
            in_specs=[SMEM, SMEM] + [HBM] * 5 + [ANY] * len(extra),
            out_specs=(VMEM,) * 3,
            scratch_shapes=[
                pltpu.VMEM((2, frames), jnp.int32),
                pltpu.VMEM((count, width), BF16),
                pltpu.VMEM((LEFT + count, width), BF16),
                pltpu.VMEM((LEFT + count, width), BF16),
                pltpu.VMEM(out_proj.shape, BF16),
                pltpu.SemaphoreType.DMA((7,)),
            ],
            compiler_params=params(16),
            cost_estimate=cost(count * 384 * width * 16, count * width * 8, count * 384 * 4),
            name=f"attend_{start}",
        )(offset, order, *in_hbm(segment_edges, queries, keys, values, out_proj), *extra)

    def add(name, keep, got, after):
        count = keep.shape[0]
        return pl.pallas_call(
            functools.partial(add_kernel, width),
            in_specs=[VMEM, VMEM, ANY],
            out_specs=(VMEM,) * (chips - 1),
            out_shape=(jax.ShapeDtypeStruct((count, width), BF16),) * (chips - 1),
            compiler_params=params(16),
            cost_estimate=cost(keep.size, keep.size * 8),
            name=f"add_{name}",
        )(keep, got, after)

    def from_chips(parts):
        return [from_chip(part, chips - by) for by, part in enumerate(parts, 1)]

    def attended(name, send, keep_x, keep):
        swapped = core_swap(send)
        return [keep, swapped, *from_chips(add(name, keep_x, swapped, swapped))]

    late = attended("late", *attend(LEFT, frames))
    early = attended("early", *attend(0, LEFT, tails))

    def blocks_of(count):
        return (jax.ShapeDtypeStruct((capacity, width), BF16),) * count

    near = n_time // 2 + 1
    state, *outgoing_0 = pl.pallas_call(
        functools.partial(state_kernel, len(early), away, n_time),
        out_shape=(jax.ShapeDtypeStruct((frames, width), BF16),) + blocks_of(near),
        in_specs=[SMEM] + [VMEM] * (2 * len(early) + 2),
        out_specs=(VMEM,) * (1 + near),
        compiler_params=params(16),
        cost_estimate=cost(frames * width * rows, 4 * MIB),
        name="state",
    )(place, *early, *late, own_frames, ranks)
    wide = [state] + [from_chip(state, by) for by in range(1, chips)]
    *far, outgoing_1 = pl.pallas_call(
        functools.partial(dispatch_kernel, chips, near, n_time),
        out_shape=blocks_of(n_time - near)
        + (jax.ShapeDtypeStruct((rows, chips * width), BF16),),
        in_specs=[SMEM] + [VMEM] * (chips + 1),
        out_specs=(VMEM,) * (n_time - near + 1),
        compiler_params=params(16),
        cost_estimate=cost(3 * frames * width * rows, 3 * MIB),
        name="dispatch",
    )(place, *wide, ranks)

    def over_time(x):
        columns = x.shape[1]
        x = x.reshape(n_time, capacity, columns)
        x = lax.all_to_all(x, "tm", split_axis=0, concat_axis=0, tiled=True)
        return x.reshape(rows, columns)

    def take(x, after):
        return pl.pallas_call(
            take_kernel,
            in_specs=[VMEM] + [ANY] * len(after),
            out_specs=VMEM,
            out_shape=jax.ShapeDtypeStruct(x.shape, x.dtype),
            compiler_params=params(16),
            cost_estimate=cost(x.size, x.size * 4),
            name="take",
        )(x, *after)

    def experts(local, parts, after):
        outs = [jax.ShapeDtypeStruct((rows, columns), BF16) for columns in (away, width)]
        outs += [jax.ShapeDtypeStruct((rows, columns), F32) for columns in (away, width)]
        return pl.pallas_call(
            functools.partial(expert_kernel, local, (0,) * len(parts), width, len(after)),
            in_specs=[SMEM] + [VMEM] * len(parts) + [HBM] * 3 + [ANY] * len(after),
            out_specs=(VMEM,) * 4,
            scratch_shapes=[
                pltpu.VMEM((model, hidden), BF16),
                pltpu.VMEM((model, hidden), BF16),
                pltpu.VMEM((hidden, model), BF16),
                pltpu.VMEM((rows, model), BF16),
                pltpu.VMEM((rows, hidden), BF16),
                pltpu.SemaphoreType.DMA((3,)),
            ],
            out_shape=tuple(outs),
            compiler_params=params(20),
            cost_estimate=cost(6 * rows * model * hidden, 12 * MIB, rows * hidden),
            name=f"experts_{local}",
        )(order, *parts, *in_hbm(w_gate, w_up, w_down), *after)

    def total(local, parts, after):
        return pl.pallas_call(
            functools.partial(total_kernel, n_time),
            in_specs=[SMEM] + [VMEM] * len(parts) + [ANY],
            out_specs=VMEM,
            out_shape=jax.ShapeDtypeStruct((rows, width), BF16),
            compiler_params=params(16),
            cost_estimate=cost(rows * width * 4, rows * width * 10),
            name=f"total_{local}",
        )(place, *parts, after)

    def spread(local, parts, after):
        return pl.pallas_call(
            functools.partial(spread_kernel, n_time),
            in_specs=[SMEM] + [VMEM] * len(parts) + [ANY],
            out_specs=(VMEM,) * n_time,
            out_shape=(jax.ShapeDtypeStruct((capacity, width), BF16),) * n_time,
            compiler_params=params(16),
            cost_estimate=cost(rows * width * 4, rows * width * 10),
            name=f"spread_{local}",
        )(place, *parts, after)

    def combine(local, back, base):
        last = local == local_experts - 1
        apart = [pltpu.VMEM((rows, width), BF16)] if len(back) > 1 else []
        return pl.pallas_call(
            functools.partial(combine_kernel, local),
            out_shape=jax.ShapeDtypeStruct((frames, width), BF16 if last else F32),
            in_specs=[SMEM] + [VMEM] * (3 + len(back)),
            out_specs=VMEM,
            scratch_shapes=apart,
            compiler_params=params(16),
            cost_estimate=cost(4 * frames * width * rows, 3 * MIB),
            name=f"combine_{local}",
        )(place, targets, gates, base, *back)

    arrived_0 = jnp.concatenate(exchanged(outgoing_0 + far), 0)
    arrived_1 = over_time(outgoing_1)
    send_x_0, send_0, keep_x_0, keep_0 = experts(0, gathered(arrived_0), [outgoing_1])
    away_0 = add("0", keep_x_0, core_swap(send_x_0), send_0)
    got_0 = from_chips(away_0)
    arrived_1 = take(arrived_1, [away_0[0]])
    parts = [arrived_1, core_swap(arrived_1)]
    send_x_1, send_1, keep_x_1, keep_1 = experts(1, parts, [away_0[0]])
    total_0 = total(0, [keep_0, core_swap(send_0), *got_0], send_1)
    back_0 = over_time(total_0)
    got_1 = from_chips(add("1", keep_x_1, core_swap(send_x_1), total_0))
    back_1 = exchanged(spread(1, [keep_1, core_swap(send_1), *got_1], back_0))
    return combine(1, back_1, combine(0, [back_0], state))


def solution(mesh):
    return jax.shard_map(
        per_device,
        mesh=mesh,
        in_specs=(
            P("tm", None),
            P("tm", "mp"),
            P("tm", "mp"),
            P("tm", "mp"),
            P(None, "tm"),
            P("mp", None),
            P("tm", None),
            P("tm", None),
            P("tm", None, "mp"),
            P("tm", None, "mp"),
            P("tm", "mp", None),
        ),
        out_specs=P("tm", "mp"),
        check_vma=False,
    )
```

```python
import functools

import jax
import jax.numpy as jnp
from jax import lax
from jax.experimental import pallas as pl
from jax.experimental.pallas import tpu as pltpu
from jax.sharding import PartitionSpec as P

HEADS = 16
TOP = 2
LEFT = 256
EPS = 1e-06
LANES = 128
MIB = 1 << 20
F32 = jnp.float32
BF16 = jnp.bfloat16

VMEM = pl.BlockSpec(memory_space=pltpu.VMEM)
SMEM = pl.BlockSpec(memory_space=pltpu.SMEM)
ANY = pl.BlockSpec(memory_space=pl.ANY)
HBM = pl.BlockSpec(memory_space=pltpu.HBM)


def params(mib):
    return pltpu.CompilerParams(vmem_limit_bytes=mib * MIB)


def cost(flops, moved, transcendentals=0):
    return pl.CostEstimate(flops=flops, bytes_accessed=moved, transcendentals=transcendentals)


def from_behind(x, axis, by):
    size = lax.axis_size(axis)
    pairs = [(i, i + by) for i in range(size) if 0 <= i + by < size]
    return lax.ppermute(x, axis, pairs)


def core_swap(x):
    size = lax.axis_size("mp")
    return lax.ppermute(x, "mp", [(i, i ^ 1) for i in range(size)])


def from_chip(x, by):
    chips = lax.axis_size("mp") // 2
    pairs = [(c * 2 + k, ((c + by) % chips) * 2 + k) for c in range(chips) for k in range(2)]
    return lax.ppermute(x, "mp", pairs)


def gathered(x):
    chips = lax.axis_size("mp") // 2
    mine = [x] + [from_chip(x, by) for by in range(1, chips)]
    return mine + [core_swap(part) for part in mine]


def exchanged(blocks):
    size = lax.axis_size("tm")
    return [blocks[0]] + [
        lax.ppermute(block, "tm", [(i, (i + s) % size) for i in range(size)])
        for s, block in enumerate(blocks)
        if s > 0
    ]


def route_kernel(capacity, local_experts, n_time, ids_ref, ranks_ref, targets_ref):
    frames = ids_ref.shape[0]
    lanes = ranks_ref.shape[0]
    ids = ids_ref[...]
    owner = ids // local_experts
    ids = (ids - owner * local_experts) * n_time + owner
    experts = lax.broadcasted_iota(jnp.int32, (frames, lanes), 1)
    hits = [ids[:, k : k + 1] == experts for k in range(TOP)]
    named = functools.reduce(jnp.logical_or, hits)
    ones = jnp.where(named, 1.0, 0.0).astype(BF16)
    row = lax.broadcasted_iota(jnp.int32, (frames, frames), 0)
    column = lax.broadcasted_iota(jnp.int32, (frames, frames), 1)
    before = jnp.where(column < row, 1.0, 0.0).astype(BF16)
    ranks = jnp.dot(before, ones, preferred_element_type=F32)
    ranks_ref[...] = jnp.where(named, ranks, -1.0).T
    places = []
    for k in range(TOP):
        slot = jnp.sum(jnp.where(hits[k], ranks, 0.0), 1, keepdims=True).astype(jnp.int32)
        places.append(ids[:, k : k + 1] * capacity + slot)
    targets_ref[...] = jnp.concatenate(places, 1)


def attend_kernel(scale, head_width, start, meta_ref, order_ref, *refs):
    tails_any = refs[5] if start == 0 else None
    edges_any, q_any, k_any, v_any, proj_any = refs[:5]
    refs = refs[6:] if start == 0 else refs[5:]
    send_ref, keep_x_ref, keep_ref, edges_ref, q_ref, k_ref, v_ref, proj_ref, sems = refs
    rows, columns = q_ref.shape
    heads = columns // head_width
    block = LANES
    window = LEFT + block
    if start == 0:
        moves = [
            (q_any.at[pl.ds(0, rows)], q_ref),
            (tails_any.at[0], k_ref.at[pl.ds(0, LEFT)]),
            (k_any.at[pl.ds(0, rows)], k_ref.at[pl.ds(LEFT, rows)]),
            (tails_any.at[1], v_ref.at[pl.ds(0, LEFT)]),
            (v_any.at[pl.ds(0, rows)], v_ref.at[pl.ds(LEFT, rows)]),
            (edges_any, edges_ref),
            (proj_any, proj_ref),
        ]
    else:
        moves = [
            (q_any.at[pl.ds(start, rows)], q_ref),
            (k_any.at[pl.ds(start - LEFT, rows + LEFT)], k_ref),
            (v_any.at[pl.ds(start - LEFT, rows + LEFT)], v_ref),
            (edges_any, edges_ref),
            (proj_any, proj_ref),
        ]
    copies = [pltpu.make_async_copy(a, b, sems.at[i]) for i, (a, b) in enumerate(moves)]
    for copy in copies:
        copy.start()
    for copy in copies[:-1]:
        copy.wait()
    edges = edges_ref[:, start : start + rows].astype(F32)
    edges = jnp.concatenate([edges, jnp.zeros((6, rows), F32)], 0).T
    lane_head = lax.broadcasted_iota(jnp.int32, (block, columns), 1) // head_width
    context = []
    for r in range(0, rows, block):
        key = k_ref[r : r + window, :]
        value = v_ref[r : r + window, :]
        query = q_ref[r : r + block, :]
        places = lax.broadcasted_iota(jnp.int32, (block, window), 1)
        places = (places + (meta_ref[0] + (start + r - LEFT))).astype(F32)
        lower = jnp.maximum(edges[r : r + block, 0:1] - LEFT, 0.0)
        upper = edges[r : r + block, 1:2]
        visible = (places >= lower) & (places <= upper)
        own = [jnp.where(lane_head == h, query, jnp.zeros_like(query)) for h in range(heads)]
        own = jnp.concatenate(own, 0)
        scores = lax.dot_general(own, key, (((1,), (1,)), ((), ())), preferred_element_type=F32)
        scores = (scores * scale).reshape(heads, block, window)
        scores = jnp.where(visible[None], scores, -1e30)
        highest = jnp.max(scores, 2, keepdims=True)
        expos = jnp.exp(scores - highest)
        weights = (expos * (1.0 / jnp.sum(expos, 2, keepdims=True))).astype(BF16)
        weights = weights.reshape(heads * block, window)
        product = jnp.dot(weights, value, preferred_element_type=F32)
        mixed = product[0:block]
        for h in range(1, heads):
            mixed = jnp.where(lane_head == h, product[h * block : (h + 1) * block], mixed)
        context.append(mixed.astype(BF16))
    context = jnp.concatenate(context, 0)
    copies[-1].wait()
    count = proj_ref.shape[1] // columns // 2
    for i in range(2 * count):
        at = pl.multiple_of(order_ref[i] * columns, columns)
        part = jnp.dot(context, proj_ref[:, pl.ds(at, columns)], preferred_element_type=F32)
        j = (i - 1) % count * columns
        if i >= count:
            send_ref[:, j : j + columns] = part.astype(BF16)
        elif i > 0:
            keep_x_ref[:, j : j + columns] = part
        else:
            keep_ref[...] = part


def picked_rows(e, capacity, ranks_ref, state):
    slot = lax.broadcasted_iota(jnp.int32, (capacity, state.shape[0]), 0).astype(F32)
    pick = jnp.where(slot == ranks_ref[pl.ds(e, 1), :], 1.0, 0.0).astype(BF16)
    return jnp.dot(pick, state, preferred_element_type=F32).astype(BF16)


def scatter_rows(local, first, n_time, at_ref, ranks_ref, state, out_refs):
    for s, out_ref in enumerate(out_refs, first):
        owner = at_ref[0] + s
        owner = jnp.where(owner >= n_time, owner - n_time, owner)
        out_ref[...] = picked_rows(local * n_time + owner, out_ref.shape[0], ranks_ref, state)


def state_kernel(parts, column, n_time, at_ref, *refs):
    frames_ref, ranks_ref, state_ref = refs[2 * parts : 2 * parts + 3]
    width = state_ref.shape[1]
    halves = []
    for keep_ref, swapped_ref, *got in (refs[:parts], refs[parts : 2 * parts]):
        half = keep_ref[...] + swapped_ref[:, column : column + width].astype(F32)
        for ref in got:
            half = half + ref[...].astype(F32)
        halves.append(half)
    attended = jnp.concatenate(halves, 0)
    state = (frames_ref[...].astype(F32) + attended).astype(BF16)
    state_ref[...] = state
    scatter_rows(0, 0, n_time, at_ref, ranks_ref, state, refs[2 * parts + 3 :])


def dispatch_kernel(pieces, first, n_time, at_ref, *refs):
    own = refs[0][...]
    ranks_ref, *blocks, out_ref = refs[pieces:]
    scatter_rows(0, first, n_time, at_ref, ranks_ref, own, blocks)
    state = jnp.concatenate([own] + [ref[...] for ref in refs[1:pieces]], 1)
    capacity = out_ref.shape[0] // n_time
    for owner in range(n_time):
        rows = picked_rows(n_time + owner, capacity, ranks_ref, state)
        out_ref[owner * capacity : (owner + 1) * capacity, :] = rows


def take_kernel(rows_ref, *refs):
    refs[-1][...] = rows_ref[...]


def expert_kernel(local, arrays, width, awaited, fetched, order_ref, *refs):
    rows_in = refs[:arrays]
    gate_any, up_any, down_any = refs[arrays : arrays + 3]
    refs = refs[arrays + 3 + awaited :]
    send_x_ref, send_ref, keep_x_any, keep_any = refs[:4]
    gate_ref, up_ref, down_ref, normed_ref, active_ref, keep_x_ref, keep_ref, sems = refs[4:12]
    rows, model = normed_ref.shape
    hidden = active_ref.shape[1]
    moves = [
        (gate_any.at[local], gate_ref),
        (up_any.at[local], up_ref),
        (down_any.at[local], down_ref),
        (keep_x_ref, keep_x_any),
        (keep_ref, keep_any),
    ]
    if fetched:
        moves += list(zip(rows_in, refs[12:]))
        rows_in = refs[12:]
    copies = [pltpu.make_async_copy(a, b, sems.at[i]) for i, (a, b) in enumerate(moves)]
    for copy in copies[5:] + copies[:3]:
        copy.start()
    for copy in copies[5:]:
        copy.wait()

    blocks = []
    for ref in rows_in:
        blocks += [(ref, c) for c in range(0, ref.shape[1], width)]
    step = min(rows, 256)

    def norm(i, carry):
        at_row = pl.multiple_of(i * step, step)
        parts = [ref[pl.ds(at_row, step), c : c + width].astype(F32) for ref, c in blocks]
        squares = sum(jnp.sum(part * part, 1, keepdims=True) for part in parts)
        factor = lax.rsqrt(squares * (1.0 / model) + EPS)
        for j, part in enumerate(parts):
            at = pl.multiple_of(order_ref[j] * width, width)
            normed_ref[pl.ds(at_row, step), pl.ds(at, width)] = (part * factor).astype(BF16)
        return carry

    lax.fori_loop(0, rows // step, norm, 0)
    copies[0].wait()
    copies[1].wait()
    tile = min(rows, 1024)
    chunk = min(hidden, 256)
    for r in range(0, rows, tile):
        normed = normed_ref[r : r + tile, :]
        for c in range(0, hidden, chunk):
            gate = jnp.dot(normed, gate_ref[:, c : c + chunk], preferred_element_type=F32)
            up = jnp.dot(normed, up_ref[:, c : c + chunk], preferred_element_type=F32)
            half = 0.5 * gate
            active = (half + half * jnp.tanh(half)) * up
            active_ref[r : r + tile, c : c + chunk] = active.astype(BF16)
    copies[2].wait()
    count = len(blocks) // 2
    def project(i, out_ref, column):
        at = pl.multiple_of(order_ref[i] * width, width)
        weight = down_ref[:, pl.ds(at, width)]
        result = jnp.dot(active_ref[...], weight, preferred_element_type=F32)
        out_ref[:, column : column + width] = result.astype(out_ref.dtype)

    for by in range(1, count):
        project(by, keep_x_ref, (by - 1) * width)
    copies[3].start()
    project(0, keep_ref, 0)
    copies[4].start()
    for by in range(1, count):
        project(count + by, send_x_ref, (by - 1) * width)
    project(count, send_ref, 0)
    copies[3].wait()
    copies[4].wait()


def fetch(source, target, sem):
    copy = pltpu.make_async_copy(source, target, sem)
    copy.start()
    copy.wait()


def add_kernel(width, awaited, keep_any, got_ref, *refs):
    *out_refs, keep_ref, sem = refs[awaited:]
    fetch(keep_any, keep_ref, sem)
    for i, out_ref in enumerate(out_refs):
        at = slice(i * width, (i + 1) * width)
        out_ref[...] = (keep_ref[:, at] + got_ref[:, at].astype(F32)).astype(BF16)


def total_kernel(n_time, at_ref, keep_any, *refs):
    *got, after_any, out_ref, keep_ref, sem = refs
    fetch(keep_any, keep_ref, sem)
    capacity = out_ref.shape[0] // n_time
    for s in range(n_time):
        rows = slice(s * capacity, (s + 1) * capacity)
        total = keep_ref[rows, :]
        for ref in got:
            total = total + ref[rows, :].astype(F32)
        place = at_ref[0] - s
        place = jnp.where(place < 0, place + n_time, place)
        out_ref[pl.ds(pl.multiple_of(place * capacity, capacity), capacity), :] = total.astype(BF16)


def spread_kernel(n_time, at_ref, keep_any, *refs):
    *got, after_any = refs[: -n_time - 2]
    *outs, keep_ref, sem = refs[-n_time - 2 :]
    fetch(keep_any, keep_ref, sem)
    capacity = outs[0].shape[0]
    for s, out_ref in enumerate(outs):
        place = at_ref[0] + s
        place = jnp.where(place >= n_time, place - n_time, place)
        at = pl.ds(pl.multiple_of(place * capacity, capacity), capacity)
        total = keep_ref[at, :]
        for ref in got:
            total = total + ref[at, :].astype(F32)
        out_ref[...] = total.astype(BF16)


def combine_kernel(local, at_ref, targets_ref, gates_ref, base_ref, *refs):
    if len(refs) == 2:
        back_ref, out_ref = refs
    else:
        *got, out_ref, back_ref = refs
        n_time, capacity = len(got), got[0].shape[0]
        for s, ref in enumerate(got):
            place = at_ref[0] - s
            place = jnp.where(place < 0, place + n_time, place)
            back_ref[pl.ds(pl.multiple_of(place * capacity, capacity), capacity), :] = ref[...]
    back = back_ref[...]
    rows = back.shape[0]
    frames = targets_ref.shape[0]
    places = lax.broadcasted_iota(jnp.int32, (frames, rows), 1) + local * rows
    total = base_ref[...].astype(F32)
    for k in range(TOP):
        pick = jnp.where(places == targets_ref[:, k : k + 1], 1.0, 0.0).astype(BF16)
        total = total + gates_ref[:, k : k + 1] * jnp.dot(pick, back, preferred_element_type=F32)
    out_ref[...] = total.astype(out_ref.dtype)


def per_device(
    frames_in,
    queries,
    keys,
    values,
    segment_edges,
    out_proj,
    expert_ids,
    gates,
    w_gate,
    w_up,
    w_down,
):
    frames, model = frames_in.shape
    width = queries.shape[1]
    n_model = lax.axis_size("mp")
    n_time = lax.axis_size("tm")
    chips = n_model // 2
    head_width = model // HEADS
    scale = head_width ** (-0.5)
    local_experts = w_gate.shape[0]
    hidden = w_gate.shape[2]
    experts_all = local_experts * n_time
    capacity = 4 * frames // experts_all
    rows = n_time * capacity
    lanes = -(-experts_all // LANES) * LANES
    at_time = lax.axis_index("tm")
    at_model = lax.axis_index("mp")
    chip, core = at_model // 2, at_model % 2
    mine = [((chip - by) % chips) * 2 + core for by in range(chips)]
    others = [((chip - by) % chips) * 2 + 1 - core for by in range(chips)]
    order = jnp.stack(mine + others).astype(jnp.int32)
    offset = (at_time * frames).astype(jnp.int32).reshape(1)
    place = at_time.astype(jnp.int32).reshape(1)
    away = (chips - 1) * width

    tails = from_behind(jnp.stack([keys[frames - LEFT :], values[frames - LEFT :]], 0), "tm", 1)
    own_frames = lax.dynamic_slice_in_dim(frames_in, at_model * width, width, 1)

    ranks, targets = pl.pallas_call(
        functools.partial(route_kernel, capacity, local_experts, n_time),
        out_shape=(
            jax.ShapeDtypeStruct((lanes, frames), F32),
            jax.ShapeDtypeStruct((frames, TOP), jnp.int32),
        ),
        in_specs=[VMEM],
        out_specs=(VMEM, VMEM),
        compiler_params=params(16),
        cost_estimate=cost(2 * frames * frames * lanes, frames * 1024),
        name="route",
    )(expert_ids)

    def in_hbm(*arrays):
        return [pltpu.with_memory_space_constraint(x, pltpu.HBM) for x in arrays]

    def attend(start, end, *extra):
        count = end - start
        return pl.pallas_call(
            functools.partial(attend_kernel, scale, head_width, start),
            out_shape=(
                jax.ShapeDtypeStruct((count, chips * width), BF16),
                jax.ShapeDtypeStruct((count, away), F32),
                jax.ShapeDtypeStruct((count, width), F32),
            ),
            in_specs=[SMEM, SMEM] + [HBM] * 5 + [ANY] * len(extra),
            out_specs=(VMEM,) * 3,
            scratch_shapes=[
                pltpu.VMEM((2, frames), jnp.int32),
                pltpu.VMEM((count, width), BF16),
                pltpu.VMEM((LEFT + count, width), BF16),
                pltpu.VMEM((LEFT + count, width), BF16),
                pltpu.VMEM(out_proj.shape, BF16),
                pltpu.SemaphoreType.DMA((7,)),
            ],
            compiler_params=params(16),
            cost_estimate=cost(count * 384 * width * 16, count * width * 8, count * 384 * 4),
            name=f"attend_{start}",
        )(offset, order, *in_hbm(segment_edges, queries, keys, values, out_proj), *extra)

    def add(name, keep, got, after=()):
        count = keep.shape[0]
        return pl.pallas_call(
            functools.partial(add_kernel, width, len(after)),
            in_specs=[ANY, VMEM] + [ANY] * len(after),
            out_specs=(VMEM,) * (chips - 1),
            out_shape=(jax.ShapeDtypeStruct((count, width), BF16),) * (chips - 1),
            scratch_shapes=[pltpu.VMEM(keep.shape, F32), pltpu.SemaphoreType.DMA],
            compiler_params=params(16),
            cost_estimate=cost(keep.size, keep.size * 8),
            name=f"add_{name}",
        )(keep, got, *after)

    def from_chips(parts):
        return [from_chip(part, chips - by) for by, part in enumerate(parts, 1)]

    def attended(name, send, keep_x, keep):
        swapped = core_swap(send)
        return [keep, swapped, *from_chips(add(name, keep_x, swapped))]

    late = attended("late", *attend(LEFT, frames))
    early = attended("early", *attend(0, LEFT, tails))

    def blocks_of(count):
        return (jax.ShapeDtypeStruct((capacity, width), BF16),) * count

    near = n_time - 1
    state, *outgoing_0 = pl.pallas_call(
        functools.partial(state_kernel, len(early), away, n_time),
        out_shape=(jax.ShapeDtypeStruct((frames, width), BF16),) + blocks_of(near),
        in_specs=[SMEM] + [VMEM] * (2 * len(early) + 2),
        out_specs=(VMEM,) * (1 + near),
        compiler_params=params(16),
        cost_estimate=cost(frames * width * rows, 4 * MIB),
        name="state",
    )(place, *early, *late, own_frames, ranks)
    wide = [state] + [from_chip(state, by) for by in range(1, chips)]
    *far, outgoing_1 = pl.pallas_call(
        functools.partial(dispatch_kernel, chips, near, n_time),
        out_shape=blocks_of(n_time - near)
        + (jax.ShapeDtypeStruct((rows, chips * width), BF16),),
        in_specs=[SMEM] + [VMEM] * (chips + 1),
        out_specs=(VMEM,) * (n_time - near + 1),
        compiler_params=params(16),
        cost_estimate=cost(3 * frames * width * rows, 3 * MIB),
        name="dispatch",
    )(place, *wide, ranks)

    def over_time(x):
        columns = x.shape[1]
        x = x.reshape(n_time, capacity, columns)
        x = lax.all_to_all(x, "tm", split_axis=0, concat_axis=0, tiled=True)
        return x.reshape(rows, columns)

    def take(x, after):
        return pl.pallas_call(
            take_kernel,
            in_specs=[VMEM] + [ANY] * len(after),
            out_specs=VMEM,
            out_shape=jax.ShapeDtypeStruct(x.shape, x.dtype),
            compiler_params=params(16),
            cost_estimate=cost(x.size, x.size * 4),
            name="take",
        )(x, *after)

    def experts(local, parts, fetched, after):
        outs = [jax.ShapeDtypeStruct((rows, columns), BF16) for columns in (away, width)]
        outs += [pltpu.HBM((rows, columns), F32) for columns in (away, width)]
        pieces = [pltpu.VMEM(part.shape, BF16) for part in parts] if fetched else []
        return pl.pallas_call(
            functools.partial(expert_kernel, local, len(parts), width, len(after), fetched),
            in_specs=[SMEM]
            + [ANY if fetched else VMEM] * len(parts)
            + [HBM] * 3
            + [ANY] * len(after),
            out_specs=(VMEM, VMEM, HBM, HBM),
            scratch_shapes=[
                pltpu.VMEM((model, hidden), BF16),
                pltpu.VMEM((model, hidden), BF16),
                pltpu.VMEM((hidden, model), BF16),
                pltpu.VMEM((rows, model), BF16),
                pltpu.VMEM((rows, hidden), BF16),
                pltpu.VMEM((rows, away), F32),
                pltpu.VMEM((rows, width), F32),
                pltpu.SemaphoreType.DMA((5 + len(pieces),)),
            ]
            + pieces,
            out_shape=tuple(outs),
            compiler_params=params(24),
            cost_estimate=cost(6 * rows * model * hidden, 12 * MIB, rows * hidden),
            name=f"experts_{local}",
        )(order, *parts, *in_hbm(w_gate, w_up, w_down), *after)

    def total(local, keep, parts, after):
        return pl.pallas_call(
            functools.partial(total_kernel, n_time),
            in_specs=[SMEM, HBM] + [VMEM] * len(parts) + [ANY],
            out_specs=VMEM,
            out_shape=jax.ShapeDtypeStruct((rows, width), BF16),
            scratch_shapes=[pltpu.VMEM(keep.shape, F32), pltpu.SemaphoreType.DMA],
            compiler_params=params(16),
            cost_estimate=cost(rows * width * 4, rows * width * 10),
            name=f"total_{local}",
        )(place, *in_hbm(keep), *parts, after)

    def spread(local, keep, parts, after):
        return pl.pallas_call(
            functools.partial(spread_kernel, n_time),
            in_specs=[SMEM, HBM] + [VMEM] * len(parts) + [ANY],
            out_specs=(VMEM,) * n_time,
            out_shape=blocks_of(n_time),
            scratch_shapes=[pltpu.VMEM(keep.shape, F32), pltpu.SemaphoreType.DMA],
            compiler_params=params(16),
            cost_estimate=cost(rows * width * 4, rows * width * 10),
            name=f"spread_{local}",
        )(place, *in_hbm(keep), *parts, after)

    def combine(local, back, base):
        last = local == local_experts - 1
        apart = [pltpu.VMEM((rows, width), BF16)] if len(back) > 1 else []
        return pl.pallas_call(
            functools.partial(combine_kernel, local),
            out_shape=jax.ShapeDtypeStruct((frames, width), BF16 if last else F32),
            in_specs=[SMEM] + [VMEM] * (3 + len(back)),
            out_specs=VMEM,
            scratch_shapes=apart,
            compiler_params=params(16),
            cost_estimate=cost(4 * frames * width * rows, 3 * MIB),
            name=f"combine_{local}",
        )(place, targets, gates, base, *back)

    arrived_0 = jnp.concatenate(exchanged(outgoing_0 + far), 0)
    arrived_1 = over_time(outgoing_1)
    parts = gathered(arrived_0)
    send_x_0, send_0, keep_x_0, keep_0 = experts(0, parts, True, [outgoing_1])
    away_0 = add("0", *in_hbm(keep_x_0), core_swap(send_x_0))
    got_0 = from_chips(away_0)
    arrived_1 = take(arrived_1, [away_0[0]])
    parts = [arrived_1, core_swap(arrived_1)]
    send_x_1, send_1, keep_x_1, keep_1 = experts(1, parts, False, [away_0[0]])
    total_0 = total(0, keep_0, [core_swap(send_0), *got_0], send_1)
    back_0 = over_time(total_0)
    got_1 = from_chips(add("1", *in_hbm(keep_x_1), core_swap(send_x_1), [total_0]))
    back_1 = exchanged(spread(1, keep_1, [core_swap(send_1), *got_1], back_0))
    return combine(1, back_1, combine(0, [back_0], state))


def solution(mesh):
    return jax.shard_map(
        per_device,
        mesh=mesh,
        in_specs=(
            P("tm", None),
            P("tm", "mp"),
            P("tm", "mp"),
            P("tm", "mp"),
            P(None, "tm"),
            P("mp", None),
            P("tm", None),
            P("tm", None),
            P("tm", None, "mp"),
            P("tm", None, "mp"),
            P("tm", "mp", None),
        ),
        out_specs=P("tm", "mp"),
        check_vma=False,
    )
```

```python
import functools

import jax
import jax.numpy as jnp
from jax import lax
from jax.experimental import pallas as pl
from jax.experimental.pallas import tpu as pltpu
from jax.sharding import PartitionSpec as P

HEADS = 16
TOP = 2
LEFT = 256
EPS = 1e-06
LANES = 128
MIB = 1 << 20
F32 = jnp.float32
BF16 = jnp.bfloat16

VMEM = pl.BlockSpec(memory_space=pltpu.VMEM)
SMEM = pl.BlockSpec(memory_space=pltpu.SMEM)
ANY = pl.BlockSpec(memory_space=pl.ANY)
HBM = pl.BlockSpec(memory_space=pltpu.HBM)


def params(mib):
    return pltpu.CompilerParams(vmem_limit_bytes=mib * MIB)


def cost(flops, moved, transcendentals=0):
    return pl.CostEstimate(flops=flops, bytes_accessed=moved, transcendentals=transcendentals)


def from_behind(x, axis, by):
    size = lax.axis_size(axis)
    pairs = [(i, i + by) for i in range(size) if 0 <= i + by < size]
    return lax.ppermute(x, axis, pairs)


def core_swap(x):
    size = lax.axis_size("mp")
    return lax.ppermute(x, "mp", [(i, i ^ 1) for i in range(size)])


def from_chip(x, by):
    chips = lax.axis_size("mp") // 2
    pairs = [(c * 2 + k, ((c + by) % chips) * 2 + k) for c in range(chips) for k in range(2)]
    return lax.ppermute(x, "mp", pairs)


def gathered(x):
    chips = lax.axis_size("mp") // 2
    mine = [x] + [from_chip(x, by) for by in range(1, chips)]
    return mine + [core_swap(part) for part in mine]


def exchanged(blocks):
    size = lax.axis_size("tm")
    return [blocks[0]] + [
        lax.ppermute(block, "tm", [(i, (i + s) % size) for i in range(size)])
        for s, block in enumerate(blocks)
        if s > 0
    ]


def route_kernel(capacity, local_experts, n_time, ids_ref, ranks_ref, targets_ref):
    frames = ids_ref.shape[0]
    lanes = ranks_ref.shape[0]
    ids = ids_ref[...]
    owner = ids // local_experts
    ids = (ids - owner * local_experts) * n_time + owner
    experts = lax.broadcasted_iota(jnp.int32, (frames, lanes), 1)
    hits = [ids[:, k : k + 1] == experts for k in range(TOP)]
    named = functools.reduce(jnp.logical_or, hits)
    ones = jnp.where(named, 1.0, 0.0).astype(BF16)
    row = lax.broadcasted_iota(jnp.int32, (frames, frames), 0)
    column = lax.broadcasted_iota(jnp.int32, (frames, frames), 1)
    before = jnp.where(column < row, 1.0, 0.0).astype(BF16)
    ranks = jnp.dot(before, ones, preferred_element_type=F32)
    ranks_ref[...] = jnp.where(named, ranks, -1.0).T
    places = []
    for k in range(TOP):
        slot = jnp.sum(jnp.where(hits[k], ranks, 0.0), 1, keepdims=True).astype(jnp.int32)
        places.append(ids[:, k : k + 1] * capacity + slot)
    targets_ref[...] = jnp.concatenate(places, 1)


def attend_kernel(scale, head_width, start, meta_ref, order_ref, *refs):
    if start > 0:
        edges_any, q_any, k_any, v_any, proj_any = refs[:5]
        send_ref, keep_x_ref, keep_ref, edges_ref, q_all, k_ref, v_ref, proj_ref, sems = refs[5:]
        moves = [
            (k_any, k_ref),
            (q_any, q_all),
            (v_any, v_ref),
            (edges_any, edges_ref),
            (proj_any, proj_ref),
        ]
    else:
        edges_ref, q_all, k_all, v_all, proj_ref, tails_any = refs[:6]
        send_ref, keep_x_ref, keep_ref, k_ref, v_ref, sems = refs[6:]
        first_rows = pl.ds(0, keep_ref.shape[0])
        moves = [
            (tails_any.at[0], k_ref.at[pl.ds(0, LEFT)]),
            (k_all.at[first_rows], k_ref.at[pl.ds(LEFT, keep_ref.shape[0])]),
            (tails_any.at[1], v_ref.at[pl.ds(0, LEFT)]),
            (v_all.at[first_rows], v_ref.at[pl.ds(LEFT, keep_ref.shape[0])]),
        ]
    rows, columns = keep_ref.shape
    heads = columns // head_width
    block = LANES
    window = LEFT + block
    copies = [pltpu.make_async_copy(a, b, sems.at[i]) for i, (a, b) in enumerate(moves)]
    for copy in copies:
        copy.start()
    for copy in copies[:4]:
        copy.wait()
    edges = edges_ref[:, start : start + rows].astype(F32)
    edges = jnp.concatenate([edges, jnp.zeros((6, rows), F32)], 0).T
    lane_head = lax.broadcasted_iota(jnp.int32, (block, columns), 1) // head_width
    context = []
    for r in range(0, rows, block):
        key = k_ref[r : r + window, :]
        value = v_ref[r : r + window, :]
        query = q_all[start + r : start + r + block, :]
        places = lax.broadcasted_iota(jnp.int32, (block, window), 1)
        places = (places + (meta_ref[0] + (start + r - LEFT))).astype(F32)
        lower = jnp.maximum(edges[r : r + block, 0:1] - LEFT, 0.0)
        upper = edges[r : r + block, 1:2]
        visible = (places >= lower) & (places <= upper)
        own = [jnp.where(lane_head == h, query, jnp.zeros_like(query)) for h in range(heads)]
        own = jnp.concatenate(own, 0)
        scores = lax.dot_general(own, key, (((1,), (1,)), ((), ())), preferred_element_type=F32)
        scores = (scores * scale).reshape(heads, block, window)
        scores = jnp.where(visible[None], scores, -1e30)
        highest = jnp.max(scores, 2, keepdims=True)
        expos = jnp.exp(scores - highest)
        weights = (expos * (1.0 / jnp.sum(expos, 2, keepdims=True))).astype(BF16)
        weights = weights.reshape(heads * block, window)
        product = jnp.dot(weights, value, preferred_element_type=F32)
        mixed = product[0:block]
        for h in range(1, heads):
            mixed = jnp.where(lane_head == h, product[h * block : (h + 1) * block], mixed)
        context.append(mixed.astype(BF16))
    context = jnp.concatenate(context, 0)
    for copy in copies[4:]:
        copy.wait()
    count = proj_ref.shape[1] // columns // 2
    for i in range(2 * count):
        at = pl.multiple_of(order_ref[i] * columns, columns)
        part = jnp.dot(context, proj_ref[:, pl.ds(at, columns)], preferred_element_type=F32)
        j = (i - 1) % count * columns
        if i >= count:
            send_ref[:, j : j + columns] = part.astype(BF16)
        elif i > 0:
            keep_x_ref[:, j : j + columns] = part
        else:
            keep_ref[...] = part


def picked_rows(e, capacity, ranks_ref, state):
    slot = lax.broadcasted_iota(jnp.int32, (capacity, state.shape[0]), 0).astype(F32)
    pick = jnp.where(slot == ranks_ref[pl.ds(e, 1), :], 1.0, 0.0).astype(BF16)
    return jnp.dot(pick, state, preferred_element_type=F32).astype(BF16)


def scatter_rows(local, first, n_time, at_ref, ranks_ref, state, out_refs):
    for s, out_ref in enumerate(out_refs, first):
        owner = at_ref[0] + s
        owner = jnp.where(owner >= n_time, owner - n_time, owner)
        out_ref[...] = picked_rows(local * n_time + owner, out_ref.shape[0], ranks_ref, state)


def state_kernel(parts, column, n_time, at_ref, *refs):
    frames_ref, ranks_ref, state_ref = refs[2 * parts : 2 * parts + 3]
    width = state_ref.shape[1]
    halves = []
    for keep_ref, swapped_ref, *got in (refs[:parts], refs[parts : 2 * parts]):
        half = keep_ref[...] + swapped_ref[:, column : column + width].astype(F32)
        for ref in got:
            half = half + ref[...].astype(F32)
        halves.append(half)
    attended = jnp.concatenate(halves, 0)
    state = (frames_ref[...].astype(F32) + attended).astype(BF16)
    state_ref[...] = state
    scatter_rows(0, 0, n_time, at_ref, ranks_ref, state, refs[2 * parts + 3 :])


def dispatch_kernel(pieces, first, n_time, at_ref, *refs):
    own = refs[0][...]
    ranks_ref, *blocks, out_ref = refs[pieces:]
    scatter_rows(0, first, n_time, at_ref, ranks_ref, own, blocks)
    state = jnp.concatenate([own] + [ref[...] for ref in refs[1:pieces]], 1)
    capacity = out_ref.shape[0] // n_time
    for owner in range(n_time):
        rows = picked_rows(n_time + owner, capacity, ranks_ref, state)
        out_ref[owner * capacity : (owner + 1) * capacity, :] = rows


def join_kernel(*refs):
    *pieces, out_ref = refs
    count = pieces[0].shape[0]
    for s, ref in enumerate(pieces):
        out_ref[s * count : (s + 1) * count, :] = ref[...]


def take_kernel(rows_ref, *refs):
    refs[-1][...] = rows_ref[...]


def expert_kernel(local, starts, width, awaited, order_ref, *refs):
    arrays = len(starts)
    rows_in = refs[:arrays]
    gate_any, up_any, down_any = refs[arrays : arrays + 3]
    *outs, gate_ref, up_ref, down_ref, normed_ref, active_ref, sems = refs[arrays + 3 + awaited :]
    *send_x_refs, send_ref, keep_x_ref, keep_ref = outs
    rows, model = normed_ref.shape
    hidden = active_ref.shape[1]
    moves = [
        (gate_any.at[local], gate_ref),
        (up_any.at[local], up_ref),
        (down_any.at[local], down_ref),
    ]
    copies = [pltpu.make_async_copy(a, b, sems.at[i]) for i, (a, b) in enumerate(moves)]
    for copy in copies:
        copy.start()

    blocks = []
    for ref, start in zip(rows_in, starts):
        blocks += [(ref, start, c) for c in range(0, ref.shape[1], width)]
    step = min(rows, 256)

    def norm(i, carry):
        at_row = pl.multiple_of(i * step, step)
        parts = [
            ref[pl.ds(pl.multiple_of(start + i * step, step), step), c : c + width].astype(F32)
            for ref, start, c in blocks
        ]
        squares = sum(jnp.sum(part * part, 1, keepdims=True) for part in parts)
        factor = lax.rsqrt(squares * (1.0 / model) + EPS)
        for j, part in enumerate(parts):
            at = pl.multiple_of(order_ref[j] * width, width)
            normed_ref[pl.ds(at_row, step), pl.ds(at, width)] = (part * factor).astype(BF16)
        return carry

    lax.fori_loop(0, rows // step, norm, 0)
    copies[0].wait()
    copies[1].wait()
    tile = min(rows, 1024)
    chunk = min(hidden, 256)
    for r in range(0, rows, tile):
        normed = normed_ref[r : r + tile, :]
        for c in range(0, hidden, chunk):
            gate = jnp.dot(normed, gate_ref[:, c : c + chunk], preferred_element_type=F32)
            up = jnp.dot(normed, up_ref[:, c : c + chunk], preferred_element_type=F32)
            half = 0.5 * gate
            active = (half + half * jnp.tanh(half)) * up
            active_ref[r : r + tile, c : c + chunk] = active.astype(BF16)
    copies[2].wait()
    count = len(blocks) // 2
    def project(i, out_refs, column):
        at = pl.multiple_of(order_ref[i] * width, width)
        weight = down_ref[:, pl.ds(at, width)]
        result = jnp.dot(active_ref[...], weight, preferred_element_type=F32)
        each = rows // len(out_refs)
        for j, out_ref in enumerate(out_refs):
            part = result[j * each : (j + 1) * each]
            out_ref[:, column : column + width] = part.astype(out_ref.dtype)

    for by in range(1, count):
        project(count + by, send_x_refs, (by - 1) * width)
    project(count, [send_ref], 0)
    for by in range(1, count):
        project(by, [keep_x_ref], (by - 1) * width)
    project(0, [keep_ref], 0)


def add_kernel(width, passed, keep_ref, got_ref, other, *out_refs):
    if passed:
        *out_refs, passed_ref = out_refs
        passed_ref[...] = other[...]
    for i, out_ref in enumerate(out_refs):
        at = slice(i * width, (i + 1) * width)
        out_ref[...] = (keep_ref[:, at] + got_ref[:, at].astype(F32)).astype(BF16)


def total_kernel(n_time, at_ref, keep_ref, *refs):
    *got, after_any, out_ref = refs
    capacity = out_ref.shape[0] // n_time
    for s in range(n_time):
        rows = slice(s * capacity, (s + 1) * capacity)
        total = keep_ref[rows, :]
        for ref in got:
            total = total + ref[rows, :].astype(F32)
        place = at_ref[0] - s
        place = jnp.where(place < 0, place + n_time, place)
        out_ref[pl.ds(pl.multiple_of(place * capacity, capacity), capacity), :] = total.astype(BF16)


def spread_kernel(n_time, at_ref, keep_ref, swapped_ref, *refs):
    got, outs = refs[: -n_time - 1], refs[-n_time:]
    capacity = outs[0].shape[0]
    for s, out_ref in enumerate(outs):
        place = at_ref[0] + s
        place = jnp.where(place >= n_time, place - n_time, place)
        at = pl.ds(pl.multiple_of(place * capacity, capacity), capacity)
        total = keep_ref[at, :] + swapped_ref[at, :].astype(F32)
        for ref in got:
            total = total + ref[at, :].astype(F32)
        out_ref[...] = total.astype(BF16)


def combine_kernel(local, at_ref, targets_ref, gates_ref, base_ref, *refs):
    if len(refs) == 2:
        back_ref, out_ref = refs
    else:
        *got, out_ref, back_ref = refs
        n_time, capacity = len(got), got[0].shape[0]
        for s, ref in enumerate(got):
            place = at_ref[0] - s
            place = jnp.where(place < 0, place + n_time, place)
            back_ref[pl.ds(pl.multiple_of(place * capacity, capacity), capacity), :] = ref[...]
    back = back_ref[...]
    rows = back.shape[0]
    frames = targets_ref.shape[0]
    places = lax.broadcasted_iota(jnp.int32, (frames, rows), 1) + local * rows
    total = base_ref[...].astype(F32)
    for k in range(TOP):
        pick = jnp.where(places == targets_ref[:, k : k + 1], 1.0, 0.0).astype(BF16)
        total = total + gates_ref[:, k : k + 1] * jnp.dot(pick, back, preferred_element_type=F32)
    out_ref[...] = total.astype(out_ref.dtype)


def per_device(
    frames_in,
    queries,
    keys,
    values,
    segment_edges,
    out_proj,
    expert_ids,
    gates,
    w_gate,
    w_up,
    w_down,
):
    frames, model = frames_in.shape
    width = queries.shape[1]
    n_model = lax.axis_size("mp")
    n_time = lax.axis_size("tm")
    chips = n_model // 2
    head_width = model // HEADS
    scale = head_width ** (-0.5)
    local_experts = w_gate.shape[0]
    hidden = w_gate.shape[2]
    experts_all = local_experts * n_time
    capacity = 4 * frames // experts_all
    rows = n_time * capacity
    lanes = -(-experts_all // LANES) * LANES
    at_time = lax.axis_index("tm")
    at_model = lax.axis_index("mp")
    chip, core = at_model // 2, at_model % 2
    mine = [((chip - by) % chips) * 2 + core for by in range(chips)]
    others = [((chip - by) % chips) * 2 + 1 - core for by in range(chips)]
    order = jnp.stack(mine + others).astype(jnp.int32)
    offset = (at_time * frames).astype(jnp.int32).reshape(1)
    place = at_time.astype(jnp.int32).reshape(1)
    away = (chips - 1) * width

    tails = from_behind(jnp.stack([keys[frames - LEFT :], values[frames - LEFT :]], 0), "tm", 1)
    own_frames = lax.dynamic_slice_in_dim(frames_in, at_model * width, width, 1)

    ranks, targets = pl.pallas_call(
        functools.partial(route_kernel, capacity, local_experts, n_time),
        out_shape=(
            jax.ShapeDtypeStruct((lanes, frames), F32),
            jax.ShapeDtypeStruct((frames, TOP), jnp.int32),
        ),
        in_specs=[VMEM],
        out_specs=(VMEM, VMEM),
        compiler_params=params(16),
        cost_estimate=cost(2 * frames * frames * lanes, frames * 1024),
        name="route",
    )(expert_ids)

    def in_hbm(*arrays):
        return [pltpu.with_memory_space_constraint(x, pltpu.HBM) for x in arrays]

    def attended_outs(count):
        return (
            jax.ShapeDtypeStruct((count, chips * width), BF16),
            jax.ShapeDtypeStruct((count, away), F32),
            jax.ShapeDtypeStruct((count, width), F32),
        )

    def attend_cost(count):
        return cost(count * 384 * width * 16, count * width * 8, count * 384 * 4)

    inputs = (segment_edges, queries, keys, values, out_proj)
    *late, edges_vmem, q_vmem, k_vmem, v_vmem, proj_vmem = pl.pallas_call(
        functools.partial(attend_kernel, scale, head_width, LEFT),
        out_shape=attended_outs(frames - LEFT)
        + tuple(jax.ShapeDtypeStruct(x.shape, x.dtype) for x in inputs),
        in_specs=[SMEM, SMEM] + [HBM] * 5,
        out_specs=(VMEM,) * 8,
        scratch_shapes=[pltpu.SemaphoreType.DMA((5,))],
        compiler_params=params(16),
        cost_estimate=attend_cost(frames - LEFT),
        name="attend_late",
    )(offset, order, *in_hbm(*inputs))
    early = pl.pallas_call(
        functools.partial(attend_kernel, scale, head_width, 0),
        out_shape=attended_outs(LEFT),
        in_specs=[SMEM, SMEM] + [VMEM] * 5 + [ANY],
        out_specs=(VMEM,) * 3,
        scratch_shapes=[
            pltpu.VMEM((2 * LEFT, width), BF16),
            pltpu.VMEM((2 * LEFT, width), BF16),
            pltpu.SemaphoreType.DMA((4,)),
        ],
        compiler_params=params(16),
        cost_estimate=attend_cost(LEFT),
        name="attend_early",
    )(offset, order, edges_vmem, q_vmem, k_vmem, v_vmem, proj_vmem, tails)

    def add(name, keep, got, other, passed=False):
        outs = (jax.ShapeDtypeStruct((keep.shape[0], width), BF16),) * (chips - 1)
        if passed:
            outs += (jax.ShapeDtypeStruct(other.shape, other.dtype),)
        return pl.pallas_call(
            functools.partial(add_kernel, width, passed),
            in_specs=[VMEM, VMEM, VMEM if passed else ANY],
            out_specs=(VMEM,) * len(outs),
            out_shape=outs,
            compiler_params=params(16),
            cost_estimate=cost(keep.size, keep.size * 8),
            name=f"add_{name}",
        )(keep, got, other)

    def from_chips(parts):
        return [from_chip(part, chips - by) for by, part in enumerate(parts, 1)]

    def attended(name, send, keep_x, keep):
        swapped = core_swap(send)
        return [keep, swapped, *from_chips(add(name, keep_x, swapped, swapped))]

    late = attended("late", *late)
    early = attended("early", *early)

    def blocks_of(count):
        return (jax.ShapeDtypeStruct((capacity, width), BF16),) * count

    near = n_time // 2 + 1
    state, *outgoing_0 = pl.pallas_call(
        functools.partial(state_kernel, len(early), away, n_time),
        out_shape=(jax.ShapeDtypeStruct((frames, width), BF16),) + blocks_of(near),
        in_specs=[SMEM] + [VMEM] * (2 * len(early) + 2),
        out_specs=(VMEM,) * (1 + near),
        compiler_params=params(16),
        cost_estimate=cost(frames * width * rows, 4 * MIB),
        name="state",
    )(place, *early, *late, own_frames, ranks)
    wide = [state] + [from_chip(state, by) for by in range(1, chips)]
    *far, outgoing_1 = pl.pallas_call(
        functools.partial(dispatch_kernel, chips, near, n_time),
        out_shape=blocks_of(n_time - near)
        + (jax.ShapeDtypeStruct((rows, chips * width), BF16),),
        in_specs=[SMEM] + [VMEM] * (chips + 1),
        out_specs=(VMEM,) * (n_time - near + 1),
        compiler_params=params(16),
        cost_estimate=cost(3 * frames * width * rows, 3 * MIB),
        name="dispatch",
    )(place, *wide, ranks)

    def over_time(x):
        columns = x.shape[1]
        x = x.reshape(n_time, capacity, columns)
        x = lax.all_to_all(x, "tm", split_axis=0, concat_axis=0, tiled=True)
        return x.reshape(rows, columns)

    def take(x, after):
        return pl.pallas_call(
            take_kernel,
            in_specs=[VMEM] + [ANY] * len(after),
            out_specs=VMEM,
            out_shape=jax.ShapeDtypeStruct(x.shape, x.dtype),
            compiler_params=params(16),
            cost_estimate=cost(x.size, x.size * 4),
            name="take",
        )(x, *after)

    def experts(local, parts, after):
        outs = [jax.ShapeDtypeStruct((rows, columns), BF16) for columns in (away, width)]
        outs += [jax.ShapeDtypeStruct((rows, columns), F32) for columns in (away, width)]
        return pl.pallas_call(
            functools.partial(expert_kernel, local, (0,) * len(parts), width, len(after)),
            in_specs=[SMEM] + [VMEM] * len(parts) + [HBM] * 3 + [ANY] * len(after),
            out_specs=(VMEM,) * 4,
            scratch_shapes=[
                pltpu.VMEM((model, hidden), BF16),
                pltpu.VMEM((model, hidden), BF16),
                pltpu.VMEM((hidden, model), BF16),
                pltpu.VMEM((rows, model), BF16),
                pltpu.VMEM((rows, hidden), BF16),
                pltpu.SemaphoreType.DMA((3,)),
            ],
            out_shape=tuple(outs),
            compiler_params=params(20),
            cost_estimate=cost(6 * rows * model * hidden, 12 * MIB, rows * hidden),
            name=f"experts_{local}",
        )(order, *parts, *in_hbm(w_gate, w_up, w_down), *after)

    def total(local, parts, after):
        return pl.pallas_call(
            functools.partial(total_kernel, n_time),
            in_specs=[SMEM] + [VMEM] * len(parts) + [ANY],
            out_specs=VMEM,
            out_shape=jax.ShapeDtypeStruct((rows, width), BF16),
            compiler_params=params(16),
            cost_estimate=cost(rows * width * 4, rows * width * 10),
            name=f"total_{local}",
        )(place, *parts, after)

    def spread(local, parts, after):
        return pl.pallas_call(
            functools.partial(spread_kernel, n_time),
            in_specs=[SMEM] + [VMEM] * len(parts) + [ANY],
            out_specs=(VMEM,) * n_time,
            out_shape=(jax.ShapeDtypeStruct((capacity, width), BF16),) * n_time,
            compiler_params=params(16),
            cost_estimate=cost(rows * width * 4, rows * width * 10),
            name=f"spread_{local}",
        )(place, *parts, after)

    def combine(local, back, base):
        last = local == local_experts - 1
        apart = [pltpu.VMEM((rows, width), BF16)] if len(back) > 1 else []
        return pl.pallas_call(
            functools.partial(combine_kernel, local),
            out_shape=jax.ShapeDtypeStruct((frames, width), BF16 if last else F32),
            in_specs=[SMEM] + [VMEM] * (3 + len(back)),
            out_specs=VMEM,
            scratch_shapes=apart,
            compiler_params=params(16),
            cost_estimate=cost(4 * frames * width * rows, 3 * MIB),
            name=f"combine_{local}",
        )(place, targets, gates, base, *back)

    arrived_0 = pl.pallas_call(
        join_kernel,
        in_specs=[VMEM] * n_time,
        out_specs=VMEM,
        out_shape=jax.ShapeDtypeStruct((rows, width), BF16),
        compiler_params=params(16),
        cost_estimate=cost(rows * width, rows * width * 4),
        name="join",
    )(*exchanged(outgoing_0 + far))
    arrived_1 = over_time(outgoing_1)
    send_x_0, send_0, keep_x_0, keep_0 = experts(0, gathered(arrived_0), [outgoing_1])
    *away_0, send_0 = add("0", keep_x_0, core_swap(send_x_0), send_0, True)
    swapped_0 = core_swap(send_0)
    got_0 = from_chips(away_0)
    arrived_1 = take(arrived_1, [swapped_0])
    parts = [arrived_1, core_swap(arrived_1)]
    send_x_1, send_1, keep_x_1, keep_1 = experts(1, parts, [away_0[0]])
    total_0 = total(0, [keep_0, swapped_0, *got_0], send_1)
    back_0 = over_time(total_0)
    got_1 = from_chips(add("1", keep_x_1, core_swap(send_x_1), total_0))
    back_1 = exchanged(spread(1, [keep_1, core_swap(send_1), *got_1], back_0))
    return combine(1, back_1, combine(0, [back_0], state))


def solution(mesh):
    return jax.shard_map(
        per_device,
        mesh=mesh,
        in_specs=(
            P("tm", None),
            P("tm", "mp"),
            P("tm", "mp"),
            P("tm", "mp"),
            P(None, "tm"),
            P("mp", None),
            P("tm", None),
            P("tm", None),
            P("tm", None, "mp"),
            P("tm", None, "mp"),
            P("tm", "mp", None),
        ),
        out_specs=P("tm", "mp"),
        check_vma=False,
    )
```

```python
import functools

import jax
import jax.numpy as jnp
from jax import lax
from jax.experimental import pallas as pl
from jax.experimental.pallas import tpu as pltpu
from jax.sharding import PartitionSpec as P

HEADS = 16
TOP = 2
LEFT = 256
EPS = 1e-06
LANES = 128
MIB = 1 << 20
F32 = jnp.float32
BF16 = jnp.bfloat16

VMEM = pl.BlockSpec(memory_space=pltpu.VMEM)
SMEM = pl.BlockSpec(memory_space=pltpu.SMEM)
ANY = pl.BlockSpec(memory_space=pl.ANY)
HBM = pl.BlockSpec(memory_space=pltpu.HBM)


def params(mib):
    return pltpu.CompilerParams(vmem_limit_bytes=mib * MIB)


def cost(flops, moved, transcendentals=0):
    return pl.CostEstimate(flops=flops, bytes_accessed=moved, transcendentals=transcendentals)


def from_behind(x, axis, by):
    size = lax.axis_size(axis)
    pairs = [(i, i + by) for i in range(size) if 0 <= i + by < size]
    return lax.ppermute(x, axis, pairs)


def core_swap(x):
    size = lax.axis_size("mp")
    return lax.ppermute(x, "mp", [(i, i ^ 1) for i in range(size)])


def from_chip(x, by):
    chips = lax.axis_size("mp") // 2
    pairs = [(c * 2 + k, ((c + by) % chips) * 2 + k) for c in range(chips) for k in range(2)]
    return lax.ppermute(x, "mp", pairs)


def gathered(x):
    chips = lax.axis_size("mp") // 2
    mine = [x] + [from_chip(x, by) for by in range(1, chips)]
    return mine + [core_swap(part) for part in mine]


def exchanged(blocks):
    size = lax.axis_size("tm")
    return [blocks[0]] + [
        lax.ppermute(block, "tm", [(i, (i + s) % size) for i in range(size)])
        for s, block in enumerate(blocks)
        if s > 0
    ]


def route_kernel(capacity, local_experts, n_time, ids_ref, ranks_ref, targets_ref):
    frames = ids_ref.shape[0]
    lanes = ranks_ref.shape[0]
    ids = ids_ref[...]
    owner = ids // local_experts
    ids = (ids - owner * local_experts) * n_time + owner
    experts = lax.broadcasted_iota(jnp.int32, (frames, lanes), 1)
    hits = [ids[:, k : k + 1] == experts for k in range(TOP)]
    named = functools.reduce(jnp.logical_or, hits)
    ones = jnp.where(named, 1.0, 0.0).astype(BF16)
    row = lax.broadcasted_iota(jnp.int32, (frames, frames), 0)
    column = lax.broadcasted_iota(jnp.int32, (frames, frames), 1)
    before = jnp.where(column < row, 1.0, 0.0).astype(BF16)
    ranks = jnp.dot(before, ones, preferred_element_type=F32)
    ranks_ref[...] = jnp.where(named, ranks, -1.0).T
    places = []
    for k in range(TOP):
        slot = jnp.sum(jnp.where(hits[k], ranks, 0.0), 1, keepdims=True).astype(jnp.int32)
        places.append(ids[:, k : k + 1] * capacity + slot)
    targets_ref[...] = jnp.concatenate(places, 1)


def attend_kernel(scale, head_width, start, meta_ref, order_ref, *refs):
    if start > 0:
        edges_any, q_any, k_any, v_any, proj_any = refs[:5]
        send_ref, keep_x_ref, keep_ref, edges_ref, q_all, k_ref, v_ref, proj_ref, sems = refs[5:]
        moves = [
            (k_any, k_ref),
            (q_any, q_all),
            (v_any, v_ref),
            (edges_any, edges_ref),
            (proj_any, proj_ref),
        ]
    else:
        edges_ref, q_all, k_all, v_all, proj_ref, tails_any = refs[:6]
        send_ref, keep_x_ref, keep_ref, k_ref, v_ref, sems = refs[6:]
        first_rows = pl.ds(0, keep_ref.shape[0])
        moves = [
            (tails_any.at[0], k_ref.at[pl.ds(0, LEFT)]),
            (k_all.at[first_rows], k_ref.at[pl.ds(LEFT, keep_ref.shape[0])]),
            (tails_any.at[1], v_ref.at[pl.ds(0, LEFT)]),
            (v_all.at[first_rows], v_ref.at[pl.ds(LEFT, keep_ref.shape[0])]),
        ]
    rows, columns = keep_ref.shape
    heads = columns // head_width
    block = LANES
    window = LEFT + block
    copies = [pltpu.make_async_copy(a, b, sems.at[i]) for i, (a, b) in enumerate(moves)]
    for copy in copies:
        copy.start()
    for copy in copies[:4]:
        copy.wait()
    edges = edges_ref[:, start : start + rows].astype(F32)
    edges = jnp.concatenate([edges, jnp.zeros((6, rows), F32)], 0).T
    lane_head = lax.broadcasted_iota(jnp.int32, (block, columns), 1) // head_width
    context = []
    for r in range(0, rows, block):
        key = k_ref[r : r + window, :]
        value = v_ref[r : r + window, :]
        query = q_all[start + r : start + r + block, :]
        places = lax.broadcasted_iota(jnp.int32, (block, window), 1)
        places = (places + (meta_ref[0] + (start + r - LEFT))).astype(F32)
        lower = jnp.maximum(edges[r : r + block, 0:1] - LEFT, 0.0)
        upper = edges[r : r + block, 1:2]
        visible = (places >= lower) & (places <= upper)
        own = [jnp.where(lane_head == h, query, jnp.zeros_like(query)) for h in range(heads)]
        own = jnp.concatenate(own, 0)
        scores = lax.dot_general(own, key, (((1,), (1,)), ((), ())), preferred_element_type=F32)
        scores = (scores * scale).reshape(heads, block, window)
        scores = jnp.where(visible[None], scores, -1e30)
        highest = jnp.max(scores, 2, keepdims=True)
        expos = jnp.exp(scores - highest)
        weights = (expos * (1.0 / jnp.sum(expos, 2, keepdims=True))).astype(BF16)
        weights = weights.reshape(heads * block, window)
        product = jnp.dot(weights, value, preferred_element_type=F32)
        mixed = product[0:block]
        for h in range(1, heads):
            mixed = jnp.where(lane_head == h, product[h * block : (h + 1) * block], mixed)
        context.append(mixed.astype(BF16))
    context = jnp.concatenate(context, 0)
    for copy in copies[4:]:
        copy.wait()
    count = proj_ref.shape[1] // columns // 2
    for i in range(2 * count):
        at = pl.multiple_of(order_ref[i] * columns, columns)
        part = jnp.dot(context, proj_ref[:, pl.ds(at, columns)], preferred_element_type=F32)
        j = (i - 1) % count * columns
        if i >= count:
            send_ref[:, j : j + columns] = part.astype(BF16)
        elif i > 0:
            keep_x_ref[:, j : j + columns] = part
        else:
            keep_ref[...] = part


def picked_rows(e, capacity, ranks_ref, state):
    slot = lax.broadcasted_iota(jnp.int32, (capacity, state.shape[0]), 0).astype(F32)
    pick = jnp.where(slot == ranks_ref[pl.ds(e, 1), :], 1.0, 0.0).astype(BF16)
    return jnp.dot(pick, state, preferred_element_type=F32).astype(BF16)


def scatter_rows(local, first, n_time, at_ref, ranks_ref, state, out_refs):
    for s, out_ref in enumerate(out_refs, first):
        owner = at_ref[0] + s
        owner = jnp.where(owner >= n_time, owner - n_time, owner)
        out_ref[...] = picked_rows(local * n_time + owner, out_ref.shape[0], ranks_ref, state)


def state_kernel(parts, column, n_time, at_ref, *refs):
    frames_ref, ranks_ref, state_ref = refs[2 * parts : 2 * parts + 3]
    width = state_ref.shape[1]
    halves = []
    for keep_ref, swapped_ref, *got in (refs[:parts], refs[parts : 2 * parts]):
        half = keep_ref[...] + swapped_ref[:, column : column + width].astype(F32)
        for ref in got:
            half = half + ref[...].astype(F32)
        halves.append(half)
    attended = jnp.concatenate(halves, 0)
    state = (frames_ref[...].astype(F32) + attended).astype(BF16)
    state_ref[...] = state
    scatter_rows(0, 0, n_time, at_ref, ranks_ref, state, refs[2 * parts + 3 :])


def dispatch_kernel(pieces, first, n_time, at_ref, *refs):
    own = refs[0][...]
    ranks_ref, *blocks, out_ref = refs[pieces:]
    scatter_rows(0, first, n_time, at_ref, ranks_ref, own, blocks)
    state = jnp.concatenate([own] + [ref[...] for ref in refs[1:pieces]], 1)
    capacity = out_ref.shape[0] // n_time
    for owner in range(n_time):
        rows = picked_rows(n_time + owner, capacity, ranks_ref, state)
        out_ref[owner * capacity : (owner + 1) * capacity, :] = rows


def join_kernel(*refs):
    *pieces, out_ref = refs
    count = pieces[0].shape[0]
    for s, ref in enumerate(pieces):
        out_ref[s * count : (s + 1) * count, :] = ref[...]


def take_kernel(rows_ref, *refs):
    refs[-1][...] = rows_ref[...]


def expert_kernel(local, starts, width, awaited, order_ref, *refs):
    arrays = len(starts)
    rows_in = refs[:arrays]
    gate_any, up_any, down_any = refs[arrays : arrays + 3]
    *outs, gate_ref, up_ref, down_ref, normed_ref, active_ref, sems = refs[arrays + 3 + awaited :]
    *send_x_refs, send_ref, keep_x_ref, keep_ref = outs
    rows, model = normed_ref.shape
    hidden = active_ref.shape[1]
    moves = [
        (gate_any.at[local], gate_ref),
        (up_any.at[local], up_ref),
        (down_any.at[local], down_ref),
    ]
    copies = [pltpu.make_async_copy(a, b, sems.at[i]) for i, (a, b) in enumerate(moves)]
    for copy in copies:
        copy.start()

    blocks = []
    for ref, start in zip(rows_in, starts):
        blocks += [(ref, start, c) for c in range(0, ref.shape[1], width)]
    step = min(rows, 256)

    def norm(i, carry):
        at_row = pl.multiple_of(i * step, step)
        parts = [
            ref[pl.ds(pl.multiple_of(start + i * step, step), step), c : c + width].astype(F32)
            for ref, start, c in blocks
        ]
        squares = sum(jnp.sum(part * part, 1, keepdims=True) for part in parts)
        factor = lax.rsqrt(squares * (1.0 / model) + EPS)
        for j, part in enumerate(parts):
            at = pl.multiple_of(order_ref[j] * width, width)
            normed_ref[pl.ds(at_row, step), pl.ds(at, width)] = (part * factor).astype(BF16)
        return carry

    lax.fori_loop(0, rows // step, norm, 0)
    copies[0].wait()
    copies[1].wait()
    tile = min(rows, 1024)
    chunk = min(hidden, 256)
    for r in range(0, rows, tile):
        normed = normed_ref[r : r + tile, :]
        for c in range(0, hidden, chunk):
            gate = jnp.dot(normed, gate_ref[:, c : c + chunk], preferred_element_type=F32)
            up = jnp.dot(normed, up_ref[:, c : c + chunk], preferred_element_type=F32)
            half = 0.5 * gate
            active = (half + half * jnp.tanh(half)) * up
            active_ref[r : r + tile, c : c + chunk] = active.astype(BF16)
    copies[2].wait()
    count = len(blocks) // 2
    def project(i, out_refs, column):
        at = pl.multiple_of(order_ref[i] * width, width)
        weight = down_ref[:, pl.ds(at, width)]
        result = jnp.dot(active_ref[...], weight, preferred_element_type=F32)
        each = rows // len(out_refs)
        for j, out_ref in enumerate(out_refs):
            part = result[j * each : (j + 1) * each]
            out_ref[:, column : column + width] = part.astype(out_ref.dtype)

    for by in range(1, count):
        project(count + by, send_x_refs, (by - 1) * width)
    project(count, [send_ref], 0)
    for by in range(1, count):
        project(by, [keep_x_ref], (by - 1) * width)
    project(0, [keep_ref], 0)


def add_kernel(width, keep_ref, got_ref, after_any, *out_refs):
    for i, out_ref in enumerate(out_refs):
        at = slice(i * width, (i + 1) * width)
        out_ref[...] = (keep_ref[:, at] + got_ref[:, at].astype(F32)).astype(BF16)


def total_kernel(n_time, at_ref, keep_ref, *refs):
    *got, after_any, out_ref = refs
    capacity = out_ref.shape[0] // n_time
    for s in range(n_time):
        rows = slice(s * capacity, (s + 1) * capacity)
        total = keep_ref[rows, :]
        for ref in got:
            total = total + ref[rows, :].astype(F32)
        place = at_ref[0] - s
        place = jnp.where(place < 0, place + n_time, place)
        out_ref[pl.ds(pl.multiple_of(place * capacity, capacity), capacity), :] = total.astype(BF16)


def spread_kernel(n_time, at_ref, keep_ref, swapped_ref, *refs):
    got, outs = refs[: -n_time - 1], refs[-n_time:]
    capacity = outs[0].shape[0]
    for s, out_ref in enumerate(outs):
        place = at_ref[0] + s
        place = jnp.where(place >= n_time, place - n_time, place)
        at = pl.ds(pl.multiple_of(place * capacity, capacity), capacity)
        total = keep_ref[at, :] + swapped_ref[at, :].astype(F32)
        for ref in got:
            total = total + ref[at, :].astype(F32)
        out_ref[...] = total.astype(BF16)


def combine_kernel(local, at_ref, targets_ref, gates_ref, base_ref, *refs):
    if len(refs) == 2:
        back_ref, out_ref = refs
    else:
        *got, out_ref, back_ref = refs
        n_time, capacity = len(got), got[0].shape[0]
        for s, ref in enumerate(got):
            place = at_ref[0] - s
            place = jnp.where(place < 0, place + n_time, place)
            back_ref[pl.ds(pl.multiple_of(place * capacity, capacity), capacity), :] = ref[...]
    back = back_ref[...]
    rows = back.shape[0]
    frames = targets_ref.shape[0]
    places = lax.broadcasted_iota(jnp.int32, (frames, rows), 1) + local * rows
    total = base_ref[...].astype(F32)
    for k in range(TOP):
        pick = jnp.where(places == targets_ref[:, k : k + 1], 1.0, 0.0).astype(BF16)
        total = total + gates_ref[:, k : k + 1] * jnp.dot(pick, back, preferred_element_type=F32)
    out_ref[...] = total.astype(out_ref.dtype)


def per_device(
    frames_in,
    queries,
    keys,
    values,
    segment_edges,
    out_proj,
    expert_ids,
    gates,
    w_gate,
    w_up,
    w_down,
):
    frames, model = frames_in.shape
    width = queries.shape[1]
    n_model = lax.axis_size("mp")
    n_time = lax.axis_size("tm")
    chips = n_model // 2
    head_width = model // HEADS
    scale = head_width ** (-0.5)
    local_experts = w_gate.shape[0]
    hidden = w_gate.shape[2]
    experts_all = local_experts * n_time
    capacity = 4 * frames // experts_all
    rows = n_time * capacity
    lanes = -(-experts_all // LANES) * LANES
    at_time = lax.axis_index("tm")
    at_model = lax.axis_index("mp")
    chip, core = at_model // 2, at_model % 2
    mine = [((chip - by) % chips) * 2 + core for by in range(chips)]
    others = [((chip - by) % chips) * 2 + 1 - core for by in range(chips)]
    order = jnp.stack(mine + others).astype(jnp.int32)
    offset = (at_time * frames).astype(jnp.int32).reshape(1)
    place = at_time.astype(jnp.int32).reshape(1)
    away = (chips - 1) * width

    tails = from_behind(jnp.stack([keys[frames - LEFT :], values[frames - LEFT :]], 0), "tm", 1)
    own_frames = lax.dynamic_slice_in_dim(frames_in, at_model * width, width, 1)

    ranks, targets = pl.pallas_call(
        functools.partial(route_kernel, capacity, local_experts, n_time),
        out_shape=(
            jax.ShapeDtypeStruct((lanes, frames), F32),
            jax.ShapeDtypeStruct((frames, TOP), jnp.int32),
        ),
        in_specs=[VMEM],
        out_specs=(VMEM, VMEM),
        compiler_params=params(16),
        cost_estimate=cost(2 * frames * frames * lanes, frames * 1024),
        name="route",
    )(expert_ids)

    def in_hbm(*arrays):
        return [pltpu.with_memory_space_constraint(x, pltpu.HBM) for x in arrays]

    def attended_outs(count):
        return (
            jax.ShapeDtypeStruct((count, chips * width), BF16),
            jax.ShapeDtypeStruct((count, away), F32),
            jax.ShapeDtypeStruct((count, width), F32),
        )

    def attend_cost(count):
        return cost(count * 384 * width * 16, count * width * 8, count * 384 * 4)

    inputs = (segment_edges, queries, keys, values, out_proj)
    *late, edges_vmem, q_vmem, k_vmem, v_vmem, proj_vmem = pl.pallas_call(
        functools.partial(attend_kernel, scale, head_width, LEFT),
        out_shape=attended_outs(frames - LEFT)
        + tuple(jax.ShapeDtypeStruct(x.shape, x.dtype) for x in inputs),
        in_specs=[SMEM, SMEM] + [HBM] * 5,
        out_specs=(VMEM,) * 8,
        scratch_shapes=[pltpu.SemaphoreType.DMA((5,))],
        compiler_params=params(16),
        cost_estimate=attend_cost(frames - LEFT),
        name="attend_late",
    )(offset, order, *in_hbm(*inputs))
    early = pl.pallas_call(
        functools.partial(attend_kernel, scale, head_width, 0),
        out_shape=attended_outs(LEFT),
        in_specs=[SMEM, SMEM] + [VMEM] * 5 + [ANY],
        out_specs=(VMEM,) * 3,
        scratch_shapes=[
            pltpu.VMEM((2 * LEFT, width), BF16),
            pltpu.VMEM((2 * LEFT, width), BF16),
            pltpu.SemaphoreType.DMA((4,)),
        ],
        compiler_params=params(16),
        cost_estimate=attend_cost(LEFT),
        name="attend_early",
    )(offset, order, edges_vmem, q_vmem, k_vmem, v_vmem, proj_vmem, tails)

    def add(name, keep, got, after):
        return pl.pallas_call(
            functools.partial(add_kernel, width),
            in_specs=[VMEM, VMEM, ANY],
            out_specs=(VMEM,) * (chips - 1),
            out_shape=(jax.ShapeDtypeStruct((keep.shape[0], width), BF16),) * (chips - 1),
            compiler_params=params(16),
            cost_estimate=cost(keep.size, keep.size * 8),
            name=f"add_{name}",
        )(keep, got, after)

    def from_chips(parts):
        return [from_chip(part, chips - by) for by, part in enumerate(parts, 1)]

    def attended(name, send, keep_x, keep):
        swapped = core_swap(send)
        return [keep, swapped, *from_chips(add(name, keep_x, swapped, swapped))]

    late = attended("late", *late)
    early = attended("early", *early)

    def blocks_of(count):
        return (jax.ShapeDtypeStruct((capacity, width), BF16),) * count

    near = n_time // 2 + 1
    state, *outgoing_0 = pl.pallas_call(
        functools.partial(state_kernel, len(early), away, n_time),
        out_shape=(jax.ShapeDtypeStruct((frames, width), BF16),) + blocks_of(near),
        in_specs=[SMEM] + [VMEM] * (2 * len(early) + 2),
        out_specs=(VMEM,) * (1 + near),
        compiler_params=params(16),
        cost_estimate=cost(frames * width * rows, 4 * MIB),
        name="state",
    )(place, *early, *late, own_frames, ranks)
    wide = [state] + [from_chip(state, by) for by in range(1, chips)]
    *far, outgoing_1 = pl.pallas_call(
        functools.partial(dispatch_kernel, chips, near, n_time),
        out_shape=blocks_of(n_time - near)
        + (jax.ShapeDtypeStruct((rows, chips * width), BF16),),
        in_specs=[SMEM] + [VMEM] * (chips + 1),
        out_specs=(VMEM,) * (n_time - near + 1),
        compiler_params=params(16),
        cost_estimate=cost(3 * frames * width * rows, 3 * MIB),
        name="dispatch",
    )(place, *wide, ranks)

    def over_time(x):
        columns = x.shape[1]
        x = x.reshape(n_time, capacity, columns)
        x = lax.all_to_all(x, "tm", split_axis=0, concat_axis=0, tiled=True)
        return x.reshape(rows, columns)

    def take(x, after):
        return pl.pallas_call(
            take_kernel,
            in_specs=[VMEM] + [ANY] * len(after),
            out_specs=VMEM,
            out_shape=jax.ShapeDtypeStruct(x.shape, x.dtype),
            compiler_params=params(16),
            cost_estimate=cost(x.size, x.size * 4),
            name="take",
        )(x, *after)

    def experts(local, parts, after):
        outs = [jax.ShapeDtypeStruct((rows, columns), BF16) for columns in (away, width)]
        outs += [jax.ShapeDtypeStruct((rows, columns), F32) for columns in (away, width)]
        return pl.pallas_call(
            functools.partial(expert_kernel, local, (0,) * len(parts), width, len(after)),
            in_specs=[SMEM] + [VMEM] * len(parts) + [HBM] * 3 + [ANY] * len(after),
            out_specs=(VMEM,) * 4,
            scratch_shapes=[
                pltpu.VMEM((model, hidden), BF16),
                pltpu.VMEM((model, hidden), BF16),
                pltpu.VMEM((hidden, model), BF16),
                pltpu.VMEM((rows, model), BF16),
                pltpu.VMEM((rows, hidden), BF16),
                pltpu.SemaphoreType.DMA((3,)),
            ],
            out_shape=tuple(outs),
            compiler_params=params(20),
            cost_estimate=cost(rows * hidden, rows * width),
            name=f"experts_{local}",
        )(order, *parts, *in_hbm(w_gate, w_up, w_down), *after)

    def total(local, parts, after):
        return pl.pallas_call(
            functools.partial(total_kernel, n_time),
            in_specs=[SMEM] + [VMEM] * len(parts) + [ANY],
            out_specs=VMEM,
            out_shape=jax.ShapeDtypeStruct((rows, width), BF16),
            compiler_params=params(16),
            cost_estimate=cost(rows * width * 4, rows * width * 10),
            name=f"total_{local}",
        )(place, *parts, after)

    def spread(local, parts, after):
        return pl.pallas_call(
            functools.partial(spread_kernel, n_time),
            in_specs=[SMEM] + [VMEM] * len(parts) + [ANY],
            out_specs=(VMEM,) * n_time,
            out_shape=(jax.ShapeDtypeStruct((capacity, width), BF16),) * n_time,
            compiler_params=params(16),
            cost_estimate=cost(rows * width * 4, rows * width * 10),
            name=f"spread_{local}",
        )(place, *parts, after)

    def combine(local, back, base):
        last = local == local_experts - 1
        apart = [pltpu.VMEM((rows, width), BF16)] if len(back) > 1 else []
        return pl.pallas_call(
            functools.partial(combine_kernel, local),
            out_shape=jax.ShapeDtypeStruct((frames, width), BF16 if last else F32),
            in_specs=[SMEM] + [VMEM] * (3 + len(back)),
            out_specs=VMEM,
            scratch_shapes=apart,
            compiler_params=params(16),
            cost_estimate=cost(4 * frames * width * rows, 3 * MIB),
            name=f"combine_{local}",
        )(place, targets, gates, base, *back)

    arrived_0 = pl.pallas_call(
        join_kernel,
        in_specs=[VMEM] * n_time,
        out_specs=VMEM,
        out_shape=jax.ShapeDtypeStruct((rows, width), BF16),
        compiler_params=params(16),
        cost_estimate=cost(rows * width, rows * width * 4),
        name="join",
    )(*exchanged(outgoing_0 + far))
    arrived_1 = over_time(outgoing_1)
    send_x_0, send_0, keep_x_0, keep_0 = experts(0, gathered(arrived_0), [outgoing_1])
    away_0 = add("0", keep_x_0, core_swap(send_x_0), send_0)
    got_0 = from_chips(away_0)
    arrived_1 = take(arrived_1, [away_0[0]])
    parts = [arrived_1, core_swap(arrived_1)]
    send_x_1, send_1, keep_x_1, keep_1 = experts(1, parts, [away_0[0]])
    total_0 = total(0, [keep_0, core_swap(send_0), *got_0], send_1)
    back_0 = over_time(total_0)
    got_1 = from_chips(add("1", keep_x_1, core_swap(send_x_1), total_0))
    back_1 = exchanged(spread(1, [keep_1, core_swap(send_1), *got_1], back_0))
    return combine(1, back_1, combine(0, [back_0], state))


def solution(mesh):
    return jax.shard_map(
        per_device,
        mesh=mesh,
        in_specs=(
            P("tm", None),
            P("tm", "mp"),
            P("tm", "mp"),
            P("tm", "mp"),
            P(None, "tm"),
            P("mp", None),
            P("tm", None),
            P("tm", None),
            P("tm", None, "mp"),
            P("tm", None, "mp"),
            P("tm", "mp", None),
        ),
        out_specs=P("tm", "mp"),
        check_vma=False,
    )
```

```python
import functools

import jax
import jax.numpy as jnp
from jax import lax
from jax.experimental import pallas as pl
from jax.experimental.pallas import tpu as pltpu
from jax.sharding import PartitionSpec as P

HEADS = 16
TOP = 2
LEFT = 256
EPS = 1e-06
LANES = 128
MIB = 1 << 20
F32 = jnp.float32
BF16 = jnp.bfloat16

VMEM = pl.BlockSpec(memory_space=pltpu.VMEM)
SMEM = pl.BlockSpec(memory_space=pltpu.SMEM)
ANY = pl.BlockSpec(memory_space=pl.ANY)
HBM = pl.BlockSpec(memory_space=pltpu.HBM)


def params(mib):
    return pltpu.CompilerParams(vmem_limit_bytes=mib * MIB)


def cost(flops, moved, transcendentals=0):
    return pl.CostEstimate(flops=flops, bytes_accessed=moved, transcendentals=transcendentals)


def from_behind(x, axis, by):
    size = lax.axis_size(axis)
    pairs = [(i, i + by) for i in range(size) if 0 <= i + by < size]
    return lax.ppermute(x, axis, pairs)


def core_swap(x):
    size = lax.axis_size("mp")
    return lax.ppermute(x, "mp", [(i, i ^ 1) for i in range(size)])


def from_chip(x, by):
    chips = lax.axis_size("mp") // 2
    pairs = [(c * 2 + k, ((c + by) % chips) * 2 + k) for c in range(chips) for k in range(2)]
    return lax.ppermute(x, "mp", pairs)


def gathered(x):
    chips = lax.axis_size("mp") // 2
    mine = [x] + [from_chip(x, by) for by in range(1, chips)]
    return mine + [core_swap(part) for part in mine]


def exchanged(blocks):
    size = lax.axis_size("tm")
    return [blocks[0]] + [
        lax.ppermute(block, "tm", [(i, (i + s) % size) for i in range(size)])
        for s, block in enumerate(blocks)
        if s > 0
    ]


def route_kernel(capacity, local_experts, n_time, ids_ref, ranks_ref, targets_ref):
    frames = ids_ref.shape[0]
    lanes = ranks_ref.shape[0]
    ids = ids_ref[...]
    owner = ids // local_experts
    ids = (ids - owner * local_experts) * n_time + owner
    experts = lax.broadcasted_iota(jnp.int32, (frames, lanes), 1)
    hits = [ids[:, k : k + 1] == experts for k in range(TOP)]
    named = functools.reduce(jnp.logical_or, hits)
    ones = jnp.where(named, 1.0, 0.0).astype(BF16)
    row = lax.broadcasted_iota(jnp.int32, (frames, frames), 0)
    column = lax.broadcasted_iota(jnp.int32, (frames, frames), 1)
    before = jnp.where(column < row, 1.0, 0.0).astype(BF16)
    ranks = jnp.dot(before, ones, preferred_element_type=F32)
    ranks_ref[...] = jnp.where(named, ranks, -1.0).T
    places = []
    for k in range(TOP):
        slot = jnp.sum(jnp.where(hits[k], ranks, 0.0), 1, keepdims=True).astype(jnp.int32)
        places.append(ids[:, k : k + 1] * capacity + slot)
    targets_ref[...] = jnp.concatenate(places, 1)


def attend_kernel(scale, head_width, start, meta_ref, order_ref, *refs):
    if start > 0:
        edges_any, q_any, k_any, v_any, proj_any = refs[:5]
        send_ref, keep_x_ref, keep_ref, edges_ref, q_all, k_ref, v_ref, proj_ref, sems = refs[5:]
        moves = [
            (k_any, k_ref),
            (q_any, q_all),
            (v_any, v_ref),
            (edges_any, edges_ref),
            (proj_any, proj_ref),
        ]
    else:
        edges_ref, q_all, k_all, v_all, proj_ref, tails_any = refs[:6]
        send_ref, keep_x_ref, keep_ref, k_ref, v_ref, sems = refs[6:]
        first_rows = pl.ds(0, keep_ref.shape[0])
        moves = [
            (tails_any.at[0], k_ref.at[pl.ds(0, LEFT)]),
            (k_all.at[first_rows], k_ref.at[pl.ds(LEFT, keep_ref.shape[0])]),
            (tails_any.at[1], v_ref.at[pl.ds(0, LEFT)]),
            (v_all.at[first_rows], v_ref.at[pl.ds(LEFT, keep_ref.shape[0])]),
        ]
    rows, columns = keep_ref.shape
    heads = columns // head_width
    block = LANES
    window = LEFT + block
    copies = [pltpu.make_async_copy(a, b, sems.at[i]) for i, (a, b) in enumerate(moves)]
    for copy in copies:
        copy.start()
    for copy in copies[:4]:
        copy.wait()
    edges = edges_ref[:, start : start + rows].astype(F32)
    edges = jnp.concatenate([edges, jnp.zeros((6, rows), F32)], 0).T
    lane_head = lax.broadcasted_iota(jnp.int32, (block, columns), 1) // head_width
    context = []
    for r in range(0, rows, block):
        key = k_ref[r : r + window, :]
        value = v_ref[r : r + window, :]
        query = q_all[start + r : start + r + block, :]
        places = lax.broadcasted_iota(jnp.int32, (block, window), 1)
        places = (places + (meta_ref[0] + (start + r - LEFT))).astype(F32)
        lower = jnp.maximum(edges[r : r + block, 0:1] - LEFT, 0.0)
        upper = edges[r : r + block, 1:2]
        visible = (places >= lower) & (places <= upper)
        own = [jnp.where(lane_head == h, query, jnp.zeros_like(query)) for h in range(heads)]
        own = jnp.concatenate(own, 0)
        scores = lax.dot_general(own, key, (((1,), (1,)), ((), ())), preferred_element_type=F32)
        scores = (scores * scale).reshape(heads, block, window)
        scores = jnp.where(visible[None], scores, -1e30)
        highest = jnp.max(scores, 2, keepdims=True)
        expos = jnp.exp(scores - highest)
        weights = (expos * (1.0 / jnp.sum(expos, 2, keepdims=True))).astype(BF16)
        weights = weights.reshape(heads * block, window)
        product = jnp.dot(weights, value, preferred_element_type=F32)
        mixed = product[0:block]
        for h in range(1, heads):
            mixed = jnp.where(lane_head == h, product[h * block : (h + 1) * block], mixed)
        context.append(mixed.astype(BF16))
    context = jnp.concatenate(context, 0)
    for copy in copies[4:]:
        copy.wait()
    count = proj_ref.shape[1] // columns // 2
    for i in range(2 * count):
        at = pl.multiple_of(order_ref[i] * columns, columns)
        part = jnp.dot(context, proj_ref[:, pl.ds(at, columns)], preferred_element_type=F32)
        j = (i - 1) % count * columns
        if i >= count:
            send_ref[:, j : j + columns] = part.astype(BF16)
        elif i > 0:
            keep_x_ref[:, j : j + columns] = part
        else:
            keep_ref[...] = part


def picked_rows(e, capacity, ranks_ref, state):
    slot = lax.broadcasted_iota(jnp.int32, (capacity, state.shape[0]), 0).astype(F32)
    pick = jnp.where(slot == ranks_ref[pl.ds(e, 1), :], 1.0, 0.0).astype(BF16)
    return jnp.dot(pick, state, preferred_element_type=F32).astype(BF16)


def scatter_rows(local, first, n_time, at_ref, ranks_ref, state, out_refs):
    for s, out_ref in enumerate(out_refs, first):
        owner = at_ref[0] + s
        owner = jnp.where(owner >= n_time, owner - n_time, owner)
        out_ref[...] = picked_rows(local * n_time + owner, out_ref.shape[0], ranks_ref, state)


def state_kernel(parts, column, n_time, at_ref, *refs):
    frames_ref, ranks_ref, state_ref = refs[2 * parts : 2 * parts + 3]
    width = state_ref.shape[1]
    halves = []
    for keep_ref, swapped_ref, *got in (refs[:parts], refs[parts : 2 * parts]):
        half = keep_ref[...] + swapped_ref[:, column : column + width].astype(F32)
        for ref in got:
            half = half + ref[...].astype(F32)
        halves.append(half)
    attended = jnp.concatenate(halves, 0)
    state = (frames_ref[...].astype(F32) + attended).astype(BF16)
    state_ref[...] = state
    scatter_rows(0, 0, n_time, at_ref, ranks_ref, state, refs[2 * parts + 3 :])


def dispatch_kernel(pieces, first, n_time, at_ref, *refs):
    own = refs[0][...]
    ranks_ref, *blocks, out_ref = refs[pieces:]
    scatter_rows(0, first, n_time, at_ref, ranks_ref, own, blocks)
    state = jnp.concatenate([own] + [ref[...] for ref in refs[1:pieces]], 1)
    capacity = out_ref.shape[0] // n_time
    for owner in range(n_time):
        rows = picked_rows(n_time + owner, capacity, ranks_ref, state)
        out_ref[owner * capacity : (owner + 1) * capacity, :] = rows


def join_kernel(*refs):
    *pieces, out_ref = refs
    count = pieces[0].shape[0]
    for s, ref in enumerate(pieces):
        out_ref[s * count : (s + 1) * count, :] = ref[...]


def take_kernel(rows_ref, *refs):
    refs[-1][...] = rows_ref[...]


def expert_kernel(local, starts, width, awaited, order_ref, *refs):
    arrays = len(starts)
    rows_in = refs[:arrays]
    gate_any, up_any, down_any = refs[arrays : arrays + 3]
    *outs, gate_ref, up_ref, down_ref, normed_ref, active_ref, sems = refs[arrays + 3 + awaited :]
    *send_x_refs, send_ref, keep_x_ref, keep_ref = outs
    rows, model = normed_ref.shape
    hidden = active_ref.shape[1]
    moves = [
        (gate_any.at[local], gate_ref),
        (up_any.at[local], up_ref),
        (down_any.at[local], down_ref),
    ]
    copies = [pltpu.make_async_copy(a, b, sems.at[i]) for i, (a, b) in enumerate(moves)]
    for copy in copies:
        copy.start()

    blocks = []
    for ref, start in zip(rows_in, starts):
        blocks += [(ref, start, c) for c in range(0, ref.shape[1], width)]
    step = min(rows, 256)

    def norm(i, carry):
        at_row = pl.multiple_of(i * step, step)
        parts = [
            ref[pl.ds(pl.multiple_of(start + i * step, step), step), c : c + width].astype(F32)
            for ref, start, c in blocks
        ]
        squares = sum(jnp.sum(part * part, 1, keepdims=True) for part in parts)
        factor = lax.rsqrt(squares * (1.0 / model) + EPS)
        for j, part in enumerate(parts):
            at = pl.multiple_of(order_ref[j] * width, width)
            normed_ref[pl.ds(at_row, step), pl.ds(at, width)] = (part * factor).astype(BF16)
        return carry

    lax.fori_loop(0, rows // step, norm, 0)
    copies[0].wait()
    copies[1].wait()
    tile = min(rows, 1024)
    chunk = min(hidden, 256)
    for r in range(0, rows, tile):
        normed = normed_ref[r : r + tile, :]
        for c in range(0, hidden, chunk):
            gate = jnp.dot(normed, gate_ref[:, c : c + chunk], preferred_element_type=F32)
            up = jnp.dot(normed, up_ref[:, c : c + chunk], preferred_element_type=F32)
            half = 0.5 * gate
            active = (half + half * jnp.tanh(half)) * up
            active_ref[r : r + tile, c : c + chunk] = active.astype(BF16)
    copies[2].wait()
    count = len(blocks) // 2
    def project(i, out_refs, column):
        at = pl.multiple_of(order_ref[i] * width, width)
        weight = down_ref[:, pl.ds(at, width)]
        result = jnp.dot(active_ref[...], weight, preferred_element_type=F32)
        each = rows // len(out_refs)
        for j, out_ref in enumerate(out_refs):
            part = result[j * each : (j + 1) * each]
            out_ref[:, column : column + width] = part.astype(out_ref.dtype)

    for by in range(1, count):
        project(count + by, send_x_refs, (by - 1) * width)
    project(count, [send_ref], 0)
    for by in range(1, count):
        project(by, [keep_x_ref], (by - 1) * width)
    project(0, [keep_ref], 0)


def add_kernel(width, keep_ref, got_ref, after_any, *out_refs):
    for i, out_ref in enumerate(out_refs):
        at = slice(i * width, (i + 1) * width)
        out_ref[...] = (keep_ref[:, at] + got_ref[:, at].astype(F32)).astype(BF16)


def total_kernel(n_time, at_ref, keep_ref, *refs):
    *got, after_any, out_ref = refs
    capacity = out_ref.shape[0] // n_time
    for s in range(n_time):
        rows = slice(s * capacity, (s + 1) * capacity)
        total = keep_ref[rows, :]
        for ref in got:
            total = total + ref[rows, :].astype(F32)
        place = at_ref[0] - s
        place = jnp.where(place < 0, place + n_time, place)
        out_ref[pl.ds(pl.multiple_of(place * capacity, capacity), capacity), :] = total.astype(BF16)


def spread_kernel(n_time, at_ref, keep_ref, swapped_ref, *refs):
    got, outs = refs[: -n_time - 1], refs[-n_time:]
    capacity = outs[0].shape[0]
    for s, out_ref in enumerate(outs):
        place = at_ref[0] + s
        place = jnp.where(place >= n_time, place - n_time, place)
        at = pl.ds(pl.multiple_of(place * capacity, capacity), capacity)
        total = keep_ref[at, :] + swapped_ref[at, :].astype(F32)
        for ref in got:
            total = total + ref[at, :].astype(F32)
        out_ref[...] = total.astype(BF16)


def combine_kernel(local, at_ref, targets_ref, gates_ref, base_ref, *refs):
    if len(refs) == 2:
        back_ref, out_ref = refs
    else:
        *got, out_ref, back_ref = refs
        n_time, capacity = len(got), got[0].shape[0]
        for s, ref in enumerate(got):
            place = at_ref[0] - s
            place = jnp.where(place < 0, place + n_time, place)
            back_ref[pl.ds(pl.multiple_of(place * capacity, capacity), capacity), :] = ref[...]
    back = back_ref[...]
    rows = back.shape[0]
    frames = targets_ref.shape[0]
    places = lax.broadcasted_iota(jnp.int32, (frames, rows), 1) + local * rows
    total = base_ref[...].astype(F32)
    for k in range(TOP):
        pick = jnp.where(places == targets_ref[:, k : k + 1], 1.0, 0.0).astype(BF16)
        total = total + gates_ref[:, k : k + 1] * jnp.dot(pick, back, preferred_element_type=F32)
    out_ref[...] = total.astype(out_ref.dtype)


def per_device(
    frames_in,
    queries,
    keys,
    values,
    segment_edges,
    out_proj,
    expert_ids,
    gates,
    w_gate,
    w_up,
    w_down,
):
    frames, model = frames_in.shape
    width = queries.shape[1]
    n_model = lax.axis_size("mp")
    n_time = lax.axis_size("tm")
    chips = n_model // 2
    head_width = model // HEADS
    scale = head_width ** (-0.5)
    local_experts = w_gate.shape[0]
    hidden = w_gate.shape[2]
    experts_all = local_experts * n_time
    capacity = 4 * frames // experts_all
    rows = n_time * capacity
    lanes = -(-experts_all // LANES) * LANES
    at_time = lax.axis_index("tm")
    at_model = lax.axis_index("mp")
    chip, core = at_model // 2, at_model % 2
    mine = [((chip - by) % chips) * 2 + core for by in range(chips)]
    others = [((chip - by) % chips) * 2 + 1 - core for by in range(chips)]
    order = jnp.stack(mine + others).astype(jnp.int32)
    offset = (at_time * frames).astype(jnp.int32).reshape(1)
    place = at_time.astype(jnp.int32).reshape(1)
    away = (chips - 1) * width

    tails = from_behind(jnp.stack([keys[frames - LEFT :], values[frames - LEFT :]], 0), "tm", 1)
    own_frames = lax.dynamic_slice_in_dim(frames_in, at_model * width, width, 1)

    ranks, targets = pl.pallas_call(
        functools.partial(route_kernel, capacity, local_experts, n_time),
        out_shape=(
            jax.ShapeDtypeStruct((lanes, frames), F32),
            jax.ShapeDtypeStruct((frames, TOP), jnp.int32),
        ),
        in_specs=[VMEM],
        out_specs=(VMEM, VMEM),
        compiler_params=params(16),
        cost_estimate=cost(2 * frames * frames * lanes, frames * 1024),
        name="route",
    )(expert_ids)

    def in_hbm(*arrays):
        return [pltpu.with_memory_space_constraint(x, pltpu.HBM) for x in arrays]

    def attended_outs(count):
        return (
            jax.ShapeDtypeStruct((count, chips * width), BF16),
            jax.ShapeDtypeStruct((count, away), F32),
            jax.ShapeDtypeStruct((count, width), F32),
        )

    def attend_cost(count):
        return cost(count * 384 * width * 16, count * width * 8, count * 384 * 4)

    inputs = (segment_edges, queries, keys, values, out_proj)
    *late, edges_vmem, q_vmem, k_vmem, v_vmem, proj_vmem = pl.pallas_call(
        functools.partial(attend_kernel, scale, head_width, LEFT),
        out_shape=attended_outs(frames - LEFT)
        + tuple(jax.ShapeDtypeStruct(x.shape, x.dtype) for x in inputs),
        in_specs=[SMEM, SMEM] + [HBM] * 5,
        out_specs=(VMEM,) * 8,
        scratch_shapes=[pltpu.SemaphoreType.DMA((5,))],
        compiler_params=params(16),
        cost_estimate=attend_cost(frames - LEFT),
        name="attend_late",
    )(offset, order, *in_hbm(*inputs))
    early = pl.pallas_call(
        functools.partial(attend_kernel, scale, head_width, 0),
        out_shape=attended_outs(LEFT),
        in_specs=[SMEM, SMEM] + [VMEM] * 5 + [ANY],
        out_specs=(VMEM,) * 3,
        scratch_shapes=[
            pltpu.VMEM((2 * LEFT, width), BF16),
            pltpu.VMEM((2 * LEFT, width), BF16),
            pltpu.SemaphoreType.DMA((4,)),
        ],
        compiler_params=params(16),
        cost_estimate=attend_cost(LEFT),
        name="attend_early",
    )(offset, order, edges_vmem, q_vmem, k_vmem, v_vmem, proj_vmem, tails)

    def add(name, keep, got, after):
        return pl.pallas_call(
            functools.partial(add_kernel, width),
            in_specs=[VMEM, VMEM, ANY],
            out_specs=(VMEM,) * (chips - 1),
            out_shape=(jax.ShapeDtypeStruct((keep.shape[0], width), BF16),) * (chips - 1),
            compiler_params=params(16),
            cost_estimate=cost(keep.size, keep.size * 8),
            name=f"add_{name}",
        )(keep, got, after)

    def from_chips(parts):
        return [from_chip(part, chips - by) for by, part in enumerate(parts, 1)]

    def attended(name, send, keep_x, keep):
        swapped = core_swap(send)
        return [keep, swapped, *from_chips(add(name, keep_x, swapped, swapped))]

    late = attended("late", *late)
    early = attended("early", *early)

    def blocks_of(count):
        return (jax.ShapeDtypeStruct((capacity, width), BF16),) * count

    near = n_time // 2 + 1
    state, *outgoing_0 = pl.pallas_call(
        functools.partial(state_kernel, len(early), away, n_time),
        out_shape=(jax.ShapeDtypeStruct((frames, width), BF16),) + blocks_of(near),
        in_specs=[SMEM] + [VMEM] * (2 * len(early) + 2),
        out_specs=(VMEM,) * (1 + near),
        compiler_params=params(16),
        cost_estimate=cost(frames * width * rows, 4 * MIB),
        name="state",
    )(place, *early, *late, own_frames, ranks)
    wide = [state] + [from_chip(state, by) for by in range(1, chips)]
    *far, outgoing_1 = pl.pallas_call(
        functools.partial(dispatch_kernel, chips, near, n_time),
        out_shape=blocks_of(n_time - near)
        + (jax.ShapeDtypeStruct((rows, chips * width), BF16),),
        in_specs=[SMEM] + [VMEM] * (chips + 1),
        out_specs=(VMEM,) * (n_time - near + 1),
        compiler_params=params(16),
        cost_estimate=cost(3 * frames * width * rows, 3 * MIB),
        name="dispatch",
    )(place, *wide, ranks)

    def over_time(x):
        columns = x.shape[1]
        x = x.reshape(n_time, capacity, columns)
        x = lax.all_to_all(x, "tm", split_axis=0, concat_axis=0, tiled=True)
        return x.reshape(rows, columns)

    def take(x, after):
        return pl.pallas_call(
            take_kernel,
            in_specs=[VMEM] + [ANY] * len(after),
            out_specs=VMEM,
            out_shape=jax.ShapeDtypeStruct(x.shape, x.dtype),
            compiler_params=params(16),
            cost_estimate=cost(x.size, x.size * 4),
            name="take",
        )(x, *after)

    def experts(local, parts, after):
        outs = [jax.ShapeDtypeStruct((rows, columns), BF16) for columns in (away, width)]
        outs += [jax.ShapeDtypeStruct((rows, columns), F32) for columns in (away, width)]
        return pl.pallas_call(
            functools.partial(expert_kernel, local, (0,) * len(parts), width, len(after)),
            in_specs=[SMEM] + [VMEM] * len(parts) + [HBM] * 3 + [ANY] * len(after),
            out_specs=(VMEM,) * 4,
            scratch_shapes=[
                pltpu.VMEM((model, hidden), BF16),
                pltpu.VMEM((model, hidden), BF16),
                pltpu.VMEM((hidden, model), BF16),
                pltpu.VMEM((rows, model), BF16),
                pltpu.VMEM((rows, hidden), BF16),
                pltpu.SemaphoreType.DMA((3,)),
            ],
            out_shape=tuple(outs),
            compiler_params=params(20),
            cost_estimate=cost(rows * hidden, rows * width),
            name=f"experts_{local}",
        )(order, *parts, *in_hbm(w_gate, w_up, w_down), *after)

    def total(local, parts, after):
        return pl.pallas_call(
            functools.partial(total_kernel, n_time),
            in_specs=[SMEM] + [VMEM] * len(parts) + [ANY],
            out_specs=VMEM,
            out_shape=jax.ShapeDtypeStruct((rows, width), BF16),
            compiler_params=params(16),
            cost_estimate=cost(rows * width * 4, rows * width * 10),
            name=f"total_{local}",
        )(place, *parts, after)

    def spread(local, parts, after):
        return pl.pallas_call(
            functools.partial(spread_kernel, n_time),
            in_specs=[SMEM] + [VMEM] * len(parts) + [ANY],
            out_specs=(VMEM,) * n_time,
            out_shape=(jax.ShapeDtypeStruct((capacity, width), BF16),) * n_time,
            compiler_params=params(16),
            cost_estimate=cost(rows * width * 4, rows * width * 10),
            name=f"spread_{local}",
        )(place, *parts, after)

    def combine(local, back, base):
        last = local == local_experts - 1
        apart = [pltpu.VMEM((rows, width), BF16)] if len(back) > 1 else []
        return pl.pallas_call(
            functools.partial(combine_kernel, local),
            out_shape=jax.ShapeDtypeStruct((frames, width), BF16 if last else F32),
            in_specs=[SMEM] + [VMEM] * (3 + len(back)),
            out_specs=VMEM,
            scratch_shapes=apart,
            compiler_params=params(16),
            cost_estimate=cost(4 * frames * width * rows, 3 * MIB),
            name=f"combine_{local}",
        )(place, targets, gates, base, *back)

    arrived_0 = pl.pallas_call(
        join_kernel,
        in_specs=[VMEM] * n_time,
        out_specs=VMEM,
        out_shape=jax.ShapeDtypeStruct((rows, width), BF16),
        compiler_params=params(16),
        cost_estimate=cost(rows * width, rows * width * 4),
        name="join",
    )(*exchanged(outgoing_0 + far))
    outgoing_1 = take(outgoing_1, [arrived_0])
    arrived_1 = over_time(outgoing_1)
    send_x_0, send_0, keep_x_0, keep_0 = experts(0, gathered(arrived_0), [outgoing_1])
    away_0 = add("0", keep_x_0, core_swap(send_x_0), send_0)
    got_0 = from_chips(away_0)
    arrived_1 = take(arrived_1, [away_0[0]])
    parts = [arrived_1, core_swap(arrived_1)]
    send_x_1, send_1, keep_x_1, keep_1 = experts(1, parts, [away_0[0]])
    total_0 = total(0, [keep_0, core_swap(send_0), *got_0], send_1)
    back_0 = over_time(total_0)
    got_1 = from_chips(add("1", keep_x_1, core_swap(send_x_1), total_0))
    back_1 = exchanged(spread(1, [keep_1, core_swap(send_1), *got_1], back_0))
    return combine(1, back_1, combine(0, [back_0], state))


def solution(mesh):
    return jax.shard_map(
        per_device,
        mesh=mesh,
        in_specs=(
            P("tm", None),
            P("tm", "mp"),
            P("tm", "mp"),
            P("tm", "mp"),
            P(None, "tm"),
            P("mp", None),
            P("tm", None),
            P("tm", None),
            P("tm", None, "mp"),
            P("tm", None, "mp"),
            P("tm", "mp", None),
        ),
        out_specs=P("tm", "mp"),
        check_vma=False,
    )
```

```python
import functools

import jax
import jax.numpy as jnp
from jax import lax
from jax.experimental import pallas as pl
from jax.experimental.pallas import tpu as pltpu
from jax.sharding import PartitionSpec as P

HEADS = 16
TOP = 2
LEFT = 256
EPS = 1e-06
LANES = 128
MIB = 1 << 20
F32 = jnp.float32
BF16 = jnp.bfloat16

VMEM = pl.BlockSpec(memory_space=pltpu.VMEM)
SMEM = pl.BlockSpec(memory_space=pltpu.SMEM)
ANY = pl.BlockSpec(memory_space=pl.ANY)
HBM = pl.BlockSpec(memory_space=pltpu.HBM)


def params(mib):
    return pltpu.CompilerParams(vmem_limit_bytes=mib * MIB)


def cost(flops, moved, transcendentals=0):
    return pl.CostEstimate(flops=flops, bytes_accessed=moved, transcendentals=transcendentals)


def from_behind(x, axis, by):
    size = lax.axis_size(axis)
    pairs = [(i, i + by) for i in range(size) if 0 <= i + by < size]
    return lax.ppermute(x, axis, pairs)


def core_swap(x):
    size = lax.axis_size("mp")
    return lax.ppermute(x, "mp", [(i, i ^ 1) for i in range(size)])


def from_chip(x, by):
    chips = lax.axis_size("mp") // 2
    pairs = [(c * 2 + k, ((c + by) % chips) * 2 + k) for c in range(chips) for k in range(2)]
    return lax.ppermute(x, "mp", pairs)


def gathered(x):
    chips = lax.axis_size("mp") // 2
    mine = [x] + [from_chip(x, by) for by in range(1, chips)]
    return mine + [core_swap(part) for part in mine]


def exchanged(blocks, sign=1):
    size = lax.axis_size("tm")
    return [blocks[0]] + [
        lax.ppermute(block, "tm", [(i, (i + sign * s) % size) for i in range(size)])
        for s, block in enumerate(blocks)
        if s > 0
    ]


def route_kernel(capacity, local_experts, n_time, ids_ref, ranks_ref, targets_ref):
    frames = ids_ref.shape[0]
    lanes = ranks_ref.shape[0]
    ids = ids_ref[...]
    owner = ids // local_experts
    ids = (ids - owner * local_experts) * n_time + owner
    experts = lax.broadcasted_iota(jnp.int32, (frames, lanes), 1)
    hits = [ids[:, k : k + 1] == experts for k in range(TOP)]
    named = functools.reduce(jnp.logical_or, hits)
    ones = jnp.where(named, 1.0, 0.0).astype(BF16)
    row = lax.broadcasted_iota(jnp.int32, (frames, frames), 0)
    column = lax.broadcasted_iota(jnp.int32, (frames, frames), 1)
    before = jnp.where(column < row, 1.0, 0.0).astype(BF16)
    ranks = jnp.dot(before, ones, preferred_element_type=F32)
    ranks_ref[...] = jnp.where(named, ranks, -1.0).T
    places = []
    for k in range(TOP):
        slot = jnp.sum(jnp.where(hits[k], ranks, 0.0), 1, keepdims=True).astype(jnp.int32)
        places.append(ids[:, k : k + 1] * capacity + slot)
    targets_ref[...] = jnp.concatenate(places, 1)


def attend_kernel(scale, head_width, start, meta_ref, order_ref, *refs):
    if start > 0:
        edges_any, q_any, k_any, v_any, proj_any = refs[:5]
        send_ref, keep_x_ref, keep_ref, edges_ref, q_all, k_ref, v_ref, proj_ref, sems = refs[5:]
        moves = [
            (k_any, k_ref),
            (q_any, q_all),
            (v_any, v_ref),
            (edges_any, edges_ref),
            (proj_any, proj_ref),
        ]
    else:
        edges_ref, q_all, k_all, v_all, proj_ref, tails_any = refs[:6]
        send_ref, keep_x_ref, keep_ref, k_ref, v_ref, sems = refs[6:]
        first_rows = pl.ds(0, keep_ref.shape[0])
        moves = [
            (tails_any.at[0], k_ref.at[pl.ds(0, LEFT)]),
            (k_all.at[first_rows], k_ref.at[pl.ds(LEFT, keep_ref.shape[0])]),
            (tails_any.at[1], v_ref.at[pl.ds(0, LEFT)]),
            (v_all.at[first_rows], v_ref.at[pl.ds(LEFT, keep_ref.shape[0])]),
        ]
    rows, columns = keep_ref.shape
    heads = columns // head_width
    block = LANES
    window = LEFT + block
    copies = [pltpu.make_async_copy(a, b, sems.at[i]) for i, (a, b) in enumerate(moves)]
    for copy in copies:
        copy.start()
    for copy in copies[:4]:
        copy.wait()
    edges = edges_ref[:, start : start + rows].astype(F32)
    edges = jnp.concatenate([edges, jnp.zeros((6, rows), F32)], 0).T
    lane_head = lax.broadcasted_iota(jnp.int32, (block, columns), 1) // head_width
    context = []
    for r in range(0, rows, block):
        key = k_ref[r : r + window, :]
        value = v_ref[r : r + window, :]
        query = q_all[start + r : start + r + block, :]
        places = lax.broadcasted_iota(jnp.int32, (block, window), 1)
        places = (places + (meta_ref[0] + (start + r - LEFT))).astype(F32)
        lower = jnp.maximum(edges[r : r + block, 0:1] - LEFT, 0.0)
        upper = edges[r : r + block, 1:2]
        visible = (places >= lower) & (places <= upper)
        own = [jnp.where(lane_head == h, query, jnp.zeros_like(query)) for h in range(heads)]
        own = jnp.concatenate(own, 0)
        scores = lax.dot_general(own, key, (((1,), (1,)), ((), ())), preferred_element_type=F32)
        scores = (scores * scale).reshape(heads, block, window)
        scores = jnp.where(visible[None], scores, -1e30)
        highest = jnp.max(scores, 2, keepdims=True)
        expos = jnp.exp(scores - highest)
        weights = (expos * (1.0 / jnp.sum(expos, 2, keepdims=True))).astype(BF16)
        weights = weights.reshape(heads * block, window)
        product = jnp.dot(weights, value, preferred_element_type=F32)
        mixed = product[0:block]
        for h in range(1, heads):
            mixed = jnp.where(lane_head == h, product[h * block : (h + 1) * block], mixed)
        context.append(mixed.astype(BF16))
    context = jnp.concatenate(context, 0)
    for copy in copies[4:]:
        copy.wait()
    count = proj_ref.shape[1] // columns // 2
    for i in range(2 * count):
        at = pl.multiple_of(order_ref[i] * columns, columns)
        part = jnp.dot(context, proj_ref[:, pl.ds(at, columns)], preferred_element_type=F32)
        j = (i - 1) % count * columns
        if i >= count:
            send_ref[:, j : j + columns] = part.astype(BF16)
        elif i > 0:
            keep_x_ref[:, j : j + columns] = part
        else:
            keep_ref[...] = part


def picked_rows(e, capacity, ranks_ref, state):
    slot = lax.broadcasted_iota(jnp.int32, (capacity, state.shape[0]), 0).astype(F32)
    pick = jnp.where(slot == ranks_ref[pl.ds(e, 1), :], 1.0, 0.0).astype(BF16)
    return jnp.dot(pick, state, preferred_element_type=F32).astype(BF16)


def scatter_rows(local, first, n_time, at_ref, ranks_ref, state, out_refs):
    for s, out_ref in enumerate(out_refs, first):
        owner = at_ref[0] + s
        owner = jnp.where(owner >= n_time, owner - n_time, owner)
        out_ref[...] = picked_rows(local * n_time + owner, out_ref.shape[0], ranks_ref, state)


def state_kernel(parts, column, n_time, at_ref, *refs):
    frames_ref, ranks_ref, state_ref = refs[2 * parts : 2 * parts + 3]
    width = state_ref.shape[1]
    halves = []
    for keep_ref, swapped_ref, *got in (refs[:parts], refs[parts : 2 * parts]):
        half = keep_ref[...] + swapped_ref[:, column : column + width].astype(F32)
        for ref in got:
            half = half + ref[...].astype(F32)
        halves.append(half)
    attended = jnp.concatenate(halves, 0)
    state = (frames_ref[...].astype(F32) + attended).astype(BF16)
    state_ref[...] = state
    scatter_rows(0, 0, n_time, at_ref, ranks_ref, state, refs[2 * parts + 3 :])


def dispatch_kernel(pieces, first, n_time, at_ref, *refs):
    own = refs[0][...]
    ranks_ref, *blocks, out_ref = refs[pieces:]
    scatter_rows(0, first, n_time, at_ref, ranks_ref, own, blocks)
    state = jnp.concatenate([own] + [ref[...] for ref in refs[1:pieces]], 1)
    capacity = out_ref.shape[0] // n_time
    for owner in range(n_time):
        rows = picked_rows(n_time + owner, capacity, ranks_ref, state)
        out_ref[owner * capacity : (owner + 1) * capacity, :] = rows


def join_kernel(*refs):
    *pieces, out_ref = refs
    count = pieces[0].shape[0]
    for s, ref in enumerate(pieces):
        out_ref[s * count : (s + 1) * count, :] = ref[...]


def take_kernel(rows_ref, *refs):
    refs[-1][...] = rows_ref[...]


def expert_kernel(local, starts, width, awaited, order_ref, *refs):
    arrays = len(starts)
    rows_in = refs[:arrays]
    gate_any, up_any, down_any = refs[arrays : arrays + 3]
    *outs, gate_ref, up_ref, down_ref, normed_ref, active_ref, sems = refs[arrays + 3 + awaited :]
    *send_x_refs, send_ref, keep_x_ref, keep_ref = outs
    rows, model = normed_ref.shape
    hidden = active_ref.shape[1]
    moves = [
        (gate_any.at[local], gate_ref),
        (up_any.at[local], up_ref),
        (down_any.at[local], down_ref),
    ]
    copies = [pltpu.make_async_copy(a, b, sems.at[i]) for i, (a, b) in enumerate(moves)]
    for copy in copies:
        copy.start()

    blocks = []
    for ref, start in zip(rows_in, starts):
        blocks += [(ref, start, c) for c in range(0, ref.shape[1], width)]
    step = min(rows, 256)

    def norm(i, carry):
        at_row = pl.multiple_of(i * step, step)
        parts = [
            ref[pl.ds(pl.multiple_of(start + i * step, step), step), c : c + width].astype(F32)
            for ref, start, c in blocks
        ]
        squares = sum(jnp.sum(part * part, 1, keepdims=True) for part in parts)
        factor = lax.rsqrt(squares * (1.0 / model) + EPS)
        for j, part in enumerate(parts):
            at = pl.multiple_of(order_ref[j] * width, width)
            normed_ref[pl.ds(at_row, step), pl.ds(at, width)] = (part * factor).astype(BF16)
        return carry

    lax.fori_loop(0, rows // step, norm, 0)
    copies[0].wait()
    copies[1].wait()
    tile = min(rows, 1024)
    chunk = min(hidden, 256)
    for r in range(0, rows, tile):
        normed = normed_ref[r : r + tile, :]
        for c in range(0, hidden, chunk):
            gate = jnp.dot(normed, gate_ref[:, c : c + chunk], preferred_element_type=F32)
            up = jnp.dot(normed, up_ref[:, c : c + chunk], preferred_element_type=F32)
            half = 0.5 * gate
            active = (half + half * jnp.tanh(half)) * up
            active_ref[r : r + tile, c : c + chunk] = active.astype(BF16)
    copies[2].wait()
    count = len(blocks) // 2
    def project(i, out_refs, column):
        at = pl.multiple_of(order_ref[i] * width, width)
        weight = down_ref[:, pl.ds(at, width)]
        result = jnp.dot(active_ref[...], weight, preferred_element_type=F32)
        each = rows // len(out_refs)
        for j, out_ref in enumerate(out_refs):
            part = result[j * each : (j + 1) * each]
            out_ref[:, column : column + width] = part.astype(out_ref.dtype)

    for by in range(1, count):
        project(count + by, send_x_refs, (by - 1) * width)
    project(count, [send_ref], 0)
    for by in range(1, count):
        project(by, [keep_x_ref], (by - 1) * width)
    project(0, [keep_ref], 0)


def add_kernel(width, keep_ref, got_ref, after_any, *out_refs):
    for i, out_ref in enumerate(out_refs):
        at = slice(i * width, (i + 1) * width)
        out_ref[...] = (keep_ref[:, at] + got_ref[:, at].astype(F32)).astype(BF16)


def wrapped(place, n_time):
    place = jnp.where(place < 0, place + n_time, place)
    return jnp.where(place >= n_time, place - n_time, place)


def spread_kernel(n_time, turned, at_ref, keep_ref, *refs):
    got, outs = refs[: -n_time - 1], refs[-n_time:]
    capacity = outs[0].shape[0]
    for s, out_ref in enumerate(outs):
        place = wrapped(at_ref[0] + s, n_time) if turned else s
        at = pl.ds(pl.multiple_of(place * capacity, capacity), capacity)
        total = keep_ref[at, :]
        for ref in got:
            total = total + ref[at, :].astype(F32)
        out_ref[...] = total.astype(BF16)


def combine_kernel(local, sign, at_ref, targets_ref, gates_ref, base_ref, *refs):
    *got, out_ref, back_ref = refs
    n_time, capacity = len(got), got[0].shape[0]
    for s, ref in enumerate(got):
        place = wrapped(at_ref[0] + sign * s, n_time)
        back_ref[pl.ds(pl.multiple_of(place * capacity, capacity), capacity), :] = ref[...]
    back = back_ref[...]
    rows = back.shape[0]
    frames = targets_ref.shape[0]
    places = lax.broadcasted_iota(jnp.int32, (frames, rows), 1) + local * rows
    total = base_ref[...].astype(F32)
    for k in range(TOP):
        pick = jnp.where(places == targets_ref[:, k : k + 1], 1.0, 0.0).astype(BF16)
        total = total + gates_ref[:, k : k + 1] * jnp.dot(pick, back, preferred_element_type=F32)
    out_ref[...] = total.astype(out_ref.dtype)


def per_device(
    frames_in,
    queries,
    keys,
    values,
    segment_edges,
    out_proj,
    expert_ids,
    gates,
    w_gate,
    w_up,
    w_down,
):
    frames, model = frames_in.shape
    width = queries.shape[1]
    n_model = lax.axis_size("mp")
    n_time = lax.axis_size("tm")
    chips = n_model // 2
    head_width = model // HEADS
    scale = head_width ** (-0.5)
    local_experts = w_gate.shape[0]
    hidden = w_gate.shape[2]
    experts_all = local_experts * n_time
    capacity = 4 * frames // experts_all
    rows = n_time * capacity
    lanes = -(-experts_all // LANES) * LANES
    at_time = lax.axis_index("tm")
    at_model = lax.axis_index("mp")
    chip, core = at_model // 2, at_model % 2
    mine = [((chip - by) % chips) * 2 + core for by in range(chips)]
    others = [((chip - by) % chips) * 2 + 1 - core for by in range(chips)]
    order = jnp.stack(mine + others).astype(jnp.int32)
    offset = (at_time * frames).astype(jnp.int32).reshape(1)
    place = at_time.astype(jnp.int32).reshape(1)
    away = (chips - 1) * width

    tails = from_behind(jnp.stack([keys[frames - LEFT :], values[frames - LEFT :]], 0), "tm", 1)
    own_frames = lax.dynamic_slice_in_dim(frames_in, at_model * width, width, 1)

    ranks, targets = pl.pallas_call(
        functools.partial(route_kernel, capacity, local_experts, n_time),
        out_shape=(
            jax.ShapeDtypeStruct((lanes, frames), F32),
            jax.ShapeDtypeStruct((frames, TOP), jnp.int32),
        ),
        in_specs=[VMEM],
        out_specs=(VMEM, VMEM),
        compiler_params=params(16),
        cost_estimate=cost(2 * frames * frames * lanes, frames * 1024),
        name="route",
    )(expert_ids)

    def in_hbm(*arrays):
        return [pltpu.with_memory_space_constraint(x, pltpu.HBM) for x in arrays]

    def attended_outs(count):
        return (
            jax.ShapeDtypeStruct((count, chips * width), BF16),
            jax.ShapeDtypeStruct((count, away), F32),
            jax.ShapeDtypeStruct((count, width), F32),
        )

    def attend_cost(count):
        return cost(count * 384 * width * 16, count * width * 8, count * 384 * 4)

    inputs = (segment_edges, queries, keys, values, out_proj)
    *late, edges_vmem, q_vmem, k_vmem, v_vmem, proj_vmem = pl.pallas_call(
        functools.partial(attend_kernel, scale, head_width, LEFT),
        out_shape=attended_outs(frames - LEFT)
        + tuple(jax.ShapeDtypeStruct(x.shape, x.dtype) for x in inputs),
        in_specs=[SMEM, SMEM] + [HBM] * 5,
        out_specs=(VMEM,) * 8,
        scratch_shapes=[pltpu.SemaphoreType.DMA((5,))],
        compiler_params=params(16),
        cost_estimate=attend_cost(frames - LEFT),
        name="attend_late",
    )(offset, order, *in_hbm(*inputs))
    early = pl.pallas_call(
        functools.partial(attend_kernel, scale, head_width, 0),
        out_shape=attended_outs(LEFT),
        in_specs=[SMEM, SMEM] + [VMEM] * 5 + [ANY],
        out_specs=(VMEM,) * 3,
        scratch_shapes=[
            pltpu.VMEM((2 * LEFT, width), BF16),
            pltpu.VMEM((2 * LEFT, width), BF16),
            pltpu.SemaphoreType.DMA((4,)),
        ],
        compiler_params=params(16),
        cost_estimate=attend_cost(LEFT),
        name="attend_early",
    )(offset, order, edges_vmem, q_vmem, k_vmem, v_vmem, proj_vmem, tails)

    def add(name, keep, got, after):
        return pl.pallas_call(
            functools.partial(add_kernel, width),
            in_specs=[VMEM, VMEM, ANY],
            out_specs=(VMEM,) * (chips - 1),
            out_shape=(jax.ShapeDtypeStruct((keep.shape[0], width), BF16),) * (chips - 1),
            compiler_params=params(16),
            cost_estimate=cost(keep.size, keep.size * 8),
            name=f"add_{name}",
        )(keep, got, after)

    def from_chips(parts):
        return [from_chip(part, chips - by) for by, part in enumerate(parts, 1)]

    def attended(name, send, keep_x, keep):
        swapped = core_swap(send)
        return [keep, swapped, *from_chips(add(name, keep_x, swapped, swapped))]

    late = attended("late", *late)
    early = attended("early", *early)

    def blocks_of(count):
        return (jax.ShapeDtypeStruct((capacity, width), BF16),) * count

    near = n_time // 2 + 1
    state, *outgoing_0 = pl.pallas_call(
        functools.partial(state_kernel, len(early), away, n_time),
        out_shape=(jax.ShapeDtypeStruct((frames, width), BF16),) + blocks_of(near),
        in_specs=[SMEM] + [VMEM] * (2 * len(early) + 2),
        out_specs=(VMEM,) * (1 + near),
        compiler_params=params(16),
        cost_estimate=cost(frames * width * rows, 4 * MIB),
        name="state",
    )(place, *early, *late, own_frames, ranks)
    wide = [state] + [from_chip(state, by) for by in range(1, chips)]
    *far, outgoing_1 = pl.pallas_call(
        functools.partial(dispatch_kernel, chips, near, n_time),
        out_shape=blocks_of(n_time - near)
        + (jax.ShapeDtypeStruct((rows, chips * width), BF16),),
        in_specs=[SMEM] + [VMEM] * (chips + 1),
        out_specs=(VMEM,) * (n_time - near + 1),
        compiler_params=params(16),
        cost_estimate=cost(3 * frames * width * rows, 3 * MIB),
        name="dispatch",
    )(place, *wide, ranks)

    def over_time(x):
        columns = x.shape[1]
        x = x.reshape(n_time, capacity, columns)
        x = lax.all_to_all(x, "tm", split_axis=0, concat_axis=0, tiled=True)
        return x.reshape(rows, columns)

    def take(x, after):
        return pl.pallas_call(
            take_kernel,
            in_specs=[VMEM] + [ANY] * len(after),
            out_specs=VMEM,
            out_shape=jax.ShapeDtypeStruct(x.shape, x.dtype),
            compiler_params=params(16),
            cost_estimate=cost(x.size, x.size * 4),
            name="take",
        )(x, *after)

    def experts(local, parts, after):
        outs = [jax.ShapeDtypeStruct((rows, columns), BF16) for columns in (away, width)]
        outs += [jax.ShapeDtypeStruct((rows, columns), F32) for columns in (away, width)]
        return pl.pallas_call(
            functools.partial(expert_kernel, local, (0,) * len(parts), width, len(after)),
            in_specs=[SMEM] + [VMEM] * len(parts) + [HBM] * 3 + [ANY] * len(after),
            out_specs=(VMEM,) * 4,
            scratch_shapes=[
                pltpu.VMEM((model, hidden), BF16),
                pltpu.VMEM((model, hidden), BF16),
                pltpu.VMEM((hidden, model), BF16),
                pltpu.VMEM((rows, model), BF16),
                pltpu.VMEM((rows, hidden), BF16),
                pltpu.SemaphoreType.DMA((3,)),
            ],
            out_shape=tuple(outs),
            compiler_params=params(20),
            cost_estimate=cost(6 * rows * model * hidden, 12 * MIB, rows * hidden),
            name=f"experts_{local}",
        )(order, *parts, *in_hbm(w_gate, w_up, w_down), *after)

    def spread(local, turned, parts, after):
        return pl.pallas_call(
            functools.partial(spread_kernel, n_time, turned),
            in_specs=[SMEM] + [VMEM] * len(parts) + [ANY],
            out_specs=(VMEM,) * n_time,
            out_shape=blocks_of(n_time),
            compiler_params=params(16),
            cost_estimate=cost(rows * width * 4, rows * width * 10),
            name=f"spread_{local}",
        )(place, *parts, after)

    def combine(local, sign, back, base):
        last = local == local_experts - 1
        return pl.pallas_call(
            functools.partial(combine_kernel, local, sign),
            out_shape=jax.ShapeDtypeStruct((frames, width), BF16 if last else F32),
            in_specs=[SMEM] + [VMEM] * (3 + len(back)),
            out_specs=VMEM,
            scratch_shapes=[pltpu.VMEM((rows, width), BF16)],
            compiler_params=params(16),
            cost_estimate=cost(4 * frames * width * rows, 3 * MIB),
            name=f"combine_{local}",
        )(place, targets, gates, base, *back)

    arrived_0 = pl.pallas_call(
        join_kernel,
        in_specs=[VMEM] * n_time,
        out_specs=VMEM,
        out_shape=jax.ShapeDtypeStruct((rows, width), BF16),
        compiler_params=params(16),
        cost_estimate=cost(rows * width, rows * width * 4),
        name="join",
    )(*exchanged(outgoing_0 + far))
    arrived_1 = over_time(outgoing_1)
    send_x_0, send_0, keep_x_0, keep_0 = experts(0, gathered(arrived_0), [outgoing_1])
    away_0 = add("0", keep_x_0, core_swap(send_x_0), send_0)
    got_0 = from_chips(away_0)
    swapped_0 = core_swap(send_0)
    arrived_1 = take(arrived_1, [away_0[0]])
    parts = [arrived_1, core_swap(arrived_1)]
    send_x_1, send_1, keep_x_1, keep_1 = experts(1, parts, [away_0[0]])
    away_1 = add("1", keep_x_1, core_swap(send_x_1), got_0[0])
    got_1 = from_chips(away_1)
    total_0 = spread(0, False, [keep_0, swapped_0, *got_0], away_1[0])
    back_0 = exchanged(total_0, -1)
    total_1 = spread(1, True, [keep_1, core_swap(send_1), *got_1], total_0[0])
    back_1 = exchanged(total_1)
    return combine(1, -1, back_1, combine(0, 1, back_0, state))


def solution(mesh):
    return jax.shard_map(
        per_device,
        mesh=mesh,
        in_specs=(
            P("tm", None),
            P("tm", "mp"),
            P("tm", "mp"),
            P("tm", "mp"),
            P(None, "tm"),
            P("mp", None),
            P("tm", None),
            P("tm", None),
            P("tm", None, "mp"),
            P("tm", None, "mp"),
            P("tm", "mp", None),
        ),
        out_specs=P("tm", "mp"),
        check_vma=False,
    )
```

```python
import functools

import jax
import jax.numpy as jnp
from jax import lax
from jax.experimental import pallas as pl
from jax.experimental.pallas import tpu as pltpu
from jax.sharding import PartitionSpec as P

HEADS = 16
TOP = 2
LEFT = 256
EPS = 1e-06
LANES = 128
MIB = 1 << 20
F32 = jnp.float32
BF16 = jnp.bfloat16

VMEM = pl.BlockSpec(memory_space=pltpu.VMEM)
SMEM = pl.BlockSpec(memory_space=pltpu.SMEM)
ANY = pl.BlockSpec(memory_space=pl.ANY)
HBM = pl.BlockSpec(memory_space=pltpu.HBM)


def params(mib):
    return pltpu.CompilerParams(vmem_limit_bytes=mib * MIB)


def cost(flops, moved, transcendentals=0):
    return pl.CostEstimate(flops=flops, bytes_accessed=moved, transcendentals=transcendentals)


def from_behind(x, axis, by):
    size = lax.axis_size(axis)
    pairs = [(i, i + by) for i in range(size) if 0 <= i + by < size]
    return lax.ppermute(x, axis, pairs)


def core_swap(x):
    size = lax.axis_size("mp")
    return lax.ppermute(x, "mp", [(i, i ^ 1) for i in range(size)])


def from_chip(x, by):
    chips = lax.axis_size("mp") // 2
    pairs = [(c * 2 + k, ((c + by) % chips) * 2 + k) for c in range(chips) for k in range(2)]
    return lax.ppermute(x, "mp", pairs)


def gathered(x):
    chips = lax.axis_size("mp") // 2
    mine = [x] + [from_chip(x, by) for by in range(1, chips)]
    return mine + [core_swap(part) for part in mine]


def exchanged(blocks, sign=1):
    size = lax.axis_size("tm")
    return [blocks[0]] + [
        lax.ppermute(block, "tm", [(i, (i + sign * s) % size) for i in range(size)])
        for s, block in enumerate(blocks)
        if s > 0
    ]


def route_kernel(capacity, local_experts, n_time, ids_ref, ranks_ref, targets_ref):
    frames = ids_ref.shape[0]
    lanes = ranks_ref.shape[0]
    ids = ids_ref[...]
    owner = ids // local_experts
    ids = (ids - owner * local_experts) * n_time + owner
    experts = lax.broadcasted_iota(jnp.int32, (frames, lanes), 1)
    hits = [ids[:, k : k + 1] == experts for k in range(TOP)]
    named = functools.reduce(jnp.logical_or, hits)
    ones = jnp.where(named, 1.0, 0.0).astype(BF16)
    row = lax.broadcasted_iota(jnp.int32, (frames, frames), 0)
    column = lax.broadcasted_iota(jnp.int32, (frames, frames), 1)
    before = jnp.where(column < row, 1.0, 0.0).astype(BF16)
    ranks = jnp.dot(before, ones, preferred_element_type=F32)
    ranks_ref[...] = jnp.where(named, ranks, -1.0).T
    places = []
    for k in range(TOP):
        slot = jnp.sum(jnp.where(hits[k], ranks, 0.0), 1, keepdims=True).astype(jnp.int32)
        places.append(ids[:, k : k + 1] * capacity + slot)
    targets_ref[...] = jnp.concatenate(places, 1)


def attend_kernel(scale, head_width, start, meta_ref, order_ref, *refs):
    if start > 0:
        edges_any, q_any, k_any, v_any, proj_any = refs[:5]
        send_ref, keep_x_ref, keep_ref, edges_ref, q_all, k_ref, v_ref, proj_ref, sems = refs[5:]
        moves = [
            (k_any, k_ref),
            (q_any, q_all),
            (v_any, v_ref),
            (edges_any, edges_ref),
            (proj_any, proj_ref),
        ]
    else:
        edges_ref, q_all, k_all, v_all, proj_ref, tails_any = refs[:6]
        send_ref, keep_x_ref, keep_ref, k_ref, v_ref, sems = refs[6:]
        first_rows = pl.ds(0, keep_ref.shape[0])
        moves = [
            (tails_any.at[0], k_ref.at[pl.ds(0, LEFT)]),
            (k_all.at[first_rows], k_ref.at[pl.ds(LEFT, keep_ref.shape[0])]),
            (tails_any.at[1], v_ref.at[pl.ds(0, LEFT)]),
            (v_all.at[first_rows], v_ref.at[pl.ds(LEFT, keep_ref.shape[0])]),
        ]
    rows, columns = keep_ref.shape
    heads = columns // head_width
    block = LANES
    window = LEFT + block
    copies = [pltpu.make_async_copy(a, b, sems.at[i]) for i, (a, b) in enumerate(moves)]
    for copy in copies:
        copy.start()
    for copy in copies[:4]:
        copy.wait()
    edges = edges_ref[:, start : start + rows].astype(F32)
    edges = jnp.concatenate([edges, jnp.zeros((6, rows), F32)], 0).T
    lane_head = lax.broadcasted_iota(jnp.int32, (block, columns), 1) // head_width
    context = []
    for r in range(0, rows, block):
        key = k_ref[r : r + window, :]
        value = v_ref[r : r + window, :]
        query = q_all[start + r : start + r + block, :]
        places = lax.broadcasted_iota(jnp.int32, (block, window), 1)
        places = (places + (meta_ref[0] + (start + r - LEFT))).astype(F32)
        lower = jnp.maximum(edges[r : r + block, 0:1] - LEFT, 0.0)
        upper = edges[r : r + block, 1:2]
        visible = (places >= lower) & (places <= upper)
        own = [jnp.where(lane_head == h, query, jnp.zeros_like(query)) for h in range(heads)]
        own = jnp.concatenate(own, 0)
        scores = lax.dot_general(own, key, (((1,), (1,)), ((), ())), preferred_element_type=F32)
        scores = (scores * scale).reshape(heads, block, window)
        scores = jnp.where(visible[None], scores, -1e30)
        highest = jnp.max(scores, 2, keepdims=True)
        expos = jnp.exp(scores - highest)
        weights = (expos * (1.0 / jnp.sum(expos, 2, keepdims=True))).astype(BF16)
        weights = weights.reshape(heads * block, window)
        product = jnp.dot(weights, value, preferred_element_type=F32)
        mixed = product[0:block]
        for h in range(1, heads):
            mixed = jnp.where(lane_head == h, product[h * block : (h + 1) * block], mixed)
        context.append(mixed.astype(BF16))
    context = jnp.concatenate(context, 0)
    for copy in copies[4:]:
        copy.wait()
    count = proj_ref.shape[1] // columns // 2
    for i in range(2 * count):
        at = pl.multiple_of(order_ref[i] * columns, columns)
        part = jnp.dot(context, proj_ref[:, pl.ds(at, columns)], preferred_element_type=F32)
        j = (i - 1) % count * columns
        if i >= count:
            send_ref[:, j : j + columns] = part.astype(BF16)
        elif i > 0:
            keep_x_ref[:, j : j + columns] = part
        else:
            keep_ref[...] = part


def picked_rows(e, capacity, ranks_ref, state):
    slot = lax.broadcasted_iota(jnp.int32, (capacity, state.shape[0]), 0).astype(F32)
    pick = jnp.where(slot == ranks_ref[pl.ds(e, 1), :], 1.0, 0.0).astype(BF16)
    return jnp.dot(pick, state, preferred_element_type=F32).astype(BF16)


def scatter_rows(local, at_ref, ranks_ref, state, out_refs):
    n_time = len(out_refs)
    for s, out_ref in enumerate(out_refs):
        owner = at_ref[0] + s
        owner = jnp.where(owner >= n_time, owner - n_time, owner)
        out_ref[...] = picked_rows(local * n_time + owner, out_ref.shape[0], ranks_ref, state)


def state_kernel(parts, column, at_ref, *refs):
    frames_ref, ranks_ref, state_ref = refs[2 * parts : 2 * parts + 3]
    width = state_ref.shape[1]
    halves = []
    for keep_ref, swapped_ref, *got in (refs[:parts], refs[parts : 2 * parts]):
        half = keep_ref[...] + swapped_ref[:, column : column + width].astype(F32)
        for ref in got:
            half = half + ref[...].astype(F32)
        halves.append(half)
    attended = jnp.concatenate(halves, 0)
    state = (frames_ref[...].astype(F32) + attended).astype(BF16)
    state_ref[...] = state
    scatter_rows(0, at_ref, ranks_ref, state, refs[2 * parts + 3 :])


def dispatch_kernel(pieces, n_time, *refs):
    state = jnp.concatenate([ref[...] for ref in refs[:pieces]], 1)
    ranks_ref, out_ref = refs[pieces:]
    capacity = out_ref.shape[0] // n_time
    for owner in range(n_time):
        rows = picked_rows(n_time + owner, capacity, ranks_ref, state)
        out_ref[owner * capacity : (owner + 1) * capacity, :] = rows


def join_kernel(*refs):
    *pieces, after_any, out_ref = refs
    count = pieces[0].shape[0]
    for s, ref in enumerate(pieces):
        out_ref[s * count : (s + 1) * count, :] = ref[...]


def take_kernel(rows_ref, *refs):
    refs[-1][...] = rows_ref[...]


def expert_kernel(local, starts, width, awaited, order_ref, *refs):
    arrays = len(starts)
    rows_in = refs[:arrays]
    gate_any, up_any, down_any = refs[arrays : arrays + 3]
    *outs, gate_ref, up_ref, down_ref, normed_ref, active_ref, sems = refs[arrays + 3 + awaited :]
    *send_x_refs, send_ref, keep_x_ref, keep_ref = outs
    rows, model = normed_ref.shape
    hidden = active_ref.shape[1]
    moves = [
        (gate_any.at[local], gate_ref),
        (up_any.at[local], up_ref),
        (down_any.at[local], down_ref),
    ]
    copies = [pltpu.make_async_copy(a, b, sems.at[i]) for i, (a, b) in enumerate(moves)]
    for copy in copies:
        copy.start()

    blocks = []
    for ref, start in zip(rows_in, starts):
        blocks += [(ref, start, c) for c in range(0, ref.shape[1], width)]
    step = min(rows, 256)

    def norm(i, carry):
        at_row = pl.multiple_of(i * step, step)
        parts = [
            ref[pl.ds(pl.multiple_of(start + i * step, step), step), c : c + width].astype(F32)
            for ref, start, c in blocks
        ]
        squares = sum(jnp.sum(part * part, 1, keepdims=True) for part in parts)
        factor = lax.rsqrt(squares * (1.0 / model) + EPS)
        for j, part in enumerate(parts):
            at = pl.multiple_of(order_ref[j] * width, width)
            normed_ref[pl.ds(at_row, step), pl.ds(at, width)] = (part * factor).astype(BF16)
        return carry

    lax.fori_loop(0, rows // step, norm, 0)
    copies[0].wait()
    copies[1].wait()
    tile = min(rows, 1024)
    chunk = min(hidden, 512)
    for r in range(0, rows, tile):
        normed = normed_ref[r : r + tile, :]
        for c in range(0, hidden, chunk):
            gate = jnp.dot(normed, gate_ref[:, c : c + chunk], preferred_element_type=F32)
            up = jnp.dot(normed, up_ref[:, c : c + chunk], preferred_element_type=F32)
            half = 0.5 * gate
            active = (half + half * jnp.tanh(half)) * up
            active_ref[r : r + tile, c : c + chunk] = active.astype(BF16)
    copies[2].wait()
    count = len(blocks) // 2
    def project(i, out_refs, column):
        at = pl.multiple_of(order_ref[i] * width, width)
        weight = down_ref[:, pl.ds(at, width)]
        result = jnp.dot(active_ref[...], weight, preferred_element_type=F32)
        each = rows // len(out_refs)
        for j, out_ref in enumerate(out_refs):
            part = result[j * each : (j + 1) * each]
            out_ref[:, column : column + width] = part.astype(out_ref.dtype)

    for by in range(1, count):
        project(count + by, send_x_refs, (by - 1) * width)
    project(count, [send_ref], 0)
    for by in range(1, count):
        project(by, [keep_x_ref], (by - 1) * width)
    project(0, [keep_ref], 0)


def add_kernel(width, keep_ref, got_ref, after_any, *out_refs):
    for i, out_ref in enumerate(out_refs):
        at = slice(i * width, (i + 1) * width)
        out_ref[...] = (keep_ref[:, at] + got_ref[:, at].astype(F32)).astype(BF16)


def wrapped(place, n_time):
    place = jnp.where(place < 0, place + n_time, place)
    return jnp.where(place >= n_time, place - n_time, place)


def spread_kernel(n_time, awaited, turned, at_ref, keep_ref, *refs):
    got, outs = refs[: -n_time - awaited], refs[-n_time:]
    capacity = outs[0].shape[0]
    for s, out_ref in enumerate(outs):
        place = wrapped(at_ref[0] + s, n_time) if turned else s
        at = pl.ds(pl.multiple_of(place * capacity, capacity), capacity)
        total = keep_ref[at, :]
        for ref in got:
            total = total + ref[at, :].astype(F32)
        out_ref[...] = total.astype(BF16)


def combine_kernel(local, sign, at_ref, targets_ref, gates_ref, base_ref, *refs):
    *got, out_ref, back_ref = refs
    n_time, capacity = len(got), got[0].shape[0]
    for s, ref in enumerate(got):
        place = wrapped(at_ref[0] + sign * s, n_time)
        back_ref[pl.ds(pl.multiple_of(place * capacity, capacity), capacity), :] = ref[...]
    back = back_ref[...]
    rows = back.shape[0]
    frames = targets_ref.shape[0]
    places = lax.broadcasted_iota(jnp.int32, (frames, rows), 1) + local * rows
    total = base_ref[...].astype(F32)
    for k in range(TOP):
        pick = jnp.where(places == targets_ref[:, k : k + 1], 1.0, 0.0).astype(BF16)
        total = total + gates_ref[:, k : k + 1] * jnp.dot(pick, back, preferred_element_type=F32)
    out_ref[...] = total.astype(out_ref.dtype)


def per_device(
    frames_in,
    queries,
    keys,
    values,
    segment_edges,
    out_proj,
    expert_ids,
    gates,
    w_gate,
    w_up,
    w_down,
):
    frames, model = frames_in.shape
    width = queries.shape[1]
    n_model = lax.axis_size("mp")
    n_time = lax.axis_size("tm")
    chips = n_model // 2
    head_width = model // HEADS
    scale = head_width ** (-0.5)
    local_experts = w_gate.shape[0]
    hidden = w_gate.shape[2]
    experts_all = local_experts * n_time
    capacity = 4 * frames // experts_all
    rows = n_time * capacity
    lanes = -(-experts_all // LANES) * LANES
    at_time = lax.axis_index("tm")
    at_model = lax.axis_index("mp")
    chip, core = at_model // 2, at_model % 2
    mine = [((chip - by) % chips) * 2 + core for by in range(chips)]
    others = [((chip - by) % chips) * 2 + 1 - core for by in range(chips)]
    order = jnp.stack(mine + others).astype(jnp.int32)
    offset = (at_time * frames).astype(jnp.int32).reshape(1)
    place = at_time.astype(jnp.int32).reshape(1)
    away = (chips - 1) * width

    tails = from_behind(jnp.stack([keys[frames - LEFT :], values[frames - LEFT :]], 0), "tm", 1)
    own_frames = lax.dynamic_slice_in_dim(frames_in, at_model * width, width, 1)

    ranks, targets = pl.pallas_call(
        functools.partial(route_kernel, capacity, local_experts, n_time),
        out_shape=(
            jax.ShapeDtypeStruct((lanes, frames), F32),
            jax.ShapeDtypeStruct((frames, TOP), jnp.int32),
        ),
        in_specs=[VMEM],
        out_specs=(VMEM, VMEM),
        compiler_params=params(16),
        cost_estimate=cost(2 * frames * frames * lanes, frames * 1024),
        name="route",
    )(expert_ids)

    def in_hbm(*arrays):
        return [pltpu.with_memory_space_constraint(x, pltpu.HBM) for x in arrays]

    def attended_outs(count):
        return (
            jax.ShapeDtypeStruct((count, chips * width), BF16),
            jax.ShapeDtypeStruct((count, away), F32),
            jax.ShapeDtypeStruct((count, width), F32),
        )

    def attend_cost(count):
        return cost(count * 384 * width * 16, count * width * 8, count * 384 * 4)

    inputs = (segment_edges, queries, keys, values, out_proj)
    *late, edges_vmem, q_vmem, k_vmem, v_vmem, proj_vmem = pl.pallas_call(
        functools.partial(attend_kernel, scale, head_width, LEFT),
        out_shape=attended_outs(frames - LEFT)
        + tuple(jax.ShapeDtypeStruct(x.shape, x.dtype) for x in inputs),
        in_specs=[SMEM, SMEM] + [HBM] * 5,
        out_specs=(VMEM,) * 8,
        scratch_shapes=[pltpu.SemaphoreType.DMA((5,))],
        compiler_params=params(16),
        cost_estimate=attend_cost(frames - LEFT),
        name="attend_late",
    )(offset, order, *in_hbm(*inputs))
    early = pl.pallas_call(
        functools.partial(attend_kernel, scale, head_width, 0),
        out_shape=attended_outs(LEFT),
        in_specs=[SMEM, SMEM] + [VMEM] * 5 + [ANY],
        out_specs=(VMEM,) * 3,
        scratch_shapes=[
            pltpu.VMEM((2 * LEFT, width), BF16),
            pltpu.VMEM((2 * LEFT, width), BF16),
            pltpu.SemaphoreType.DMA((4,)),
        ],
        compiler_params=params(16),
        cost_estimate=attend_cost(LEFT),
        name="attend_early",
    )(offset, order, edges_vmem, q_vmem, k_vmem, v_vmem, proj_vmem, tails)

    def add(name, keep, got, after):
        return pl.pallas_call(
            functools.partial(add_kernel, width),
            in_specs=[VMEM, VMEM, ANY],
            out_specs=(VMEM,) * (chips - 1),
            out_shape=(jax.ShapeDtypeStruct((keep.shape[0], width), BF16),) * (chips - 1),
            compiler_params=params(16),
            cost_estimate=cost(keep.size, keep.size * 8),
            name=f"add_{name}",
        )(keep, got, after)

    def from_chips(parts):
        return [from_chip(part, chips - by) for by, part in enumerate(parts, 1)]

    def attended(name, send, keep_x, keep):
        swapped = core_swap(send)
        return [keep, swapped, *from_chips(add(name, keep_x, swapped, swapped))]

    late = attended("late", *late)
    early = attended("early", *early)

    def blocks_of(count):
        return (jax.ShapeDtypeStruct((capacity, width), BF16),) * count

    state, *outgoing_0 = pl.pallas_call(
        functools.partial(state_kernel, len(early), away),
        out_shape=(jax.ShapeDtypeStruct((frames, width), BF16),) + blocks_of(n_time),
        in_specs=[SMEM] + [VMEM] * (2 * len(early) + 2),
        out_specs=(VMEM,) * (1 + n_time),
        compiler_params=params(16),
        cost_estimate=cost(2 * frames * width * rows, 4 * MIB),
        name="state",
    )(place, *early, *late, own_frames, ranks)
    wide = [state] + [from_chip(state, by) for by in range(1, chips)]
    outgoing_1 = pl.pallas_call(
        functools.partial(dispatch_kernel, chips, n_time),
        out_shape=jax.ShapeDtypeStruct((rows, chips * width), BF16),
        in_specs=[VMEM] * (chips + 1),
        out_specs=VMEM,
        compiler_params=params(16),
        cost_estimate=cost(4 * frames * width * rows, 3 * MIB),
        name="dispatch",
    )(*wide, ranks)

    def over_time(x):
        columns = x.shape[1]
        x = x.reshape(n_time, capacity, columns)
        x = lax.all_to_all(x, "tm", split_axis=0, concat_axis=0, tiled=True)
        return x.reshape(rows, columns)

    def take(x, after):
        return pl.pallas_call(
            take_kernel,
            in_specs=[VMEM] + [ANY] * len(after),
            out_specs=VMEM,
            out_shape=jax.ShapeDtypeStruct(x.shape, x.dtype),
            compiler_params=params(16),
            cost_estimate=cost(x.size, x.size * 4),
            name="take",
        )(x, *after)

    def experts(local, parts, after):
        outs = [jax.ShapeDtypeStruct((rows, columns), BF16) for columns in (away, width)]
        outs += [jax.ShapeDtypeStruct((rows, columns), F32) for columns in (away, width)]
        return pl.pallas_call(
            functools.partial(expert_kernel, local, (0,) * len(parts), width, len(after)),
            in_specs=[SMEM] + [VMEM] * len(parts) + [HBM] * 3 + [ANY] * len(after),
            out_specs=(VMEM,) * 4,
            scratch_shapes=[
                pltpu.VMEM((model, hidden), BF16),
                pltpu.VMEM((model, hidden), BF16),
                pltpu.VMEM((hidden, model), BF16),
                pltpu.VMEM((rows, model), BF16),
                pltpu.VMEM((rows, hidden), BF16),
                pltpu.SemaphoreType.DMA((3,)),
            ],
            out_shape=tuple(outs),
            compiler_params=params(20),
            cost_estimate=cost(6 * rows * model * hidden, 12 * MIB, rows * hidden),
            name=f"experts_{local}",
        )(order, *parts, *in_hbm(w_gate, w_up, w_down), *after)

    def spread(local, turned, parts, after):
        return pl.pallas_call(
            functools.partial(spread_kernel, n_time, len(after), turned),
            in_specs=[SMEM] + [VMEM] * len(parts) + [ANY] * len(after),
            out_specs=(VMEM,) * n_time,
            out_shape=blocks_of(n_time),
            compiler_params=params(16),
            cost_estimate=cost(rows * width * 4, rows * width * 10),
            name=f"spread_{local}",
        )(place, *parts, *after)

    def combine(local, sign, back, base):
        last = local == local_experts - 1
        return pl.pallas_call(
            functools.partial(combine_kernel, local, sign),
            out_shape=jax.ShapeDtypeStruct((frames, width), BF16 if last else F32),
            in_specs=[SMEM] + [VMEM] * (3 + len(back)),
            out_specs=VMEM,
            scratch_shapes=[pltpu.VMEM((rows, width), BF16)],
            compiler_params=params(16),
            cost_estimate=cost(4 * frames * width * rows, 3 * MIB),
            name=f"combine_{local}",
        )(place, targets, gates, base, *back)

    outgoing_0[-1] = take(outgoing_0[-1], wide[1:])
    arrived_0 = pl.pallas_call(
        join_kernel,
        in_specs=[VMEM] * n_time + [ANY],
        out_specs=VMEM,
        out_shape=jax.ShapeDtypeStruct((rows, width), BF16),
        compiler_params=params(16),
        cost_estimate=cost(rows * width, rows * width * 4),
        name="join",
    )(*exchanged(outgoing_0), outgoing_1)
    arrived_1 = over_time(outgoing_1)
    send_x_0, send_0, keep_x_0, keep_0 = experts(0, gathered(arrived_0), [outgoing_1])
    away_0 = add("0", keep_x_0, core_swap(send_x_0), send_0)
    got_0 = from_chips(away_0)
    swapped_0 = core_swap(send_0)
    arrived_1 = take(arrived_1, [away_0[0]])
    parts = [arrived_1, core_swap(arrived_1)]
    send_x_1, send_1, keep_x_1, keep_1 = experts(1, parts, [away_0[0]])
    away_1 = add("1", keep_x_1, core_swap(send_x_1), got_0[0])
    got_1 = from_chips(away_1)
    total_0 = spread(0, False, [keep_0, swapped_0, *got_0], [away_1[0]])
    back_0 = exchanged(total_0, -1)
    total_1 = spread(1, True, [keep_1, core_swap(send_1), *got_1], back_0[1 : n_time // 2 + 1])
    back_1 = exchanged(total_1)
    return combine(1, -1, back_1, combine(0, 1, back_0, state))


def solution(mesh):
    return jax.shard_map(
        per_device,
        mesh=mesh,
        in_specs=(
            P("tm", None),
            P("tm", "mp"),
            P("tm", "mp"),
            P("tm", "mp"),
            P(None, "tm"),
            P("mp", None),
            P("tm", None),
            P("tm", None),
            P("tm", None, "mp"),
            P("tm", None, "mp"),
            P("tm", "mp", None),
        ),
        out_specs=P("tm", "mp"),
        check_vma=False,
    )
```

```python
import functools

import jax
import jax.numpy as jnp
from jax import lax
from jax.experimental import pallas as pl
from jax.experimental.pallas import tpu as pltpu
from jax.sharding import PartitionSpec as P

HEADS = 16
TOP = 2
LEFT = 256
EPS = 1e-06
LANES = 128
MIB = 1 << 20
F32 = jnp.float32
BF16 = jnp.bfloat16

VMEM = pl.BlockSpec(memory_space=pltpu.VMEM)
SMEM = pl.BlockSpec(memory_space=pltpu.SMEM)
ANY = pl.BlockSpec(memory_space=pl.ANY)
HBM = pl.BlockSpec(memory_space=pltpu.HBM)


def params(mib):
    return pltpu.CompilerParams(vmem_limit_bytes=mib * MIB)


def cost(flops, moved, transcendentals=0):
    return pl.CostEstimate(flops=flops, bytes_accessed=moved, transcendentals=transcendentals)


def from_behind(x, axis, by):
    size = lax.axis_size(axis)
    pairs = [(i, i + by) for i in range(size) if 0 <= i + by < size]
    return lax.ppermute(x, axis, pairs)


def core_swap(x):
    size = lax.axis_size("mp")
    return lax.ppermute(x, "mp", [(i, i ^ 1) for i in range(size)])


def from_chip(x, by):
    chips = lax.axis_size("mp") // 2
    pairs = [(c * 2 + k, ((c + by) % chips) * 2 + k) for c in range(chips) for k in range(2)]
    return lax.ppermute(x, "mp", pairs)


def gathered(x):
    chips = lax.axis_size("mp") // 2
    mine = [x] + [from_chip(x, by) for by in range(1, chips)]
    return mine + [core_swap(part) for part in mine]


def exchanged(blocks, sign=1):
    size = lax.axis_size("tm")
    return [blocks[0]] + [
        lax.ppermute(block, "tm", [(i, (i + sign * s) % size) for i in range(size)])
        for s, block in enumerate(blocks)
        if s > 0
    ]


def route_kernel(capacity, local_experts, n_time, ids_ref, ranks_ref, targets_ref):
    frames = ids_ref.shape[0]
    lanes = ranks_ref.shape[0]
    ids = ids_ref[...]
    owner = ids // local_experts
    ids = (ids - owner * local_experts) * n_time + owner
    experts = lax.broadcasted_iota(jnp.int32, (frames, lanes), 1)
    hits = [ids[:, k : k + 1] == experts for k in range(TOP)]
    named = functools.reduce(jnp.logical_or, hits)
    ones = jnp.where(named, 1.0, 0.0).astype(BF16)
    row = lax.broadcasted_iota(jnp.int32, (frames, frames), 0)
    column = lax.broadcasted_iota(jnp.int32, (frames, frames), 1)
    before = jnp.where(column < row, 1.0, 0.0).astype(BF16)
    ranks = jnp.dot(before, ones, preferred_element_type=F32)
    ranks_ref[...] = jnp.where(named, ranks, -1.0).T
    places = []
    for k in range(TOP):
        slot = jnp.sum(jnp.where(hits[k], ranks, 0.0), 1, keepdims=True).astype(jnp.int32)
        places.append(ids[:, k : k + 1] * capacity + slot)
    targets_ref[...] = jnp.concatenate(places, 1)


def tails_kernel(first, k_any, v_any, out_ref, sems):
    copies = [
        pltpu.make_async_copy(source.at[pl.ds(first, LEFT)], out_ref.at[i], sems.at[i])
        for i, source in enumerate((k_any, v_any))
    ]
    for copy in copies:
        copy.start()
    for copy in copies:
        copy.wait()


def attend_kernel(scale, head_width, start, meta_ref, order_ref, *refs):
    if start > 0:
        edges_any, q_any, k_any, v_any, proj_any = refs[:5]
        send_ref, keep_x_ref, keep_ref, edges_ref, q_all, k_ref, v_ref, proj_ref, sems = refs[5:]
        moves = [
            (k_any, k_ref),
            (q_any, q_all),
            (v_any, v_ref),
            (edges_any, edges_ref),
            (proj_any, proj_ref),
        ]
    else:
        edges_ref, q_all, k_all, v_all, proj_ref, tails_any = refs[:6]
        send_ref, keep_x_ref, keep_ref, k_ref, v_ref, sems = refs[6:]
        first_rows = pl.ds(0, keep_ref.shape[0])
        moves = [
            (tails_any.at[0], k_ref.at[pl.ds(0, LEFT)]),
            (k_all.at[first_rows], k_ref.at[pl.ds(LEFT, keep_ref.shape[0])]),
            (tails_any.at[1], v_ref.at[pl.ds(0, LEFT)]),
            (v_all.at[first_rows], v_ref.at[pl.ds(LEFT, keep_ref.shape[0])]),
        ]
    rows, columns = keep_ref.shape
    heads = columns // head_width
    block = LANES
    window = LEFT + block
    copies = [pltpu.make_async_copy(a, b, sems.at[i]) for i, (a, b) in enumerate(moves)]
    for copy in copies:
        copy.start()
    for copy in copies[:4]:
        copy.wait()
    edges = edges_ref[:, start : start + rows].astype(F32)
    edges = jnp.concatenate([edges, jnp.zeros((6, rows), F32)], 0).T
    lane_head = lax.broadcasted_iota(jnp.int32, (block, columns), 1) // head_width
    context = []
    for r in range(0, rows, block):
        key = k_ref[r : r + window, :]
        value = v_ref[r : r + window, :]
        query = q_all[start + r : start + r + block, :]
        places = lax.broadcasted_iota(jnp.int32, (block, window), 1)
        places = (places + (meta_ref[0] + (start + r - LEFT))).astype(F32)
        lower = jnp.maximum(edges[r : r + block, 0:1] - LEFT, 0.0)
        upper = edges[r : r + block, 1:2]
        visible = (places >= lower) & (places <= upper)
        own = [jnp.where(lane_head == h, query, jnp.zeros_like(query)) for h in range(heads)]
        own = jnp.concatenate(own, 0)
        scores = lax.dot_general(own, key, (((1,), (1,)), ((), ())), preferred_element_type=F32)
        scores = (scores * scale).reshape(heads, block, window)
        scores = jnp.where(visible[None], scores, -1e30)
        highest = jnp.max(scores, 2, keepdims=True)
        expos = jnp.exp(scores - highest)
        weights = (expos * (1.0 / jnp.sum(expos, 2, keepdims=True))).astype(BF16)
        weights = weights.reshape(heads * block, window)
        product = jnp.dot(weights, value, preferred_element_type=F32)
        mixed = product[0:block]
        for h in range(1, heads):
            mixed = jnp.where(lane_head == h, product[h * block : (h + 1) * block], mixed)
        context.append(mixed.astype(BF16))
    context = jnp.concatenate(context, 0)
    for copy in copies[4:]:
        copy.wait()
    count = proj_ref.shape[1] // columns // 2
    for i in range(2 * count):
        at = pl.multiple_of(order_ref[i] * columns, columns)
        part = jnp.dot(context, proj_ref[:, pl.ds(at, columns)], preferred_element_type=F32)
        j = (i - 1) % count * columns
        if i >= count:
            send_ref[:, j : j + columns] = part.astype(BF16)
        elif i > 0:
            keep_x_ref[:, j : j + columns] = part
        else:
            keep_ref[...] = part


def picked_rows(e, capacity, ranks_ref, state):
    slot = lax.broadcasted_iota(jnp.int32, (capacity, state.shape[0]), 0).astype(F32)
    pick = jnp.where(slot == ranks_ref[pl.ds(e, 1), :], 1.0, 0.0).astype(BF16)
    return jnp.dot(pick, state, preferred_element_type=F32).astype(BF16)


def scatter_rows(local, at_ref, ranks_ref, state, out_refs):
    n_time = len(out_refs)
    for s, out_ref in enumerate(out_refs):
        owner = at_ref[0] + s
        owner = jnp.where(owner >= n_time, owner - n_time, owner)
        out_ref[...] = picked_rows(local * n_time + owner, out_ref.shape[0], ranks_ref, state)


def both_kernel(width, *refs):
    keeps, gots, out_refs = refs[0:4:2], refs[1:4:2], refs[4:]
    for j, (keep_ref, got_ref) in enumerate(zip(keeps, gots)):
        count = keep_ref.shape[0]
        for i, out_ref in enumerate(out_refs):
            at = slice(i * width, (i + 1) * width)
            part = keep_ref[:, at] + got_ref[:, at].astype(F32)
            out_ref[j * count : (j + 1) * count, :] = part.astype(BF16)


def state_kernel(column, parts, at_ref, *refs):
    got = refs[4:parts]
    frames_ref, ranks_ref, state_ref = refs[parts : parts + 3]
    width = state_ref.shape[1]
    halves = []
    for keep_ref, swapped_ref in (refs[0:2], refs[2:4]):
        halves.append(keep_ref[...] + swapped_ref[:, column : column + width].astype(F32))
    attended = jnp.concatenate(halves, 0)
    for ref in got:
        attended = attended + ref[...].astype(F32)
    state = (frames_ref[...].astype(F32) + attended).astype(BF16)
    state_ref[...] = state
    scatter_rows(0, at_ref, ranks_ref, state, refs[parts + 3 :])


def dispatch_kernel(pieces, n_time, *refs):
    state = jnp.concatenate([ref[...] for ref in refs[:pieces]], 1)
    ranks_ref, out_ref = refs[pieces:]
    capacity = out_ref.shape[0] // n_time
    for owner in range(n_time):
        rows = picked_rows(n_time + owner, capacity, ranks_ref, state)
        out_ref[owner * capacity : (owner + 1) * capacity, :] = rows


def join_kernel(*refs):
    *pieces, after_any, out_ref = refs
    count = pieces[0].shape[0]
    for s, ref in enumerate(pieces):
        out_ref[s * count : (s + 1) * count, :] = ref[...]


def take_kernel(rows_ref, *refs):
    refs[-1][...] = rows_ref[...]


def expert_kernel(local, starts, width, awaited, order_ref, *refs):
    arrays = len(starts)
    rows_in = refs[:arrays]
    gate_any, up_any, down_any = refs[arrays : arrays + 3]
    *outs, gate_ref, up_ref, down_ref, normed_ref, active_ref, sems = refs[arrays + 3 + awaited :]
    *send_x_refs, send_ref, keep_x_ref, keep_ref = outs
    rows, model = normed_ref.shape
    hidden = active_ref.shape[1]
    moves = [
        (gate_any.at[local], gate_ref),
        (up_any.at[local], up_ref),
        (down_any.at[local], down_ref),
    ]
    copies = [pltpu.make_async_copy(a, b, sems.at[i]) for i, (a, b) in enumerate(moves)]
    for copy in copies:
        copy.start()

    blocks = []
    for ref, start in zip(rows_in, starts):
        blocks += [(ref, start, c) for c in range(0, ref.shape[1], width)]
    tile = min(rows, 512)
    step = min(tile, 256)
    chunk = min(hidden, 256)

    def norm(first):
        for r in range(first, first + tile, step):
            parts = [ref[r : r + step, c : c + width].astype(F32) for ref, _, c in blocks]
            squares = sum(jnp.sum(part * part, 1, keepdims=True) for part in parts)
            factor = lax.rsqrt(squares * (1.0 / model) + EPS)
            for j, part in enumerate(parts):
                at = pl.multiple_of(order_ref[j] * width, width)
                normed_ref[r : r + step, pl.ds(at, width)] = (part * factor).astype(BF16)

    norm(0)
    copies[0].wait()
    copies[1].wait()
    for r in range(0, rows, tile):
        normed = normed_ref[r : r + tile, :]
        if r + tile < rows:
            norm(r + tile)
        for c in range(0, hidden, chunk):
            gate = jnp.dot(normed, gate_ref[:, c : c + chunk], preferred_element_type=F32)
            up = jnp.dot(normed, up_ref[:, c : c + chunk], preferred_element_type=F32)
            half = 0.5 * gate
            active = (half + half * jnp.tanh(half)) * up
            active_ref[r : r + tile, c : c + chunk] = active.astype(BF16)
    copies[2].wait()
    count = len(blocks) // 2
    def project(i, out_refs, column):
        at = pl.multiple_of(order_ref[i] * width, width)
        weight = down_ref[:, pl.ds(at, width)]
        result = jnp.dot(active_ref[...], weight, preferred_element_type=F32)
        each = rows // len(out_refs)
        for j, out_ref in enumerate(out_refs):
            part = result[j * each : (j + 1) * each]
            out_ref[:, column : column + width] = part.astype(out_ref.dtype)

    for by in range(1, count):
        project(count + by, send_x_refs, (by - 1) * width)
    project(count, [send_ref], 0)
    for by in range(1, count):
        project(by, [keep_x_ref], (by - 1) * width)
    project(0, [keep_ref], 0)


def add_kernel(width, keep_ref, got_ref, after_any, *out_refs):
    for i, out_ref in enumerate(out_refs):
        at = slice(i * width, (i + 1) * width)
        out_ref[...] = (keep_ref[:, at] + got_ref[:, at].astype(F32)).astype(BF16)


def wrapped(place, n_time):
    place = jnp.where(place < 0, place + n_time, place)
    return jnp.where(place >= n_time, place - n_time, place)


def spread_kernel(n_time, awaited, turned, at_ref, keep_ref, *refs):
    got, outs = refs[: -n_time - awaited], refs[-n_time:]
    capacity = outs[0].shape[0]
    for s, out_ref in enumerate(outs):
        place = wrapped(at_ref[0] + s, n_time) if turned else s
        at = pl.ds(pl.multiple_of(place * capacity, capacity), capacity)
        total = keep_ref[at, :]
        for ref in got:
            total = total + ref[at, :].astype(F32)
        out_ref[...] = total.astype(BF16)


def combine_kernel(local, sign, at_ref, targets_ref, gates_ref, base_ref, *refs):
    *got, out_ref, back_ref = refs
    n_time, capacity = len(got), got[0].shape[0]
    for s, ref in enumerate(got):
        place = wrapped(at_ref[0] + sign * s, n_time)
        back_ref[pl.ds(pl.multiple_of(place * capacity, capacity), capacity), :] = ref[...]
    back = back_ref[...]
    rows = back.shape[0]
    frames = targets_ref.shape[0]
    places = lax.broadcasted_iota(jnp.int32, (frames, rows), 1) + local * rows
    total = base_ref[...].astype(F32)
    for k in range(TOP):
        pick = jnp.where(places == targets_ref[:, k : k + 1], 1.0, 0.0).astype(BF16)
        total = total + gates_ref[:, k : k + 1] * jnp.dot(pick, back, preferred_element_type=F32)
    out_ref[...] = total.astype(out_ref.dtype)


def per_device(
    frames_in,
    queries,
    keys,
    values,
    segment_edges,
    out_proj,
    expert_ids,
    gates,
    w_gate,
    w_up,
    w_down,
):
    frames, model = frames_in.shape
    width = queries.shape[1]
    n_model = lax.axis_size("mp")
    n_time = lax.axis_size("tm")
    chips = n_model // 2
    head_width = model // HEADS
    scale = head_width ** (-0.5)
    local_experts = w_gate.shape[0]
    hidden = w_gate.shape[2]
    experts_all = local_experts * n_time
    capacity = 4 * frames // experts_all
    rows = n_time * capacity
    lanes = -(-experts_all // LANES) * LANES
    at_time = lax.axis_index("tm")
    at_model = lax.axis_index("mp")
    chip, core = at_model // 2, at_model % 2
    mine = [((chip - by) % chips) * 2 + core for by in range(chips)]
    others = [((chip - by) % chips) * 2 + 1 - core for by in range(chips)]
    order = jnp.stack(mine + others).astype(jnp.int32)
    offset = (at_time * frames).astype(jnp.int32).reshape(1)
    place = at_time.astype(jnp.int32).reshape(1)
    away = (chips - 1) * width

    def in_hbm(*arrays):
        return [pltpu.with_memory_space_constraint(x, pltpu.HBM) for x in arrays]

    last = pl.pallas_call(
        functools.partial(tails_kernel, frames - LEFT),
        in_specs=[HBM] * 2,
        out_specs=VMEM,
        out_shape=jax.ShapeDtypeStruct((2, LEFT, width), BF16),
        scratch_shapes=[pltpu.SemaphoreType.DMA((2,))],
        compiler_params=params(16),
        cost_estimate=cost(0, 4 * LEFT * width * 2),
        name="tails",
    )(*in_hbm(keys, values))
    tails = from_behind(last, "tm", 1)
    own_frames = lax.dynamic_slice_in_dim(frames_in, at_model * width, width, 1)

    ranks, targets = pl.pallas_call(
        functools.partial(route_kernel, capacity, local_experts, n_time),
        out_shape=(
            jax.ShapeDtypeStruct((lanes, frames), F32),
            jax.ShapeDtypeStruct((frames, TOP), jnp.int32),
        ),
        in_specs=[VMEM],
        out_specs=(VMEM, VMEM),
        compiler_params=params(16),
        cost_estimate=cost(2 * frames * frames * lanes, frames * 1024),
        name="route",
    )(expert_ids)

    def attended_outs(count):
        return (
            jax.ShapeDtypeStruct((count, chips * width), BF16),
            jax.ShapeDtypeStruct((count, away), F32),
            jax.ShapeDtypeStruct((count, width), F32),
        )

    def attend_cost(count):
        return cost(count * 384 * width * 16, count * width * 8, count * 384 * 4)

    inputs = (segment_edges, queries, keys, values, out_proj)
    *late, edges_vmem, q_vmem, k_vmem, v_vmem, proj_vmem = pl.pallas_call(
        functools.partial(attend_kernel, scale, head_width, LEFT),
        out_shape=attended_outs(frames - LEFT)
        + tuple(jax.ShapeDtypeStruct(x.shape, x.dtype) for x in inputs),
        in_specs=[SMEM, SMEM] + [HBM] * 5,
        out_specs=(VMEM,) * 8,
        scratch_shapes=[pltpu.SemaphoreType.DMA((5,))],
        compiler_params=params(16),
        cost_estimate=attend_cost(frames - LEFT),
        name="attend_late",
    )(offset, order, *in_hbm(*inputs))
    early = pl.pallas_call(
        functools.partial(attend_kernel, scale, head_width, 0),
        out_shape=attended_outs(LEFT),
        in_specs=[SMEM, SMEM] + [VMEM] * 5 + [ANY],
        out_specs=(VMEM,) * 3,
        scratch_shapes=[
            pltpu.VMEM((2 * LEFT, width), BF16),
            pltpu.VMEM((2 * LEFT, width), BF16),
            pltpu.SemaphoreType.DMA((4,)),
        ],
        compiler_params=params(16),
        cost_estimate=attend_cost(LEFT),
        name="attend_early",
    )(offset, order, edges_vmem, q_vmem, k_vmem, v_vmem, proj_vmem, tails)

    def add(name, keep, got, after):
        return pl.pallas_call(
            functools.partial(add_kernel, width),
            in_specs=[VMEM, VMEM, ANY],
            out_specs=(VMEM,) * (chips - 1),
            out_shape=(jax.ShapeDtypeStruct((keep.shape[0], width), BF16),) * (chips - 1),
            compiler_params=params(16),
            cost_estimate=cost(keep.size, keep.size * 8),
            name=f"add_{name}",
        )(keep, got, after)

    def from_chips(parts):
        return [from_chip(part, chips - by) for by, part in enumerate(parts, 1)]

    send_late, keep_x_late, keep_late = late
    send_early, keep_x_early, keep_early = early
    swapped_late, swapped_early = core_swap(send_late), core_swap(send_early)
    both = pl.pallas_call(
        functools.partial(both_kernel, width),
        in_specs=[VMEM] * 4,
        out_specs=(VMEM,) * (chips - 1),
        out_shape=(jax.ShapeDtypeStruct((frames, width), BF16),) * (chips - 1),
        compiler_params=params(16),
        cost_estimate=cost(frames * away, frames * away * 8),
        name="both",
    )(keep_x_early, swapped_early, keep_x_late, swapped_late)
    sums = [keep_early, swapped_early, keep_late, swapped_late, *from_chips(both)]

    def blocks_of(count):
        return (jax.ShapeDtypeStruct((capacity, width), BF16),) * count

    state, *outgoing_0 = pl.pallas_call(
        functools.partial(state_kernel, away, len(sums)),
        out_shape=(jax.ShapeDtypeStruct((frames, width), BF16),) + blocks_of(n_time),
        in_specs=[SMEM] + [VMEM] * (len(sums) + 2),
        out_specs=(VMEM,) * (1 + n_time),
        compiler_params=params(16),
        cost_estimate=cost(2 * frames * width * rows, 4 * MIB),
        name="state",
    )(place, *sums, own_frames, ranks)
    wide = [state] + [from_chip(state, by) for by in range(1, chips)]
    outgoing_1 = pl.pallas_call(
        functools.partial(dispatch_kernel, chips, n_time),
        out_shape=jax.ShapeDtypeStruct((rows, chips * width), BF16),
        in_specs=[VMEM] * (chips + 1),
        out_specs=VMEM,
        compiler_params=params(16),
        cost_estimate=cost(4 * frames * width * rows, 3 * MIB),
        name="dispatch",
    )(*wide, ranks)

    def over_time(x):
        columns = x.shape[1]
        x = x.reshape(n_time, capacity, columns)
        x = lax.all_to_all(x, "tm", split_axis=0, concat_axis=0, tiled=True)
        return x.reshape(rows, columns)

    def take(x, after):
        return pl.pallas_call(
            take_kernel,
            in_specs=[VMEM] + [ANY] * len(after),
            out_specs=VMEM,
            out_shape=jax.ShapeDtypeStruct(x.shape, x.dtype),
            compiler_params=params(16),
            cost_estimate=cost(x.size, x.size * 4),
            name="take",
        )(x, *after)

    def experts(local, parts, after):
        outs = [jax.ShapeDtypeStruct((rows, columns), BF16) for columns in (away, width)]
        outs += [jax.ShapeDtypeStruct((rows, columns), F32) for columns in (away, width)]
        return pl.pallas_call(
            functools.partial(expert_kernel, local, (0,) * len(parts), width, len(after)),
            in_specs=[SMEM] + [VMEM] * len(parts) + [HBM] * 3 + [ANY] * len(after),
            out_specs=(VMEM,) * 4,
            scratch_shapes=[
                pltpu.VMEM((model, hidden), BF16),
                pltpu.VMEM((model, hidden), BF16),
                pltpu.VMEM((hidden, model), BF16),
                pltpu.VMEM((rows, model), BF16),
                pltpu.VMEM((rows, hidden), BF16),
                pltpu.SemaphoreType.DMA((3,)),
            ],
            out_shape=tuple(outs),
            compiler_params=params(20),
            cost_estimate=cost(6 * rows * model * hidden, 12 * MIB, rows * hidden),
            name=f"experts_{local}",
        )(order, *parts, *in_hbm(w_gate, w_up, w_down), *after)

    def spread(local, turned, parts, after):
        return pl.pallas_call(
            functools.partial(spread_kernel, n_time, len(after), turned),
            in_specs=[SMEM] + [VMEM] * len(parts) + [ANY] * len(after),
            out_specs=(VMEM,) * n_time,
            out_shape=blocks_of(n_time),
            compiler_params=params(16),
            cost_estimate=cost(rows * width * 4, rows * width * 10),
            name=f"spread_{local}",
        )(place, *parts, *after)

    def combine(local, sign, back, base):
        last = local == local_experts - 1
        return pl.pallas_call(
            functools.partial(combine_kernel, local, sign),
            out_shape=jax.ShapeDtypeStruct((frames, width), BF16 if last else F32),
            in_specs=[SMEM] + [VMEM] * (3 + len(back)),
            out_specs=VMEM,
            scratch_shapes=[pltpu.VMEM((rows, width), BF16)],
            compiler_params=params(16),
            cost_estimate=cost(4 * frames * width * rows, 3 * MIB),
            name=f"combine_{local}",
        )(place, targets, gates, base, *back)

    outgoing_0[-1] = take(outgoing_0[-1], wide[1:])
    arrived_0 = pl.pallas_call(
        join_kernel,
        in_specs=[VMEM] * n_time + [ANY],
        out_specs=VMEM,
        out_shape=jax.ShapeDtypeStruct((rows, width), BF16),
        compiler_params=params(16),
        cost_estimate=cost(rows * width, rows * width * 4),
        name="join",
    )(*exchanged(outgoing_0), outgoing_1)
    arrived_1 = over_time(outgoing_1)
    send_x_0, send_0, keep_x_0, keep_0 = experts(0, gathered(arrived_0), [outgoing_1])
    away_0 = add("0", keep_x_0, core_swap(send_x_0), send_0)
    got_0 = from_chips(away_0)
    swapped_0 = core_swap(send_0)
    arrived_1 = take(arrived_1, [away_0[0]])
    parts = [arrived_1, core_swap(arrived_1)]
    send_x_1, send_1, keep_x_1, keep_1 = experts(1, parts, [away_0[0]])
    away_1 = add("1", keep_x_1, core_swap(send_x_1), got_0[0])
    got_1 = from_chips(away_1)
    total_0 = spread(0, False, [keep_0, swapped_0, *got_0], [away_1[0]])
    back_0 = exchanged(total_0, -1)
    total_1 = spread(1, True, [keep_1, core_swap(send_1), *got_1], back_0[1 : n_time // 2 + 1])
    back_1 = exchanged(total_1)
    return combine(1, -1, back_1, combine(0, 1, back_0, state))


def solution(mesh):
    return jax.shard_map(
        per_device,
        mesh=mesh,
        in_specs=(
            P("tm", None),
            P("tm", "mp"),
            P("tm", "mp"),
            P("tm", "mp"),
            P(None, "tm"),
            P("mp", None),
            P("tm", None),
            P("tm", None),
            P("tm", None, "mp"),
            P("tm", None, "mp"),
            P("tm", "mp", None),
        ),
        out_specs=P("tm", "mp"),
        check_vma=False,
    )
```

```python
import functools

import jax
import jax.numpy as jnp
from jax import lax
from jax.experimental import pallas as pl
from jax.experimental.pallas import tpu as pltpu
from jax.sharding import PartitionSpec as P

HEADS = 16
TOP = 2
LEFT = 256
EPS = 1e-06
LANES = 128
MIB = 1 << 20
F32 = jnp.float32
BF16 = jnp.bfloat16

VMEM = pl.BlockSpec(memory_space=pltpu.VMEM)
SMEM = pl.BlockSpec(memory_space=pltpu.SMEM)
ANY = pl.BlockSpec(memory_space=pl.ANY)
HBM = pl.BlockSpec(memory_space=pltpu.HBM)


def params(mib):
    return pltpu.CompilerParams(vmem_limit_bytes=mib * MIB)


def cost(flops, moved, transcendentals=0):
    return pl.CostEstimate(flops=flops, bytes_accessed=moved, transcendentals=transcendentals)


def from_behind(x, axis, by):
    size = lax.axis_size(axis)
    pairs = [(i, i + by) for i in range(size) if 0 <= i + by < size]
    return lax.ppermute(x, axis, pairs)


def core_swap(x):
    size = lax.axis_size("mp")
    return lax.ppermute(x, "mp", [(i, i ^ 1) for i in range(size)])


def from_chip(x, by):
    chips = lax.axis_size("mp") // 2
    pairs = [(c * 2 + k, ((c + by) % chips) * 2 + k) for c in range(chips) for k in range(2)]
    return lax.ppermute(x, "mp", pairs)


def gathered(x):
    chips = lax.axis_size("mp") // 2
    mine = [x] + [from_chip(x, by) for by in range(1, chips)]
    return mine + [core_swap(part) for part in mine]


def exchanged(blocks):
    size = lax.axis_size("tm")
    assert size & (size - 1) == 0, size
    moved = list(blocks)
    for s in range(size - 1, 0, -1):
        moved[s] = lax.ppermute(blocks[s], "tm", [(i, i ^ s) for i in range(size)])
    return moved


def route_kernel(capacity, local_experts, n_time, ids_ref, ranks_ref, targets_ref):
    frames = ids_ref.shape[0]
    lanes = ranks_ref.shape[0]
    ids = ids_ref[...]
    owner = ids // local_experts
    ids = (ids - owner * local_experts) * n_time + owner
    experts = lax.broadcasted_iota(jnp.int32, (frames, lanes), 1)
    hits = [ids[:, k : k + 1] == experts for k in range(TOP)]
    named = functools.reduce(jnp.logical_or, hits)
    ones = jnp.where(named, 1.0, 0.0).astype(BF16)
    row = lax.broadcasted_iota(jnp.int32, (frames, frames), 0)
    column = lax.broadcasted_iota(jnp.int32, (frames, frames), 1)
    before = jnp.where(column < row, 1.0, 0.0).astype(BF16)
    ranks = jnp.dot(before, ones, preferred_element_type=F32)
    ranks_ref[...] = jnp.where(named, ranks, -1.0).T
    places = []
    for k in range(TOP):
        slot = jnp.sum(jnp.where(hits[k], ranks, 0.0), 1, keepdims=True).astype(jnp.int32)
        places.append(ids[:, k : k + 1] * capacity + slot)
    targets_ref[...] = jnp.concatenate(places, 1)


def attend_kernel(scale, head_width, start, meta_ref, order_ref, *refs):
    if start > 0:
        edges_any, q_any, k_any, v_any, proj_any = refs[:5]
        send_ref, keep_x_ref, keep_ref, edges_ref, q_all, k_ref, v_ref, proj_ref, sems = refs[5:]
        moves = [
            (k_any, k_ref),
            (q_any, q_all),
            (v_any, v_ref),
            (edges_any, edges_ref),
            (proj_any, proj_ref),
        ]
    else:
        edges_ref, q_all, k_all, v_all, proj_ref, tails_any = refs[:6]
        send_ref, keep_x_ref, keep_ref, k_ref, v_ref, sems = refs[6:]
        first_rows = pl.ds(0, keep_ref.shape[0])
        moves = [
            (tails_any.at[0], k_ref.at[pl.ds(0, LEFT)]),
            (k_all.at[first_rows], k_ref.at[pl.ds(LEFT, keep_ref.shape[0])]),
            (tails_any.at[1], v_ref.at[pl.ds(0, LEFT)]),
            (v_all.at[first_rows], v_ref.at[pl.ds(LEFT, keep_ref.shape[0])]),
        ]
    rows, columns = keep_ref.shape
    heads = columns // head_width
    block = LANES
    window = LEFT + block
    copies = [pltpu.make_async_copy(a, b, sems.at[i]) for i, (a, b) in enumerate(moves)]
    for copy in copies:
        copy.start()
    for copy in copies[:4]:
        copy.wait()
    edges = edges_ref[:, start : start + rows].astype(F32)
    edges = jnp.concatenate([edges, jnp.zeros((6, rows), F32)], 0).T
    lane_head = lax.broadcasted_iota(jnp.int32, (block, columns), 1) // head_width
    context = []
    for r in range(0, rows, block):
        key = k_ref[r : r + window, :]
        value = v_ref[r : r + window, :]
        query = q_all[start + r : start + r + block, :]
        places = lax.broadcasted_iota(jnp.int32, (block, window), 1)
        places = (places + (meta_ref[0] + (start + r - LEFT))).astype(F32)
        lower = jnp.maximum(edges[r : r + block, 0:1] - LEFT, 0.0)
        upper = edges[r : r + block, 1:2]
        visible = (places >= lower) & (places <= upper)
        own = [jnp.where(lane_head == h, query, jnp.zeros_like(query)) for h in range(heads)]
        own = jnp.concatenate(own, 0)
        scores = lax.dot_general(own, key, (((1,), (1,)), ((), ())), preferred_element_type=F32)
        scores = (scores * scale).reshape(heads, block, window)
        scores = jnp.where(visible[None], scores, -1e30)
        highest = jnp.max(scores, 2, keepdims=True)
        expos = jnp.exp(scores - highest)
        weights = (expos * (1.0 / jnp.sum(expos, 2, keepdims=True))).astype(BF16)
        weights = weights.reshape(heads * block, window)
        product = jnp.dot(weights, value, preferred_element_type=F32)
        mixed = product[0:block]
        for h in range(1, heads):
            mixed = jnp.where(lane_head == h, product[h * block : (h + 1) * block], mixed)
        context.append(mixed.astype(BF16))
    context = jnp.concatenate(context, 0)
    for copy in copies[4:]:
        copy.wait()
    count = proj_ref.shape[1] // columns // 2
    for i in range(2 * count):
        at = pl.multiple_of(order_ref[i] * columns, columns)
        part = jnp.dot(context, proj_ref[:, pl.ds(at, columns)], preferred_element_type=F32)
        j = (i - 1) % count * columns
        if i >= count:
            send_ref[:, j : j + columns] = part.astype(BF16)
        elif i > 0:
            keep_x_ref[:, j : j + columns] = part
        else:
            keep_ref[...] = part


def picked_rows(e, capacity, ranks_ref, state):
    slot = lax.broadcasted_iota(jnp.int32, (capacity, state.shape[0]), 0).astype(F32)
    pick = jnp.where(slot == ranks_ref[pl.ds(e, 1), :], 1.0, 0.0).astype(BF16)
    return jnp.dot(pick, state, preferred_element_type=F32).astype(BF16)


def scatter_rows(local, at_ref, ranks_ref, state, out_refs):
    n_time = len(out_refs)
    for s, out_ref in enumerate(out_refs):
        owner = at_ref[0] ^ s
        out_ref[...] = picked_rows(local * n_time + owner, out_ref.shape[0], ranks_ref, state)


def state_kernel(parts, column, at_ref, *refs):
    frames_ref, ranks_ref, state_ref = refs[2 * parts : 2 * parts + 3]
    width = state_ref.shape[1]
    halves = []
    for keep_ref, swapped_ref, *got in (refs[:parts], refs[parts : 2 * parts]):
        half = keep_ref[...] + swapped_ref[:, column : column + width].astype(F32)
        for ref in got:
            half = half + ref[...].astype(F32)
        halves.append(half)
    attended = jnp.concatenate(halves, 0)
    state = (frames_ref[...].astype(F32) + attended).astype(BF16)
    state_ref[...] = state
    scatter_rows(0, at_ref, ranks_ref, state, refs[2 * parts + 3 :])


def dispatch_kernel(pieces, n_time, *refs):
    state = jnp.concatenate([ref[...] for ref in refs[:pieces]], 1)
    ranks_ref, out_ref = refs[pieces:]
    capacity = out_ref.shape[0] // n_time
    for owner in range(n_time):
        rows = picked_rows(n_time + owner, capacity, ranks_ref, state)
        out_ref[owner * capacity : (owner + 1) * capacity, :] = rows


def join_kernel(*refs):
    *pieces, after_any, out_ref = refs
    count = pieces[0].shape[0]
    for s, ref in enumerate(pieces):
        out_ref[s * count : (s + 1) * count, :] = ref[...]


def take_kernel(rows_ref, *refs):
    refs[-1][...] = rows_ref[...]


def expert_kernel(local, starts, width, awaited, order_ref, *refs):
    arrays = len(starts)
    rows_in = refs[:arrays]
    gate_any, up_any, down_any = refs[arrays : arrays + 3]
    *outs, gate_ref, up_ref, down_ref, normed_ref, active_ref, sems = refs[arrays + 3 + awaited :]
    *send_x_refs, send_ref, keep_x_ref, keep_ref = outs
    rows, model = normed_ref.shape
    hidden = active_ref.shape[1]
    moves = [
        (gate_any.at[local], gate_ref),
        (up_any.at[local], up_ref),
        (down_any.at[local], down_ref),
    ]
    copies = [pltpu.make_async_copy(a, b, sems.at[i]) for i, (a, b) in enumerate(moves)]
    for copy in copies:
        copy.start()

    blocks = []
    for ref, start in zip(rows_in, starts):
        blocks += [(ref, start, c) for c in range(0, ref.shape[1], width)]
    step = min(rows, 256)

    def norm(i, carry):
        at_row = pl.multiple_of(i * step, step)
        parts = [
            ref[pl.ds(pl.multiple_of(start + i * step, step), step), c : c + width].astype(F32)
            for ref, start, c in blocks
        ]
        squares = sum(jnp.sum(part * part, 1, keepdims=True) for part in parts)
        factor = lax.rsqrt(squares * (1.0 / model) + EPS)
        for j, part in enumerate(parts):
            at = pl.multiple_of(order_ref[j] * width, width)
            normed_ref[pl.ds(at_row, step), pl.ds(at, width)] = (part * factor).astype(BF16)
        return carry

    lax.fori_loop(0, rows // step, norm, 0)
    copies[0].wait()
    copies[1].wait()
    tile = min(rows, 1024)
    chunk = min(hidden, 256)
    for r in range(0, rows, tile):
        normed = normed_ref[r : r + tile, :]
        for c in range(0, hidden, chunk):
            gate = jnp.dot(normed, gate_ref[:, c : c + chunk], preferred_element_type=F32)
            up = jnp.dot(normed, up_ref[:, c : c + chunk], preferred_element_type=F32)
            half = 0.5 * gate
            active = (half + half * jnp.tanh(half)) * up
            active_ref[r : r + tile, c : c + chunk] = active.astype(BF16)
    copies[2].wait()
    count = len(blocks) // 2
    def project(i, out_refs, column):
        at = pl.multiple_of(order_ref[i] * width, width)
        weight = down_ref[:, pl.ds(at, width)]
        result = jnp.dot(active_ref[...], weight, preferred_element_type=F32)
        each = rows // len(out_refs)
        for j, out_ref in enumerate(out_refs):
            part = result[j * each : (j + 1) * each]
            out_ref[:, column : column + width] = part.astype(out_ref.dtype)

    for by in range(1, count):
        project(count + by, send_x_refs, (by - 1) * width)
    project(count, [send_ref], 0)
    for by in range(1, count):
        project(by, [keep_x_ref], (by - 1) * width)
    project(0, [keep_ref], 0)


def add_kernel(width, keep_ref, got_ref, after_any, *out_refs):
    for i, out_ref in enumerate(out_refs):
        at = slice(i * width, (i + 1) * width)
        out_ref[...] = (keep_ref[:, at] + got_ref[:, at].astype(F32)).astype(BF16)


def spread_kernel(n_time, awaited, turned, at_ref, keep_ref, *refs):
    got, outs = refs[: -n_time - awaited], refs[-n_time:]
    capacity = outs[0].shape[0]
    for s, out_ref in enumerate(outs):
        place = at_ref[0] ^ s if turned else s
        at = pl.ds(pl.multiple_of(place * capacity, capacity), capacity)
        total = keep_ref[at, :]
        for ref in got:
            total = total + ref[at, :].astype(F32)
        out_ref[...] = total.astype(BF16)


def combine_kernel(local, at_ref, targets_ref, gates_ref, base_ref, *refs):
    *got, out_ref, back_ref = refs
    capacity = got[0].shape[0]
    for s, ref in enumerate(reversed(got)):
        place = at_ref[0] ^ s
        back_ref[pl.ds(pl.multiple_of(place * capacity, capacity), capacity), :] = ref[...]
    back = back_ref[...]
    rows = back.shape[0]
    frames = targets_ref.shape[0]
    places = lax.broadcasted_iota(jnp.int32, (frames, rows), 1) + local * rows
    total = base_ref[...].astype(F32)
    for k in range(TOP):
        pick = jnp.where(places == targets_ref[:, k : k + 1], 1.0, 0.0).astype(BF16)
        total = total + gates_ref[:, k : k + 1] * jnp.dot(pick, back, preferred_element_type=F32)
    out_ref[...] = total.astype(out_ref.dtype)


def per_device(
    frames_in,
    queries,
    keys,
    values,
    segment_edges,
    out_proj,
    expert_ids,
    gates,
    w_gate,
    w_up,
    w_down,
):
    frames, model = frames_in.shape
    width = queries.shape[1]
    n_model = lax.axis_size("mp")
    n_time = lax.axis_size("tm")
    chips = n_model // 2
    head_width = model // HEADS
    scale = head_width ** (-0.5)
    local_experts = w_gate.shape[0]
    hidden = w_gate.shape[2]
    experts_all = local_experts * n_time
    capacity = 4 * frames // experts_all
    rows = n_time * capacity
    lanes = -(-experts_all // LANES) * LANES
    at_time = lax.axis_index("tm")
    at_model = lax.axis_index("mp")
    chip, core = at_model // 2, at_model % 2
    mine = [((chip - by) % chips) * 2 + core for by in range(chips)]
    others = [((chip - by) % chips) * 2 + 1 - core for by in range(chips)]
    order = jnp.stack(mine + others).astype(jnp.int32)
    offset = (at_time * frames).astype(jnp.int32).reshape(1)
    place = at_time.astype(jnp.int32).reshape(1)
    away = (chips - 1) * width

    tails = from_behind(jnp.stack([keys[frames - LEFT :], values[frames - LEFT :]], 0), "tm", 1)
    own_frames = lax.dynamic_slice_in_dim(frames_in, at_model * width, width, 1)

    ranks, targets = pl.pallas_call(
        functools.partial(route_kernel, capacity, local_experts, n_time),
        out_shape=(
            jax.ShapeDtypeStruct((lanes, frames), F32),
            jax.ShapeDtypeStruct((frames, TOP), jnp.int32),
        ),
        in_specs=[VMEM],
        out_specs=(VMEM, VMEM),
        compiler_params=params(16),
        cost_estimate=cost(2 * frames * frames * lanes, frames * 1024),
        name="route",
    )(expert_ids)

    def in_hbm(*arrays):
        return [pltpu.with_memory_space_constraint(x, pltpu.HBM) for x in arrays]

    def attended_outs(count):
        return (
            jax.ShapeDtypeStruct((count, chips * width), BF16),
            jax.ShapeDtypeStruct((count, away), F32),
            jax.ShapeDtypeStruct((count, width), F32),
        )

    def attend_cost(count):
        return cost(count * 384 * width * 16, count * width * 8, count * 384 * 4)

    inputs = (segment_edges, queries, keys, values, out_proj)
    *late, edges_vmem, q_vmem, k_vmem, v_vmem, proj_vmem = pl.pallas_call(
        functools.partial(attend_kernel, scale, head_width, LEFT),
        out_shape=attended_outs(frames - LEFT)
        + tuple(jax.ShapeDtypeStruct(x.shape, x.dtype) for x in inputs),
        in_specs=[SMEM, SMEM] + [HBM] * 5,
        out_specs=(VMEM,) * 8,
        scratch_shapes=[pltpu.SemaphoreType.DMA((5,))],
        compiler_params=params(16),
        cost_estimate=attend_cost(frames - LEFT),
        name="attend_late",
    )(offset, order, *in_hbm(*inputs))
    early = pl.pallas_call(
        functools.partial(attend_kernel, scale, head_width, 0),
        out_shape=attended_outs(LEFT),
        in_specs=[SMEM, SMEM] + [VMEM] * 5 + [ANY],
        out_specs=(VMEM,) * 3,
        scratch_shapes=[
            pltpu.VMEM((2 * LEFT, width), BF16),
            pltpu.VMEM((2 * LEFT, width), BF16),
            pltpu.SemaphoreType.DMA((4,)),
        ],
        compiler_params=params(16),
        cost_estimate=attend_cost(LEFT),
        name="attend_early",
    )(offset, order, edges_vmem, q_vmem, k_vmem, v_vmem, proj_vmem, tails)

    def add(name, keep, got, after):
        return pl.pallas_call(
            functools.partial(add_kernel, width),
            in_specs=[VMEM, VMEM, ANY],
            out_specs=(VMEM,) * (chips - 1),
            out_shape=(jax.ShapeDtypeStruct((keep.shape[0], width), BF16),) * (chips - 1),
            compiler_params=params(16),
            cost_estimate=cost(keep.size, keep.size * 8),
            name=f"add_{name}",
        )(keep, got, after)

    def from_chips(parts):
        return [from_chip(part, chips - by) for by, part in enumerate(parts, 1)]

    def attended(name, send, keep_x, keep):
        swapped = core_swap(send)
        return [keep, swapped, *from_chips(add(name, keep_x, swapped, swapped))]

    late = attended("late", *late)
    early = attended("early", *early)

    def blocks_of(count):
        return (jax.ShapeDtypeStruct((capacity, width), BF16),) * count

    state, *outgoing_0 = pl.pallas_call(
        functools.partial(state_kernel, len(early), away),
        out_shape=(jax.ShapeDtypeStruct((frames, width), BF16),) + blocks_of(n_time),
        in_specs=[SMEM] + [VMEM] * (2 * len(early) + 2),
        out_specs=(VMEM,) * (1 + n_time),
        compiler_params=params(16),
        cost_estimate=cost(2 * frames * width * rows, 4 * MIB),
        name="state",
    )(place, *early, *late, own_frames, ranks)
    wide = [state] + [from_chip(state, by) for by in range(1, chips)]
    outgoing_1 = pl.pallas_call(
        functools.partial(dispatch_kernel, chips, n_time),
        out_shape=jax.ShapeDtypeStruct((rows, chips * width), BF16),
        in_specs=[VMEM] * (chips + 1),
        out_specs=VMEM,
        compiler_params=params(16),
        cost_estimate=cost(4 * frames * width * rows, 3 * MIB),
        name="dispatch",
    )(*wide, ranks)

    def over_time(x):
        columns = x.shape[1]
        x = x.reshape(n_time, capacity, columns)
        x = lax.all_to_all(x, "tm", split_axis=0, concat_axis=0, tiled=True)
        return x.reshape(rows, columns)

    def take(x, after):
        return pl.pallas_call(
            take_kernel,
            in_specs=[VMEM] + [ANY] * len(after),
            out_specs=VMEM,
            out_shape=jax.ShapeDtypeStruct(x.shape, x.dtype),
            compiler_params=params(16),
            cost_estimate=cost(x.size, x.size * 4),
            name="take",
        )(x, *after)

    def experts(local, parts, after):
        outs = [jax.ShapeDtypeStruct((rows, columns), BF16) for columns in (away, width)]
        outs += [jax.ShapeDtypeStruct((rows, columns), F32) for columns in (away, width)]
        return pl.pallas_call(
            functools.partial(expert_kernel, local, (0,) * len(parts), width, len(after)),
            in_specs=[SMEM] + [VMEM] * len(parts) + [HBM] * 3 + [ANY] * len(after),
            out_specs=(VMEM,) * 4,
            scratch_shapes=[
                pltpu.VMEM((model, hidden), BF16),
                pltpu.VMEM((model, hidden), BF16),
                pltpu.VMEM((hidden, model), BF16),
                pltpu.VMEM((rows, model), BF16),
                pltpu.VMEM((rows, hidden), BF16),
                pltpu.SemaphoreType.DMA((3,)),
            ],
            out_shape=tuple(outs),
            compiler_params=params(20),
            cost_estimate=cost(6 * rows * model * hidden, 12 * MIB, rows * hidden),
            name=f"experts_{local}",
        )(order, *parts, *in_hbm(w_gate, w_up, w_down), *after)

    def spread(local, turned, parts, after):
        return pl.pallas_call(
            functools.partial(spread_kernel, n_time, len(after), turned),
            in_specs=[SMEM] + [VMEM] * len(parts) + [ANY] * len(after),
            out_specs=(VMEM,) * n_time,
            out_shape=blocks_of(n_time),
            compiler_params=params(16),
            cost_estimate=cost(rows * width * 4, rows * width * 10),
            name=f"spread_{local}",
        )(place, *parts, *after)

    def combine(local, back, base):
        last = local == local_experts - 1
        return pl.pallas_call(
            functools.partial(combine_kernel, local),
            out_shape=jax.ShapeDtypeStruct((frames, width), BF16 if last else F32),
            in_specs=[SMEM] + [VMEM] * (3 + len(back)),
            out_specs=VMEM,
            scratch_shapes=[pltpu.VMEM((rows, width), BF16)],
            compiler_params=params(16),
            cost_estimate=cost(4 * frames * width * rows, 3 * MIB),
            name=f"combine_{local}",
        )(place, targets, gates, base, *reversed(back))

    outgoing_0[1] = take(outgoing_0[1], wide[1:])
    arrived_0 = pl.pallas_call(
        join_kernel,
        in_specs=[VMEM] * n_time + [ANY],
        out_specs=VMEM,
        out_shape=jax.ShapeDtypeStruct((rows, width), BF16),
        compiler_params=params(16),
        cost_estimate=cost(rows * width, rows * width * 4),
        name="join",
    )(*exchanged(outgoing_0), outgoing_1)
    arrived_1 = over_time(outgoing_1)
    send_x_0, send_0, keep_x_0, keep_0 = experts(0, gathered(arrived_0), [outgoing_1])
    away_0 = add("0", keep_x_0, core_swap(send_x_0), send_0)
    got_0 = from_chips(away_0)
    swapped_0 = core_swap(send_0)
    arrived_1 = take(arrived_1, [away_0[0]])
    parts = [arrived_1, core_swap(arrived_1)]
    send_x_1, send_1, keep_x_1, keep_1 = experts(1, parts, [away_0[0]])
    away_1 = add("1", keep_x_1, core_swap(send_x_1), got_0[0])
    got_1 = from_chips(away_1)
    total_0 = spread(0, False, [keep_0, swapped_0, *got_0], [away_1[0]])
    back_0 = exchanged(total_0)
    total_1 = spread(1, True, [keep_1, core_swap(send_1), *got_1], back_0[n_time // 2 + 1 :])
    back_1 = exchanged(total_1)
    return combine(1, back_1, combine(0, back_0, state))


def solution(mesh):
    return jax.shard_map(
        per_device,
        mesh=mesh,
        in_specs=(
            P("tm", None),
            P("tm", "mp"),
            P("tm", "mp"),
            P("tm", "mp"),
            P(None, "tm"),
            P("mp", None),
            P("tm", None),
            P("tm", None),
            P("tm", None, "mp"),
            P("tm", None, "mp"),
            P("tm", "mp", None),
        ),
        out_specs=P("tm", "mp"),
        check_vma=False,
    )
```

```python
import functools

import jax
import jax.numpy as jnp
from jax import lax
from jax.experimental import pallas as pl
from jax.experimental.pallas import tpu as pltpu
from jax.sharding import PartitionSpec as P

HEADS = 16
TOP = 2
LEFT = 256
EPS = 1e-06
LANES = 128
MIB = 1 << 20
F32 = jnp.float32
BF16 = jnp.bfloat16

VMEM = pl.BlockSpec(memory_space=pltpu.VMEM)
SMEM = pl.BlockSpec(memory_space=pltpu.SMEM)
ANY = pl.BlockSpec(memory_space=pl.ANY)
HBM = pl.BlockSpec(memory_space=pltpu.HBM)


def params(mib):
    return pltpu.CompilerParams(vmem_limit_bytes=mib * MIB)


def cost(flops, moved, transcendentals=0):
    return pl.CostEstimate(flops=flops, bytes_accessed=moved, transcendentals=transcendentals)


def from_behind(x, axis, by):
    size = lax.axis_size(axis)
    pairs = [(i, i + by) for i in range(size) if 0 <= i + by < size]
    return lax.ppermute(x, axis, pairs)


def core_swap(x):
    size = lax.axis_size("mp")
    return lax.ppermute(x, "mp", [(i, i ^ 1) for i in range(size)])


def from_chip(x, by):
    chips = lax.axis_size("mp") // 2
    pairs = [(c * 2 + k, ((c + by) % chips) * 2 + k) for c in range(chips) for k in range(2)]
    return lax.ppermute(x, "mp", pairs)


def gathered(x):
    chips = lax.axis_size("mp") // 2
    mine = [x] + [from_chip(x, by) for by in range(1, chips)]
    return mine + [core_swap(part) for part in mine]


def exchanged(blocks):
    size = lax.axis_size("tm")
    assert size & (size - 1) == 0, size
    moved = list(blocks)
    for s in range(size - 1, 0, -1):
        moved[s] = lax.ppermute(blocks[s], "tm", [(i, i ^ s) for i in range(size)])
    return moved


def route_kernel(capacity, local_experts, n_time, ids_ref, ranks_ref, targets_ref):
    frames = ids_ref.shape[0]
    lanes = ranks_ref.shape[0]
    ids = ids_ref[...]
    owner = ids // local_experts
    ids = (ids - owner * local_experts) * n_time + owner
    experts = lax.broadcasted_iota(jnp.int32, (frames, lanes), 1)
    hits = [ids[:, k : k + 1] == experts for k in range(TOP)]
    named = functools.reduce(jnp.logical_or, hits)
    ones = jnp.where(named, 1.0, 0.0).astype(BF16)
    row = lax.broadcasted_iota(jnp.int32, (frames, frames), 0)
    column = lax.broadcasted_iota(jnp.int32, (frames, frames), 1)
    before = jnp.where(column < row, 1.0, 0.0).astype(BF16)
    ranks = jnp.dot(before, ones, preferred_element_type=F32)
    ranks_ref[...] = jnp.where(named, ranks, -1.0).T
    places = []
    for k in range(TOP):
        slot = jnp.sum(jnp.where(hits[k], ranks, 0.0), 1, keepdims=True).astype(jnp.int32)
        places.append(ids[:, k : k + 1] * capacity + slot)
    targets_ref[...] = jnp.concatenate(places, 1)


def attend_kernel(scale, head_width, start, meta_ref, order_ref, *refs):
    if start > 0:
        edges_any, q_any, k_any, v_any, proj_any = refs[:5]
        send_ref, keep_x_ref, keep_ref, edges_ref, q_all, k_ref, v_ref, proj_ref, sems = refs[5:]
        moves = [
            (k_any, k_ref),
            (q_any, q_all),
            (v_any, v_ref),
            (edges_any, edges_ref),
            (proj_any, proj_ref),
        ]
    else:
        edges_ref, q_all, k_ref, v_ref, proj_ref, tails_ref = refs[:6]
        send_ref, keep_x_ref, keep_ref = refs[6:]
        moves = []
    rows, columns = keep_ref.shape
    heads = columns // head_width
    block = LANES
    window = LEFT + block
    copies = [pltpu.make_async_copy(a, b, sems.at[i]) for i, (a, b) in enumerate(moves)]
    for copy in copies:
        copy.start()
    for copy in copies[:4]:
        copy.wait()
    edges = edges_ref[:, start : start + rows].astype(F32)
    edges = jnp.concatenate([edges, jnp.zeros((6, rows), F32)], 0).T
    lane_head = lax.broadcasted_iota(jnp.int32, (block, columns), 1) // head_width
    context = []
    for r in range(0, rows, block):
        if start > 0:
            key = k_ref[start - LEFT + r : start + r + block, :]
            value = v_ref[start - LEFT + r : start + r + block, :]
        else:
            key = jnp.concatenate([tails_ref[0, r:LEFT, :], k_ref[0 : r + block, :]], 0)
            value = jnp.concatenate([tails_ref[1, r:LEFT, :], v_ref[0 : r + block, :]], 0)
        query = q_all[start + r : start + r + block, :]
        places = lax.broadcasted_iota(jnp.int32, (block, window), 1)
        places = (places + (meta_ref[0] + (start + r - LEFT))).astype(F32)
        lower = jnp.maximum(edges[r : r + block, 0:1] - LEFT, 0.0)
        upper = edges[r : r + block, 1:2]
        visible = (places >= lower) & (places <= upper)
        own = [jnp.where(lane_head == h, query, jnp.zeros_like(query)) for h in range(heads)]
        own = jnp.concatenate(own, 0)
        scores = lax.dot_general(own, key, (((1,), (1,)), ((), ())), preferred_element_type=F32)
        scores = (scores * scale).reshape(heads, block, window)
        scores = jnp.where(visible[None], scores, -1e30)
        highest = jnp.max(scores, 2, keepdims=True)
        expos = jnp.exp(scores - highest)
        weights = (expos * (1.0 / jnp.sum(expos, 2, keepdims=True))).astype(BF16)
        weights = weights.reshape(heads * block, window)
        product = jnp.dot(weights, value, preferred_element_type=F32)
        mixed = product[0:block]
        for h in range(1, heads):
            mixed = jnp.where(lane_head == h, product[h * block : (h + 1) * block], mixed)
        context.append(mixed.astype(BF16))
    context = jnp.concatenate(context, 0)
    for copy in copies[4:]:
        copy.wait()
    count = proj_ref.shape[1] // columns // 2
    for i in range(2 * count):
        at = pl.multiple_of(order_ref[i] * columns, columns)
        part = jnp.dot(context, proj_ref[:, pl.ds(at, columns)], preferred_element_type=F32)
        j = (i - 1) % count * columns
        if i >= count:
            send_ref[:, j : j + columns] = part.astype(BF16)
        elif i > 0:
            keep_x_ref[:, j : j + columns] = part
        else:
            keep_ref[...] = part


def picked_rows(e, capacity, ranks_ref, state):
    slot = lax.broadcasted_iota(jnp.int32, (capacity, state.shape[0]), 0).astype(F32)
    pick = jnp.where(slot == ranks_ref[pl.ds(e, 1), :], 1.0, 0.0).astype(BF16)
    return jnp.dot(pick, state, preferred_element_type=F32).astype(BF16)


def scatter_rows(local, at_ref, ranks_ref, state, out_refs):
    n_time = len(out_refs)
    for s, out_ref in enumerate(out_refs):
        owner = at_ref[0] ^ s
        out_ref[...] = picked_rows(local * n_time + owner, out_ref.shape[0], ranks_ref, state)


def state_kernel(parts, column, at_ref, *refs):
    frames_ref, ranks_ref, state_ref = refs[2 * parts : 2 * parts + 3]
    width = state_ref.shape[1]
    halves = []
    for keep_ref, swapped_ref, *got in (refs[:parts], refs[parts : 2 * parts]):
        half = keep_ref[...] + swapped_ref[:, column : column + width].astype(F32)
        for ref in got:
            half = half + ref[...].astype(F32)
        halves.append(half)
    attended = jnp.concatenate(halves, 0)
    state = (frames_ref[...].astype(F32) + attended).astype(BF16)
    state_ref[...] = state
    scatter_rows(0, at_ref, ranks_ref, state, refs[2 * parts + 3 :])


def dispatch_kernel(pieces, n_time, *refs):
    state = jnp.concatenate([ref[...] for ref in refs[:pieces]], 1)
    ranks_ref, out_ref = refs[pieces:]
    capacity = out_ref.shape[0] // n_time
    for owner in range(n_time):
        rows = picked_rows(n_time + owner, capacity, ranks_ref, state)
        out_ref[owner * capacity : (owner + 1) * capacity, :] = rows


def join_kernel(*refs):
    *pieces, after_any, out_ref = refs
    count = pieces[0].shape[0]
    for s, ref in enumerate(pieces):
        out_ref[s * count : (s + 1) * count, :] = ref[...]


def take_kernel(rows_ref, *refs):
    refs[-1][...] = rows_ref[...]


def expert_kernel(local, starts, width, awaited, order_ref, *refs):
    arrays = len(starts)
    rows_in = refs[:arrays]
    gate_any, up_any, down_any = refs[arrays : arrays + 3]
    *outs, gate_ref, up_ref, down_ref, normed_ref, active_ref, sems = refs[arrays + 3 + awaited :]
    *send_x_refs, send_ref, keep_x_ref, keep_ref = outs
    rows, model = normed_ref.shape
    hidden = active_ref.shape[1]
    moves = [
        (gate_any.at[local], gate_ref),
        (up_any.at[local], up_ref),
        (down_any.at[local], down_ref),
    ]
    copies = [pltpu.make_async_copy(a, b, sems.at[i]) for i, (a, b) in enumerate(moves)]
    for copy in copies:
        copy.start()

    blocks = []
    for ref, start in zip(rows_in, starts):
        blocks += [(ref, start, c) for c in range(0, ref.shape[1], width)]
    step = min(rows, 256)

    def norm(i, carry):
        at_row = pl.multiple_of(i * step, step)
        parts = [
            ref[pl.ds(pl.multiple_of(start + i * step, step), step), c : c + width].astype(F32)
            for ref, start, c in blocks
        ]
        squares = sum(jnp.sum(part * part, 1, keepdims=True) for part in parts)
        factor = lax.rsqrt(squares * (1.0 / model) + EPS)
        for j, part in enumerate(parts):
            at = pl.multiple_of(order_ref[j] * width, width)
            normed_ref[pl.ds(at_row, step), pl.ds(at, width)] = (part * factor).astype(BF16)
        return carry

    lax.fori_loop(0, rows // step, norm, 0)
    copies[0].wait()
    copies[1].wait()
    tile = min(rows, 1024)
    chunk = min(hidden, 256)
    for r in range(0, rows, tile):
        normed = normed_ref[r : r + tile, :]
        for c in range(0, hidden, chunk):
            gate = jnp.dot(normed, gate_ref[:, c : c + chunk], preferred_element_type=F32)
            up = jnp.dot(normed, up_ref[:, c : c + chunk], preferred_element_type=F32)
            half = 0.5 * gate
            active = (half + half * jnp.tanh(half)) * up
            active_ref[r : r + tile, c : c + chunk] = active.astype(BF16)
    copies[2].wait()
    count = len(blocks) // 2
    def project(i, out_refs, column):
        at = pl.multiple_of(order_ref[i] * width, width)
        weight = down_ref[:, pl.ds(at, width)]
        result = jnp.dot(active_ref[...], weight, preferred_element_type=F32)
        each = rows // len(out_refs)
        for j, out_ref in enumerate(out_refs):
            part = result[j * each : (j + 1) * each]
            out_ref[:, column : column + width] = part.astype(out_ref.dtype)

    for by in range(1, count):
        project(count + by, send_x_refs, (by - 1) * width)
    project(count, [send_ref], 0)
    for by in range(1, count):
        project(by, [keep_x_ref], (by - 1) * width)
    project(0, [keep_ref], 0)


def add_kernel(width, keep_ref, got_ref, after_any, *out_refs):
    for i, out_ref in enumerate(out_refs):
        at = slice(i * width, (i + 1) * width)
        out_ref[...] = (keep_ref[:, at] + got_ref[:, at].astype(F32)).astype(BF16)


def spread_kernel(n_time, awaited, turned, at_ref, keep_ref, *refs):
    got, outs = refs[: -n_time - awaited], refs[-n_time:]
    capacity = outs[0].shape[0]
    for s, out_ref in enumerate(outs):
        place = at_ref[0] ^ s if turned else s
        at = pl.ds(pl.multiple_of(place * capacity, capacity), capacity)
        total = keep_ref[at, :]
        for ref in got:
            total = total + ref[at, :].astype(F32)
        out_ref[...] = total.astype(BF16)


def combine_kernel(local, at_ref, targets_ref, gates_ref, base_ref, *refs):
    *got, out_ref, back_ref = refs
    capacity = got[0].shape[0]
    for s, ref in enumerate(reversed(got)):
        place = at_ref[0] ^ s
        back_ref[pl.ds(pl.multiple_of(place * capacity, capacity), capacity), :] = ref[...]
    back = back_ref[...]
    rows = back.shape[0]
    frames = targets_ref.shape[0]
    places = lax.broadcasted_iota(jnp.int32, (frames, rows), 1) + local * rows
    total = base_ref[...].astype(F32)
    for k in range(TOP):
        pick = jnp.where(places == targets_ref[:, k : k + 1], 1.0, 0.0).astype(BF16)
        total = total + gates_ref[:, k : k + 1] * jnp.dot(pick, back, preferred_element_type=F32)
    out_ref[...] = total.astype(out_ref.dtype)


def per_device(
    frames_in,
    queries,
    keys,
    values,
    segment_edges,
    out_proj,
    expert_ids,
    gates,
    w_gate,
    w_up,
    w_down,
):
    frames, model = frames_in.shape
    width = queries.shape[1]
    n_model = lax.axis_size("mp")
    n_time = lax.axis_size("tm")
    chips = n_model // 2
    head_width = model // HEADS
    scale = head_width ** (-0.5)
    local_experts = w_gate.shape[0]
    hidden = w_gate.shape[2]
    experts_all = local_experts * n_time
    capacity = 4 * frames // experts_all
    rows = n_time * capacity
    lanes = -(-experts_all // LANES) * LANES
    at_time = lax.axis_index("tm")
    at_model = lax.axis_index("mp")
    chip, core = at_model // 2, at_model % 2
    mine = [((chip - by) % chips) * 2 + core for by in range(chips)]
    others = [((chip - by) % chips) * 2 + 1 - core for by in range(chips)]
    order = jnp.stack(mine + others).astype(jnp.int32)
    offset = (at_time * frames).astype(jnp.int32).reshape(1)
    place = at_time.astype(jnp.int32).reshape(1)
    away = (chips - 1) * width

    tails = from_behind(jnp.stack([keys[frames - LEFT :], values[frames - LEFT :]], 0), "tm", 1)
    own_frames = lax.dynamic_slice_in_dim(frames_in, at_model * width, width, 1)

    ranks, targets = pl.pallas_call(
        functools.partial(route_kernel, capacity, local_experts, n_time),
        out_shape=(
            jax.ShapeDtypeStruct((lanes, frames), F32),
            jax.ShapeDtypeStruct((frames, TOP), jnp.int32),
        ),
        in_specs=[VMEM],
        out_specs=(VMEM, VMEM),
        compiler_params=params(16),
        cost_estimate=cost(2 * frames * frames * lanes, frames * 1024),
        name="route",
    )(expert_ids)

    def in_hbm(*arrays):
        return [pltpu.with_memory_space_constraint(x, pltpu.HBM) for x in arrays]

    def attended_outs(count):
        return (
            jax.ShapeDtypeStruct((count, chips * width), BF16),
            jax.ShapeDtypeStruct((count, away), F32),
            jax.ShapeDtypeStruct((count, width), F32),
        )

    def attend_cost(count):
        return cost(count * 384 * width * 16, count * width * 8, count * 384 * 4)

    inputs = (segment_edges, queries, keys, values, out_proj)
    *late, edges_vmem, q_vmem, k_vmem, v_vmem, proj_vmem = pl.pallas_call(
        functools.partial(attend_kernel, scale, head_width, LEFT),
        out_shape=attended_outs(frames - LEFT)
        + tuple(jax.ShapeDtypeStruct(x.shape, x.dtype) for x in inputs),
        in_specs=[SMEM, SMEM] + [HBM] * 5,
        out_specs=(VMEM,) * 8,
        scratch_shapes=[pltpu.SemaphoreType.DMA((5,))],
        compiler_params=params(16),
        cost_estimate=attend_cost(frames - LEFT),
        name="attend_late",
    )(offset, order, *in_hbm(*inputs))
    early = pl.pallas_call(
        functools.partial(attend_kernel, scale, head_width, 0),
        out_shape=attended_outs(LEFT),
        in_specs=[SMEM, SMEM] + [VMEM] * 6,
        out_specs=(VMEM,) * 3,
        compiler_params=params(16),
        cost_estimate=attend_cost(LEFT),
        name="attend_early",
    )(offset, order, edges_vmem, q_vmem, k_vmem, v_vmem, proj_vmem, tails)

    def add(name, keep, got, after):
        return pl.pallas_call(
            functools.partial(add_kernel, width),
            in_specs=[VMEM, VMEM, ANY],
            out_specs=(VMEM,) * (chips - 1),
            out_shape=(jax.ShapeDtypeStruct((keep.shape[0], width), BF16),) * (chips - 1),
            compiler_params=params(16),
            cost_estimate=cost(keep.size, keep.size * 8),
            name=f"add_{name}",
        )(keep, got, after)

    def from_chips(parts):
        return [from_chip(part, chips - by) for by, part in enumerate(parts, 1)]

    def attended(name, send, keep_x, keep):
        swapped = core_swap(send)
        return [keep, swapped, *from_chips(add(name, keep_x, swapped, swapped))]

    late = attended("late", *late)
    early = attended("early", *early)

    def blocks_of(count):
        return (jax.ShapeDtypeStruct((capacity, width), BF16),) * count

    state, *outgoing_0 = pl.pallas_call(
        functools.partial(state_kernel, len(early), away),
        out_shape=(jax.ShapeDtypeStruct((frames, width), BF16),) + blocks_of(n_time),
        in_specs=[SMEM] + [VMEM] * (2 * len(early) + 2),
        out_specs=(VMEM,) * (1 + n_time),
        compiler_params=params(16),
        cost_estimate=cost(2 * frames * width * rows, 4 * MIB),
        name="state",
    )(place, *early, *late, own_frames, ranks)
    wide = [state] + [from_chip(state, by) for by in range(1, chips)]
    outgoing_1 = pl.pallas_call(
        functools.partial(dispatch_kernel, chips, n_time),
        out_shape=jax.ShapeDtypeStruct((rows, chips * width), BF16),
        in_specs=[VMEM] * (chips + 1),
        out_specs=VMEM,
        compiler_params=params(16),
        cost_estimate=cost(4 * frames * width * rows, 3 * MIB),
        name="dispatch",
    )(*wide, ranks)

    def over_time(x):
        columns = x.shape[1]
        x = x.reshape(n_time, capacity, columns)
        x = lax.all_to_all(x, "tm", split_axis=0, concat_axis=0, tiled=True)
        return x.reshape(rows, columns)

    def take(x, after):
        return pl.pallas_call(
            take_kernel,
            in_specs=[VMEM] + [ANY] * len(after),
            out_specs=VMEM,
            out_shape=jax.ShapeDtypeStruct(x.shape, x.dtype),
            compiler_params=params(16),
            cost_estimate=cost(x.size, x.size * 4),
            name="take",
        )(x, *after)

    def experts(local, parts, after):
        outs = [jax.ShapeDtypeStruct((rows, columns), BF16) for columns in (away, width)]
        outs += [jax.ShapeDtypeStruct((rows, columns), F32) for columns in (away, width)]
        return pl.pallas_call(
            functools.partial(expert_kernel, local, (0,) * len(parts), width, len(after)),
            in_specs=[SMEM] + [VMEM] * len(parts) + [HBM] * 3 + [ANY] * len(after),
            out_specs=(VMEM,) * 4,
            scratch_shapes=[
                pltpu.VMEM((model, hidden), BF16),
                pltpu.VMEM((model, hidden), BF16),
                pltpu.VMEM((hidden, model), BF16),
                pltpu.VMEM((rows, model), BF16),
                pltpu.VMEM((rows, hidden), BF16),
                pltpu.SemaphoreType.DMA((3,)),
            ],
            out_shape=tuple(outs),
            compiler_params=params(20),
            cost_estimate=cost(6 * rows * model * hidden, 12 * MIB, rows * hidden),
            name=f"experts_{local}",
        )(order, *parts, *in_hbm(w_gate, w_up, w_down), *after)

    def spread(local, turned, parts, after):
        return pl.pallas_call(
            functools.partial(spread_kernel, n_time, len(after), turned),
            in_specs=[SMEM] + [VMEM] * len(parts) + [ANY] * len(after),
            out_specs=(VMEM,) * n_time,
            out_shape=blocks_of(n_time),
            compiler_params=params(16),
            cost_estimate=cost(rows * width * 4, rows * width * 10),
            name=f"spread_{local}",
        )(place, *parts, *after)

    def combine(local, back, base):
        last = local == local_experts - 1
        return pl.pallas_call(
            functools.partial(combine_kernel, local),
            out_shape=jax.ShapeDtypeStruct((frames, width), BF16 if last else F32),
            in_specs=[SMEM] + [VMEM] * (3 + len(back)),
            out_specs=VMEM,
            scratch_shapes=[pltpu.VMEM((rows, width), BF16)],
            compiler_params=params(16),
            cost_estimate=cost(4 * frames * width * rows, 3 * MIB),
            name=f"combine_{local}",
        )(place, targets, gates, base, *reversed(back))

    outgoing_0[1] = take(outgoing_0[1], wide[1:])
    arrived_0 = pl.pallas_call(
        join_kernel,
        in_specs=[VMEM] * n_time + [ANY],
        out_specs=VMEM,
        out_shape=jax.ShapeDtypeStruct((rows, width), BF16),
        compiler_params=params(16),
        cost_estimate=cost(rows * width, rows * width * 4),
        name="join",
    )(*exchanged(outgoing_0), outgoing_1)
    arrived_1 = over_time(outgoing_1)
    send_x_0, send_0, keep_x_0, keep_0 = experts(0, gathered(arrived_0), [outgoing_1])
    away_0 = add("0", keep_x_0, core_swap(send_x_0), send_0)
    got_0 = from_chips(away_0)
    swapped_0 = core_swap(send_0)
    arrived_1 = take(arrived_1, [away_0[0]])
    parts = [arrived_1, core_swap(arrived_1)]
    send_x_1, send_1, keep_x_1, keep_1 = experts(1, parts, [away_0[0]])
    away_1 = add("1", keep_x_1, core_swap(send_x_1), got_0[0])
    got_1 = from_chips(away_1)
    total_0 = spread(0, False, [keep_0, swapped_0, *got_0], [away_1[0]])
    back_0 = exchanged(total_0)
    total_1 = spread(1, True, [keep_1, core_swap(send_1), *got_1], back_0[n_time // 2 + 1 :])
    back_1 = exchanged(total_1)
    return combine(1, back_1, combine(0, back_0, state))


def solution(mesh):
    return jax.shard_map(
        per_device,
        mesh=mesh,
        in_specs=(
            P("tm", None),
            P("tm", "mp"),
            P("tm", "mp"),
            P("tm", "mp"),
            P(None, "tm"),
            P("mp", None),
            P("tm", None),
            P("tm", None),
            P("tm", None, "mp"),
            P("tm", None, "mp"),
            P("tm", "mp", None),
        ),
        out_specs=P("tm", "mp"),
        check_vma=False,
    )
```

```python
import functools

import jax
import jax.numpy as jnp
from jax import lax
from jax.experimental import pallas as pl
from jax.experimental.pallas import tpu as pltpu
from jax.sharding import PartitionSpec as P

HEADS = 16
TOP = 2
LEFT = 256
EPS = 1e-06
LANES = 128
MIB = 1 << 20
F32 = jnp.float32
BF16 = jnp.bfloat16

VMEM = pl.BlockSpec(memory_space=pltpu.VMEM)
SMEM = pl.BlockSpec(memory_space=pltpu.SMEM)
ANY = pl.BlockSpec(memory_space=pl.ANY)
HBM = pl.BlockSpec(memory_space=pltpu.HBM)


def params(mib):
    return pltpu.CompilerParams(vmem_limit_bytes=mib * MIB)


def cost(flops, moved, transcendentals=0):
    return pl.CostEstimate(flops=flops, bytes_accessed=moved, transcendentals=transcendentals)


def from_behind(x, axis, by):
    size = lax.axis_size(axis)
    pairs = [(i, i + by) for i in range(size) if 0 <= i + by < size]
    return lax.ppermute(x, axis, pairs)


def core_swap(x):
    size = lax.axis_size("mp")
    return lax.ppermute(x, "mp", [(i, i ^ 1) for i in range(size)])


def from_chip(x, by):
    chips = lax.axis_size("mp") // 2
    pairs = [(c * 2 + k, ((c + by) % chips) * 2 + k) for c in range(chips) for k in range(2)]
    return lax.ppermute(x, "mp", pairs)


def gathered(x):
    chips = lax.axis_size("mp") // 2
    mine = [x] + [from_chip(x, by) for by in range(1, chips)]
    return mine + [core_swap(part) for part in mine]


def exchanged(blocks):
    size = lax.axis_size("tm")
    assert size & (size - 1) == 0, size
    moved = list(blocks)
    for s in range(size - 1, 0, -1):
        moved[s] = lax.ppermute(blocks[s], "tm", [(i, i ^ s) for i in range(size)])
    return moved


def route_kernel(capacity, local_experts, n_time, ids_ref, ranks_ref, targets_ref):
    frames = ids_ref.shape[0]
    lanes = ranks_ref.shape[0]
    ids = ids_ref[...]
    owner = ids // local_experts
    ids = (ids - owner * local_experts) * n_time + owner
    experts = lax.broadcasted_iota(jnp.int32, (frames, lanes), 1)
    hits = [ids[:, k : k + 1] == experts for k in range(TOP)]
    named = functools.reduce(jnp.logical_or, hits)
    ones = jnp.where(named, 1.0, 0.0).astype(BF16)
    row = lax.broadcasted_iota(jnp.int32, (frames, frames), 0)
    column = lax.broadcasted_iota(jnp.int32, (frames, frames), 1)
    before = jnp.where(column < row, 1.0, 0.0).astype(BF16)
    ranks = jnp.dot(before, ones, preferred_element_type=F32)
    ranks_ref[...] = jnp.where(named, ranks, -1.0).T
    places = []
    for k in range(TOP):
        slot = jnp.sum(jnp.where(hits[k], ranks, 0.0), 1, keepdims=True).astype(jnp.int32)
        places.append(ids[:, k : k + 1] * capacity + slot)
    targets_ref[...] = jnp.concatenate(places, 1)


def attend_kernel(scale, head_width, start, meta_ref, order_ref, *refs):
    if start > 0:
        edges_any, q_any, k_any, v_any, proj_any = refs[:5]
        send_ref, keep_x_ref, keep_ref, edges_ref, q_all, k_ref, v_ref, proj_ref, sems = refs[5:]
        moves = [
            (k_any, k_ref),
            (q_any, q_all),
            (v_any, v_ref),
            (edges_any, edges_ref),
            (proj_any, proj_ref),
        ]
    else:
        edges_ref, q_all, k_ref, v_ref, proj_ref, tails_ref = refs[:6]
        send_ref, keep_x_ref, keep_ref = refs[6:]
        moves = []
    rows, columns = keep_ref.shape
    heads = columns // head_width
    block = LANES
    window = LEFT + block
    copies = [pltpu.make_async_copy(a, b, sems.at[i]) for i, (a, b) in enumerate(moves)]
    for copy in copies:
        copy.start()
    for copy in copies[:4]:
        copy.wait()
    edges = edges_ref[:, start : start + rows].astype(F32)
    edges = jnp.concatenate([edges, jnp.zeros((6, rows), F32)], 0).T
    lane_head = lax.broadcasted_iota(jnp.int32, (block, columns), 1) // head_width
    context = []
    for r in range(0, rows, block):
        if start > 0:
            key = k_ref[start - LEFT + r : start + r + block, :]
            value = v_ref[start - LEFT + r : start + r + block, :]
        else:
            key = jnp.concatenate([tails_ref[0, r:LEFT, :], k_ref[0 : r + block, :]], 0)
            value = jnp.concatenate([tails_ref[1, r:LEFT, :], v_ref[0 : r + block, :]], 0)
        query = q_all[start + r : start + r + block, :]
        places = lax.broadcasted_iota(jnp.int32, (block, window), 1)
        places = (places + (meta_ref[0] + (start + r - LEFT))).astype(F32)
        lower = jnp.maximum(edges[r : r + block, 0:1] - LEFT, 0.0)
        upper = edges[r : r + block, 1:2]
        visible = (places >= lower) & (places <= upper)
        own = [jnp.where(lane_head == h, query, jnp.zeros_like(query)) for h in range(heads)]
        own = jnp.concatenate(own, 0)
        scores = lax.dot_general(own, key, (((1,), (1,)), ((), ())), preferred_element_type=F32)
        scores = (scores * scale).reshape(heads, block, window)
        scores = jnp.where(visible[None], scores, -1e30)
        highest = jnp.max(scores, 2, keepdims=True)
        expos = jnp.exp(scores - highest)
        weights = (expos * (1.0 / jnp.sum(expos, 2, keepdims=True))).astype(BF16)
        weights = weights.reshape(heads * block, window)
        product = jnp.dot(weights, value, preferred_element_type=F32)
        mixed = product[0:block]
        for h in range(1, heads):
            mixed = jnp.where(lane_head == h, product[h * block : (h + 1) * block], mixed)
        context.append(mixed.astype(BF16))
    context = jnp.concatenate(context, 0)
    for copy in copies[4:]:
        copy.wait()
    count = proj_ref.shape[1] // columns // 2
    for i in range(2 * count):
        at = pl.multiple_of(order_ref[i] * columns, columns)
        part = jnp.dot(context, proj_ref[:, pl.ds(at, columns)], preferred_element_type=F32)
        j = (i - 1) % count * columns
        if i >= count:
            send_ref[:, j : j + columns] = part.astype(BF16)
        elif i > 0:
            keep_x_ref[:, j : j + columns] = part
        else:
            keep_ref[...] = part


def picked_rows(e, capacity, ranks_ref, state):
    slot = lax.broadcasted_iota(jnp.int32, (capacity, state.shape[0]), 0).astype(F32)
    pick = jnp.where(slot == ranks_ref[pl.ds(e, 1), :], 1.0, 0.0).astype(BF16)
    return jnp.dot(pick, state, preferred_element_type=F32).astype(BF16)


def scatter_rows(local, at_ref, ranks_ref, state, out_refs):
    n_time = len(out_refs)
    for s, out_ref in enumerate(out_refs):
        owner = at_ref[0] ^ s
        out_ref[...] = picked_rows(local * n_time + owner, out_ref.shape[0], ranks_ref, state)


def state_kernel(parts, column, at_ref, *refs):
    frames_ref, ranks_ref, state_ref = refs[2 * parts : 2 * parts + 3]
    width = state_ref.shape[1]
    halves = []
    for keep_ref, swapped_ref, *got in (refs[:parts], refs[parts : 2 * parts]):
        half = keep_ref[...] + swapped_ref[:, column : column + width].astype(F32)
        for ref in got:
            half = half + ref[...].astype(F32)
        halves.append(half)
    attended = jnp.concatenate(halves, 0)
    state = (frames_ref[...].astype(F32) + attended).astype(BF16)
    state_ref[...] = state
    scatter_rows(0, at_ref, ranks_ref, state, refs[2 * parts + 3 :])


def dispatch_kernel(pieces, n_time, *refs):
    state = jnp.concatenate([ref[...] for ref in refs[:pieces]], 1)
    ranks_ref, out_ref = refs[pieces:]
    capacity = out_ref.shape[0] // n_time
    for owner in range(n_time):
        rows = picked_rows(n_time + owner, capacity, ranks_ref, state)
        out_ref[owner * capacity : (owner + 1) * capacity, :] = rows


def join_kernel(*refs):
    *pieces, after_any, out_ref = refs
    count = pieces[0].shape[0]
    for s, ref in enumerate(pieces):
        out_ref[s * count : (s + 1) * count, :] = ref[...]


def take_kernel(rows_ref, *refs):
    refs[-1][...] = rows_ref[...]


def expert_kernel(local, starts, width, awaited, order_ref, *refs):
    arrays = len(starts)
    rows_in = refs[:arrays]
    gate_any, up_any, down_any = refs[arrays : arrays + 3]
    *outs, gate_ref, up_ref, down_ref, normed_ref, active_ref, sems = refs[arrays + 3 + awaited :]
    *send_x_refs, send_ref, keep_x_ref, keep_ref = outs
    rows, model = normed_ref.shape
    hidden = active_ref.shape[1]
    moves = [
        (gate_any.at[local], gate_ref),
        (up_any.at[local], up_ref),
        (down_any.at[local], down_ref),
    ]
    copies = [pltpu.make_async_copy(a, b, sems.at[i]) for i, (a, b) in enumerate(moves)]
    for copy in copies:
        copy.start()

    blocks = []
    for ref, start in zip(rows_in, starts):
        blocks += [(ref, start, c) for c in range(0, ref.shape[1], width)]
    step = min(rows, 256)

    def norm(i, carry):
        at_row = pl.multiple_of(i * step, step)
        parts = [
            ref[pl.ds(pl.multiple_of(start + i * step, step), step), c : c + width].astype(F32)
            for ref, start, c in blocks
        ]
        squares = sum(jnp.sum(part * part, 1, keepdims=True) for part in parts)
        factor = lax.rsqrt(squares * (1.0 / model) + EPS)
        for j, part in enumerate(parts):
            at = pl.multiple_of(order_ref[j] * width, width)
            normed_ref[pl.ds(at_row, step), pl.ds(at, width)] = (part * factor).astype(BF16)
        return carry

    lax.fori_loop(0, rows // step, norm, 0, unroll=True)
    copies[0].wait()
    copies[1].wait()
    tile = min(rows, 1024)
    chunk = min(hidden, 256)
    for r in range(0, rows, tile):
        normed = normed_ref[r : r + tile, :]
        for c in range(0, hidden, chunk):
            gate = jnp.dot(normed, gate_ref[:, c : c + chunk], preferred_element_type=F32)
            up = jnp.dot(normed, up_ref[:, c : c + chunk], preferred_element_type=F32)
            half = 0.5 * gate
            active = (half + half * jnp.tanh(half)) * up
            active_ref[r : r + tile, c : c + chunk] = active.astype(BF16)
    copies[2].wait()
    count = len(blocks) // 2
    def project(i, out_refs, column):
        at = pl.multiple_of(order_ref[i] * width, width)
        weight = down_ref[:, pl.ds(at, width)]
        result = jnp.dot(active_ref[...], weight, preferred_element_type=F32)
        each = rows // len(out_refs)
        for j, out_ref in enumerate(out_refs):
            part = result[j * each : (j + 1) * each]
            out_ref[:, column : column + width] = part.astype(out_ref.dtype)

    for by in range(1, count):
        project(count + by, send_x_refs, (by - 1) * width)
    project(count, [send_ref], 0)
    for by in range(1, count):
        project(by, [keep_x_ref], (by - 1) * width)
    project(0, [keep_ref], 0)


def add_kernel(width, keep_ref, got_ref, after_any, *out_refs):
    for i, out_ref in enumerate(out_refs):
        at = slice(i * width, (i + 1) * width)
        out_ref[...] = (keep_ref[:, at] + got_ref[:, at].astype(F32)).astype(BF16)


def spread_kernel(n_time, awaited, turned, at_ref, keep_ref, *refs):
    got, outs = refs[: -n_time - awaited], refs[-n_time:]
    capacity = outs[0].shape[0]
    for s, out_ref in enumerate(outs):
        place = at_ref[0] ^ s if turned else s
        at = pl.ds(pl.multiple_of(place * capacity, capacity), capacity)
        total = keep_ref[at, :]
        for ref in got:
            total = total + ref[at, :].astype(F32)
        out_ref[...] = total.astype(BF16)


def combine_kernel(local, at_ref, targets_ref, gates_ref, base_ref, *refs):
    *got, out_ref, back_ref = refs
    capacity = got[0].shape[0]
    for s, ref in enumerate(reversed(got)):
        place = at_ref[0] ^ s
        back_ref[pl.ds(pl.multiple_of(place * capacity, capacity), capacity), :] = ref[...]
    back = back_ref[...]
    rows = back.shape[0]
    frames = targets_ref.shape[0]
    places = lax.broadcasted_iota(jnp.int32, (frames, rows), 1) + local * rows
    total = base_ref[...].astype(F32)
    for k in range(TOP):
        pick = jnp.where(places == targets_ref[:, k : k + 1], 1.0, 0.0).astype(BF16)
        total = total + gates_ref[:, k : k + 1] * jnp.dot(pick, back, preferred_element_type=F32)
    out_ref[...] = total.astype(out_ref.dtype)


def per_device(
    frames_in,
    queries,
    keys,
    values,
    segment_edges,
    out_proj,
    expert_ids,
    gates,
    w_gate,
    w_up,
    w_down,
):
    frames, model = frames_in.shape
    width = queries.shape[1]
    n_model = lax.axis_size("mp")
    n_time = lax.axis_size("tm")
    chips = n_model // 2
    head_width = model // HEADS
    scale = head_width ** (-0.5)
    local_experts = w_gate.shape[0]
    hidden = w_gate.shape[2]
    experts_all = local_experts * n_time
    capacity = 4 * frames // experts_all
    rows = n_time * capacity
    lanes = -(-experts_all // LANES) * LANES
    at_time = lax.axis_index("tm")
    at_model = lax.axis_index("mp")
    chip, core = at_model // 2, at_model % 2
    mine = [((chip - by) % chips) * 2 + core for by in range(chips)]
    others = [((chip - by) % chips) * 2 + 1 - core for by in range(chips)]
    order = jnp.stack(mine + others).astype(jnp.int32)
    offset = (at_time * frames).astype(jnp.int32).reshape(1)
    place = at_time.astype(jnp.int32).reshape(1)
    away = (chips - 1) * width

    tails = from_behind(jnp.stack([keys[frames - LEFT :], values[frames - LEFT :]], 0), "tm", 1)
    own_frames = lax.dynamic_slice_in_dim(frames_in, at_model * width, width, 1)

    ranks, targets = pl.pallas_call(
        functools.partial(route_kernel, capacity, local_experts, n_time),
        out_shape=(
            jax.ShapeDtypeStruct((lanes, frames), F32),
            jax.ShapeDtypeStruct((frames, TOP), jnp.int32),
        ),
        in_specs=[VMEM],
        out_specs=(VMEM, VMEM),
        compiler_params=params(16),
        cost_estimate=cost(2 * frames * frames * lanes, frames * 1024),
        name="route",
    )(expert_ids)

    def in_hbm(*arrays):
        return [pltpu.with_memory_space_constraint(x, pltpu.HBM) for x in arrays]

    def attended_outs(count):
        return (
            jax.ShapeDtypeStruct((count, chips * width), BF16),
            jax.ShapeDtypeStruct((count, away), F32),
            jax.ShapeDtypeStruct((count, width), F32),
        )

    def attend_cost(count):
        return cost(count * 384 * width * 16, count * width * 8, count * 384 * 4)

    inputs = (segment_edges, queries, keys, values, out_proj)
    *late, edges_vmem, q_vmem, k_vmem, v_vmem, proj_vmem = pl.pallas_call(
        functools.partial(attend_kernel, scale, head_width, LEFT),
        out_shape=attended_outs(frames - LEFT)
        + tuple(jax.ShapeDtypeStruct(x.shape, x.dtype) for x in inputs),
        in_specs=[SMEM, SMEM] + [HBM] * 5,
        out_specs=(VMEM,) * 8,
        scratch_shapes=[pltpu.SemaphoreType.DMA((5,))],
        compiler_params=params(16),
        cost_estimate=attend_cost(frames - LEFT),
        name="attend_late",
    )(offset, order, *in_hbm(*inputs))
    early = pl.pallas_call(
        functools.partial(attend_kernel, scale, head_width, 0),
        out_shape=attended_outs(LEFT),
        in_specs=[SMEM, SMEM] + [VMEM] * 6,
        out_specs=(VMEM,) * 3,
        compiler_params=params(16),
        cost_estimate=attend_cost(LEFT),
        name="attend_early",
    )(offset, order, edges_vmem, q_vmem, k_vmem, v_vmem, proj_vmem, tails)

    def add(name, keep, got, after):
        return pl.pallas_call(
            functools.partial(add_kernel, width),
            in_specs=[VMEM, VMEM, ANY],
            out_specs=(VMEM,) * (chips - 1),
            out_shape=(jax.ShapeDtypeStruct((keep.shape[0], width), BF16),) * (chips - 1),
            compiler_params=params(16),
            cost_estimate=cost(keep.size, keep.size * 8),
            name=f"add_{name}",
        )(keep, got, after)

    def from_chips(parts):
        return [from_chip(part, chips - by) for by, part in enumerate(parts, 1)]

    def attended(name, send, keep_x, keep):
        swapped = core_swap(send)
        return [keep, swapped, *from_chips(add(name, keep_x, swapped, swapped))]

    late = attended("late", *late)
    early = attended("early", *early)

    def blocks_of(count):
        return (jax.ShapeDtypeStruct((capacity, width), BF16),) * count

    state, *outgoing_0 = pl.pallas_call(
        functools.partial(state_kernel, len(early), away),
        out_shape=(jax.ShapeDtypeStruct((frames, width), BF16),) + blocks_of(n_time),
        in_specs=[SMEM] + [VMEM] * (2 * len(early) + 2),
        out_specs=(VMEM,) * (1 + n_time),
        compiler_params=params(16),
        cost_estimate=cost(2 * frames * width * rows, 4 * MIB),
        name="state",
    )(place, *early, *late, own_frames, ranks)
    wide = [state] + [from_chip(state, by) for by in range(1, chips)]
    outgoing_1 = pl.pallas_call(
        functools.partial(dispatch_kernel, chips, n_time),
        out_shape=jax.ShapeDtypeStruct((rows, chips * width), BF16),
        in_specs=[VMEM] * (chips + 1),
        out_specs=VMEM,
        compiler_params=params(16),
        cost_estimate=cost(4 * frames * width * rows, 3 * MIB),
        name="dispatch",
    )(*wide, ranks)

    def over_time(x):
        columns = x.shape[1]
        x = x.reshape(n_time, capacity, columns)
        x = lax.all_to_all(x, "tm", split_axis=0, concat_axis=0, tiled=True)
        return x.reshape(rows, columns)

    def take(x, after):
        return pl.pallas_call(
            take_kernel,
            in_specs=[VMEM] + [ANY] * len(after),
            out_specs=VMEM,
            out_shape=jax.ShapeDtypeStruct(x.shape, x.dtype),
            compiler_params=params(16),
            cost_estimate=cost(x.size, x.size * 4),
            name="take",
        )(x, *after)

    def experts(local, parts, after):
        outs = [jax.ShapeDtypeStruct((rows, columns), BF16) for columns in (away, width)]
        outs += [jax.ShapeDtypeStruct((rows, columns), F32) for columns in (away, width)]
        return pl.pallas_call(
            functools.partial(expert_kernel, local, (0,) * len(parts), width, len(after)),
            in_specs=[SMEM] + [VMEM] * len(parts) + [HBM] * 3 + [ANY] * len(after),
            out_specs=(VMEM,) * 4,
            scratch_shapes=[
                pltpu.VMEM((model, hidden), BF16),
                pltpu.VMEM((model, hidden), BF16),
                pltpu.VMEM((hidden, model), BF16),
                pltpu.VMEM((rows, model), BF16),
                pltpu.VMEM((rows, hidden), BF16),
                pltpu.SemaphoreType.DMA((3,)),
            ],
            out_shape=tuple(outs),
            compiler_params=params(20),
            cost_estimate=cost(6 * rows * model * hidden, 12 * MIB, rows * hidden),
            name=f"experts_{local}",
        )(order, *parts, *in_hbm(w_gate, w_up, w_down), *after)

    def spread(local, turned, parts, after):
        return pl.pallas_call(
            functools.partial(spread_kernel, n_time, len(after), turned),
            in_specs=[SMEM] + [VMEM] * len(parts) + [ANY] * len(after),
            out_specs=(VMEM,) * n_time,
            out_shape=blocks_of(n_time),
            compiler_params=params(16),
            cost_estimate=cost(rows * width * 4, rows * width * 10),
            name=f"spread_{local}",
        )(place, *parts, *after)

    def combine(local, back, base):
        last = local == local_experts - 1
        return pl.pallas_call(
            functools.partial(combine_kernel, local),
            out_shape=jax.ShapeDtypeStruct((frames, width), BF16 if last else F32),
            in_specs=[SMEM] + [VMEM] * (3 + len(back)),
            out_specs=VMEM,
            scratch_shapes=[pltpu.VMEM((rows, width), BF16)],
            compiler_params=params(16),
            cost_estimate=cost(4 * frames * width * rows, 3 * MIB),
            name=f"combine_{local}",
        )(place, targets, gates, base, *reversed(back))

    outgoing_0[1] = take(outgoing_0[1], wide[1:])
    arrived_0 = pl.pallas_call(
        join_kernel,
        in_specs=[VMEM] * n_time + [ANY],
        out_specs=VMEM,
        out_shape=jax.ShapeDtypeStruct((rows, width), BF16),
        compiler_params=params(16),
        cost_estimate=cost(rows * width, rows * width * 4),
        name="join",
    )(*exchanged(outgoing_0), outgoing_1)
    arrived_1 = over_time(outgoing_1)
    send_x_0, send_0, keep_x_0, keep_0 = experts(0, gathered(arrived_0), [outgoing_1])
    away_0 = add("0", keep_x_0, core_swap(send_x_0), send_0)
    got_0 = from_chips(away_0)
    swapped_0 = core_swap(send_0)
    arrived_1 = take(arrived_1, [away_0[0]])
    parts = [arrived_1, core_swap(arrived_1)]
    send_x_1, send_1, keep_x_1, keep_1 = experts(1, parts, [away_0[0]])
    away_1 = add("1", keep_x_1, core_swap(send_x_1), got_0[0])
    got_1 = from_chips(away_1)
    total_0 = spread(0, False, [keep_0, swapped_0, *got_0], [away_1[0]])
    back_0 = exchanged(total_0)
    total_1 = spread(1, True, [keep_1, core_swap(send_1), *got_1], back_0[n_time // 2 + 1 :])
    back_1 = exchanged(total_1)
    return combine(1, back_1, combine(0, back_0, state))


def solution(mesh):
    return jax.shard_map(
        per_device,
        mesh=mesh,
        in_specs=(
            P("tm", None),
            P("tm", "mp"),
            P("tm", "mp"),
            P("tm", "mp"),
            P(None, "tm"),
            P("mp", None),
            P("tm", None),
            P("tm", None),
            P("tm", None, "mp"),
            P("tm", None, "mp"),
            P("tm", "mp", None),
        ),
        out_specs=P("tm", "mp"),
        check_vma=False,
    )
```
